32 devices in a mesh: dp: 16 (over z, y, x), mp: 2 (over core).
Axes of the slice: x: 2, y: 2, z: 4, core: 2. Of those that a mesh axis runs over, the one named last changes fastest.
Arguments:
- tokens: bfloat16 [2, 16, 1024, 768], P(None, 'dp', 'mp'), may hold values from -6 to 6
- segment: int32 [2, 16, 1024], P(None, 'dp'), may hold values from 0 to 7, never falling along the last dimension, each value on 1 to 768 neighbouring positions
- ln1_gain: float32 [768], replicated, may hold values from 0.25 to 1.75
- ln1_bias: float32 [768], replicated, may hold values from -3 to 3
- w_qkv: bfloat16 [768, 3, 768], P('dp', None, 'mp'), may hold values from -0.21875 to 0.21875
- w_out: bfloat16 [768, 768], P('mp', 'dp'), may hold values from -1.25 to 1.25
- ln2_gain: float32 [768], replicated, may hold values from 0.25 to 1.75
- ln2_bias: float32 [768], replicated, may hold values from -3 to 3
- w_up: bfloat16 [768, 3072], P('dp', 'mp'), may hold values from -0.21875 to 0.21875
- w_down: bfloat16 [3072, 768], P('mp', 'dp'), may hold values from -0.109375 to 0.109375
- cotangent: bfloat16 [2, 16, 1024, 768], P(None, 'dp', 'mp'), may hold values from -6 to 6
Outputs:
- mixed: bfloat16 [2, 16, 1024, 768], P(None, 'dp', 'mp')
- grad_tokens: float32 [2, 16, 1024, 768], P(None, 'dp', 'mp')
- grad_ln1_gain: float32 [768], replicated
- grad_ln1_bias: float32 [768], replicated
- grad_w_qkv: float32 [768, 3, 768], P('dp', None, 'mp')
- grad_w_out: float32 [768, 768], P('mp', 'dp')
- grad_ln2_gain: float32 [768], replicated
- grad_ln2_bias: float32 [768], replicated
- grad_w_up: float32 [768, 3072], P('dp', 'mp')
- grad_w_down: float32 [3072, 768], P('mp', 'dp')
The draws below stay inside these ranges and needn't reach their ends.
Inputs may be any that keep to these rules, and one draw needn't show every extreme that they name: `segment`: episode numbers never fall along a sequence; an episode has 1 to 768 positions, and one episode of each sequence has exactly 768.
All inputs are finite; a program needn't handle non-finite values.
Results may differ from the reference program's by a relative error of at most 0.014.
Values may be sent and summed in bfloat16 or wider, within the bound.
No kernel may reach another device: no remote copies, remote signals or barrier semaphores. Data moves between devices by JAX's collectives and lax.ppermute only.
A program may use at most 384 MiB of HBM per device.

```python
import math
import jax
import jax.numpy as jnp
import numpy as np
from jax import lax

D = 768
HEADS = 24
HD = 32
FF = 3072
LEN = 1024
MICRO = 2
SEGS = 8
QBLOCK = 512
SEQS = 16


def block_levels(own_key, shape, shards, low, high):
    def one(dim, blocks):
        draws = jax.random.uniform(jax.random.fold_in(jax.random.fold_in(own_key, 6), dim), (blocks,), jnp.float32, low / len(shards), high / len(shards))
        return jnp.repeat(jnp.exp(draws), shape[dim] // blocks).reshape((-1,) + (1,) * (len(shape) - dim - 1))

    factor_of = one(*shards[0])
    for cut in shards[1:]:
        factor_of = factor_of * one(*cut)
    return factor_of


def split_up(number_of, total, most, skew):
    portions = [(1 << 20) // math.isqrt(rank ** skew) + 1 for rank in range(2, number_of + 1)]
    surplus, counts = total - most - (number_of - 1), [1] * (number_of - 1)
    while surplus > 0:
        candidates = [i for i in range(number_of - 1) if counts[i] < most]
        pool, left = sum([portions[i] for i in candidates]), surplus
        for i in candidates:
            extra = min(most - counts[i], max(1, left * portions[i] // pool), surplus)
            counts[i] = counts[i] + extra
            surplus = surplus - extra
    return np.array([most] + counts)


def uneven_parts(rng, amount, total, limit, slope):
    if amount == 2:
        one = jax.random.randint(rng, (), max(1, total - limit), min(limit, total - 1) + 1)
        return jnp.stack([one, total - one])
    tallies = jnp.asarray(split_up(amount, total, limit, slope), jnp.int32)
    pairs = (amount - 1) // 2
    giver, taker = tallies[1:1 + 2 * pairs:2], tallies[2:2 + 2 * pairs:2]
    room = jnp.minimum(giver - 1, limit - taker)
    shifted = jax.random.randint(jax.random.fold_in(rng, 1), (pairs,), 0, 1 << 20) % (room + 1)
    tallies = tallies.at[1:1 + 2 * pairs:2].set(giver - shifted).at[2:2 + 2 * pairs:2].set(taker + shifted)
    return tallies[jax.random.permutation(jax.random.fold_in(rng, 2), amount)]


def centred(own_key, dims, width, most, shards=(), kind=jnp.bfloat16):
    factor_of = block_levels(own_key, dims, shards, -0.22, 0.18) if shards else 1.0
    values = jax.random.normal(own_key, dims, jnp.float32) * width * factor_of
    return jnp.minimum(jnp.maximum(values, -most), most).astype(kind)


def setup_inputs(seed: int = 0) -> dict:
    streams_of = jax.random.split(jax.random.key(seed), 12)
    tokens = centred(streams_of[0], (MICRO, SEQS, LEN, D), 1.0, 6.0, ((1, 16), (2, 2)))
    segment = jax.vmap(lambda own: jnp.searchsorted(jnp.cumsum(uneven_parts(own, SEGS, LEN, LEN * 3 // 4, 2)), jnp.arange(LEN), side="right"))(jax.random.split(streams_of[1], MICRO * SEQS)).reshape((MICRO, SEQS, LEN)).astype(jnp.int32)
    ln1_gain = jnp.clip(1.0 + 0.15 * jax.random.normal(streams_of[2], (D,), jnp.float32), 0.25, 1.75)
    ln1_bias = centred(streams_of[3], (D,), 0.5, 3.0, (), jnp.float32)
    w_qkv = centred(streams_of[4], (D, 3, D), D ** -0.5, 0.21875, ((0, 16), (2, 2)))
    w_out = centred(streams_of[5], (D, D), (D // 32) ** -0.5, 1.25, ((0, 2), (1, 16)))
    ln2_gain = jnp.clip(1.0 + 0.15 * jax.random.normal(streams_of[6], (D,), jnp.float32), 0.25, 1.75)
    ln2_bias = centred(streams_of[7], (D,), 0.5, 3.0, (), jnp.float32)
    w_up = centred(streams_of[8], (D, FF), D ** -0.5, 0.21875, ((0, 16), (1, 2)))
    w_down = centred(streams_of[9], (FF, D), FF ** -0.5, 0.109375, ((0, 2), (1, 16)))
    cotangent = centred(streams_of[10], (MICRO, SEQS, LEN, D), 1.0, 6.0, ((1, 16), (2, 2)))
    return dict(tokens=tokens, segment=segment, ln1_gain=ln1_gain, ln1_bias=ln1_bias, w_qkv=w_qkv, w_out=w_out, ln2_gain=ln2_gain, ln2_bias=ln2_bias, w_up=w_up, w_down=w_down, cotangent=cotangent)


precise = lax.Precision.HIGHEST

@jax.custom_vjp
def low(v):
    return lax.optimization_barrier(v.astype(jnp.bfloat16)).astype(jnp.float32)

@jax.custom_vjp
def low_back(v):
    return v

def low_keep(v):
    return (low(v), None)

def low_pass(kept, grad):
    return (grad,)

def back_keep(v):
    return (v, None)

def back_low(kept, grad):
    return (low(grad),)
low.defvjp(low_keep, low_pass)
low_back.defvjp(back_keep, back_low)

def layer_norm(values, gain_vec, offset):
    centered = values - lax.optimization_barrier(jnp.mean(values, axis=-1, keepdims=True))
    spread = lax.optimization_barrier(jnp.mean(centered * centered, axis=-1, keepdims=True))
    return centered * lax.rsqrt(spread + 1e-05) * gain_vec + offset

def forward(inputs, ln1_gain, ln1_bias, w_qkv, w_out, ln2_gain, ln2_bias, w_up, w_down, segment):
    groups = inputs.shape[0]
    length = inputs.shape[1]
    score_scale = 1.0 / math.sqrt(HD)
    normed = low(layer_norm(inputs, ln1_gain, ln1_bias))
    projected = low(low_back(jnp.einsum('gld,dce->glce', normed, w_qkv, precision=precise)))
    query_heads = projected[:, :, 0].reshape(groups, length, HEADS, HD)
    key_heads = projected[:, :, 1].reshape(groups, length, HEADS, HD)
    value_heads = projected[:, :, 2].reshape(groups, length, HEADS, HD)
    places = jnp.arange(length, dtype=jnp.int32)

    def attend(block_index):
        first_row = (block_index * QBLOCK).astype(jnp.int32)
        query_block = lax.dynamic_slice_in_dim(query_heads, first_row, QBLOCK, 1)
        query_seg = lax.dynamic_slice_in_dim(segment, first_row, QBLOCK, 1)
        query_pos = first_row + jnp.arange(QBLOCK, dtype=jnp.int32)
        scores = low_back(jnp.einsum('gqhe,gkhe->ghqk', query_block, key_heads, precision=precise) * score_scale)
        allowed = (query_pos[:, None] >= places[None, :])[None] & (query_seg[:, :, None] == segment[:, None, :])
        scores = jnp.where(allowed[:, None], scores, -1e+30)
        row_peak = lax.optimization_barrier(jnp.max(scores, axis=-1, keepdims=True))
        exponent = jnp.exp(scores - row_peak)
        probabilities = exponent / lax.optimization_barrier(jnp.sum(exponent, axis=-1, keepdims=True))
        return jnp.einsum('ghqk,gkhe->gqhe', low(probabilities), value_heads, precision=precise)
    blocks = lax.map(jax.checkpoint(attend), jnp.arange(length // QBLOCK, dtype=jnp.int32))
    attention_output = jnp.moveaxis(blocks, 0, 1).reshape(groups, length, HEADS * HD)
    attention_output = low(low_back(attention_output))
    branch = low_back(jnp.einsum('gle,ed->gld', attention_output, w_out, precision=precise))
    middle = inputs + branch
    normed_ffn = low(layer_norm(middle, ln2_gain, ln2_bias))
    hidden = low_back(jnp.einsum('gld,df->glf', normed_ffn, w_up, precision=precise))
    gelu_output = low(jax.nn.gelu(hidden, approximate=False))
    ffn_out = low_back(jnp.einsum('glf,fd->gld', gelu_output, w_down, precision=precise))
    return middle + ffn_out

def reference(tokens, segment, ln1_gain, ln1_bias, w_qkv, w_out, ln2_gain, ln2_bias, w_up, w_down, cotangent):
    weights = tuple((array_item.astype(jnp.float32) for array_item in (ln1_gain, ln1_bias, w_qkv, w_out, ln2_gain, ln2_bias, w_up, w_down)))
    seq_total = MICRO * SEQS
    group_size = math.gcd(seq_total, max(1, 4096 // LEN))
    grouped_tokens = tokens.astype(jnp.float32).reshape(seq_total // group_size, group_size, LEN, D)
    grouped_segments = segment.astype(jnp.int32).reshape(seq_total // group_size, group_size, LEN)
    grouped_cotangent = cotangent.astype(jnp.float32).reshape(seq_total // group_size, group_size, LEN, D)

    def scan_step(totals, pieces):
        inputs, seg_piece, cot_piece = pieces
        output, pullback = jax.vjp(lambda values, *params: forward(values, *params, seg_piece), inputs, *weights)
        gradients = pullback(cot_piece)
        updated = tuple((held + fresh for held, fresh in zip(totals, gradients[1:])))
        return (updated, (output.astype(jnp.bfloat16), gradients[0]))
    initial = tuple((jnp.zeros_like(array_item) for array_item in weights))
    totals, (outputs, input_grads) = lax.scan(scan_step, initial, (grouped_tokens, grouped_segments, grouped_cotangent))
    return (outputs.reshape(tokens.shape), input_grads.reshape(tokens.shape), totals[0], totals[1], totals[2], totals[3], totals[4], totals[5], totals[6], totals[7])
```

```python
import functools
import math

import jax
import jax.numpy as jnp
from jax import lax
from jax.experimental import pallas as pl
from jax.experimental.pallas import tpu as pltpu
from jax.sharding import PartitionSpec as P

HD = 32
QB = 256
EPS = 1e-05
BF = jnp.bfloat16
F32 = jnp.float32
NEG = -1e30
SCALE = 1.0 / math.sqrt(HD)
LOG2E = math.log2(math.e)
C2 = SCALE * LOG2E
MIB = 1024 * 1024
SDS = jax.ShapeDtypeStruct


def nn(a, b):
    return lax.dot_general(a, b, (((1,), (0,)), ((), ())), preferred_element_type=F32)


def nt(a, b):
    return lax.dot_general(a, b, (((1,), (1,)), ((), ())), preferred_element_type=F32)


def params(mib):
    return pltpu.CompilerParams(vmem_limit_bytes=mib * MIB)


def in_hbm(values):
    return [pltpu.with_memory_space_constraint(v, pltpu.HBM) for v in values]


def in_vmem(values):
    return [pltpu.with_memory_space_constraint(v, pltpu.VMEM) for v in values]


def cost(gflop, mbytes):
    return pl.CostEstimate(flops=int(gflop * 1e9), bytes_accessed=int(mbytes * 1e6), transcendentals=0)


def any_spec():
    return pl.BlockSpec(memory_space=pl.ANY)


def smem_spec():
    return pl.BlockSpec(memory_space=pltpu.SMEM)


def vmem_spec():
    return pl.BlockSpec(memory_space=pltpu.VMEM)


def row_spec(width):
    return pl.BlockSpec((QB, width), lambda r: (r, 0))


def column_spec(height):
    return pl.BlockSpec((height, QB), lambda r: (0, r))


def whole_spec(shape):
    return pl.BlockSpec(shape, lambda r: tuple(0 for _ in shape))


MASKS = (0, 1, 2, 3)


class Rows:
    def __init__(self, dp_count, depth):
        self.dp_count = dp_count
        self.depth = depth
        self.split = (depth // dp_count) % 16 == 0 and dp_count == 16
        self.near = 4 if self.split else 1
        self.far = dp_count // 4 if self.split else 1
        self.block = depth // (self.near * self.far)
        self.shape = (self.far, self.near, self.block)


class Piece:
    def __init__(self, rows, kind, start=0, width=0, masks=MASKS):
        self.rows = rows
        self.masks = masks
        self.kind = kind if rows.split else "whole"
        self.start = start
        self.count = 2 * len(MASKS) if self.kind == "slabs" else 2
        if self.kind == "stack":
            self.shape = (len(MASKS), rows.far, rows.block, width)
        else:
            self.shape = rows.shape + (width,)


def piece_copies(piece, me, refs, moves, sem, outward):
    copies = []
    each = piece.count // 2
    for half, column, width, view in moves:
        cols = pl.ds(piece.start + column, width)
        if piece.kind == "whole":
            pairs = [(refs[half].at[:, :, :, cols], view)]
        else:
            pairs = []
            for k, mask in enumerate(piece.masks):
                ref = refs[half].at[k] if piece.kind == "stack" else refs[half * each + k]
                near = lax.bitwise_xor(lax.rem(me, 4), mask)
                pairs.append((ref.at[:, :, cols], view.at[:, near]))
        for outside, inside in pairs:
            if outward:
                copies.append(pltpu.make_async_copy(inside, outside, sem))
            else:
                copies.append(pltpu.make_async_copy(outside, inside, sem))
    return copies


def start_all(copies):
    for copy in copies:
        copy.start()


def wait_bytes(ref, sem):
    pltpu.make_async_copy(ref, ref, sem).wait()


def flat(value):
    return value.reshape(-1, value.shape[-1])


def head_row(h):
    return lax.broadcasted_iota(jnp.int32, (1, 128), 1) // HD == h


def fill_bias(bias, seg_col, seg_row):
    key = lax.broadcasted_iota(jnp.int32, (QB, QB), 0)
    query = lax.broadcasted_iota(jnp.int32, (QB, QB), 1)
    bias[0] = jnp.where(query >= key, 0.0, NEG)
    bias[1] = jnp.where((query >= key) & (seg_col[...] == seg_row[...]), 0.0, NEG)


def fill_double(double, halves):
    here = halves[0].shape[0]
    for k in range(4):
        double[k * here : (k + 1) * here, :] = halves[k % 2][...]


def turned(doubles, start, r):
    coarse = pl.multiple_of(start // 16 * 16 + r * QB, 16)
    fine = start % 16
    row = lax.broadcasted_iota(jnp.int32, (QB, QB + 16), 0)
    col = lax.broadcasted_iota(jnp.int32, (QB, QB + 16), 1)
    pick = jnp.where(col - row == fine, 1.0, 0.0).astype(BF)
    total = None
    for double in doubles:
        part = nn(pick, double[pl.ds(coarse, QB + 16), :])
        total = part if total is None else total + part
    return total


def norm_parts(values):
    centered = values - jnp.mean(values, axis=-1, keepdims=True)
    spread = jnp.mean(centered * centered, axis=-1, keepdims=True)
    root = lax.rsqrt(spread + EPS)
    return centered * root, root


def prepare_body(
    start,
    own,
    other,
    cot_own,
    cot_other,
    gain,
    offset,
    x_out,
    normed,
    normed_t_out,
    cot,
    cot_t,
    double,
    x,
    normed_t,
    sems,
):
    fill_double(double, [own, other])

    def step(r, carry):
        at = pl.ds(pl.multiple_of(r * QB, QB), QB)
        value = turned([double], start[0], r)
        x[at, :] = value.astype(BF)
        hat, _ = norm_parts(value)
        low = (hat * gain[...] + offset[...]).astype(BF)
        normed[at, :] = low
        normed_t[:, at] = low.T
        return carry

    count = x.shape[0] // QB
    lax.fori_loop(0, count, step, 0)
    copies = [
        pltpu.make_async_copy(x, x_out, sems.at[0]),
        pltpu.make_async_copy(normed_t, normed_t_out, sems.at[1]),
    ]
    start_all(copies)
    fill_double(double, [cot_own, cot_other])

    def second(r, carry):
        at = pl.ds(pl.multiple_of(r * QB, QB), QB)
        low = turned([double], start[0], r).astype(BF)
        cot[at, :] = low
        cot_t[:, at] = low.T
        return carry

    lax.fori_loop(0, count, second, 0)
    for copy in copies:
        copy.wait()


def prepare(start, own, other, cot_own, cot_other, gain, offset):
    here, depth = own.shape
    shape, shape_t = (2 * here, depth), (depth, 2 * here)
    return pl.pallas_call(
        prepare_body,
        in_specs=[smem_spec()] + [vmem_spec()] * 6,
        out_specs=[any_spec(), vmem_spec(), any_spec(), vmem_spec(), vmem_spec()],
        out_shape=[
            pltpu.HBM(shape, BF),
            pltpu.VMEM(shape, BF),
            pltpu.HBM(shape_t, BF),
            pltpu.VMEM(shape, BF),
            pltpu.VMEM(shape_t, BF),
        ],
        scratch_shapes=[
            pltpu.VMEM((4 * here, depth), BF),
            pltpu.VMEM(shape, BF),
            pltpu.VMEM(shape_t, BF),
            pltpu.SemaphoreType.DMA((2,)),
        ],
        compiler_params=params(20),
        cost_estimate=cost(4, 8),
        name="prepare",
    )(start, own, other, cot_own, cot_other, gain, offset)


def turn_back_body(start, values, own, other, double):
    here = own.shape[0]
    double[: 2 * here, :] = values[...]
    double[2 * here :, :] = values[...]
    count = here // QB

    def step(r, carry):
        at = pl.ds(pl.multiple_of(r * QB, QB), QB)
        own[at, :] = turned([double], start[0], r).astype(BF)
        other[at, :] = turned([double], start[0], r + count).astype(BF)
        return carry

    lax.fori_loop(0, count, step, 0)


def turn_back(start, values):
    length, depth = values.shape
    return pl.pallas_call(
        turn_back_body,
        in_specs=[smem_spec(), vmem_spec()],
        out_specs=[vmem_spec()] * 2,
        out_shape=[SDS((length // 2, depth), BF)] * 2,
        scratch_shapes=[pltpu.VMEM((2 * length, depth), BF)],
        compiler_params=params(16),
        cost_estimate=cost(2, 4),
        name="turn_back",
    )(start, values)


def arrange_body(widths, me, *refs):
    pieces, outs = refs[:4], refs[4:]
    far = me[0] // 4
    for m, piece in enumerate(pieces):
        begin = 0
        for out, width in zip(outs, widths):
            out[lax.bitwise_xor(far, m)] = piece[:, begin : begin + width]
            begin += width


def arrange(rows, me, pieces, widths):
    return pl.pallas_call(
        functools.partial(arrange_body, widths),
        in_specs=[smem_spec()] + [vmem_spec()] * 4,
        out_specs=[vmem_spec()] * len(widths),
        out_shape=[SDS((rows.far, rows.block, w), BF) for w in widths],
        compiler_params=params(8),
        cost_estimate=cost(1, 1),
        name="arrange",
    )(me, *pieces)


def project_attend_body(piece, me, normed, seg_col, seg_row, *refs):
    slabs = refs[: piece.count]
    proj_out, att, lse, weight, proj, bias, keys_m, values_t, att_t, sem, out_sem = refs[piece.count :]
    moves = [(half, 0, 384, weight.at[:, :, :, pl.ds(384 * half, 384)]) for half in range(2)]
    start_all(piece_copies(piece, me[0], slabs, moves, sem, False))
    fill_bias(bias, seg_col, seg_row)
    values_t[...] = jnp.ones_like(values_t)
    wait_bytes(weight, sem)
    length = normed.shape[0]

    def project(r, carry):
        at = pl.ds(pl.multiple_of(r * 512, 512), 512)
        proj[at, :] = nn(normed[at, :], flat(weight[...])).astype(BF)
        return carry

    lax.fori_loop(0, length // 512, project, 0)
    proj_copy = pltpu.make_async_copy(proj, proj_out, out_sem)
    proj_copy.start()
    for half in range(2):
        flipped = proj[:, half * 384 + 256 : half * 384 + 384].T
        for h in range(4):
            values_t[half * 4 + h, 0:HD, :] = flipped[h * HD : (h + 1) * HD]

    units = [(h, i) for i in (2, 1, 0, 3) for h in range(4)]

    def step(half, carry):
        col = pl.multiple_of(half * 384, 128)
        for h in range(4):
            keys_m[h] = jnp.where(head_row(h), proj[:, pl.ds(col + 128, 128)], 0)

        def score(h, i):
            first = 768 if i == 3 else 0
            scores = nt(keys_m[h, first : (i + 1) * QB, :], proj[i * QB : (i + 1) * QB, pl.ds(col, 128)])
            edge = scores[-QB:] + bias[1 if i == 3 else 0]
            return jnp.concatenate([scores[:-QB], edge], 0) if scores.shape[0] > QB else edge

        ahead = score(*units[0])
        for k, (h, i) in enumerate(units):
            scores = ahead
            if k + 1 < len(units):
                ahead = score(*units[k + 1])
            first = 768 if i == 3 else 0
            last = (i + 1) * QB
            at = slice(i * QB, last)
            peak = jnp.max(scores, axis=0, keepdims=True) * C2
            probs = jnp.exp2(scores * C2 - peak).astype(BF)
            summed = nn(values_t[half * 4 + h, :, first:last], probs)
            total = summed[HD : HD + 1]
            att_t[pl.ds(pl.multiple_of(half * 128 + h * HD, HD), HD), at] = summed[:HD] / total
            lse[pl.ds(half * 4 + h, 1), at] = peak + jnp.log2(total)
        return carry

    lax.fori_loop(0, 2, step, 0)
    for half in range(2):
        cols = slice(half * 128, half * 128 + 128)
        att[:, cols] = att_t[cols, :].T.astype(BF)
    proj_copy.wait()


def project_attend(piece, me, normed, seg_col, seg_row, slabs):
    length, depth = normed.shape
    rows = piece.rows
    return pl.pallas_call(
        functools.partial(project_attend_body, piece),
        in_specs=[smem_spec()] + [vmem_spec()] * 3 + [any_spec()] * len(slabs),
        out_specs=[any_spec()] + [vmem_spec()] * 2,
        out_shape=[
            pltpu.HBM((length, 768), BF),
            pltpu.HBM((length, 256), BF),
            pltpu.HBM((8, length), F32),
        ],
        scratch_shapes=[
            pltpu.VMEM(rows.shape + (768,), BF),
            pltpu.VMEM((length, 768), BF),
            pltpu.VMEM((2, QB, QB), F32),
            pltpu.VMEM((4, length, 128), BF),
            pltpu.VMEM((8, HD + 16, length), BF),
            pltpu.VMEM((256, length), F32),
            pltpu.SemaphoreType.DMA,
            pltpu.SemaphoreType.DMA,
        ],
        compiler_params=params(20),
        cost_estimate=cost(8, 8),
        name="project_attend",
    )(me, *in_vmem([normed]), seg_col, seg_row, *in_hbm(slabs))


def join_heads(attended):
    return jnp.concatenate([a[:, :128] for a in attended] + [a[:, 128:] for a in attended], 1)


def out_norm_body(piece, groups, me, tokens, gain, offset, *refs):
    attended = refs[:groups]
    slabs = refs[groups : groups + piece.count]
    middle, normed, normed_t, weight, sem = refs[groups + piece.count :]
    width = weight.shape[3] // 2

    @pl.when(pl.program_id(0) == 0)
    def _():
        moves = [(half, 0, width, weight.at[:, :, :, pl.ds(width * half, width)]) for half in range(2)]
        start_all(piece_copies(piece, me[0], slabs, moves, sem, False))
        wait_bytes(weight, sem)

    value = tokens[...].astype(F32) + nt(join_heads([a[...] for a in attended]), flat(weight[...]))
    middle[...] = value
    hat, _ = norm_parts(value)
    low = (hat * gain[...] + offset[...]).astype(BF)
    normed[...] = low
    normed_t[...] = low.T


def out_norm(piece, me, tokens, gain, offset, attended, slabs):
    length, depth = tokens.shape
    return pl.pallas_call(
        functools.partial(out_norm_body, piece, len(attended)),
        grid=(length // QB,),
        in_specs=[smem_spec(), row_spec(depth), whole_spec((1, depth)), whole_spec((1, depth))]
        + [row_spec(256)] * len(attended)
        + [any_spec()] * len(slabs),
        out_specs=[row_spec(depth)] * 2 + [column_spec(depth)],
        out_shape=[
            pltpu.HBM((length, depth), F32),
            pltpu.VMEM((length, depth), BF),
            pltpu.VMEM((depth, length), BF),
        ],
        scratch_shapes=[pltpu.VMEM(piece.rows.shape + (depth,), BF), pltpu.SemaphoreType.DMA],
        compiler_params=params(16),
        cost_estimate=cost(3, 8),
        name="out_norm",
    )(me, *in_hbm([tokens]), gain, offset, *in_hbm(attended), *in_hbm(slabs))


def gelu_parts(values):
    size = jnp.abs(values)
    density = jnp.exp2(values * values * (-0.5 * LOG2E) + math.log2(1.0 / math.sqrt(2 * math.pi)))
    t = 1.0 / (1.0 + 0.2316419 * size)
    poly = t * (
        0.319381530
        + t * (-0.356563782 + t * (1.781477937 + t * (-1.821255978 + t * 1.330274429)))
    )
    tail = density * poly
    below = jnp.where(values >= 0, 1.0 - tail, tail)
    return values * below, below + values * density


def feed_forward_body(piece, out_piece, first, final, aliased, me, normed, normed_t, cot, cot_t, *refs):
    refs = list(refs)
    held = [] if first else [refs.pop(0), refs.pop(0)]
    middle = refs.pop(0) if final else None
    slabs, refs = refs[: piece.count], refs[piece.count + aliased :]
    mixed, grad_in = refs[:2]
    outs, refs = refs[2:4], refs[4:]
    weight, staged, act, grad_hidden, mixed_acc, grad_acc, sems = refs[:7]
    mixed_low, middle_here = refs[7:] if final else (None, None)
    length, depth = normed.shape
    moves = []
    for half in range(2):
        for which in range(2):
            at = pl.ds(which * 768 + half * 384, 384)
            moves.append((half, which * 384, 384, at))
    into = [(h, c, w, weight.at[:, :, :, at]) for h, c, w, at in moves]
    outof = [(h, c, w, staged.at[:, :, :, at]) for h, c, w, at in moves]
    start_all(piece_copies(piece, me[0], slabs, into, sems.at[0], False))
    held_copies = []
    if not first:
        held_copies.append(pltpu.make_async_copy(held[0], mixed_acc, sems.at[1]))
        held_copies.append(pltpu.make_async_copy(held[1], grad_acc, sems.at[2]))
    if final:
        held_copies.append(pltpu.make_async_copy(middle, middle_here, sems.at[4]))
    start_all(held_copies)
    wait_bytes(weight, sems.at[0])
    block = 512

    def hidden_step(r, carry):
        at = pl.ds(pl.multiple_of(r * block, block), block)
        for c in range(3):
            cols = slice(c * 256, c * 256 + 256)
            hidden = nn(normed[at, :], flat(weight[:, :, :, cols]))
            grad_act = nn(cot[at, :], flat(weight[:, :, :, 768 + c * 256 : 1024 + c * 256]))
            value, slope = gelu_parts(hidden)
            act[at, cols] = value.astype(BF)
            grad_hidden[at, cols] = (grad_act * slope).astype(BF)
        return carry

    lax.fori_loop(0, length // block, hidden_step, 0)
    for copy in held_copies:
        copy.wait()

    def sum_step(r, carry):
        at = pl.ds(pl.multiple_of(r * QB, QB), QB)
        mixed_part = nt(act[at, :], flat(weight[:, :, :, 768:1536]))
        grad_part = nt(grad_hidden[at, :], flat(weight[:, :, :, 0:768]))
        if not first:
            mixed_part = mixed_part + mixed_acc[at, :]
            grad_part = grad_part + grad_acc[at, :]
        if final:
            mixed_low[at, :] = (middle_here[at, :] + mixed_part).astype(BF)
        else:
            mixed_acc[at, :] = mixed_part
        grad_acc[at, :] = grad_part
        return carry

    lax.fori_loop(0, length // QB, sum_step, 0)
    out_copies = [
        pltpu.make_async_copy(mixed_low if final else mixed_acc, mixed, sems.at[1]),
        pltpu.make_async_copy(grad_acc, grad_in, sems.at[2]),
    ]
    start_all(out_copies)
    for c in range(3):
        cols = slice(c * 256, c * 256 + 256)
        up = nn(normed_t[...], grad_hidden[:, cols]).astype(BF)
        staged[:, :, :, cols] = up.reshape(staged.shape[:3] + (256,))
        down = nn(cot_t[...], act[:, cols]).astype(BF)
        staged[:, :, :, 768 + c * 256 : 1024 + c * 256] = down.reshape(staged.shape[:3] + (256,))
    start_all(piece_copies(out_piece, me[0], outs, outof, sems.at[3], True))
    for copy in out_copies:
        copy.wait()
    wait_bytes(staged, sems.at[3])


def feed_forward(piece, out_piece, me, normed, normed_t, cot, cot_t, held, middle, slabs, onto):
    length, depth = normed.shape
    rows = piece.rows
    first, final = held is None, middle is not None
    ins = [me] + in_vmem([normed, normed_t, cot, cot_t]) + ([] if first else in_hbm(held))
    specs = [smem_spec()] + [vmem_spec()] * 4 + [any_spec()] * (0 if first else 2)
    if final:
        ins += in_hbm([middle])
        specs.append(any_spec())
    scratch = [
        pltpu.VMEM(rows.shape + (1536,), BF),
        pltpu.VMEM(rows.shape + (1536,), BF),
        pltpu.VMEM((length, 768), BF),
        pltpu.VMEM((length, 768), BF),
        pltpu.VMEM((length, depth), F32),
        pltpu.VMEM((length, depth), F32),
        pltpu.SemaphoreType.DMA((5,)),
    ]
    if final:
        scratch += [pltpu.VMEM((length, depth), BF), pltpu.VMEM((length, depth), F32)]
    got = pl.pallas_call(
        functools.partial(feed_forward_body, piece, out_piece, first, final, len(onto)),
        in_specs=specs + [any_spec()] * (piece.count + len(onto)),
        out_specs=[any_spec()] * 4,
        out_shape=[pltpu.HBM((length, depth), BF if final else F32), pltpu.HBM((length, depth), F32)]
        + [pltpu.HBM(out_piece.shape, BF)] * 2,
        input_output_aliases={len(ins) + piece.count + k: 2 + k for k in range(len(onto))},
        scratch_shapes=scratch,
        compiler_params=params(28 if final else 24),
        cost_estimate=cost(11, 20),
        name="feed_forward",
    )(*ins, *in_hbm(slabs), *in_hbm(onto))
    return got[0], got[1], got[2:]


def norm_pull(grad, hat, root, gain):
    scaled = grad * gain
    first = jnp.mean(scaled, axis=-1, keepdims=True)
    second = jnp.mean(scaled * hat, axis=-1, keepdims=True)
    return root * (scaled - first - hat * second)


def add_sums(sums, grad, hat):
    @pl.when(pl.program_id(0) == 0)
    def _():
        sums[...] = jnp.zeros_like(sums)

    sums[0:1, :] += jnp.sum(grad * hat, axis=0, keepdims=True)
    sums[1:2, :] += jnp.sum(grad, axis=0, keepdims=True)


def out_back_body(piece, groups, me, middle, grad_in, cot, gain, *refs):
    slabs, refs = refs[: piece.count], refs[piece.count :]
    grad_middle, branch_t, sums = refs[:3]
    grad_att = refs[3 : 3 + groups]
    weight, sem = refs[3 + groups :]
    width = weight.shape[3] // 2

    @pl.when(pl.program_id(0) == 0)
    def _():
        moves = [(half, 0, width, weight.at[:, :, :, pl.ds(width * half, width)]) for half in range(2)]
        start_all(piece_copies(piece, me[0], slabs, moves, sem, False))
        wait_bytes(weight, sem)

    hat, root = norm_parts(middle[...])
    grad = grad_in[...]
    value = cot[...].astype(F32) + norm_pull(grad, hat, root, gain[...])
    grad_middle[...] = value
    low = value.astype(BF)
    branch_t[...] = low.T
    add_sums(sums, grad, hat)
    back = nn(low, flat(weight[...])).astype(BF)
    for g in range(groups):
        grad_att[g][:, 0:128] = back[:, g * 128 : g * 128 + 128]
        grad_att[g][:, 128:256] = back[:, width + g * 128 : width + g * 128 + 128]


def out_back(piece, groups, me, middle, grad_in, cot, gain, slabs):
    length, depth = middle.shape
    got = pl.pallas_call(
        functools.partial(out_back_body, piece, groups),
        grid=(length // QB,),
        in_specs=[smem_spec()] + [row_spec(depth)] * 3 + [whole_spec((1, depth))] + [any_spec()] * len(slabs),
        out_specs=[row_spec(depth), column_spec(depth), whole_spec((8, depth))] + [row_spec(256)] * groups,
        out_shape=[pltpu.HBM((length, depth), F32), pltpu.VMEM((depth, length), BF), SDS((8, depth), F32)]
        + [pltpu.HBM((length, 256), BF)] * groups,
        scratch_shapes=[pltpu.VMEM(piece.rows.shape + (depth,), BF), pltpu.SemaphoreType.DMA],
        compiler_params=params(16),
        cost_estimate=cost(4, 16),
        name="out_back",
    )(me, *in_hbm([middle, grad_in]), *in_vmem([cot]), gain, *in_hbm(slabs))
    return got[0], got[1], got[2], got[3:]


def attend_back_body(piece, out_piece, extra, aliased, final, me, normed_t_in, proj, att, grad_att, lse, seg_col, seg_row, *refs):
    refs = list(refs)
    slabs, refs = refs[: piece.count], refs[piece.count :]
    if extra:
        branch_t = refs.pop(0)
        attended, refs = refs[:extra], refs[extra:]
    else:
        held = refs.pop(0)
    if final:
        tokens_in = refs.pop(0)
    refs = refs[aliased:]
    grad_normed, outs, refs = refs[0], refs[1:3], refs[3:]
    if final:
        sums = refs.pop(0)
    grad_proj = refs.pop(0)
    bias, delta, keys_t, query_t, query_m, grad_m, staged, normed_t, total, weight, sems = refs[:11]
    copies = [pltpu.make_async_copy(normed_t_in, normed_t, sems.at[1])]
    if not extra:
        copies.append(pltpu.make_async_copy(held, total, sems.at[2]))
    if final:
        copies.append(pltpu.make_async_copy(tokens_in, refs[11], sems.at[3]))
    moves = [(half, 0, 384, weight.at[:, :, :, pl.ds(384 * half, 384)]) for half in range(2)]
    start_all(copies + piece_copies(piece, me[0], slabs, moves, sems.at[4], False))
    length = proj.shape[0]
    fill_bias(bias, seg_col, seg_row)
    if extra:
        joined = join_heads([a[...] for a in attended])
        out_grad = nn(branch_t[...], joined).astype(BF)
        staged[:, :, :, 768:] = out_grad.reshape(staged.shape[:3] + (768,))
    for half in range(2):
        cols = slice(half * 128, half * 128 + 128)
        product = (grad_att[:, cols].astype(F32) * att[:, cols].astype(F32)).T
        for h in range(4):
            delta[half * 4 + h : half * 4 + h + 1, :] = jnp.sum(
                product[h * HD : (h + 1) * HD], axis=0, keepdims=True
            )
        keys_t[cols, :] = proj[:, half * 384 + 128 : half * 384 + 256].T

    def step(half, carry):
        col = pl.multiple_of(half * 384, 128)
        out = pl.multiple_of(half * 128, 128)
        for h in range(4):
            mine = head_row(h)
            query_m[h] = jnp.where(mine, proj[:, pl.ds(col, 128)], 0)
            grad_m[h] = jnp.where(mine, grad_att[:, pl.ds(out, 128)], 0)
        for j in range(4):
            first = j * QB
            last = length if j == 3 else 768
            here = slice(first, first + QB)
            there = slice(first, last)
            keys = proj[here, pl.ds(col + 128, 128)]
            values = proj[here, pl.ds(col + 256, 128)]
            all_probs, all_grads = [], []
            for h in range(4):
                stat = pl.ds(half * 4 + h, 1)
                lanes = pl.ds(pl.multiple_of(half * 128 + h * HD, HD), HD)
                scores = nt(keys, query_m[h, there, :])
                edge = scores[:, :QB] + bias[1 if j == 3 else 0]
                scores = jnp.concatenate([edge, scores[:, QB:]], 1) if last - first > QB else edge
                probs = jnp.exp2(scores * C2 - lse[stat, there])
                grad_probs = nt(values, grad_m[h, there, :])
                grad_scores = (probs * (grad_probs - delta[stat, there])).astype(BF)
                all_probs.append(probs.astype(BF))
                all_grads.append(grad_scores)
                query_grad = nn(keys_t[lanes, here], grad_scores)
                if j == 0 or j == 3:
                    query_t[lanes, there] = query_grad
                else:
                    query_t[lanes, there] += query_grad
            stacked = jnp.concatenate([grad_m[h, there, :] for h in range(4)], 0)
            value_grad = nn(jnp.concatenate(all_probs, 1), stacked)
            stacked = jnp.concatenate([query_m[h, there, :] for h in range(4)], 0)
            key_grad = nn(jnp.concatenate(all_grads, 1), stacked) * SCALE
            grad_proj[here, pl.ds(col + 128, 128)] = key_grad.astype(BF)
            grad_proj[here, pl.ds(col + 256, 128)] = value_grad.astype(BF)
        return carry

    lax.fori_loop(0, 2, step, 0)
    for half in range(2):
        grad_proj[:, half * 384 : half * 384 + 128] = (
            query_t[half * 128 : half * 128 + 128, :].T * SCALE
        ).astype(BF)
    for copy in copies:
        copy.wait()
    wait_bytes(weight, sems.at[4])
    for c in range(3):
        cols = slice(c * 256, c * 256 + 256)
        part = nn(normed_t[...], grad_proj[:, cols]).astype(BF)
        staged[:, :, :, cols] = part.reshape(staged.shape[:3] + (256,))
    moves = [(half, 0, 384, staged.at[:, :, :, pl.ds(384 * half, 384)]) for half in range(2)]
    if extra:
        moves += [
            (half, -384, 384, staged.at[:, :, :, pl.ds(768 + 384 * half, 384)]) for half in range(2)
        ]
    start_all(piece_copies(out_piece, me[0], outs, moves, sems.at[0], True))
    if final:
        sums[...] = jnp.zeros_like(sums)

    def normed_step(r, carry):
        at = pl.ds(pl.multiple_of(r * QB, QB), QB)
        value = nt(grad_proj[at, :], flat(weight[...]))
        if not extra:
            value = value + total[at, :]
        total[at, :] = value
        if final:
            hat, _ = norm_parts(refs[11][at, :].astype(F32))
            sums[0:1, :] += jnp.sum(value * hat, axis=0, keepdims=True)
            sums[1:2, :] += jnp.sum(value, axis=0, keepdims=True)
        return carry

    lax.fori_loop(0, length // QB, normed_step, 0)
    total_copy = pltpu.make_async_copy(total, grad_normed, sems.at[2])
    total_copy.start()
    wait_bytes(staged, sems.at[0])
    total_copy.wait()


def attend_back(
    piece,
    out_piece,
    me,
    normed_t,
    proj,
    att,
    grad_att,
    lse,
    seg_col,
    seg_row,
    slabs,
    branch_t,
    attended,
    held,
    tokens,
    onto,
):
    depth, length = normed_t.shape
    extra = len(attended)
    final = tokens is not None
    columns = 1536 if extra else 768
    ins = [me] + in_hbm([normed_t, proj, att, grad_att, lse]) + [seg_col, seg_row] + in_hbm(slabs)
    specs = [smem_spec(), any_spec()] + [vmem_spec()] * 6 + [any_spec()] * len(slabs)
    if extra:
        ins += in_vmem([branch_t]) + in_hbm(attended)
        specs += [vmem_spec()] * (1 + extra)
    else:
        ins += in_hbm([held])
        specs += [any_spec()]
    if final:
        ins += in_hbm([tokens])
        specs += [any_spec()]
    outs = [pltpu.HBM((length, depth), F32)] + [pltpu.HBM(out_piece.shape, BF)] * 2
    scratch = [
        pltpu.VMEM((2, QB, QB), F32),
        pltpu.VMEM((8, length), F32),
        pltpu.VMEM((256, length), BF),
        pltpu.VMEM((256, length), F32),
        pltpu.VMEM((4, length, 128), BF),
        pltpu.VMEM((4, length, 128), BF),
        pltpu.VMEM(out_piece.rows.shape + (columns,), BF),
        pltpu.VMEM((depth, length), BF),
        pltpu.VMEM((length, depth), F32),
        pltpu.VMEM(piece.rows.shape + (768,), BF),
        pltpu.SemaphoreType.DMA((5,)),
    ]
    if final:
        outs.append(SDS((8, depth), F32))
        scratch.append(pltpu.VMEM((length, depth), BF))
    got = pl.pallas_call(
        functools.partial(attend_back_body, piece, out_piece, extra, len(onto), final),
        in_specs=specs + [any_spec()] * len(onto),
        out_specs=[any_spec()] * 3 + ([vmem_spec()] if final else []),
        out_shape=outs,
        input_output_aliases={len(ins) + k: 1 + k for k in range(len(onto))},
        scratch_shapes=[pltpu.VMEM((length, 768), BF)] + scratch,
        compiler_params=params(32),
        cost_estimate=cost(12, 8),
        name="attend_back",
    )(*ins, *in_hbm(onto))
    return got[0], got[1:3], got[3] if final else None


def norm_back_body(start, tokens, grad_normed, grad_middle, gain, own, other, high, low):
    length = high.shape[0] // 2
    r = pl.program_id(0)
    hat, root = norm_parts(tokens[...].astype(F32))
    value = grad_middle[...] + norm_pull(grad_normed[...], hat, root, gain[...])
    top = value.astype(BF)
    rest = (value - top.astype(F32)).astype(BF)
    for base in (0, length):
        at = pl.ds(pl.multiple_of(base + r * QB, QB), QB)
        high[at, :] = top
        low[at, :] = rest

    @pl.when(r == pl.num_programs(0) - 1)
    def _():
        count = own.shape[0] // QB
        for k in range(count):
            at = slice(k * QB, k * QB + QB)
            own[at, :] = turned([high, low], start[0], k)
            other[at, :] = turned([high, low], start[0], k + count)


def norm_back(start, tokens, grad_normed, grad_middle, gain):
    length, depth = tokens.shape
    half = (length // 2, depth)
    return pl.pallas_call(
        norm_back_body,
        grid=(length // QB,),
        in_specs=[smem_spec()] + [row_spec(depth)] * 3 + [whole_spec((1, depth))],
        out_specs=[whole_spec(half)] * 2,
        out_shape=[SDS(half, F32)] * 2,
        scratch_shapes=[pltpu.VMEM((2 * length, depth), BF), pltpu.VMEM((2 * length, depth), BF)],
        compiler_params=params(24),
        cost_estimate=cost(4, 16),
        name="norm_back",
    )(start, *in_hbm([tokens, grad_normed, grad_middle]), gain)


def split_far_body(counts, me, *refs):
    keep, send = refs[-2:]
    far = me[0] // 4
    begin = 0
    for count in counts:
        pieces, refs = refs[:count], refs[count:]
        cols = pl.ds(begin, pieces[0].shape[-1])
        begin += pieces[0].shape[-1]
        for k, out in enumerate((keep, send)):
            for slot in range(2):
                at = lax.bitwise_xor(far, k + 2 * slot)
                total = pieces[0][at].astype(F32)
                for piece in pieces[1:]:
                    total = total + piece[at].astype(F32)
                out[slot, :, cols] = total.astype(BF)


def split_far(me, groups):
    width, specs = 0, []
    for pieces in groups:
        far, block, columns = pieces[0].shape[-3:]
        width += columns
        for piece in pieces:
            if piece.ndim == 4:
                specs.append(pl.BlockSpec((None, far, block, columns), lambda i: (0, 0, 0, 0)))
            else:
                specs.append(whole_spec(piece.shape))
    return pl.pallas_call(
        functools.partial(split_far_body, [len(pieces) for pieces in groups]),
        grid=(1,),
        in_specs=[smem_spec()] + specs,
        out_specs=[whole_spec((2, block, width))] * 2,
        out_shape=[SDS((2, block, width), BF)] * 2,
        compiler_params=params(16),
        cost_estimate=cost(1, 2),
        name="split_far",
    )(me, *[piece for pieces in groups for piece in pieces])


def swap(value):
    return lax.ppermute(value, "mp", [(0, 1), (1, 0)])


def tie(*values):
    return lax.optimization_barrier(values)


def hop(value, mask, count):
    return lax.ppermute(value, "dp", [(i, i ^ mask) for i in range(count)])


def hops(value, masks, count):
    return [(value, functools.partial(hop, mask=m, count=count)) for m in masks]


def far_hops(rows, values):
    return [
        (v, functools.partial(hop, mask=rows.near * m, count=rows.dp_count))
        for m, v in zip(range(1, rows.far), values)
    ]


def swaps(values):
    return [(v, swap) for v in values]


def send_all(requests):
    return [send(value) for value, send in requests]


def low_sum(values):
    total = values[0].astype(F32)
    for value in values[1:]:
        total = total + value.astype(F32)
    return total


class Flow:
    def __init__(self, me):
        self.me = me
        self.active = []

    def add(self, transfer, name, results, seeds=()):
        self.active.append([transfer, list(seeds), name, results])

    def step(self, *pivots):
        values = [v for item in self.active for v in item[1]]
        tied = list(tie(self.me, *pivots, *values))
        self.me = tied.pop(0)
        pivots, tied = tied[: len(pivots)], tied[len(pivots) :]
        going, self.active, requests = self.active, [], []
        for item in going:
            transfer, values, name, results = item
            got, tied = tied[: len(values)], tied[len(values) :]
            try:
                if callable(transfer):
                    item[0] = transfer(*got)
                    asked = next(item[0])
                else:
                    asked = transfer.send(got)
                self.active.append(item)
                requests.append(asked)
            except StopIteration as stop:
                results[name] = stop.value
        tied = list(tie(self.me, *(operand for asked in requests for operand, _ in asked)))
        self.me = tied.pop(0)
        for item, asked in zip(self.active, requests):
            item[1] = [send(operand) for (_, send), operand in zip(asked, tied)]
            tied = tied[len(asked) :]
        return pivots


def add_low(a, b):
    return (a.astype(F32) + b.astype(F32)).astype(BF)


def on_device(
    tokens, segment, ln1_gain, ln1_bias, w_qkv, w_out, ln2_gain, ln2_bias, w_up, w_down, cotangent
):
    dp_count = lax.axis_size("dp")
    core = lax.axis_index("mp")
    me = lax.axis_index("dp").astype(jnp.int32).reshape(1)
    here, depth = tokens.shape[2], tokens.shape[3]
    length = 2 * here
    rows = Rows(dp_count, depth)

    groups = w_qkv.shape[2] // 128
    part = 384
    subs = w_up.shape[1] // part
    down = w_down.T
    qkv = [w_qkv[:, :, g * 128 : (g + 1) * 128].reshape(-1, part) for g in range(groups)]
    feed = [
        jnp.concatenate([w_up[:, s * part : (s + 1) * part], down[:, s * part : (s + 1) * part]], 1)
        for s in range(subs)
    ]
    cut = subs // 2
    shards = {
        "q": jnp.concatenate(qkv, 1),
        "a": jnp.concatenate([w_out.T] + feed[:cut], 1),
        "c": jnp.concatenate(feed[cut:], 1),
    }

    def halves(values):
        own = lax.dynamic_index_in_dim(values[:, 0], core, 0, keepdims=False)
        away = lax.dynamic_index_in_dim(values[:, 0], 1 - core, 0, keepdims=False)
        return own, swap(away)

    seg = lax.dynamic_index_in_dim(segment[:, 0], core, 0, keepdims=False)
    run = length * 3 // 4
    begin = jnp.argmax(seg[: length - run + 1] == seg[run - 1 :]).astype(jnp.int32)
    start = ((begin - here * core) % length).reshape(1)
    back = (length - start) % length
    seg_tail = lax.dynamic_slice_in_dim(jnp.concatenate([seg, seg]), begin + run, length - run)
    seg_col = seg_tail.reshape(-1, 1)
    seg_row = seg_tail.reshape(1, -1)
    gain1, bias1, gain2, bias2 = (
        v.reshape(1, -1) for v in (ln1_gain, ln1_bias, ln2_gain, ln2_bias)
    )

    flow = Flow(me)
    token_halves = halves(tokens)
    cot_halves = halves(cotangent)
    wide = 2 * part
    qkv_pieces = [Piece(rows, "slabs")] + [Piece(rows, "slabs", part * g) for g in range(groups - 1)]
    out_piece = Piece(rows, "slabs")
    feed_pieces = [Piece(rows, "slabs", part), Piece(rows, "slabs")]
    feed_pieces += [Piece(rows, "whole", wide * s) for s in range(subs - cut)]
    orders = [(1, 2), (2, 1)]
    turns = [(0, 2, 1, 3), MASKS]
    feed_outs = [
        Piece(rows, "stack", wide * (s % cut), wide * cut, turns[s // cut]) for s in range(subs)
    ]
    qkv_outs = [Piece(rows, "stack", part, wide, turns[0])]
    qkv_outs += [Piece(rows, "stack", part * g, part * (groups - 1)) for g in range(groups - 1)]
    far = lax.axis_index("dp") // rows.near

    def gather_whole(shard):
        return lax.all_gather(shard, "dp", axis=0, tiled=True).reshape(rows.shape + (-1,))

    def fetch_near(near):
        got = yield hops(near, MASKS[1:], dp_count)
        own = [near] + got
        return own + [swap(x) for x in own]

    def via(mask):
        return functools.partial(hop, mask=mask, count=dp_count)

    def fetch_two(widths, shard, away):
        got = yield [(shard, via(4)), (away, via(4))]
        a0, b0 = arrange(rows, flow.me, [shard, got[0], away, got[1]], widths)
        a1, a2, c0 = yield [(a0, via(1)), (a0, via(2))] + swaps([a0])
        a3, c1, c2 = yield [(a1, via(2))] + swaps([a1, a2])
        slabs["a"] = [a0, a1, a2, a3, c0, c1, c2, swap(a3)]
        b1, b2, d0 = yield [(b0, via(1)), (b0, via(2))] + swaps([b0])
        b3, d1, d2 = yield [(b2, via(1))] + swaps([b1, b2])
        return [b0, b1, b2, b3, d0, d1, d2, swap(b3)]

    def fetch_whole(own):
        (other,) = yield swaps([own])
        return [own, other]

    def halve(first, second, own, other):
        (other,) = yield swaps([other])
        keep, send = (low_sum([own[k : k + 2], other[k : k + 2]]).astype(BF) for k in (0, 2))
        (near,) = yield [(send, via(first))]
        (away,) = yield [(low_sum([keep[1], near[1]]).astype(BF), via(second))]
        return [keep, near, away]

    def direct(own, other):
        other = swap(other)
        mine = [low_sum([own[k], other[k]]).astype(BF) for k in range(4)]
        got = yield hops_of(mine, (1, 2, 3))
        return [mine[0]] + got

    def hops_of(values, masks):
        return [(values[m], via(m)) for m in masks]

    def reduce_far(groups):
        keep, send = split_far(flow.me, groups)
        (near,) = yield [(send, via(4))]
        (away,) = yield [(low_sum([keep[1], near[1]]).astype(BF), via(8))]
        return low_sum([keep[0], near[0], away])

    def reduce_all(first, second, own, other):
        pieces = yield from halve(first, second, own, other)
        return (yield from reduce_far([pieces]))

    def plain(own, other):
        value = low_sum([own, swap(other)]).astype(BF).reshape(depth, -1)
        return lax.psum_scatter(value, "dp", scatter_dimension=0, tiled=True).astype(F32)

    def run(transfer):
        requests = next(transfer)
        while True:
            try:
                requests = transfer.send(send_all(requests))
            except StopIteration as stop:
                return stop.value

    slabs, forward = {}, []

    def project(g):
        name = "q0" if g == 0 else "q1"
        forward.append(
            project_attend(qkv_pieces[g], flow.me, normed, seg_col, seg_row, slabs[name])
        )

    if rows.split:
        shard_q, shard_a, shard_c = shards["q"], shards["a"], shards["c"]
        tied = tie(shard_q, *token_halves, *cot_halves)
        shard_q, token_halves, cot_halves = tied[0], tied[1:3], tied[3:]
        got = send_all(far_hops(rows, [shard_q] * (rows.far - 1)))
        prepared = prepare(start, *token_halves, *cot_halves, gain1, bias1)
        tied = tie(*got, *prepared)
        got, prepared = tied[:3], tied[3:]
        near_q0, near_q1 = arrange(rows, me, [shard_q] + list(got), [part, wide])
        near_q0, near_q1, shard_a, shard_c = tie(near_q0, near_q1, shard_a, shard_c)
        own = [near_q0] + [hop(near_q0, m, dp_count) for m in MASKS[1:]]
        away_a = hop(shard_a, 8, dp_count)
        slabs["q0"] = own + [swap(v) for v in own]
        flow.add(fetch_near, "q1", slabs, [near_q1])
        flow.add(
            functools.partial(fetch_two, [part + wide, wide]), "b", slabs, [shard_a, away_a]
        )
        shard_c, _ = flow.step(shard_c, own[3])
        whole_c = gather_whole(shard_c)
    else:
        for name, shard in (
            ("q0", shards["q"][:, :part]),
            ("q1", shards["q"][:, part:]),
            ("a", shards["a"][:, : part + wide]),
            ("b", shards["a"][:, part + wide :]),
            ("c", shards["c"]),
        ):
            slabs[name] = run(fetch_whole(gather_whole(shard)))
        prepared = prepare(start, *token_halves, *cot_halves, gain1, bias1)
    x, normed, normed_t, cot, cot_t = prepared
    for g in range(groups):
        project(g)
        flow.step(forward[g][2])
    atts = [f[1] for f in forward]
    middle, normed_ffn, normed_ffn_t = out_norm(
        out_piece, flow.me, x, gain2, bias2, atts, slabs["a"]
    )
    flow.step(normed_ffn)

    held = None
    sums_of = {}
    onto = []
    feed_names = ["a", "b"] + ["c"] * (subs - cut)
    for s in range(subs):
        mixed, grad_in, grads = feed_forward(
            feed_pieces[s],
            feed_outs[s],
            flow.me,
            normed_ffn,
            normed_ffn_t,
            cot,
            cot_t,
            held,
            middle if s == subs - 1 else None,
            slabs[feed_names[s]],
            onto,
        )
        held = (mixed, grad_in)
        onto = grads
        if s == 0 and rows.split:
            flow.add(fetch_whole, "c", slabs, [whole_c])
        if s % cut == cut - 1:
            k = s // cut
            if rows.split:
                flow.add(functools.partial(reduce_all, *orders[k]), k, sums_of, grads)
            else:
                sums_of[k] = plain(*grads)
            onto = []
        flow.step(grad_in)
    grad_middle, branch_t, sums2, grad_atts = out_back(
        out_piece, groups, flow.me, middle, grad_in, cot, gain2, slabs["a"]
    )
    flow.step(sums2)
    grad_projs = []
    onto = []

    held = None
    qkv_slabs = [slabs["q0"]] + [slabs["q1"]] * (groups - 1)
    for g in range(groups):
        proj, att, lse = forward[g]
        held, grads, sums1 = attend_back(
            qkv_pieces[g],
            qkv_outs[g],
            flow.me,
            normed_t,
            proj,
            att,
            grad_atts[g],
            lse,
            seg_col,
            seg_row,
            qkv_slabs[g],
            branch_t,
            atts if g == 0 else [],
            held,
            x if g == groups - 1 else None,
            onto,
        )
        onto = grads
        if g == 0:
            if rows.split:
                flow.add(functools.partial(halve, *orders[0]), "first", sums_of, grads)
            else:
                sums_of["first"] = plain(*grads)
            onto = []
        if g < groups - 1:
            flow.step(held)
    if rows.split:
        flow.add(direct, "last", sums_of, grads)
    else:
        sums_of["last"] = plain(*grads)
    held, sums1, sums2, mixed = flow.step(held, sums1, sums2, mixed)
    sums = jnp.concatenate([sums1[:2], sums2[:2]], 0)
    away = swap(sums)
    start_late, _ = tie(back, flow.me)
    tokens_own, tokens_other = norm_back(start_late, x, held, grad_middle, gain1)
    tokens_own, tokens_other, mixed, sums, away = flow.step(
        tokens_own, tokens_other, mixed, sums, away
    )
    sums = sums + away
    if rows.split:
        while flow.active:
            flow.step()
        keep, send = split_far(flow.me, [sums_of["first"], sums_of["last"]])
        near = hop(send, 4, dp_count)
        away = [hop(sums, m, dp_count) for m in MASKS[1:]]
        sums = (sums + away[0]) + (away[1] + away[2])
        mixed, _ = tie(mixed, away[0])
        mixed_own, mixed_other = turn_back(back, mixed)
        far_sum = hop(low_sum([keep[1], near[1]]).astype(BF), 8, dp_count)
        last_sum = low_sum([keep[0], near[0], far_sum])
        away = [hop(sums, rows.near * m, dp_count) for m in range(1, rows.far)]
        norm_sums = (sums + away[0]) + (away[1] + away[2])
        feed_sums = [sums_of[0], sums_of[1]]
    else:
        mixed_own, mixed_other = turn_back(back, mixed)
        last_sum = jnp.concatenate([sums_of["first"], sums_of["last"]], -1)
        feed_sums = [sums_of[0], sums_of[1]]
        norm_sums = jnp.sum(lax.all_gather(sums, "dp", axis=0), 0)
    feed_list = []
    for value in feed_sums:
        feed_list += [value[:, wide * s : wide * (s + 1)] for s in range(cut)]
    qkv_list = [last_sum[:, part * (g + 1) : part * (g + 2)] for g in range(groups)]
    grad_out = last_sum[:, :part].T
    def place(own, other):
        other = swap(other)
        return jnp.stack([jnp.where(core == 0, own, other), jnp.where(core == 0, other, own)], 0)[:, None]

    grad_qkv = jnp.concatenate([r.reshape(-1, 3, 128) for r in qkv_list], 2)
    return (
        place(mixed_own, mixed_other),
        place(tokens_own, tokens_other),
        norm_sums[0],
        norm_sums[1],
        grad_qkv,
        grad_out,
        norm_sums[2],
        norm_sums[3],
        jnp.concatenate([r[:, :part] for r in feed_list], 1),
        jnp.concatenate([r[:, part:] for r in feed_list], 1).T,
    )


def solution(mesh):
    in_specs = (
        P(None, "dp", "mp", None),
        P(None, "dp", None),
        P(),
        P(),
        P("dp", None, "mp"),
        P("mp", "dp"),
        P(),
        P(),
        P("dp", "mp"),
        P("mp", "dp"),
        P(None, "dp", "mp", None),
    )
    out_specs = (
        P(None, "dp", "mp", None),
        P(None, "dp", "mp", None),
        P(),
        P(),
        P("dp", None, "mp"),
        P("mp", "dp"),
        P(),
        P(),
        P("dp", "mp"),
        P("mp", "dp"),
    )
    return jax.shard_map(
        on_device, mesh=mesh, in_specs=in_specs, out_specs=out_specs, check_vma=False
    )
```

```python
import functools
import math

import jax
import jax.numpy as jnp
from jax import lax
from jax.experimental import pallas as pl
from jax.experimental.pallas import tpu as pltpu
from jax.sharding import PartitionSpec as P

HD = 32
QB = 256
EPS = 1e-05
BF = jnp.bfloat16
F32 = jnp.float32
NEG = -1e30
SCALE = 1.0 / math.sqrt(HD)
LOG2E = math.log2(math.e)
C2 = SCALE * LOG2E
MIB = 1024 * 1024
SDS = jax.ShapeDtypeStruct


def nn(a, b):
    return lax.dot_general(a, b, (((1,), (0,)), ((), ())), preferred_element_type=F32)


def nt(a, b):
    return lax.dot_general(a, b, (((1,), (1,)), ((), ())), preferred_element_type=F32)


def params(mib):
    return pltpu.CompilerParams(vmem_limit_bytes=mib * MIB)


def in_hbm(values):
    return [pltpu.with_memory_space_constraint(v, pltpu.HBM) for v in values]


def in_vmem(values):
    return [pltpu.with_memory_space_constraint(v, pltpu.VMEM) for v in values]


def cost(gflop, mbytes):
    return pl.CostEstimate(flops=int(gflop * 1e9), bytes_accessed=int(mbytes * 1e6), transcendentals=0)


def any_spec():
    return pl.BlockSpec(memory_space=pl.ANY)


def smem_spec():
    return pl.BlockSpec(memory_space=pltpu.SMEM)


def vmem_spec():
    return pl.BlockSpec(memory_space=pltpu.VMEM)


def row_spec(width, rows=512):
    return pl.BlockSpec((rows, width), lambda r: (r, 0))


def column_spec(height, rows=512):
    return pl.BlockSpec((height, rows), lambda r: (0, r))


def whole_spec(shape):
    return pl.BlockSpec(shape, lambda r: tuple(0 for _ in shape))


MASKS = (0, 1, 2, 3)


class Rows:
    def __init__(self, dp_count, depth):
        self.dp_count = dp_count
        self.depth = depth
        self.split = (depth // dp_count) % 16 == 0 and dp_count == 16
        self.near = 4 if self.split else 1
        self.far = dp_count // 4 if self.split else 1
        self.block = depth // (self.near * self.far)
        self.shape = (self.far, self.near, self.block)


class Piece:
    def __init__(self, rows, kind, start=0, width=0, masks=MASKS):
        self.rows = rows
        self.masks = masks
        self.kind = kind if rows.split else "whole"
        self.start = start
        self.count = 2 * len(MASKS) if self.kind == "slabs" else 2
        if self.kind == "stack":
            self.shape = (len(MASKS), rows.far, rows.block, width)
        else:
            self.shape = rows.shape + (width,)


def piece_copies(piece, me, refs, moves, sem, outward):
    copies = []
    each = piece.count // 2
    for half, column, width, view in moves:
        cols = pl.ds(piece.start + column, width)
        if piece.kind == "whole":
            pairs = [(refs[half].at[:, :, :, cols], view)]
        else:
            pairs = []
            for k, mask in enumerate(piece.masks):
                ref = refs[half].at[k] if piece.kind == "stack" else refs[half * each + k]
                near = lax.bitwise_xor(lax.rem(me, 4), mask)
                pairs.append((ref.at[:, :, cols], view.at[:, near]))
        for outside, inside in pairs:
            if outward:
                copies.append(pltpu.make_async_copy(inside, outside, sem))
            else:
                copies.append(pltpu.make_async_copy(outside, inside, sem))
    return copies


def start_all(copies):
    for copy in copies:
        copy.start()


def wait_bytes(ref, sem):
    pltpu.make_async_copy(ref, ref, sem).wait()


def flat(value):
    return value.reshape(-1, value.shape[-1])


def head_row(h):
    return lax.broadcasted_iota(jnp.int32, (1, 128), 1) // HD == h


def fill_bias(bias, seg_col, seg_row):
    key = lax.broadcasted_iota(jnp.int32, (QB, QB), 0)
    query = lax.broadcasted_iota(jnp.int32, (QB, QB), 1)
    bias[0] = jnp.where(query >= key, 0.0, NEG)
    bias[1] = jnp.where((query >= key) & (seg_col[...] == seg_row[...]), 0.0, NEG)


def fill_double(double, halves):
    here = halves[0].shape[0]
    for k in range(4):
        double[k * here : (k + 1) * here, :] = halves[k % 2][...]


def turned(doubles, start, r):
    coarse = pl.multiple_of(start // 16 * 16 + r * QB, 16)
    fine = start % 16
    row = lax.broadcasted_iota(jnp.int32, (QB, QB + 16), 0)
    col = lax.broadcasted_iota(jnp.int32, (QB, QB + 16), 1)
    pick = jnp.where(col - row == fine, 1.0, 0.0).astype(BF)
    total = None
    for double in doubles:
        part = nn(pick, double[pl.ds(coarse, QB + 16), :])
        total = part if total is None else total + part
    return total


def norm_parts(values):
    centered = values - jnp.mean(values, axis=-1, keepdims=True)
    spread = jnp.mean(centered * centered, axis=-1, keepdims=True)
    root = lax.rsqrt(spread + EPS)
    return centered * root, root


def prepare_body(
    start,
    own,
    other,
    cot_own,
    cot_other,
    gain,
    offset,
    x_out,
    normed,
    normed_t_out,
    cot,
    cot_t,
    double,
    x,
    normed_t,
    sems,
):
    fill_double(double, [own, other])

    def step(r, carry):
        at = pl.ds(pl.multiple_of(r * QB, QB), QB)
        value = turned([double], start[0], r)
        x[at, :] = value.astype(BF)
        hat, _ = norm_parts(value)
        low = (hat * gain[...] + offset[...]).astype(BF)
        normed[at, :] = low
        normed_t[:, at] = low.T
        return carry

    count = x.shape[0] // QB
    lax.fori_loop(0, count, step, 0)
    copies = [
        pltpu.make_async_copy(x, x_out, sems.at[0]),
        pltpu.make_async_copy(normed_t, normed_t_out, sems.at[1]),
    ]
    start_all(copies)
    fill_double(double, [cot_own, cot_other])

    def second(r, carry):
        at = pl.ds(pl.multiple_of(r * QB, QB), QB)
        low = turned([double], start[0], r).astype(BF)
        cot[at, :] = low
        cot_t[:, at] = low.T
        return carry

    lax.fori_loop(0, count, second, 0)
    for copy in copies:
        copy.wait()


def prepare(start, own, other, cot_own, cot_other, gain, offset):
    here, depth = own.shape
    shape, shape_t = (2 * here, depth), (depth, 2 * here)
    return pl.pallas_call(
        prepare_body,
        in_specs=[smem_spec()] + [vmem_spec()] * 6,
        out_specs=[any_spec(), vmem_spec(), any_spec(), vmem_spec(), vmem_spec()],
        out_shape=[
            pltpu.HBM(shape, BF),
            pltpu.VMEM(shape, BF),
            pltpu.HBM(shape_t, BF),
            pltpu.VMEM(shape, BF),
            pltpu.VMEM(shape_t, BF),
        ],
        scratch_shapes=[
            pltpu.VMEM((4 * here, depth), BF),
            pltpu.VMEM(shape, BF),
            pltpu.VMEM(shape_t, BF),
            pltpu.SemaphoreType.DMA((2,)),
        ],
        compiler_params=params(20),
        cost_estimate=cost(4, 8),
        name="prepare",
    )(start, own, other, cot_own, cot_other, gain, offset)


def turn_back_body(start, values, own, other, double):
    here = own.shape[0]
    double[: 2 * here, :] = values[...]
    double[2 * here :, :] = values[...]
    count = here // QB

    def step(r, carry):
        at = pl.ds(pl.multiple_of(r * QB, QB), QB)
        own[at, :] = turned([double], start[0], r).astype(BF)
        other[at, :] = turned([double], start[0], r + count).astype(BF)
        return carry

    lax.fori_loop(0, count, step, 0)


def turn_back(start, values):
    length, depth = values.shape
    return pl.pallas_call(
        turn_back_body,
        in_specs=[smem_spec(), vmem_spec()],
        out_specs=[vmem_spec()] * 2,
        out_shape=[SDS((length // 2, depth), BF)] * 2,
        scratch_shapes=[pltpu.VMEM((2 * length, depth), BF)],
        compiler_params=params(16),
        cost_estimate=cost(2, 4),
        name="turn_back",
    )(start, values)


def arrange_body(widths, me, *refs):
    pieces, outs = refs[:4], refs[4:]
    far = me[0] // 4
    for m, piece in enumerate(pieces):
        begin = 0
        for out, width in zip(outs, widths):
            out[lax.bitwise_xor(far, m)] = piece[:, begin : begin + width]
            begin += width


def arrange(rows, me, pieces, widths):
    return pl.pallas_call(
        functools.partial(arrange_body, widths),
        in_specs=[smem_spec()] + [vmem_spec()] * 4,
        out_specs=[vmem_spec()] * len(widths),
        out_shape=[SDS((rows.far, rows.block, w), BF) for w in widths],
        compiler_params=params(8),
        cost_estimate=cost(1, 1),
        name="arrange",
    )(me, *pieces)


def project_attend_body(piece, me, normed, seg_col, seg_row, *refs):
    slabs = refs[: piece.count]
    proj_out, att, lse, weight, proj, bias, keys_m, values_t, att_t, sem, out_sem = refs[piece.count :]
    moves = [(half, 0, 384, weight.at[:, :, :, pl.ds(384 * half, 384)]) for half in range(2)]
    start_all(piece_copies(piece, me[0], slabs, moves, sem, False))
    fill_bias(bias, seg_col, seg_row)
    values_t[...] = jnp.ones_like(values_t)
    wait_bytes(weight, sem)
    length = normed.shape[0]

    def project(r, carry):
        at = pl.ds(pl.multiple_of(r * 512, 512), 512)
        proj[at, :] = nn(normed[at, :], flat(weight[...])).astype(BF)
        return carry

    lax.fori_loop(0, length // 512, project, 0)
    proj_copy = pltpu.make_async_copy(proj, proj_out, out_sem)
    proj_copy.start()
    for half in range(2):
        flipped = proj[:, half * 384 + 256 : half * 384 + 384].T
        for h in range(4):
            values_t[half * 4 + h, 0:HD, :] = flipped[h * HD : (h + 1) * HD]

    units = [(h, i) for i in (2, 1, 0, 3) for h in range(4)]

    def step(half, carry):
        col = pl.multiple_of(half * 384, 128)
        for h in range(4):
            keys_m[h] = jnp.where(head_row(h), proj[:, pl.ds(col + 128, 128)], 0)

        def score(h, i):
            first = 768 if i == 3 else 0
            scores = nt(keys_m[h, first : (i + 1) * QB, :], proj[i * QB : (i + 1) * QB, pl.ds(col, 128)])
            edge = scores[-QB:] + bias[1 if i == 3 else 0]
            return jnp.concatenate([scores[:-QB], edge], 0) if scores.shape[0] > QB else edge

        ahead = score(*units[0])
        for k, (h, i) in enumerate(units):
            scores = ahead
            if k + 1 < len(units):
                ahead = score(*units[k + 1])
            first = 768 if i == 3 else 0
            last = (i + 1) * QB
            at = slice(i * QB, last)
            peak = jnp.max(scores, axis=0, keepdims=True) * C2
            probs = jnp.exp2(scores * C2 - peak).astype(BF)
            summed = nn(values_t[half * 4 + h, :, first:last], probs)
            total = summed[HD : HD + 1]
            att_t[pl.ds(pl.multiple_of(half * 128 + h * HD, HD), HD), at] = summed[:HD] / total
            lse[pl.ds(half * 4 + h, 1), at] = peak + jnp.log2(total)
        return carry

    lax.fori_loop(0, 2, step, 0)
    for half in range(2):
        cols = slice(half * 128, half * 128 + 128)
        att[:, cols] = att_t[cols, :].T.astype(BF)
    proj_copy.wait()


def project_attend(piece, me, normed, seg_col, seg_row, slabs):
    length, depth = normed.shape
    rows = piece.rows
    return pl.pallas_call(
        functools.partial(project_attend_body, piece),
        in_specs=[smem_spec()] + [vmem_spec()] * 3 + [any_spec()] * len(slabs),
        out_specs=[any_spec()] + [vmem_spec()] * 2,
        out_shape=[
            pltpu.HBM((length, 768), BF),
            pltpu.HBM((length, 256), BF),
            pltpu.HBM((8, length), F32),
        ],
        scratch_shapes=[
            pltpu.VMEM(rows.shape + (768,), BF),
            pltpu.VMEM((length, 768), BF),
            pltpu.VMEM((2, QB, QB), F32),
            pltpu.VMEM((4, length, 128), BF),
            pltpu.VMEM((8, HD + 16, length), BF),
            pltpu.VMEM((256, length), F32),
            pltpu.SemaphoreType.DMA,
            pltpu.SemaphoreType.DMA,
        ],
        compiler_params=params(20),
        cost_estimate=cost(8, 8),
        name="project_attend",
    )(me, *in_vmem([normed]), seg_col, seg_row, *in_hbm(slabs))


def join_heads(attended):
    return jnp.concatenate([a[:, :128] for a in attended] + [a[:, 128:] for a in attended], 1)


def out_norm_body(piece, groups, me, tokens, gain, offset, *refs):
    attended = refs[:groups]
    slabs = refs[groups : groups + piece.count]
    middle, normed, normed_t, weight, sem = refs[groups + piece.count :]
    width = weight.shape[3] // 2

    @pl.when(pl.program_id(0) == 0)
    def _():
        moves = [(half, 0, width, weight.at[:, :, :, pl.ds(width * half, width)]) for half in range(2)]
        start_all(piece_copies(piece, me[0], slabs, moves, sem, False))
        wait_bytes(weight, sem)

    value = tokens[...].astype(F32) + nt(join_heads([a[...] for a in attended]), flat(weight[...]))
    middle[...] = value
    hat, _ = norm_parts(value)
    low = (hat * gain[...] + offset[...]).astype(BF)
    normed[...] = low
    normed_t[...] = low.T


def out_norm(piece, me, tokens, gain, offset, attended, slabs):
    length, depth = tokens.shape
    return pl.pallas_call(
        functools.partial(out_norm_body, piece, len(attended)),
        grid=(length // 512,),
        in_specs=[smem_spec(), row_spec(depth), whole_spec((1, depth)), whole_spec((1, depth))]
        + [row_spec(256)] * len(attended)
        + [any_spec()] * len(slabs),
        out_specs=[row_spec(depth)] * 2 + [column_spec(depth)],
        out_shape=[
            pltpu.HBM((length, depth), F32),
            pltpu.VMEM((length, depth), BF),
            pltpu.VMEM((depth, length), BF),
        ],
        scratch_shapes=[pltpu.VMEM(piece.rows.shape + (depth,), BF), pltpu.SemaphoreType.DMA],
        compiler_params=params(28),
        cost_estimate=cost(3, 8),
        name="out_norm",
    )(me, *in_hbm([tokens]), gain, offset, *in_hbm(attended), *in_hbm(slabs))


def gelu_parts(values):
    size = jnp.abs(values)
    density = jnp.exp2(values * values * (-0.5 * LOG2E) + math.log2(1.0 / math.sqrt(2 * math.pi)))
    t = 1.0 / (1.0 + 0.2316419 * size)
    poly = t * (
        0.319381530
        + t * (-0.356563782 + t * (1.781477937 + t * (-1.821255978 + t * 1.330274429)))
    )
    tail = density * poly
    below = jnp.where(values >= 0, 1.0 - tail, tail)
    return values * below, below + values * density


def feed_forward_body(piece, out_piece, first, final, aliased, me, normed, normed_t, cot, cot_t, *refs):
    refs = list(refs)
    held = [] if first else [refs.pop(0), refs.pop(0)]
    middle = refs.pop(0) if final else None
    slabs, refs = refs[: piece.count], refs[piece.count + aliased :]
    mixed, grad_in = refs[:2]
    outs, refs = refs[2:4], refs[4:]
    weight, staged, act, grad_hidden, mixed_acc, grad_acc, sems = refs[:7]
    mixed_low, middle_here = refs[7:] if final else (None, None)
    length, depth = normed.shape
    moves = []
    for half in range(2):
        for which in range(2):
            at = pl.ds(which * 768 + half * 384, 384)
            moves.append((half, which * 384, 384, at))
    into = [(h, c, w, weight.at[:, :, :, at]) for h, c, w, at in moves]
    outof = [(h, c, w, staged.at[:, :, :, at]) for h, c, w, at in moves]
    start_all(piece_copies(piece, me[0], slabs, into, sems.at[0], False))
    held_copies = []
    if not first:
        held_copies.append(pltpu.make_async_copy(held[0], mixed_acc, sems.at[1]))
        held_copies.append(pltpu.make_async_copy(held[1], grad_acc, sems.at[2]))
    if final:
        held_copies.append(pltpu.make_async_copy(middle, middle_here, sems.at[4]))
    start_all(held_copies)
    wait_bytes(weight, sems.at[0])
    chunks = [slice(c * 256, c * 256 + 256) for c in range(3)]

    def products(c):
        hidden = nn(normed[...], flat(weight[:, :, :, c * 256 : c * 256 + 256]))
        return hidden, nn(cot[...], flat(weight[:, :, :, 768 + c * 256 : 1024 + c * 256]))

    ahead = products(0)
    for c in range(3):
        hidden, grad_act = ahead
        if c < 2:
            ahead = products(c + 1)
        value, slope = gelu_parts(hidden)
        act[:, chunks[c]] = value.astype(BF)
        grad_hidden[:, chunks[c]] = (grad_act * slope).astype(BF)
    for copy in held_copies:
        copy.wait()
    for cols in chunks:
        mixed_part = nt(act[...], flat(weight[:, :, :, 768:1536])[cols])
        grad_part = nt(grad_hidden[...], flat(weight[:, :, :, 0:768])[cols])
        if not first:
            mixed_part = mixed_part + mixed_acc[:, cols]
            grad_part = grad_part + grad_acc[:, cols]
        if final:
            mixed_low[:, cols] = (middle_here[:, cols] + mixed_part).astype(BF)
        else:
            mixed_acc[:, cols] = mixed_part
        grad_acc[:, cols] = grad_part
    out_copies = [
        pltpu.make_async_copy(mixed_low if final else mixed_acc, mixed, sems.at[1]),
        pltpu.make_async_copy(grad_acc, grad_in, sems.at[2]),
    ]
    start_all(out_copies)
    for c in range(3):
        cols = slice(c * 256, c * 256 + 256)
        up = nn(normed_t[...], grad_hidden[:, cols]).astype(BF)
        staged[:, :, :, cols] = up.reshape(staged.shape[:3] + (256,))
        down = nn(cot_t[...], act[:, cols]).astype(BF)
        staged[:, :, :, 768 + c * 256 : 1024 + c * 256] = down.reshape(staged.shape[:3] + (256,))
    start_all(piece_copies(out_piece, me[0], outs, outof, sems.at[3], True))
    for copy in out_copies:
        copy.wait()
    wait_bytes(staged, sems.at[3])


def feed_forward(piece, out_piece, me, normed, normed_t, cot, cot_t, held, middle, slabs, onto):
    length, depth = normed.shape
    rows = piece.rows
    first, final = held is None, middle is not None
    ins = [me] + in_vmem([normed, normed_t, cot, cot_t]) + ([] if first else in_hbm(held))
    specs = [smem_spec()] + [vmem_spec()] * 4 + [any_spec()] * (0 if first else 2)
    if final:
        ins += in_hbm([middle])
        specs.append(any_spec())
    scratch = [
        pltpu.VMEM(rows.shape + (1536,), BF),
        pltpu.VMEM(rows.shape + (1536,), BF),
        pltpu.VMEM((length, 768), BF),
        pltpu.VMEM((length, 768), BF),
        pltpu.VMEM((length, depth), F32),
        pltpu.VMEM((length, depth), F32),
        pltpu.SemaphoreType.DMA((5,)),
    ]
    if final:
        scratch += [pltpu.VMEM((length, depth), BF), pltpu.VMEM((length, depth), F32)]
    got = pl.pallas_call(
        functools.partial(feed_forward_body, piece, out_piece, first, final, len(onto)),
        in_specs=specs + [any_spec()] * (piece.count + len(onto)),
        out_specs=[any_spec()] * 4,
        out_shape=[pltpu.HBM((length, depth), BF if final else F32), pltpu.HBM((length, depth), F32)]
        + [pltpu.HBM(out_piece.shape, BF)] * 2,
        input_output_aliases={len(ins) + piece.count + k: 2 + k for k in range(len(onto))},
        scratch_shapes=scratch,
        compiler_params=params(40),
        cost_estimate=cost(11, 20),
        name="feed_forward",
    )(*ins, *in_hbm(slabs), *in_hbm(onto))
    return got[0], got[1], got[2:]


def norm_pull(grad, hat, root, gain):
    scaled = grad * gain
    first = jnp.mean(scaled, axis=-1, keepdims=True)
    second = jnp.mean(scaled * hat, axis=-1, keepdims=True)
    return root * (scaled - first - hat * second)


def add_sums(sums, grad, hat):
    @pl.when(pl.program_id(0) == 0)
    def _():
        sums[...] = jnp.zeros_like(sums)

    sums[0:1, :] += jnp.sum(grad * hat, axis=0, keepdims=True)
    sums[1:2, :] += jnp.sum(grad, axis=0, keepdims=True)


def out_back_body(piece, groups, me, middle, grad_in, cot, gain, *refs):
    slabs, refs = refs[: piece.count], refs[piece.count :]
    grad_middle, branch_t, sums = refs[:3]
    grad_att = refs[3 : 3 + groups]
    weight, sem = refs[3 + groups :]
    width = weight.shape[3] // 2

    @pl.when(pl.program_id(0) == 0)
    def _():
        moves = [(half, 0, width, weight.at[:, :, :, pl.ds(width * half, width)]) for half in range(2)]
        start_all(piece_copies(piece, me[0], slabs, moves, sem, False))
        wait_bytes(weight, sem)

    hat, root = norm_parts(middle[...])
    grad = grad_in[...]
    value = cot[...].astype(F32) + norm_pull(grad, hat, root, gain[...])
    grad_middle[...] = value
    low = value.astype(BF)
    branch_t[...] = low.T
    add_sums(sums, grad, hat)
    back = nn(low, flat(weight[...])).astype(BF)
    for g in range(groups):
        grad_att[g][:, 0:128] = back[:, g * 128 : g * 128 + 128]
        grad_att[g][:, 128:256] = back[:, width + g * 128 : width + g * 128 + 128]


def out_back(piece, groups, me, middle, grad_in, cot, gain, slabs):
    length, depth = middle.shape
    got = pl.pallas_call(
        functools.partial(out_back_body, piece, groups),
        grid=(length // 512,),
        in_specs=[smem_spec()] + [row_spec(depth)] * 3 + [whole_spec((1, depth))] + [any_spec()] * len(slabs),
        out_specs=[row_spec(depth), column_spec(depth), whole_spec((8, depth))] + [row_spec(256)] * groups,
        out_shape=[pltpu.HBM((length, depth), F32), pltpu.VMEM((depth, length), BF), SDS((8, depth), F32)]
        + [pltpu.HBM((length, 256), BF)] * groups,
        scratch_shapes=[pltpu.VMEM(piece.rows.shape + (depth,), BF), pltpu.SemaphoreType.DMA],
        compiler_params=params(28),
        cost_estimate=cost(4, 16),
        name="out_back",
    )(me, *in_hbm([middle, grad_in]), *in_vmem([cot]), gain, *in_hbm(slabs))
    return got[0], got[1], got[2], got[3:]


def attend_back_body(piece, out_piece, extra, aliased, final, me, normed_t_in, proj, att, grad_att, lse, seg_col, seg_row, *refs):
    refs = list(refs)
    slabs, refs = refs[: piece.count], refs[piece.count :]
    if extra:
        branch_t = refs.pop(0)
        attended, refs = refs[:extra], refs[extra:]
    else:
        held = refs.pop(0)
    if final:
        tokens_in = refs.pop(0)
    refs = refs[aliased:]
    grad_normed, outs, refs = refs[0], refs[1:3], refs[3:]
    if final:
        sums = refs.pop(0)
    grad_proj, key_sum, value_sum = refs[:3]
    refs = refs[3:]
    bias, delta, keys_t, query_t, query_m, grad_m, staged, normed_t, total, weight, sems = refs[:11]
    copies = [pltpu.make_async_copy(normed_t_in, normed_t, sems.at[1])]
    if not extra:
        copies.append(pltpu.make_async_copy(held, total, sems.at[2]))
    if final:
        copies.append(pltpu.make_async_copy(tokens_in, refs[11], sems.at[3]))
    moves = [(half, 0, 384, weight.at[:, :, :, pl.ds(384 * half, 384)]) for half in range(2)]
    start_all(copies + piece_copies(piece, me[0], slabs, moves, sems.at[4], False))
    length = proj.shape[0]
    fill_bias(bias, seg_col, seg_row)
    if extra:
        joined = join_heads([a[...] for a in attended])
        out_grad = nn(branch_t[...], joined).astype(BF)
        staged[:, :, :, 768:] = out_grad.reshape(staged.shape[:3] + (768,))
    for half in range(2):
        cols = slice(half * 128, half * 128 + 128)
        product = (grad_att[:, cols].astype(F32) * att[:, cols].astype(F32)).T
        for h in range(4):
            delta[half * 4 + h : half * 4 + h + 1, :] = jnp.sum(
                product[h * HD : (h + 1) * HD], axis=0, keepdims=True
            )
        keys_t[cols, :] = proj[:, half * 384 + 128 : half * 384 + 256].T

    def step(half, carry):
        col = pl.multiple_of(half * 384, 128)
        out = pl.multiple_of(half * 128, 128)
        for h in range(4):
            mine = head_row(h)
            query_m[h] = jnp.where(mine, proj[:, pl.ds(col, 128)], 0)
            grad_m[h] = jnp.where(mine, grad_att[:, pl.ds(out, 128)], 0)
        key_sum[...] = jnp.zeros_like(key_sum)
        value_sum[...] = jnp.zeros_like(value_sum)
        for i in (2, 1, 0, 3):
            first = 768 if i == 3 else 0
            last = (i + 1) * QB
            here = slice(first, last)
            there = slice(i * QB, last)
            keys = proj[here, pl.ds(col + 128, 128)]
            values = proj[here, pl.ds(col + 256, 128)]

            def products(h):
                scores = nt(keys, query_m[h, there, :])
                edge = scores[-QB:] + bias[1 if i == 3 else 0]
                if last - first > QB:
                    scores = jnp.concatenate([scores[:-QB], edge], 0)
                else:
                    scores = edge
                return scores, nt(values, grad_m[h, there, :])

            all_probs, all_grads = [], []
            ahead = products(0)
            for h in range(4):
                scores, grad_probs = ahead
                if h < 3:
                    ahead = products(h + 1)
                stat = pl.ds(half * 4 + h, 1)
                lanes = pl.ds(pl.multiple_of(half * 128 + h * HD, HD), HD)
                probs = jnp.exp2(scores * C2 - lse[stat, there])
                grad_scores = (probs * (grad_probs - delta[stat, there])).astype(BF)
                all_probs.append(probs.astype(BF))
                all_grads.append(grad_scores)
                query_t[lanes, there] = nn(keys_t[lanes, here], grad_scores)
            stacked = jnp.concatenate([grad_m[h, there, :] for h in range(4)], 0)
            value_sum[here, :] += nn(jnp.concatenate(all_probs, 1), stacked)
            stacked = jnp.concatenate([query_m[h, there, :] for h in range(4)], 0)
            key_sum[here, :] += nn(jnp.concatenate(all_grads, 1), stacked)
        grad_proj[:, pl.ds(col + 128, 128)] = (key_sum[...] * SCALE).astype(BF)
        grad_proj[:, pl.ds(col + 256, 128)] = value_sum[...].astype(BF)
        return carry

    lax.fori_loop(0, 2, step, 0)
    for half in range(2):
        grad_proj[:, half * 384 : half * 384 + 128] = (
            query_t[half * 128 : half * 128 + 128, :].T * SCALE
        ).astype(BF)
    for copy in copies:
        copy.wait()
    wait_bytes(weight, sems.at[4])
    for c in range(3):
        cols = slice(c * 256, c * 256 + 256)
        part = nn(normed_t[...], grad_proj[:, cols]).astype(BF)
        staged[:, :, :, cols] = part.reshape(staged.shape[:3] + (256,))
    moves = [(half, 0, 384, staged.at[:, :, :, pl.ds(384 * half, 384)]) for half in range(2)]
    if extra:
        moves += [
            (half, -384, 384, staged.at[:, :, :, pl.ds(768 + 384 * half, 384)]) for half in range(2)
        ]
    start_all(piece_copies(out_piece, me[0], outs, moves, sems.at[0], True))
    if final:
        sums[...] = jnp.zeros_like(sums)

    total_copies = []
    for c in range(3):
        cols = slice(c * 256, c * 256 + 256)
        value = nt(grad_proj[...], flat(weight[...])[cols])
        if not extra:
            value = value + total[:, cols]
        total[:, cols] = value
        total_copies.append(
            pltpu.make_async_copy(
                total.at[:, pl.ds(c * 256, 256)], grad_normed.at[:, pl.ds(c * 256, 256)], sems.at[2]
            )
        )
        total_copies[-1].start()
    if final:

        def sum_step(r, carry):
            at = pl.ds(pl.multiple_of(r * QB, QB), QB)
            value = total[at, :]
            hat, _ = norm_parts(refs[11][at, :].astype(F32))
            sums[0:1, :] += jnp.sum(value * hat, axis=0, keepdims=True)
            sums[1:2, :] += jnp.sum(value, axis=0, keepdims=True)
            return carry

        lax.fori_loop(0, length // QB, sum_step, 0)
    wait_bytes(staged, sems.at[0])
    wait_bytes(total, sems.at[2])


def attend_back(
    piece,
    out_piece,
    me,
    normed_t,
    proj,
    att,
    grad_att,
    lse,
    seg_col,
    seg_row,
    slabs,
    branch_t,
    attended,
    held,
    tokens,
    onto,
):
    depth, length = normed_t.shape
    extra = len(attended)
    final = tokens is not None
    columns = 1536 if extra else 768
    ins = [me] + in_hbm([normed_t, proj, att, grad_att, lse]) + [seg_col, seg_row] + in_hbm(slabs)
    specs = [smem_spec(), any_spec()] + [vmem_spec()] * 6 + [any_spec()] * len(slabs)
    if extra:
        ins += in_vmem([branch_t]) + in_hbm(attended)
        specs += [vmem_spec()] * (1 + extra)
    else:
        ins += in_hbm([held])
        specs += [any_spec()]
    if final:
        ins += in_hbm([tokens])
        specs += [any_spec()]
    outs = [pltpu.HBM((length, depth), F32)] + [pltpu.HBM(out_piece.shape, BF)] * 2
    scratch = [
        pltpu.VMEM((2, QB, QB), F32),
        pltpu.VMEM((8, length), F32),
        pltpu.VMEM((256, length), BF),
        pltpu.VMEM((256, length), F32),
        pltpu.VMEM((4, length, 128), BF),
        pltpu.VMEM((4, length, 128), BF),
        pltpu.VMEM(out_piece.rows.shape + (columns,), BF),
        pltpu.VMEM((depth, length), BF),
        pltpu.VMEM((length, depth), F32),
        pltpu.VMEM(piece.rows.shape + (768,), BF),
        pltpu.SemaphoreType.DMA((5,)),
    ]
    if final:
        outs.append(SDS((8, depth), F32))
        scratch.append(pltpu.VMEM((length, depth), BF))
    got = pl.pallas_call(
        functools.partial(attend_back_body, piece, out_piece, extra, len(onto), final),
        in_specs=specs + [any_spec()] * len(onto),
        out_specs=[any_spec()] * 3 + ([vmem_spec()] if final else []),
        out_shape=outs,
        input_output_aliases={len(ins) + k: 1 + k for k in range(len(onto))},
        scratch_shapes=[
            pltpu.VMEM((length, 768), BF),
            pltpu.VMEM((length, 128), F32),
            pltpu.VMEM((length, 128), F32),
        ]
        + scratch,
        compiler_params=params(40),
        cost_estimate=cost(12, 8),
        name="attend_back",
    )(*ins, *in_hbm(onto))
    return got[0], got[1:3], got[3] if final else None


def norm_back_body(start, tokens, grad_normed, grad_middle, gain, own, other, high, low):
    length = high.shape[0] // 2
    r = pl.program_id(0)
    hat, root = norm_parts(tokens[...].astype(F32))
    value = grad_middle[...] + norm_pull(grad_normed[...], hat, root, gain[...])
    top = value.astype(BF)
    rest = (value - top.astype(F32)).astype(BF)
    for base in (0, length):
        at = pl.ds(pl.multiple_of(base + r * QB, QB), QB)
        high[at, :] = top
        low[at, :] = rest

    @pl.when(r == pl.num_programs(0) - 1)
    def _():
        count = own.shape[0] // QB
        for k in range(count):
            at = slice(k * QB, k * QB + QB)
            own[at, :] = turned([high, low], start[0], k)
            other[at, :] = turned([high, low], start[0], k + count)


def norm_back(start, tokens, grad_normed, grad_middle, gain):
    length, depth = tokens.shape
    half = (length // 2, depth)
    return pl.pallas_call(
        norm_back_body,
        grid=(length // QB,),
        in_specs=[smem_spec()] + [row_spec(depth, QB)] * 3 + [whole_spec((1, depth))],
        out_specs=[whole_spec(half)] * 2,
        out_shape=[SDS(half, F32)] * 2,
        scratch_shapes=[pltpu.VMEM((2 * length, depth), BF), pltpu.VMEM((2 * length, depth), BF)],
        compiler_params=params(24),
        cost_estimate=cost(4, 16),
        name="norm_back",
    )(start, *in_hbm([tokens, grad_normed, grad_middle]), gain)


def split_far_body(counts, me, *refs):
    keep, send = refs[-2:]
    far = me[0] // 4
    begin = 0
    for count in counts:
        pieces, refs = refs[:count], refs[count:]
        cols = pl.ds(begin, pieces[0].shape[-1])
        begin += pieces[0].shape[-1]
        for k, out in enumerate((keep, send)):
            for slot in range(2):
                at = lax.bitwise_xor(far, k + 2 * slot)
                total = pieces[0][at].astype(F32)
                for piece in pieces[1:]:
                    total = total + piece[at].astype(F32)
                out[slot, :, cols] = total.astype(BF)


def split_far(me, groups):
    width, specs = 0, []
    for pieces in groups:
        far, block, columns = pieces[0].shape[-3:]
        width += columns
        for piece in pieces:
            if piece.ndim == 4:
                specs.append(pl.BlockSpec((None, far, block, columns), lambda i: (0, 0, 0, 0)))
            else:
                specs.append(whole_spec(piece.shape))
    return pl.pallas_call(
        functools.partial(split_far_body, [len(pieces) for pieces in groups]),
        grid=(1,),
        in_specs=[smem_spec()] + specs,
        out_specs=[whole_spec((2, block, width))] * 2,
        out_shape=[SDS((2, block, width), BF)] * 2,
        compiler_params=params(16),
        cost_estimate=cost(1, 2),
        name="split_far",
    )(me, *[piece for pieces in groups for piece in pieces])


def swap(value):
    return lax.ppermute(value, "mp", [(0, 1), (1, 0)])


def tie(*values):
    return lax.optimization_barrier(values)


def hop(value, mask, count):
    return lax.ppermute(value, "dp", [(i, i ^ mask) for i in range(count)])


def hops(value, masks, count):
    return [(value, functools.partial(hop, mask=m, count=count)) for m in masks]


def far_hops(rows, values):
    return [
        (v, functools.partial(hop, mask=rows.near * m, count=rows.dp_count))
        for m, v in zip(range(1, rows.far), values)
    ]


def swaps(values):
    return [(v, swap) for v in values]


def send_all(requests):
    return [send(value) for value, send in requests]


def low_sum(values):
    total = values[0].astype(F32)
    for value in values[1:]:
        total = total + value.astype(F32)
    return total


class Flow:
    def __init__(self, me):
        self.me = me
        self.active = []

    def add(self, transfer, name, results, seeds=()):
        self.active.append([transfer, list(seeds), name, results])

    def step(self, *pivots):
        values = [v for item in self.active for v in item[1]]
        tied = list(tie(self.me, *pivots, *values))
        self.me = tied.pop(0)
        pivots, tied = tied[: len(pivots)], tied[len(pivots) :]
        going, self.active, requests = self.active, [], []
        for item in going:
            transfer, values, name, results = item
            got, tied = tied[: len(values)], tied[len(values) :]
            try:
                if callable(transfer):
                    item[0] = transfer(*got)
                    asked = next(item[0])
                else:
                    asked = transfer.send(got)
                self.active.append(item)
                requests.append(asked)
            except StopIteration as stop:
                results[name] = stop.value
        tied = list(tie(self.me, *(operand for asked in requests for operand, _ in asked)))
        self.me = tied.pop(0)
        for item, asked in zip(self.active, requests):
            item[1] = [send(operand) for (_, send), operand in zip(asked, tied)]
            tied = tied[len(asked) :]
        return pivots


def add_low(a, b):
    return (a.astype(F32) + b.astype(F32)).astype(BF)


def on_device(
    tokens, segment, ln1_gain, ln1_bias, w_qkv, w_out, ln2_gain, ln2_bias, w_up, w_down, cotangent
):
    dp_count = lax.axis_size("dp")
    core = lax.axis_index("mp")
    me = lax.axis_index("dp").astype(jnp.int32).reshape(1)
    here, depth = tokens.shape[2], tokens.shape[3]
    length = 2 * here
    rows = Rows(dp_count, depth)

    groups = w_qkv.shape[2] // 128
    part = 384
    subs = w_up.shape[1] // part
    down = w_down.T
    qkv = [w_qkv[:, :, g * 128 : (g + 1) * 128].reshape(-1, part) for g in range(groups)]
    feed = [
        jnp.concatenate([w_up[:, s * part : (s + 1) * part], down[:, s * part : (s + 1) * part]], 1)
        for s in range(subs)
    ]
    cut = subs // 2
    shards = {
        "q0": qkv[0],
        "q1": jnp.concatenate(qkv[1:], 1),
        "a": jnp.concatenate([w_out.T] + feed[:cut], 1),
        "c": jnp.concatenate(feed[cut:], 1),
    }

    def halves(values):
        own = lax.dynamic_index_in_dim(values[:, 0], core, 0, keepdims=False)
        away = lax.dynamic_index_in_dim(values[:, 0], 1 - core, 0, keepdims=False)
        return own, swap(away)

    seg = lax.dynamic_index_in_dim(segment[:, 0], core, 0, keepdims=False)
    run = length * 3 // 4
    begin = jnp.argmax(seg[: length - run + 1] == seg[run - 1 :]).astype(jnp.int32)
    start = ((begin - here * core) % length).reshape(1)
    back = (length - start) % length
    seg_tail = lax.dynamic_slice_in_dim(jnp.concatenate([seg, seg]), begin + run, length - run)
    seg_col = seg_tail.reshape(-1, 1)
    seg_row = seg_tail.reshape(1, -1)
    gain1, bias1, gain2, bias2 = (
        v.reshape(1, -1) for v in (ln1_gain, ln1_bias, ln2_gain, ln2_bias)
    )

    flow = Flow(me)
    token_halves = halves(tokens)
    cot_halves = halves(cotangent)
    wide = 2 * part
    qkv_pieces = [Piece(rows, "slabs")] + [Piece(rows, "slabs", part * g) for g in range(groups - 1)]
    out_piece = Piece(rows, "slabs")
    feed_pieces = [Piece(rows, "slabs", part), Piece(rows, "slabs")]
    feed_pieces += [Piece(rows, "whole", wide * s) for s in range(subs - cut)]
    turns = [(0, 2, 1, 3), MASKS]
    feed_outs = [
        Piece(rows, "stack", wide * (s % cut), wide * cut, turns[s % cut]) for s in range(subs)
    ]
    qkv_outs = [Piece(rows, "stack", part, wide)]
    qkv_outs += [Piece(rows, "stack", part * g, part * (groups - 1)) for g in range(groups - 1)]
    far = lax.axis_index("dp") // rows.near

    def gather_whole(shard):
        return lax.all_gather(shard, "dp", axis=0, tiled=True).reshape(rows.shape + (-1,))

    def fetch_near(near):
        got = yield hops(near, MASKS[1:], dp_count)
        own = [near] + got
        return own + [swap(x) for x in own]

    def via(mask):
        return functools.partial(hop, mask=mask, count=dp_count)

    def fetch_two(widths, shard, away):
        got = yield [(shard, via(4)), (away, via(4))]
        a0, b0 = arrange(rows, flow.me, [shard, got[0], away, got[1]], widths)
        a1, a2, c0 = yield [(a0, via(1)), (a0, via(2))] + swaps([a0])
        a3, c1, c2 = yield [(a1, via(2))] + swaps([a1, a2])
        slabs["a"] = [a0, a1, a2, a3, c0, c1, c2, swap(a3)]
        b1, b2, d0 = yield [(b0, via(1)), (b0, via(2))] + swaps([b0])
        b3, d1, d2 = yield [(b2, via(1))] + swaps([b1, b2])
        return [b0, b1, b2, b3, d0, d1, d2, swap(b3)]

    def fetch_whole(own):
        (other,) = yield swaps([own])
        return [own, other]

    def halve(own, other):
        (other,) = yield swaps([other])
        middle_col = own.shape[-1] // 2
        keep, send = [], []
        for cols in (slice(0, middle_col), slice(middle_col, None)):
            keep.append(low_sum([own[:2, ..., cols], other[:2, ..., cols]]).astype(BF))
            send.append(low_sum([own[2:, ..., cols], other[2:, ..., cols]]).astype(BF))
        near = yield [(v, via(m)) for v, m in zip(send, (1, 2))]
        send = [low_sum([k[1], n[1]]).astype(BF) for k, n in zip(keep, near)]
        away = yield [(v, via(m)) for v, m in zip(send, (2, 1))]
        return [list(group) for group in zip(keep, near, away)]

    def direct(own, other, hurry=True):
        if hurry:
            other = swap(other)
        mine = [low_sum([own[k], other[k]]).astype(BF) for k in range(4)]
        got = yield hops_of(mine, (1, 2, 3))
        return [mine[0]] + got

    def hops_of(values, masks):
        return [(values[m], via(m)) for m in masks]

    def reduce_far(groups):
        keep, send = split_far(flow.me, groups)
        (near,) = yield [(send, via(4))]
        (away,) = yield [(low_sum([keep[1], near[1]]).astype(BF), via(8))]
        return low_sum([keep[0], near[0], away])

    def reduce_all(own, other):
        groups_here = yield from halve(own, other)
        return (yield from reduce_far(groups_here))

    def reduce_direct(own, other):
        (other,) = yield swaps([other])
        pieces = yield from direct(own, other, False)
        return (yield from reduce_far([pieces]))

    def plain(own, other):
        value = low_sum([own, swap(other)]).astype(BF).reshape(depth, -1)
        return lax.psum_scatter(value, "dp", scatter_dimension=0, tiled=True).astype(F32)

    def run(transfer):
        requests = next(transfer)
        while True:
            try:
                requests = transfer.send(send_all(requests))
            except StopIteration as stop:
                return stop.value

    slabs, forward = {}, []

    def project(g):
        name = "q0" if g == 0 else "q1"
        forward.append(
            project_attend(qkv_pieces[g], flow.me, normed, seg_col, seg_row, slabs[name])
        )

    if rows.split:
        shard_q, shard_q1, shard_a, shard_c = (shards[k] for k in ("q0", "q1", "a", "c"))
        tied = tie(shard_q, *token_halves, *cot_halves)
        shard_q, token_halves, cot_halves = tied[0], tied[1:3], tied[3:]
        got = send_all(far_hops(rows, [shard_q] * (rows.far - 1)))
        prepared = prepare(start, *token_halves, *cot_halves, gain1, bias1)
        tied = tie(*got, *prepared)
        got, prepared = tied[:3], tied[3:]
        (near_q0,) = arrange(rows, me, [shard_q] + list(got), [part])
        near_q0, shard_q1, shard_a = tie(near_q0, shard_q1, shard_a)
        own = [near_q0] + [hop(near_q0, m, dp_count) for m in MASKS[1:]]
        away_q1 = [hop(shard_q1, m, dp_count) for m in (4, 8)]
        away_q1.append(hop(away_q1[1], 4, dp_count))
        away_a = hop(shard_a, 8, dp_count)
        slabs["q0"] = own + [swap(v) for v in own]
        (near_q1,) = arrange(rows, me, [shard_q1] + away_q1, [wide])
        flow.add(fetch_near, "q1", slabs, [near_q1])
        flow.add(
            functools.partial(fetch_two, [part + wide, wide]), "b", slabs, [shard_a, away_a]
        )
        shard_c, _ = flow.step(shard_c, own[3])
        whole_c = gather_whole(shard_c)
    else:
        for name, shard in (
            ("q0", shards["q0"]),
            ("q1", shards["q1"]),
            ("a", shards["a"][:, : part + wide]),
            ("b", shards["a"][:, part + wide :]),
            ("c", shards["c"]),
        ):
            slabs[name] = run(fetch_whole(gather_whole(shard)))
        prepared = prepare(start, *token_halves, *cot_halves, gain1, bias1)
    x, normed, normed_t, cot, cot_t = prepared
    for g in range(groups):
        project(g)
        flow.step(forward[g][2])
    atts = [f[1] for f in forward]
    middle, normed_ffn, normed_ffn_t = out_norm(
        out_piece, flow.me, x, gain2, bias2, atts, slabs["a"]
    )
    flow.step(normed_ffn)

    held = None
    sums_of = {}
    onto = []
    feed_names = ["a", "b"] + ["c"] * (subs - cut)
    for s in range(subs):
        mixed, grad_in, grads = feed_forward(
            feed_pieces[s],
            feed_outs[s],
            flow.me,
            normed_ffn,
            normed_ffn_t,
            cot,
            cot_t,
            held,
            middle if s == subs - 1 else None,
            slabs[feed_names[s]],
            onto,
        )
        held = (mixed, grad_in)
        onto = grads
        if s == 0 and rows.split:
            flow.add(fetch_whole, "c", slabs, [whole_c])
        if s % cut == cut - 1:
            k = s // cut
            if rows.split:
                flow.add(reduce_all, k, sums_of, grads)
            else:
                sums_of[k] = plain(*grads)
            onto = []
        flow.step(grad_in)
    grad_middle, branch_t, sums2, grad_atts = out_back(
        out_piece, groups, flow.me, middle, grad_in, cot, gain2, slabs["a"]
    )
    flow.step(sums2)
    grad_projs = []
    onto = []

    held = None
    qkv_slabs = [slabs["q0"]] + [slabs["q1"]] * (groups - 1)
    for g in range(groups):
        proj, att, lse = forward[g]
        held, grads, sums1 = attend_back(
            qkv_pieces[g],
            qkv_outs[g],
            flow.me,
            normed_t,
            proj,
            att,
            grad_atts[g],
            lse,
            seg_col,
            seg_row,
            qkv_slabs[g],
            branch_t,
            atts if g == 0 else [],
            held,
            x if g == groups - 1 else None,
            onto,
        )
        onto = grads
        if g == 0:
            if rows.split:
                flow.add(reduce_direct, "first", sums_of, grads)
            else:
                sums_of["first"] = plain(*grads)
            onto = []
        if g < groups - 1:
            flow.step(held)
    if rows.split:
        flow.add(direct, "last", sums_of, grads)
    else:
        sums_of["last"] = plain(*grads)
    held, sums1, sums2, mixed = flow.step(held, sums1, sums2, mixed)
    sums = jnp.concatenate([sums1[:2], sums2[:2]], 0)
    away = swap(sums)
    start_late, _ = tie(back, flow.me)
    tokens_own, tokens_other = norm_back(start_late, x, held, grad_middle, gain1)
    tokens_own, tokens_other, mixed, sums, away = flow.step(
        tokens_own, tokens_other, mixed, sums, away
    )
    sums = sums + away
    if rows.split:
        keep, send = split_far(flow.me, [sums_of["last"]])
        near = hop(send, 4, dp_count)
        away = [hop(sums, m, dp_count) for m in MASKS[1:]]
        sums = (sums + away[0]) + (away[1] + away[2])
        mixed, _ = tie(mixed, away[0])
        mixed_own, mixed_other = turn_back(back, mixed)
        far_sum = hop(low_sum([keep[1], near[1]]).astype(BF), 8, dp_count)
        last_sum = low_sum([keep[0], near[0], far_sum])
        while flow.active:
            flow.step()
        last_sum = jnp.concatenate([sums_of["first"], last_sum], -1)
        away = [hop(sums, rows.near * m, dp_count) for m in range(1, rows.far)]
        norm_sums = (sums + away[0]) + (away[1] + away[2])
        feed_sums = [sums_of[0], sums_of[1]]
    else:
        mixed_own, mixed_other = turn_back(back, mixed)
        last_sum = jnp.concatenate([sums_of["first"], sums_of["last"]], -1)
        feed_sums = [sums_of[0], sums_of[1]]
        norm_sums = jnp.sum(lax.all_gather(sums, "dp", axis=0), 0)
    feed_list = []
    for value in feed_sums:
        feed_list += [value[:, wide * s : wide * (s + 1)] for s in range(cut)]
    qkv_list = [last_sum[:, part * (g + 1) : part * (g + 2)] for g in range(groups)]
    grad_out = last_sum[:, :part].T
    def place(own, other):
        other = swap(other)
        return jnp.stack([jnp.where(core == 0, own, other), jnp.where(core == 0, other, own)], 0)[:, None]

    grad_qkv = jnp.concatenate([r.reshape(-1, 3, 128) for r in qkv_list], 2)
    return (
        place(mixed_own, mixed_other),
        place(tokens_own, tokens_other),
        norm_sums[0],
        norm_sums[1],
        grad_qkv,
        grad_out,
        norm_sums[2],
        norm_sums[3],
        jnp.concatenate([r[:, :part] for r in feed_list], 1),
        jnp.concatenate([r[:, part:] for r in feed_list], 1).T,
    )


def solution(mesh):
    in_specs = (
        P(None, "dp", "mp", None),
        P(None, "dp", None),
        P(),
        P(),
        P("dp", None, "mp"),
        P("mp", "dp"),
        P(),
        P(),
        P("dp", "mp"),
        P("mp", "dp"),
        P(None, "dp", "mp", None),
    )
    out_specs = (
        P(None, "dp", "mp", None),
        P(None, "dp", "mp", None),
        P(),
        P(),
        P("dp", None, "mp"),
        P("mp", "dp"),
        P(),
        P(),
        P("dp", "mp"),
        P("mp", "dp"),
    )
    return jax.shard_map(
        on_device, mesh=mesh, in_specs=in_specs, out_specs=out_specs, check_vma=False
    )
```

```python
import functools
import math

import jax
import jax.numpy as jnp
from jax import lax
from jax.experimental import pallas as pl
from jax.experimental.pallas import tpu as pltpu
from jax.sharding import PartitionSpec as P

HD = 32
QB = 256
EPS = 1e-05
BF = jnp.bfloat16
F32 = jnp.float32
NEG = -1e30
SCALE = 1.0 / math.sqrt(HD)
LOG2E = math.log2(math.e)
C2 = SCALE * LOG2E
MIB = 1024 * 1024
SDS = jax.ShapeDtypeStruct


def nn(a, b):
    return lax.dot_general(a, b, (((1,), (0,)), ((), ())), preferred_element_type=F32)


def nt(a, b):
    return lax.dot_general(a, b, (((1,), (1,)), ((), ())), preferred_element_type=F32)


def params(mib):
    return pltpu.CompilerParams(vmem_limit_bytes=mib * MIB)


def in_hbm(values):
    return [pltpu.with_memory_space_constraint(v, pltpu.HBM) for v in values]


def in_vmem(values):
    return [pltpu.with_memory_space_constraint(v, pltpu.VMEM) for v in values]


def cost(gflop, mbytes):
    return pl.CostEstimate(flops=int(gflop * 1e9), bytes_accessed=int(mbytes * 1e6), transcendentals=0)


def any_spec():
    return pl.BlockSpec(memory_space=pl.ANY)


def smem_spec():
    return pl.BlockSpec(memory_space=pltpu.SMEM)


def vmem_spec():
    return pl.BlockSpec(memory_space=pltpu.VMEM)


def row_spec(width, rows=512):
    return pl.BlockSpec((rows, width), lambda r: (r, 0))


def column_spec(height, rows=512):
    return pl.BlockSpec((height, rows), lambda r: (0, r))


def whole_spec(shape):
    return pl.BlockSpec(shape, lambda r: tuple(0 for _ in shape))


MASKS = (0, 1, 2, 3)


class Rows:
    def __init__(self, dp_count, depth):
        self.dp_count = dp_count
        self.depth = depth
        self.split = (depth // dp_count) % 16 == 0 and dp_count == 16
        self.near = 4 if self.split else 1
        self.far = dp_count // 4 if self.split else 1
        self.block = depth // (self.near * self.far)
        self.shape = (self.far, self.near, self.block)


class Piece:
    def __init__(self, rows, kind, start=0, width=0, masks=MASKS):
        self.rows = rows
        self.masks = masks
        self.kind = kind if rows.split else "whole"
        self.start = start
        self.count = 2 * len(MASKS) if self.kind == "slabs" else 2
        if self.kind == "stack":
            self.shape = (len(MASKS), rows.far, rows.block, width)
        else:
            self.shape = rows.shape + (width,)


def piece_copies(piece, me, refs, moves, sem, outward):
    copies = []
    each = piece.count // 2
    for half, column, width, view in moves:
        cols = pl.ds(piece.start + column, width)
        if piece.kind == "whole":
            pairs = [(refs[half].at[:, :, :, cols], view)]
        else:
            pairs = []
            for k, mask in enumerate(piece.masks):
                ref = refs[half].at[k] if piece.kind == "stack" else refs[half * each + k]
                near = lax.bitwise_xor(lax.rem(me, 4), mask)
                pairs.append((ref.at[:, :, cols], view.at[:, near]))
        for outside, inside in pairs:
            if outward:
                copies.append(pltpu.make_async_copy(inside, outside, sem))
            else:
                copies.append(pltpu.make_async_copy(outside, inside, sem))
    return copies


def start_all(copies):
    for copy in copies:
        copy.start()


def wait_bytes(ref, sem):
    pltpu.make_async_copy(ref, ref, sem).wait()


def flat(value):
    return value.reshape(-1, value.shape[-1])


def head_row(h):
    return lax.broadcasted_iota(jnp.int32, (1, 128), 1) // HD == h


def fill_bias(bias, seg_col, seg_row):
    key = lax.broadcasted_iota(jnp.int32, (QB, QB), 0)
    query = lax.broadcasted_iota(jnp.int32, (QB, QB), 1)
    bias[0] = jnp.where(query >= key, 0.0, NEG)
    bias[1] = jnp.where((query >= key) & (seg_col[...] == seg_row[...]), 0.0, NEG)


def fill_double(double, halves):
    here = halves[0].shape[0]
    for k in range(4):
        double[k * here : (k + 1) * here, :] = halves[k % 2][...]


def turned(doubles, start, r):
    coarse = pl.multiple_of(start // 16 * 16 + r * QB, 16)
    fine = start % 16
    row = lax.broadcasted_iota(jnp.int32, (QB, QB + 16), 0)
    col = lax.broadcasted_iota(jnp.int32, (QB, QB + 16), 1)
    pick = jnp.where(col - row == fine, 1.0, 0.0).astype(BF)
    total = None
    for double in doubles:
        part = nn(pick, double[pl.ds(coarse, QB + 16), :])
        total = part if total is None else total + part
    return total


def norm_parts(values):
    centered = values - jnp.mean(values, axis=-1, keepdims=True)
    spread = jnp.mean(centered * centered, axis=-1, keepdims=True)
    root = lax.rsqrt(spread + EPS)
    return centered * root, root


def prepare_body(
    start,
    own,
    other,
    cot_own,
    cot_other,
    gain,
    offset,
    x_out,
    normed,
    normed_t_out,
    cot,
    cot_t,
    double,
    x,
    normed_t,
    sems,
):
    fill_double(double, [own, other])

    def step(r, carry):
        at = pl.ds(pl.multiple_of(r * QB, QB), QB)
        value = turned([double], start[0], r)
        x[at, :] = value.astype(BF)
        hat, _ = norm_parts(value)
        low = (hat * gain[...] + offset[...]).astype(BF)
        normed[at, :] = low
        normed_t[:, at] = low.T
        return carry

    count = x.shape[0] // QB
    lax.fori_loop(0, count, step, 0)
    copies = [
        pltpu.make_async_copy(x, x_out, sems.at[0]),
        pltpu.make_async_copy(normed_t, normed_t_out, sems.at[1]),
    ]
    start_all(copies)
    fill_double(double, [cot_own, cot_other])

    def second(r, carry):
        at = pl.ds(pl.multiple_of(r * QB, QB), QB)
        low = turned([double], start[0], r).astype(BF)
        cot[at, :] = low
        cot_t[:, at] = low.T
        return carry

    lax.fori_loop(0, count, second, 0)
    for copy in copies:
        copy.wait()


def prepare(start, own, other, cot_own, cot_other, gain, offset):
    here, depth = own.shape
    shape, shape_t = (2 * here, depth), (depth, 2 * here)
    return pl.pallas_call(
        prepare_body,
        in_specs=[smem_spec()] + [vmem_spec()] * 6,
        out_specs=[any_spec(), vmem_spec(), any_spec(), vmem_spec(), vmem_spec()],
        out_shape=[
            pltpu.HBM(shape, BF),
            pltpu.VMEM(shape, BF),
            pltpu.HBM(shape_t, BF),
            pltpu.VMEM(shape, BF),
            pltpu.VMEM(shape_t, BF),
        ],
        scratch_shapes=[
            pltpu.VMEM((4 * here, depth), BF),
            pltpu.VMEM(shape, BF),
            pltpu.VMEM(shape_t, BF),
            pltpu.SemaphoreType.DMA((2,)),
        ],
        compiler_params=params(20),
        cost_estimate=cost(4, 8),
        name="prepare",
    )(start, own, other, cot_own, cot_other, gain, offset)


def turn_back_body(start, core, values, held, other, double, own, sem):
    here = other.shape[0]
    double[: 2 * here, :] = values[...]
    double[2 * here :, :] = values[...]
    count = here // QB

    def step(r, carry):
        at = pl.ds(pl.multiple_of(r * QB, QB), QB)
        own[at, :] = turned([double], start[0], r).astype(BF)
        other[at, :] = turned([double], start[0], r + count).astype(BF)
        return carry

    lax.fori_loop(0, count, step, 0)
    copy = pltpu.make_async_copy(own, held.at[core[0]], sem)
    copy.start()
    copy.wait()


def turn_back(start, core, values):
    length, depth = values.shape
    half = (length // 2, depth)
    return pl.pallas_call(
        turn_back_body,
        in_specs=[smem_spec()] * 2 + [vmem_spec()],
        out_specs=[any_spec(), vmem_spec()],
        out_shape=[pltpu.HBM((2,) + half, BF), SDS(half, BF)],
        scratch_shapes=[
            pltpu.VMEM((2 * length, depth), BF),
            pltpu.VMEM(half, BF),
            pltpu.SemaphoreType.DMA,
        ],
        compiler_params=params(16),
        cost_estimate=cost(2, 4),
        name="turn_back",
    )(start, core, values)


def arrange_body(widths, me, *refs):
    pieces, outs = refs[:4], refs[4:]
    far = me[0] // 4
    for m, piece in enumerate(pieces):
        begin = 0
        for out, width in zip(outs, widths):
            out[lax.bitwise_xor(far, m)] = piece[:, begin : begin + width]
            begin += width


def arrange(rows, me, pieces, widths):
    return pl.pallas_call(
        functools.partial(arrange_body, widths),
        in_specs=[smem_spec()] + [vmem_spec()] * 4,
        out_specs=[vmem_spec()] * len(widths),
        out_shape=[SDS((rows.far, rows.block, w), BF) for w in widths],
        compiler_params=params(8),
        cost_estimate=cost(1, 1),
        name="arrange",
    )(me, *pieces)


def project_attend_body(piece, me, normed, seg_col, seg_row, *refs):
    slabs = refs[: piece.count]
    proj_out, att, lse, weight, proj, bias, keys_m, values_t, att_t, sem, out_sem = refs[piece.count :]
    moves = [(half, 0, 384, weight.at[:, :, :, pl.ds(384 * half, 384)]) for half in range(2)]
    start_all(piece_copies(piece, me[0], slabs, moves, sem, False))
    fill_bias(bias, seg_col, seg_row)
    values_t[...] = jnp.ones_like(values_t)
    wait_bytes(weight, sem)
    length = normed.shape[0]

    def project(r, carry):
        at = pl.ds(pl.multiple_of(r * 512, 512), 512)
        proj[at, :] = nn(normed[at, :], flat(weight[...])).astype(BF)
        return carry

    lax.fori_loop(0, length // 512, project, 0)
    proj_copy = pltpu.make_async_copy(proj, proj_out, out_sem)
    proj_copy.start()
    for half in range(2):
        flipped = proj[:, half * 384 + 256 : half * 384 + 384].T
        for h in range(4):
            values_t[half * 4 + h, 0:HD, :] = flipped[h * HD : (h + 1) * HD]

    units = [(h, i) for i in (2, 1, 0, 3) for h in range(4)]

    def step(half, carry):
        col = pl.multiple_of(half * 384, 128)
        for h in range(4):
            keys_m[h] = jnp.where(head_row(h), proj[:, pl.ds(col + 128, 128)], 0)

        def score(h, i):
            first = 768 if i == 3 else 0
            scores = nt(keys_m[h, first : (i + 1) * QB, :], proj[i * QB : (i + 1) * QB, pl.ds(col, 128)])
            edge = scores[-QB:] + bias[1 if i == 3 else 0]
            return jnp.concatenate([scores[:-QB], edge], 0) if scores.shape[0] > QB else edge

        ahead = score(*units[0])
        for k, (h, i) in enumerate(units):
            scores = ahead
            if k + 1 < len(units):
                ahead = score(*units[k + 1])
            first = 768 if i == 3 else 0
            last = (i + 1) * QB
            at = slice(i * QB, last)
            peak = jnp.max(scores, axis=0, keepdims=True) * C2
            probs = jnp.exp2(scores * C2 - peak).astype(BF)
            summed = nn(values_t[half * 4 + h, :, first:last], probs)
            total = summed[HD : HD + 1]
            att_t[pl.ds(pl.multiple_of(half * 128 + h * HD, HD), HD), at] = summed[:HD] / total
            lse[pl.ds(half * 4 + h, 1), at] = peak + jnp.log2(total)
        return carry

    lax.fori_loop(0, 2, step, 0)
    for half in range(2):
        cols = slice(half * 128, half * 128 + 128)
        att[:, cols] = att_t[cols, :].T.astype(BF)
    proj_copy.wait()


def project_attend(piece, me, normed, seg_col, seg_row, slabs):
    length, depth = normed.shape
    rows = piece.rows
    return pl.pallas_call(
        functools.partial(project_attend_body, piece),
        in_specs=[smem_spec()] + [vmem_spec()] * 3 + [any_spec()] * len(slabs),
        out_specs=[any_spec()] + [vmem_spec()] * 2,
        out_shape=[
            pltpu.HBM((length, 768), BF),
            pltpu.HBM((length, 256), BF),
            pltpu.HBM((8, length), F32),
        ],
        scratch_shapes=[
            pltpu.VMEM(rows.shape + (768,), BF),
            pltpu.VMEM((length, 768), BF),
            pltpu.VMEM((2, QB, QB), F32),
            pltpu.VMEM((4, length, 128), BF),
            pltpu.VMEM((8, HD + 16, length), BF),
            pltpu.VMEM((256, length), F32),
            pltpu.SemaphoreType.DMA,
            pltpu.SemaphoreType.DMA,
        ],
        compiler_params=params(20),
        cost_estimate=cost(8, 8),
        name="project_attend",
    )(me, *in_vmem([normed]), seg_col, seg_row, *in_hbm(slabs))


def join_heads(attended):
    return jnp.concatenate([a[:, :128] for a in attended] + [a[:, 128:] for a in attended], 1)


def out_norm_body(piece, groups, me, tokens, gain, offset, *refs):
    attended = refs[:groups]
    slabs = refs[groups : groups + piece.count]
    middle, normed, normed_t, weight, sem = refs[groups + piece.count :]
    width = weight.shape[3] // 2

    @pl.when(pl.program_id(0) == 0)
    def _():
        moves = [(half, 0, width, weight.at[:, :, :, pl.ds(width * half, width)]) for half in range(2)]
        start_all(piece_copies(piece, me[0], slabs, moves, sem, False))
        wait_bytes(weight, sem)

    value = tokens[...].astype(F32) + nt(join_heads([a[...] for a in attended]), flat(weight[...]))
    middle[...] = value
    hat, _ = norm_parts(value)
    low = (hat * gain[...] + offset[...]).astype(BF)
    normed[...] = low
    normed_t[...] = low.T


def out_norm(piece, me, tokens, gain, offset, attended, slabs):
    length, depth = tokens.shape
    return pl.pallas_call(
        functools.partial(out_norm_body, piece, len(attended)),
        grid=(length // 512,),
        in_specs=[smem_spec(), row_spec(depth), whole_spec((1, depth)), whole_spec((1, depth))]
        + [row_spec(256)] * len(attended)
        + [any_spec()] * len(slabs),
        out_specs=[row_spec(depth)] * 2 + [column_spec(depth)],
        out_shape=[
            pltpu.HBM((length, depth), F32),
            pltpu.VMEM((length, depth), BF),
            pltpu.VMEM((depth, length), BF),
        ],
        scratch_shapes=[pltpu.VMEM(piece.rows.shape + (depth,), BF), pltpu.SemaphoreType.DMA],
        compiler_params=params(28),
        cost_estimate=cost(3, 8),
        name="out_norm",
    )(me, *in_hbm([tokens]), gain, offset, *in_hbm(attended), *in_hbm(slabs))


def gelu_parts(values):
    size = jnp.abs(values)
    density = jnp.exp2(values * values * (-0.5 * LOG2E) + math.log2(1.0 / math.sqrt(2 * math.pi)))
    t = 1.0 / (1.0 + 0.2316419 * size)
    poly = t * (
        0.319381530
        + t * (-0.356563782 + t * (1.781477937 + t * (-1.821255978 + t * 1.330274429)))
    )
    tail = density * poly
    below = jnp.where(values >= 0, 1.0 - tail, tail)
    return values * below, below + values * density


def feed_forward_body(piece, out_piece, first, final, aliased, me, normed, normed_t, cot, cot_t, *refs):
    refs = list(refs)
    held = [] if first else [refs.pop(0), refs.pop(0)]
    middle = refs.pop(0) if final else None
    slabs, refs = refs[: piece.count], refs[piece.count + aliased :]
    mixed, grad_in = refs[:2]
    outs, refs = refs[2:4], refs[4:]
    weight, staged, act, grad_hidden, mixed_acc, grad_acc, sems = refs[:7]
    mixed_low, middle_here = refs[7:] if final else (None, None)
    length, depth = normed.shape
    moves = []
    for half in range(2):
        for which in range(2):
            at = pl.ds(which * 768 + half * 384, 384)
            moves.append((half, which * 384, 384, at))
    into = [(h, c, w, weight.at[:, :, :, at]) for h, c, w, at in moves]
    outof = [(h, c, w, staged.at[:, :, :, at]) for h, c, w, at in moves]
    start_all(piece_copies(piece, me[0], slabs, into, sems.at[0], False))
    held_copies = []
    if not first:
        held_copies.append(pltpu.make_async_copy(held[0], mixed_acc, sems.at[1]))
        held_copies.append(pltpu.make_async_copy(held[1], grad_acc, sems.at[2]))
    if final:
        held_copies.append(pltpu.make_async_copy(middle, middle_here, sems.at[4]))
    start_all(held_copies)
    wait_bytes(weight, sems.at[0])
    chunks = [slice(c * 256, c * 256 + 256) for c in range(3)]

    def products(c):
        hidden = nn(normed[...], flat(weight[:, :, :, c * 256 : c * 256 + 256]))
        return hidden, nn(cot[...], flat(weight[:, :, :, 768 + c * 256 : 1024 + c * 256]))

    ahead = products(0)
    for c in range(3):
        hidden, grad_act = ahead
        if c < 2:
            ahead = products(c + 1)
        value, slope = gelu_parts(hidden)
        act[:, chunks[c]] = value.astype(BF)
        grad_hidden[:, chunks[c]] = (grad_act * slope).astype(BF)
    for copy in held_copies:
        copy.wait()
    for cols in chunks:
        mixed_part = nt(act[...], flat(weight[:, :, :, 768:1536])[cols])
        grad_part = nt(grad_hidden[...], flat(weight[:, :, :, 0:768])[cols])
        if not first:
            mixed_part = mixed_part + mixed_acc[:, cols]
            grad_part = grad_part + grad_acc[:, cols]
        if final:
            mixed_low[:, cols] = (middle_here[:, cols] + mixed_part).astype(BF)
        else:
            mixed_acc[:, cols] = mixed_part
        grad_acc[:, cols] = grad_part
    out_copies = [
        pltpu.make_async_copy(mixed_low if final else mixed_acc, mixed, sems.at[1]),
        pltpu.make_async_copy(grad_acc, grad_in, sems.at[2]),
    ]
    start_all(out_copies)
    for c in range(3):
        cols = slice(c * 256, c * 256 + 256)
        up = nn(normed_t[...], grad_hidden[:, cols]).astype(BF)
        staged[:, :, :, cols] = up.reshape(staged.shape[:3] + (256,))
        down = nn(cot_t[...], act[:, cols]).astype(BF)
        staged[:, :, :, 768 + c * 256 : 1024 + c * 256] = down.reshape(staged.shape[:3] + (256,))
    start_all(piece_copies(out_piece, me[0], outs, outof, sems.at[3], True))
    for copy in out_copies:
        copy.wait()
    wait_bytes(staged, sems.at[3])


def feed_forward(piece, out_piece, me, normed, normed_t, cot, cot_t, held, middle, slabs, onto):
    length, depth = normed.shape
    rows = piece.rows
    first, final = held is None, middle is not None
    ins = [me] + in_vmem([normed, normed_t, cot, cot_t]) + ([] if first else in_hbm(held))
    specs = [smem_spec()] + [vmem_spec()] * 4 + [any_spec()] * (0 if first else 2)
    if final:
        ins += in_hbm([middle])
        specs.append(any_spec())
    scratch = [
        pltpu.VMEM(rows.shape + (1536,), BF),
        pltpu.VMEM(rows.shape + (1536,), BF),
        pltpu.VMEM((length, 768), BF),
        pltpu.VMEM((length, 768), BF),
        pltpu.VMEM((length, depth), F32),
        pltpu.VMEM((length, depth), F32),
        pltpu.SemaphoreType.DMA((5,)),
    ]
    if final:
        scratch += [pltpu.VMEM((length, depth), BF), pltpu.VMEM((length, depth), F32)]
    got = pl.pallas_call(
        functools.partial(feed_forward_body, piece, out_piece, first, final, len(onto)),
        in_specs=specs + [any_spec()] * (piece.count + len(onto)),
        out_specs=[any_spec()] * 4,
        out_shape=[pltpu.HBM((length, depth), BF if final else F32), pltpu.HBM((length, depth), F32)]
        + [pltpu.HBM(out_piece.shape, BF)] * 2,
        input_output_aliases={len(ins) + piece.count + k: 2 + k for k in range(len(onto))},
        scratch_shapes=scratch,
        compiler_params=params(40),
        cost_estimate=cost(11, 20),
        name="feed_forward",
    )(*ins, *in_hbm(slabs), *in_hbm(onto))
    return got[0], got[1], got[2:]


def norm_pull(grad, hat, root, gain):
    scaled = grad * gain
    first = jnp.mean(scaled, axis=-1, keepdims=True)
    second = jnp.mean(scaled * hat, axis=-1, keepdims=True)
    return root * (scaled - first - hat * second)


def add_sums(sums, grad, hat):
    @pl.when(pl.program_id(0) == 0)
    def _():
        sums[...] = jnp.zeros_like(sums)

    sums[0:1, :] += jnp.sum(grad * hat, axis=0, keepdims=True)
    sums[1:2, :] += jnp.sum(grad, axis=0, keepdims=True)


def out_back_body(piece, groups, me, middle, grad_in, cot, gain, *refs):
    slabs, refs = refs[: piece.count], refs[piece.count :]
    grad_middle, branch_t, sums = refs[:3]
    grad_att = refs[3 : 3 + groups]
    weight, sem = refs[3 + groups :]
    width = weight.shape[3] // 2

    @pl.when(pl.program_id(0) == 0)
    def _():
        moves = [(half, 0, width, weight.at[:, :, :, pl.ds(width * half, width)]) for half in range(2)]
        start_all(piece_copies(piece, me[0], slabs, moves, sem, False))
        wait_bytes(weight, sem)

    hat, root = norm_parts(middle[...])
    grad = grad_in[...]
    value = cot[...].astype(F32) + norm_pull(grad, hat, root, gain[...])
    grad_middle[...] = value
    low = value.astype(BF)
    branch_t[...] = low.T
    add_sums(sums, grad, hat)
    back = nn(low, flat(weight[...])).astype(BF)
    for g in range(groups):
        grad_att[g][:, 0:128] = back[:, g * 128 : g * 128 + 128]
        grad_att[g][:, 128:256] = back[:, width + g * 128 : width + g * 128 + 128]


def out_back(piece, groups, me, middle, grad_in, cot, gain, slabs):
    length, depth = middle.shape
    got = pl.pallas_call(
        functools.partial(out_back_body, piece, groups),
        grid=(length // 512,),
        in_specs=[smem_spec()] + [row_spec(depth)] * 3 + [whole_spec((1, depth))] + [any_spec()] * len(slabs),
        out_specs=[row_spec(depth), column_spec(depth), whole_spec((8, depth))] + [row_spec(256)] * groups,
        out_shape=[pltpu.HBM((length, depth), F32), pltpu.VMEM((depth, length), BF), SDS((8, depth), F32)]
        + [pltpu.HBM((length, 256), BF)] * groups,
        scratch_shapes=[pltpu.VMEM(piece.rows.shape + (depth,), BF), pltpu.SemaphoreType.DMA],
        compiler_params=params(28),
        cost_estimate=cost(4, 16),
        name="out_back",
    )(me, *in_hbm([middle, grad_in]), *in_vmem([cot]), gain, *in_hbm(slabs))
    return got[0], got[1], got[2], got[3:]


def attend_back_body(piece, out_piece, extra, aliased, final, me, normed_t_in, proj, att, grad_att, lse, seg_col, seg_row, *refs):
    refs = list(refs)
    slabs, refs = refs[: piece.count], refs[piece.count :]
    if extra:
        branch_t = refs.pop(0)
        attended, refs = refs[:extra], refs[extra:]
    else:
        held = refs.pop(0)
    if final:
        tokens_in = refs.pop(0)
    refs = refs[aliased:]
    grad_normed, outs, refs = refs[0], refs[1:3], refs[3:]
    if final:
        sums = refs.pop(0)
    grad_proj, key_sum, value_sum = refs[:3]
    refs = refs[3:]
    bias, delta, keys_t, query_t, query_m, grad_m, staged, normed_t, total, weight, sems = refs[:11]
    copies = [pltpu.make_async_copy(normed_t_in, normed_t, sems.at[1])]
    if not extra:
        copies.append(pltpu.make_async_copy(held, total, sems.at[2]))
    if final:
        copies.append(pltpu.make_async_copy(tokens_in, refs[11], sems.at[3]))
    moves = [(half, 0, 384, weight.at[:, :, :, pl.ds(384 * half, 384)]) for half in range(2)]
    start_all(copies + piece_copies(piece, me[0], slabs, moves, sems.at[4], False))
    length = proj.shape[0]
    fill_bias(bias, seg_col, seg_row)
    if extra:
        joined = join_heads([a[...] for a in attended])
        out_grad = nn(branch_t[...], joined).astype(BF)
        staged[:, :, :, 768:] = out_grad.reshape(staged.shape[:3] + (768,))
    for half in range(2):
        cols = slice(half * 128, half * 128 + 128)
        product = (grad_att[:, cols].astype(F32) * att[:, cols].astype(F32)).T
        for h in range(4):
            delta[half * 4 + h : half * 4 + h + 1, :] = jnp.sum(
                product[h * HD : (h + 1) * HD], axis=0, keepdims=True
            )
        keys_t[cols, :] = proj[:, half * 384 + 128 : half * 384 + 256].T

    def step(half, carry):
        col = pl.multiple_of(half * 384, 128)
        out = pl.multiple_of(half * 128, 128)
        for h in range(4):
            mine = head_row(h)
            query_m[h] = jnp.where(mine, proj[:, pl.ds(col, 128)], 0)
            grad_m[h] = jnp.where(mine, grad_att[:, pl.ds(out, 128)], 0)
        key_sum[...] = jnp.zeros_like(key_sum)
        value_sum[...] = jnp.zeros_like(value_sum)
        for i in (2, 1, 0, 3):
            first = 768 if i == 3 else 0
            last = (i + 1) * QB
            here = slice(first, last)
            there = slice(i * QB, last)
            keys = proj[here, pl.ds(col + 128, 128)]
            values = proj[here, pl.ds(col + 256, 128)]

            def products(h):
                scores = nt(keys, query_m[h, there, :])
                edge = scores[-QB:] + bias[1 if i == 3 else 0]
                if last - first > QB:
                    scores = jnp.concatenate([scores[:-QB], edge], 0)
                else:
                    scores = edge
                return scores, nt(values, grad_m[h, there, :])

            all_probs, all_grads = [], []
            ahead = products(0)
            for h in range(4):
                scores, grad_probs = ahead
                if h < 3:
                    ahead = products(h + 1)
                stat = pl.ds(half * 4 + h, 1)
                lanes = pl.ds(pl.multiple_of(half * 128 + h * HD, HD), HD)
                probs = jnp.exp2(scores * C2 - lse[stat, there])
                grad_scores = (probs * (grad_probs - delta[stat, there])).astype(BF)
                all_probs.append(probs.astype(BF))
                all_grads.append(grad_scores)
                query_t[lanes, there] = nn(keys_t[lanes, here], grad_scores)
            stacked = jnp.concatenate([grad_m[h, there, :] for h in range(4)], 0)
            value_sum[here, :] += nn(jnp.concatenate(all_probs, 1), stacked)
            stacked = jnp.concatenate([query_m[h, there, :] for h in range(4)], 0)
            key_sum[here, :] += nn(jnp.concatenate(all_grads, 1), stacked)
        grad_proj[:, pl.ds(col + 128, 128)] = (key_sum[...] * SCALE).astype(BF)
        grad_proj[:, pl.ds(col + 256, 128)] = value_sum[...].astype(BF)
        return carry

    lax.fori_loop(0, 2, step, 0)
    for half in range(2):
        grad_proj[:, half * 384 : half * 384 + 128] = (
            query_t[half * 128 : half * 128 + 128, :].T * SCALE
        ).astype(BF)
    for copy in copies:
        copy.wait()
    wait_bytes(weight, sems.at[4])
    for c in range(3):
        cols = slice(c * 256, c * 256 + 256)
        part = nn(normed_t[...], grad_proj[:, cols]).astype(BF)
        staged[:, :, :, cols] = part.reshape(staged.shape[:3] + (256,))
    moves = [(half, 0, 384, staged.at[:, :, :, pl.ds(384 * half, 384)]) for half in range(2)]
    if extra:
        moves += [
            (half, -384, 384, staged.at[:, :, :, pl.ds(768 + 384 * half, 384)]) for half in range(2)
        ]
    start_all(piece_copies(out_piece, me[0], outs, moves, sems.at[0], True))
    if final:
        sums[...] = jnp.zeros_like(sums)

    total_copies = []
    for c in range(3):
        cols = slice(c * 256, c * 256 + 256)
        value = nt(grad_proj[...], flat(weight[...])[cols])
        if not extra:
            value = value + total[:, cols]
        total[:, cols] = value
        total_copies.append(
            pltpu.make_async_copy(
                total.at[:, pl.ds(c * 256, 256)], grad_normed.at[:, pl.ds(c * 256, 256)], sems.at[2]
            )
        )
        total_copies[-1].start()
    if final:

        def sum_step(r, carry):
            at = pl.ds(pl.multiple_of(r * QB, QB), QB)
            value = total[at, :]
            hat, _ = norm_parts(refs[11][at, :].astype(F32))
            sums[0:1, :] += jnp.sum(value * hat, axis=0, keepdims=True)
            sums[1:2, :] += jnp.sum(value, axis=0, keepdims=True)
            return carry

        lax.fori_loop(0, length // QB, sum_step, 0)
    wait_bytes(staged, sems.at[0])
    wait_bytes(total, sems.at[2])


def attend_back(
    piece,
    out_piece,
    me,
    normed_t,
    proj,
    att,
    grad_att,
    lse,
    seg_col,
    seg_row,
    slabs,
    branch_t,
    attended,
    held,
    tokens,
    onto,
):
    depth, length = normed_t.shape
    extra = len(attended)
    final = tokens is not None
    columns = 1536 if extra else 768
    ins = [me] + in_hbm([normed_t, proj, att, grad_att, lse]) + [seg_col, seg_row] + in_hbm(slabs)
    specs = [smem_spec(), any_spec()] + [vmem_spec()] * 6 + [any_spec()] * len(slabs)
    if extra:
        ins += in_vmem([branch_t]) + in_hbm(attended)
        specs += [vmem_spec()] * (1 + extra)
    else:
        ins += in_hbm([held])
        specs += [any_spec()]
    if final:
        ins += in_hbm([tokens])
        specs += [any_spec()]
    outs = [pltpu.HBM((length, depth), F32)] + [pltpu.HBM(out_piece.shape, BF)] * 2
    scratch = [
        pltpu.VMEM((2, QB, QB), F32),
        pltpu.VMEM((8, length), F32),
        pltpu.VMEM((256, length), BF),
        pltpu.VMEM((256, length), F32),
        pltpu.VMEM((4, length, 128), BF),
        pltpu.VMEM((4, length, 128), BF),
        pltpu.VMEM(out_piece.rows.shape + (columns,), BF),
        pltpu.VMEM((depth, length), BF),
        pltpu.VMEM((length, depth), F32),
        pltpu.VMEM(piece.rows.shape + (768,), BF),
        pltpu.SemaphoreType.DMA((5,)),
    ]
    if final:
        outs.append(SDS((8, depth), F32))
        scratch.append(pltpu.VMEM((length, depth), BF))
    got = pl.pallas_call(
        functools.partial(attend_back_body, piece, out_piece, extra, len(onto), final),
        in_specs=specs + [any_spec()] * len(onto),
        out_specs=[any_spec()] * 3 + ([vmem_spec()] if final else []),
        out_shape=outs,
        input_output_aliases={len(ins) + k: 1 + k for k in range(len(onto))},
        scratch_shapes=[
            pltpu.VMEM((length, 768), BF),
            pltpu.VMEM((length, 128), F32),
            pltpu.VMEM((length, 128), F32),
        ]
        + scratch,
        compiler_params=params(40),
        cost_estimate=cost(12, 8),
        name="attend_back",
    )(*ins, *in_hbm(onto))
    return got[0], got[1:3], got[3] if final else None


def norm_back_body(
    start, core, tokens, grad_normed, grad_middle, gain, held, other, high, low, own, sem
):
    length = high.shape[0] // 2
    r = pl.program_id(0)
    hat, root = norm_parts(tokens[...].astype(F32))
    value = grad_middle[...] + norm_pull(grad_normed[...], hat, root, gain[...])
    top = value.astype(BF)
    rest = (value - top.astype(F32)).astype(BF)
    for base in (0, length):
        at = pl.ds(pl.multiple_of(base + r * QB, QB), QB)
        high[at, :] = top
        low[at, :] = rest

    @pl.when(r == pl.num_programs(0) - 1)
    def _():
        count = own.shape[0] // QB
        for k in range(count):
            own[k * QB : k * QB + QB, :] = turned([high, low], start[0], k)
        copy = pltpu.make_async_copy(own, held.at[core[0]], sem)
        copy.start()
        for k in range(count):
            other[k * QB : k * QB + QB, :] = turned([high, low], start[0], k + count)
        copy.wait()


def norm_back(start, core, tokens, grad_normed, grad_middle, gain):
    length, depth = tokens.shape
    half = (length // 2, depth)
    return pl.pallas_call(
        norm_back_body,
        grid=(length // QB,),
        in_specs=[smem_spec()] * 2 + [row_spec(depth, QB)] * 3 + [whole_spec((1, depth))],
        out_specs=[any_spec(), whole_spec(half)],
        out_shape=[pltpu.HBM((2,) + half, F32), SDS(half, F32)],
        scratch_shapes=[
            pltpu.VMEM((2 * length, depth), BF),
            pltpu.VMEM((2 * length, depth), BF),
            pltpu.VMEM(half, F32),
            pltpu.SemaphoreType.DMA,
        ],
        compiler_params=params(24),
        cost_estimate=cost(4, 16),
        name="norm_back",
    )(start, core, *in_hbm([tokens, grad_normed, grad_middle]), gain)


def split_far_body(counts, me, *refs):
    keep, send = refs[-2:]
    far = me[0] // 4
    begin = 0
    for count in counts:
        pieces, refs = refs[:count], refs[count:]
        cols = pl.ds(begin, pieces[0].shape[-1])
        begin += pieces[0].shape[-1]
        for k, out in enumerate((keep, send)):
            for slot in range(2):
                at = lax.bitwise_xor(far, k + 2 * slot)
                total = pieces[0][at].astype(F32)
                for piece in pieces[1:]:
                    total = total + piece[at].astype(F32)
                out[slot, :, cols] = total.astype(BF)


def split_far(me, groups):
    width, specs = 0, []
    for pieces in groups:
        far, block, columns = pieces[0].shape[-3:]
        width += columns
        for piece in pieces:
            if piece.ndim == 4:
                specs.append(pl.BlockSpec((None, far, block, columns), lambda i: (0, 0, 0, 0)))
            else:
                specs.append(whole_spec(piece.shape))
    return pl.pallas_call(
        functools.partial(split_far_body, [len(pieces) for pieces in groups]),
        grid=(1,),
        in_specs=[smem_spec()] + specs,
        out_specs=[whole_spec((2, block, width))] * 2,
        out_shape=[SDS((2, block, width), BF)] * 2,
        compiler_params=params(16),
        cost_estimate=cost(1, 2),
        name="split_far",
    )(me, *[piece for pieces in groups for piece in pieces])


def put_sums(ref, base, total):
    high = total.astype(BF)
    ref[base : base + 4, :] = high
    ref[base + 4 : base + 8, :] = (total - high.astype(F32)).astype(BF)
    ref[base + 8 : base + 16, :] = jnp.zeros((8, total.shape[1]), BF)


def get_sums(ref, base):
    return ref[base : base + 4, :].astype(F32) + ref[base + 4 : base + 8, :].astype(F32)


def last_join_body(own, other, sums, sums_away, *outs):
    total = sums[...] + sums_away[...]
    rows = outs[0].shape[0] - 16
    for k, out in enumerate(outs):
        value = own[k].astype(F32) + other[k].astype(F32)
        out[:rows, :] = value.astype(BF).reshape(rows, -1)
        put_sums(out, rows, total)


def last_split_body(me, m0, m1, m2, m3, keep, send):
    far = me[0] // 4
    rows = m0.shape[0] - 16
    block = rows // 4
    for k, out in enumerate((keep, send)):
        for slot in range(2):
            at = pl.ds(pl.multiple_of(lax.bitwise_xor(far, k + 2 * slot) * block, 16), block)
            total = (m0[at, :].astype(F32) + m1[at, :].astype(F32)) + (
                m2[at, :].astype(F32) + m3[at, :].astype(F32)
            )
            out[slot * block : (slot + 1) * block, :] = total.astype(BF)
    total = (get_sums(m0, rows) + get_sums(m1, rows)) + (get_sums(m2, rows) + get_sums(m3, rows))
    put_sums(keep, 2 * block, total)
    put_sums(send, 2 * block, total)


def last_middle_body(keep, near, rest, send):
    block = (keep.shape[0] - 16) // 2
    value = keep[:block, :].astype(F32) + near[:block, :].astype(F32)
    rest[:block, :] = value.astype(BF)
    value = keep[block : 2 * block, :].astype(F32) + near[block : 2 * block, :].astype(F32)
    send[:block, :] = value.astype(BF)
    total = get_sums(keep, 2 * block) + get_sums(near, 2 * block)
    put_sums(rest, block, total)
    put_sums(send, block, total)


def last_sum_body(rest, away, first, grad_qkv, sums):
    block = rest.shape[0] - 16
    value = rest[:block, :].astype(F32) + away[:block, :].astype(F32)
    parts = [first[:, 384:], value[:, :384], value[:, 384:]]
    for which in range(3):
        cols = slice(which * 128, which * 128 + 128)
        grad_qkv[which] = jnp.concatenate([part[:, cols] for part in parts], 1)
    sums[...] = get_sums(rest, block) + get_sums(away, block)


def pack_body(part, out, up, down, packed):
    width = out.shape[1]
    packed[:, :width] = out[...]
    for s in range(up.shape[1] // part):
        cols = slice(s * part, (s + 1) * part)
        packed[:, width + 2 * s * part : width + (2 * s + 1) * part] = up[:, cols]
        packed[:, width + (2 * s + 1) * part : width + (2 * s + 2) * part] = down[:, cols]


def small_call(body, name, outs, scalars, values):
    return pl.pallas_call(
        body,
        in_specs=[smem_spec()] * len(scalars) + [vmem_spec()] * len(values),
        out_specs=[vmem_spec()] * len(outs),
        out_shape=outs,
        compiler_params=params(16),
        cost_estimate=cost(1, 3),
        name=name,
    )(*scalars, *values)


def swap(value):
    return lax.ppermute(value, "mp", [(0, 1), (1, 0)])


def tie(*values):
    return lax.optimization_barrier(values)


def hop(value, mask, count):
    return lax.ppermute(value, "dp", [(i, i ^ mask) for i in range(count)])


def hops(value, masks, count):
    return [(value, functools.partial(hop, mask=m, count=count)) for m in masks]


def far_hops(rows, values):
    return [
        (v, functools.partial(hop, mask=rows.near * m, count=rows.dp_count))
        for m, v in zip(range(1, rows.far), values)
    ]


def swaps(values):
    return [(v, swap) for v in values]


def send_all(requests):
    return [send(value) for value, send in requests]


def low_sum(values):
    total = values[0].astype(F32)
    for value in values[1:]:
        total = total + value.astype(F32)
    return total


class Flow:
    def __init__(self, me):
        self.me = me
        self.active = []

    def add(self, transfer, name, results, seeds=()):
        self.active.append([transfer, list(seeds), name, results])

    def step(self, *pivots):
        values = [v for item in self.active for v in item[1]]
        tied = list(tie(self.me, *pivots, *values))
        self.me = tied.pop(0)
        pivots, tied = tied[: len(pivots)], tied[len(pivots) :]
        going, self.active, requests = self.active, [], []
        for item in going:
            transfer, values, name, results = item
            got, tied = tied[: len(values)], tied[len(values) :]
            try:
                if callable(transfer):
                    item[0] = transfer(*got)
                    asked = next(item[0])
                else:
                    asked = transfer.send(got)
                self.active.append(item)
                requests.append(asked)
            except StopIteration as stop:
                results[name] = stop.value
        tied = list(tie(self.me, *(operand for asked in requests for operand, _ in asked)))
        self.me = tied.pop(0)
        for item, asked in zip(self.active, requests):
            item[1] = [send(operand) for (_, send), operand in zip(asked, tied)]
            tied = tied[len(asked) :]
        return pivots


def add_low(a, b):
    return (a.astype(F32) + b.astype(F32)).astype(BF)


def on_device(
    tokens, segment, ln1_gain, ln1_bias, w_qkv, w_out, ln2_gain, ln2_bias, w_up, w_down, cotangent
):
    dp_count = lax.axis_size("dp")
    core = lax.axis_index("mp")
    me = lax.axis_index("dp").astype(jnp.int32).reshape(1)
    here, depth = tokens.shape[2], tokens.shape[3]
    length = 2 * here
    rows = Rows(dp_count, depth)

    groups = w_qkv.shape[2] // 128
    part = 384
    subs = w_up.shape[1] // part
    cut = subs // 2
    qkv = [w_qkv[:, :, g * 128 : (g + 1) * 128].reshape(-1, part) for g in range(groups)]
    shards = {"q": jnp.concatenate(qkv, 1)}

    shard_a = small_call(
        functools.partial(pack_body, part),
        "pack",
        [SDS((w_up.shape[0], w_out.shape[0] + 2 * w_up.shape[1]), BF)],
        [],
        [w_out.T, w_up, w_down.T],
    )[0]

    def halves(values):
        own = lax.dynamic_index_in_dim(values[:, 0], core, 0, keepdims=False)
        away = lax.dynamic_index_in_dim(values[:, 0], 1 - core, 0, keepdims=False)
        return own, swap(away)

    seg = lax.dynamic_index_in_dim(segment[:, 0], core, 0, keepdims=False)
    run = length * 3 // 4
    begin = jnp.argmax(seg[: length - run + 1] == seg[run - 1 :]).astype(jnp.int32)
    start = ((begin - here * core) % length).reshape(1)
    back = (length - start) % length
    seg_tail = lax.dynamic_slice_in_dim(jnp.concatenate([seg, seg]), begin + run, length - run)
    seg_col = seg_tail.reshape(-1, 1)
    seg_row = seg_tail.reshape(1, -1)
    gain1, bias1, gain2, bias2 = (
        v.reshape(1, -1) for v in (ln1_gain, ln1_bias, ln2_gain, ln2_bias)
    )

    flow = Flow(me)
    token_halves = halves(tokens)
    cot_halves = halves(cotangent)
    wide = 2 * part
    qkv_pieces = [Piece(rows, "slabs")] + [Piece(rows, "slabs", part * g) for g in range(groups - 1)]
    out_piece = Piece(rows, "slabs")
    feed_pieces = [Piece(rows, "slabs", part + wide * s) for s in range(cut)]
    feed_pieces += [Piece(rows, "slabs", wide * s) for s in range(subs - cut)]
    turns = [(0, 2, 1, 3), MASKS]
    feed_outs = [
        Piece(rows, "stack", wide * (s % cut), wide * cut, turns[s % cut]) for s in range(subs)
    ]
    qkv_outs = [Piece(rows, "stack", part, wide)]
    qkv_outs += [Piece(rows, "stack", part * g, part * (groups - 1)) for g in range(groups - 1)]
    far = lax.axis_index("dp") // rows.near

    def gather_whole(shard):
        return lax.all_gather(shard, "dp", axis=0, tiled=True).reshape(rows.shape + (-1,))

    def fetch_near(near):
        got = yield hops(near, MASKS[1:], dp_count)
        own = [near] + got
        return own + [swap(x) for x in own]

    def via(mask):
        return functools.partial(hop, mask=mask, count=dp_count)

    def fetch_wide(widths, shard, near, away):
        (both_ways,) = yield [(away, via(4))]
        a0, c0 = arrange(rows, flow.me, [shard, near, away, both_ways], widths)
        a1, a2, b0 = yield [(a0, via(1)), (a0, via(2))] + swaps([a0])
        a3, c1, b1, b2, d0 = yield [(a1, via(2)), (c0, via(1))] + swaps([a1, a2, c0])
        slabs["a"] = [a0, a1, a2, a3, b0, b1, b2, swap(a3)]
        c2, d1 = yield [(c0, via(2))] + swaps([c1])
        c3, d2 = yield [(c2, via(1))] + swaps([c2])
        return [c0, c1, c2, c3, d0, d1, d2, swap(c3)]

    def whole(shard):
        own = gather_whole(shard)
        return [own, swap(own)]

    def halve(own, other):
        (other,) = yield swaps([other])
        middle_col = own.shape[-1] // 2
        keep, send = [], []
        for cols in (slice(0, middle_col), slice(middle_col, None)):
            keep.append(low_sum([own[:2, ..., cols], other[:2, ..., cols]]).astype(BF))
            send.append(low_sum([own[2:, ..., cols], other[2:, ..., cols]]).astype(BF))
        near = yield [(v, via(m)) for v, m in zip(send, (1, 2))]
        send = [low_sum([k[1], n[1]]).astype(BF) for k, n in zip(keep, near)]
        away = yield [(v, via(m)) for v, m in zip(send, (2, 1))]
        return [list(group) for group in zip(keep, near, away)]

    def direct(mine):
        got = yield hops_of(mine, (1, 2, 3))
        return [mine[0]] + got

    def hops_of(values, masks):
        return [(values[m], via(m)) for m in masks]

    def reduce_far(groups):
        keep, send = split_far(flow.me, groups)
        (near,) = yield [(send, via(4))]
        (away,) = yield [(low_sum([keep[1], near[1]]).astype(BF), via(8))]
        return low_sum([keep[0], near[0], away])

    def reduce_all(own, other):
        groups_here = yield from halve(own, other)
        return (yield from reduce_far(sums_of["early"] + groups_here))

    def reduce_last(own, other, sums):
        other, sums_away = swap(other), swap(sums)
        mine = small_call(
            last_join_body,
            "last_join",
            [SDS((rows.far * rows.block + 16, wide), BF)] * 4,
            [],
            [own, other, sums, sums_away],
        )
        return (yield from direct(mine))

    def exchange(value):
        (got,) = yield swaps([value])
        return got

    def reduce_direct(own, other):
        (other,) = yield swaps([other])
        mine = [low_sum([own[k], other[k]]).astype(BF) for k in range(4)]
        pieces = yield from direct(mine)
        return (yield from reduce_far([pieces]))

    def plain(own, other):
        value = low_sum([own, swap(other)]).astype(BF).reshape(depth, -1)
        return lax.psum_scatter(value, "dp", scatter_dimension=0, tiled=True).astype(F32)

    def run(transfer):
        requests = next(transfer)
        while True:
            try:
                requests = transfer.send(send_all(requests))
            except StopIteration as stop:
                return stop.value

    slabs, forward = {}, []

    def project(g):
        name = "q0" if g == 0 else "q1"
        forward.append(
            project_attend(qkv_pieces[g], flow.me, normed, seg_col, seg_row, slabs[name])
        )

    if rows.split:
        tied = tie(shards["q"], *token_halves, *cot_halves)
        shard_q, token_halves, cot_halves = tied[0], tied[1:3], tied[3:]
        got = send_all(far_hops(rows, [shard_q] * (rows.far - 1)))
        prepared = prepare(start, *token_halves, *cot_halves, gain1, bias1)
        tied = tie(*got, *prepared, shard_a)
        got, prepared, shard_a = tied[:3], tied[3:8], tied[8]
        near_q0, near_q1 = arrange(rows, me, [shard_q] + list(got), [part, wide])
        own = [near_q0] + [hop(near_q0, m, dp_count) for m in MASKS[1:]]
        away_a = [hop(shard_a, m, dp_count) for m in (4, 8)]
        slabs["q0"] = own + [swap(v) for v in own]
        flow.add(fetch_near, "q1", slabs, [near_q1])
        flow.add(
            functools.partial(fetch_wide, [part + wide * cut, wide * (subs - cut)]),
            "c",
            slabs,
            [shard_a] + away_a,
        )
        flow.step(own[3])
    else:
        for name, shard in (
            ("q0", shards["q"][:, :part]),
            ("q1", shards["q"][:, part:]),
            ("a", shard_a[:, : part + wide * cut]),
            ("c", shard_a[:, part + wide * cut :]),
        ):
            slabs[name] = whole(shard)
        prepared = prepare(start, *token_halves, *cot_halves, gain1, bias1)
    x, normed, normed_t, cot, cot_t = prepared
    for g in range(groups):
        project(g)
        flow.step(forward[g][2])
    atts = [f[1] for f in forward]
    middle, normed_ffn, normed_ffn_t = out_norm(
        out_piece, flow.me, x, gain2, bias2, atts, slabs["a"]
    )
    flow.step(normed_ffn)

    held = None
    sums_of = {}
    onto = []
    feed_names = ["a"] * cut + ["c"] * (subs - cut)
    for s in range(subs):
        mixed, grad_in, grads = feed_forward(
            feed_pieces[s],
            feed_outs[s],
            flow.me,
            normed_ffn,
            normed_ffn_t,
            cot,
            cot_t,
            held,
            middle if s == subs - 1 else None,
            slabs[feed_names[s]],
            onto,
        )
        held = (mixed, grad_in)
        onto = grads
        if s % cut == cut - 1:
            k = s // cut
            if rows.split and k == 0:
                flow.add(halve, "early", sums_of, grads)
            elif rows.split:
                flow.add(reduce_all, "feed", sums_of, grads)
            else:
                sums_of[k] = plain(*grads)
            onto = []
        flow.step(grad_in)
    grad_middle, branch_t, sums2, grad_atts = out_back(
        out_piece, groups, flow.me, middle, grad_in, cot, gain2, slabs["a"]
    )
    mixed, core_place, _ = flow.step(mixed, core.astype(jnp.int32).reshape(1), sums2)
    mixed_held, mixed_other = turn_back(back, core_place, mixed)
    flow.add(exchange, "mixed", sums_of, [mixed_other])
    grad_projs = []
    onto = []

    held = None
    qkv_slabs = [slabs["q0"]] + [slabs["q1"]] * (groups - 1)
    for g in range(groups):
        proj, att, lse = forward[g]
        held, grads, sums1 = attend_back(
            qkv_pieces[g],
            qkv_outs[g],
            flow.me,
            normed_t,
            proj,
            att,
            grad_atts[g],
            lse,
            seg_col,
            seg_row,
            qkv_slabs[g],
            branch_t,
            atts if g == 0 else [],
            held,
            x if g == groups - 1 else None,
            onto,
        )
        onto = grads
        if g == 0:
            if rows.split:
                flow.add(reduce_direct, "first", sums_of, grads)
            else:
                sums_of["first"] = plain(*grads)
            onto = []
        if g < groups - 1:
            flow.step(held)
    sums = jnp.concatenate([sums1[:2], sums2[:2]], 0)
    if rows.split:
        flow.add(reduce_last, "last", sums_of, [*grads, sums])
        (held,) = flow.step(held)
    else:
        sums_of["last"] = plain(*grads)
    start_late, _ = tie(back, flow.me)
    tokens_held, tokens_other = norm_back(start_late, core_place, x, held, grad_middle, gain1)
    tokens_held, tokens_other = flow.step(tokens_held, tokens_other)
    if rows.split:
        block = rows.block
        keep, send = small_call(
            last_split_body,
            "last_split",
            [SDS((2 * block + 16, wide), BF)] * 2,
            [flow.me],
            sums_of["last"],
        )
        near = hop(send, 4, dp_count)
        rest, send = small_call(
            last_middle_body, "last_middle", [SDS((block + 16, wide), BF)] * 2, [], [keep, near]
        )
        away = hop(send, 8, dp_count)
        while flow.active:
            flow.step()
        grad_qkv, norm_sums = small_call(
            last_sum_body,
            "last_sum",
            [SDS((3, block, part), F32), SDS((4, depth), F32)],
            [],
            [rest, away, sums_of["first"]],
        )
        grad_qkv = grad_qkv.transpose(1, 0, 2)
        grad_out = sums_of["first"][:, :part].T
        feed_sums = [sums_of["feed"]]
    else:
        early, last = sums_of["first"], sums_of["last"]
        parts = [early[:, part:], last[:, :part], last[:, part:]]
        grad_qkv = jnp.concatenate([r.reshape(-1, 3, 128) for r in parts], 2)
        grad_out = early[:, :part].T
        feed_sums = [sums_of[0], sums_of[1]]
        norm_sums = jnp.sum(lax.all_gather(sums + swap(sums), "dp", axis=0), 0)
    feed_sum = jnp.concatenate(feed_sums, 1) if len(feed_sums) > 1 else feed_sums[0]
    feed_list = [feed_sum[:, wide * s : wide * (s + 1)] for s in range(subs)]

    def place(values, other):
        return lax.dynamic_update_index_in_dim(values, other, 1 - core, 0)[:, None]

    return (
        place(mixed_held, sums_of["mixed"]),
        place(tokens_held, swap(tokens_other)),
        norm_sums[0],
        norm_sums[1],
        grad_qkv,
        grad_out,
        norm_sums[2],
        norm_sums[3],
        jnp.concatenate([r[:, :part] for r in feed_list], 1),
        jnp.concatenate([r[:, part:] for r in feed_list], 1).T,
    )


def solution(mesh):
    in_specs = (
        P(None, "dp", "mp", None),
        P(None, "dp", None),
        P(),
        P(),
        P("dp", None, "mp"),
        P("mp", "dp"),
        P(),
        P(),
        P("dp", "mp"),
        P("mp", "dp"),
        P(None, "dp", "mp", None),
    )
    out_specs = (
        P(None, "dp", "mp", None),
        P(None, "dp", "mp", None),
        P(),
        P(),
        P("dp", None, "mp"),
        P("mp", "dp"),
        P(),
        P(),
        P("dp", "mp"),
        P("mp", "dp"),
    )
    return jax.shard_map(
        on_device, mesh=mesh, in_specs=in_specs, out_specs=out_specs, check_vma=False
    )
```

```python
import functools
import math

import jax
import jax.numpy as jnp
from jax import lax
from jax.experimental import pallas as pl
from jax.experimental.pallas import tpu as pltpu
from jax.sharding import PartitionSpec as P

HD = 32
QB = 256
EPS = 1e-05
BF = jnp.bfloat16
F32 = jnp.float32
NEG = -1e30
SCALE = 1.0 / math.sqrt(HD)
LOG2E = math.log2(math.e)
C2 = SCALE * LOG2E
MIB = 1024 * 1024
SDS = jax.ShapeDtypeStruct


def nn(a, b):
    return lax.dot_general(a, b, (((1,), (0,)), ((), ())), preferred_element_type=F32)


def nt(a, b):
    return lax.dot_general(a, b, (((1,), (1,)), ((), ())), preferred_element_type=F32)


def params(mib):
    return pltpu.CompilerParams(vmem_limit_bytes=mib * MIB)


def in_hbm(values):
    return [pltpu.with_memory_space_constraint(v, pltpu.HBM) for v in values]


def in_vmem(values):
    return [pltpu.with_memory_space_constraint(v, pltpu.VMEM) for v in values]


def cost(gflop, mbytes):
    return pl.CostEstimate(flops=int(gflop * 1e9), bytes_accessed=int(mbytes * 1e6), transcendentals=0)


def any_spec():
    return pl.BlockSpec(memory_space=pl.ANY)


def smem_spec():
    return pl.BlockSpec(memory_space=pltpu.SMEM)


def vmem_spec():
    return pl.BlockSpec(memory_space=pltpu.VMEM)


def row_spec(width, rows=512):
    return pl.BlockSpec((rows, width), lambda r: (r, 0))


def column_spec(height, rows=512):
    return pl.BlockSpec((height, rows), lambda r: (0, r))


def whole_spec(shape):
    return pl.BlockSpec(shape, lambda r: tuple(0 for _ in shape))


MASKS = (0, 1, 2, 3)


class Rows:
    def __init__(self, dp_count, depth):
        self.dp_count = dp_count
        self.depth = depth
        self.split = (depth // dp_count) % 16 == 0 and dp_count == 16
        self.near = 4 if self.split else 1
        self.far = dp_count // 4 if self.split else 1
        self.block = depth // (self.near * self.far)
        self.shape = (self.far, self.near, self.block)


class Piece:
    def __init__(self, rows, kind, start=0, width=0, masks=MASKS):
        self.rows = rows
        self.masks = masks
        self.kind = kind if rows.split else "whole"
        self.start = start
        self.count = 2 * len(MASKS) if self.kind == "slabs" else 2
        if self.kind == "stack":
            self.shape = (len(MASKS), rows.far, rows.block, width)
        else:
            self.shape = rows.shape + (width,)


def piece_copies(piece, me, refs, moves, sem, outward):
    copies = []
    each = piece.count // 2
    for half, column, width, view in moves:
        cols = pl.ds(piece.start + column, width)
        if piece.kind == "whole":
            pairs = [(refs[half].at[:, :, :, cols], view)]
        else:
            pairs = []
            for k, mask in enumerate(piece.masks):
                ref = refs[half].at[k] if piece.kind == "stack" else refs[half * each + k]
                near = lax.bitwise_xor(lax.rem(me, 4), mask)
                pairs.append((ref.at[:, :, cols], view.at[:, near]))
        for outside, inside in pairs:
            if outward:
                copies.append(pltpu.make_async_copy(inside, outside, sem))
            else:
                copies.append(pltpu.make_async_copy(outside, inside, sem))
    return copies


def start_all(copies):
    for copy in copies:
        copy.start()


def wait_bytes(ref, sem):
    pltpu.make_async_copy(ref, ref, sem).wait()


def flat(value):
    return value.reshape(-1, value.shape[-1])


def head_row(h):
    return lax.broadcasted_iota(jnp.int32, (1, 128), 1) // HD == h


def fill_bias(bias, seg_col, seg_row):
    key = lax.broadcasted_iota(jnp.int32, (QB, QB), 0)
    query = lax.broadcasted_iota(jnp.int32, (QB, QB), 1)
    bias[0] = jnp.where(query >= key, 0.0, NEG)
    bias[1] = jnp.where((query >= key) & (seg_col[...] == seg_row[...]), 0.0, NEG)


def turned(doubles, start, r):
    coarse = pl.multiple_of(start // 16 * 16 + r * QB, 16)
    fine = start % 16
    row = lax.broadcasted_iota(jnp.int32, (QB, QB + 16), 0)
    col = lax.broadcasted_iota(jnp.int32, (QB, QB + 16), 1)
    pick = jnp.where(col - row == fine, 1.0, 0.0).astype(BF)
    total = None
    for double in doubles:
        part = nn(pick, double[pl.ds(coarse, QB + 16), :])
        total = part if total is None else total + part
    return total


def norm_parts(values):
    centered = values - jnp.mean(values, axis=-1, keepdims=True)
    spread = jnp.mean(centered * centered, axis=-1, keepdims=True)
    root = lax.rsqrt(spread + EPS)
    return centered * root, root


def prepare_body(
    start,
    core,
    own,
    other,
    cot_own,
    cot_other,
    gain,
    offset,
    x_out,
    normed_out,
    normed_t_out,
    cot_out,
    cot_t_out,
    double,
    cot_double,
    x,
    normed,
    normed_t,
    cot,
    cot_t,
    sems,
):
    here = own.shape[1]
    mine = core[0]
    for buf, halves, sem in ((double, (own, other), 5), (cot_double, (cot_own, cot_other), 6)):
        for k in range(4):
            pltpu.make_async_copy(
                halves[k % 2].at[mine], buf.at[pl.ds(k * here, here)], sems.at[sem]
            ).start()
    wait_bytes(double, sems.at[5])

    def step(r, carry):
        at = pl.ds(pl.multiple_of(r * QB, QB), QB)
        value = turned([double], start[0], r)
        x[at, :] = value.astype(BF)
        hat, _ = norm_parts(value)
        low = (hat * gain[...] + offset[...]).astype(BF)
        normed[at, :] = low
        normed_t[:, at] = low.T
        return carry

    count = x.shape[0] // QB
    lax.fori_loop(0, count, step, 0)
    copies = [
        pltpu.make_async_copy(normed, normed_out, sems.at[0]),
        pltpu.make_async_copy(x, x_out, sems.at[1]),
        pltpu.make_async_copy(normed_t, normed_t_out, sems.at[2]),
        pltpu.make_async_copy(cot, cot_out, sems.at[3]),
        pltpu.make_async_copy(cot_t, cot_t_out, sems.at[4]),
    ]
    start_all(copies[:3])
    wait_bytes(cot_double, sems.at[6])

    def second(r, carry):
        at = pl.ds(pl.multiple_of(r * QB, QB), QB)
        low = turned([cot_double], start[0], r).astype(BF)
        cot[at, :] = low
        cot_t[:, at] = low.T
        return carry

    lax.fori_loop(0, count, second, 0)
    start_all(copies[3:])
    for copy in copies:
        copy.wait()


def prepare(start, core, own, other, cot_own, cot_other, gain, offset):
    _, here, depth = own.shape
    shape, shape_t = (2 * here, depth), (depth, 2 * here)
    shapes = [shape, shape, shape_t, shape, shape_t]
    return pl.pallas_call(
        prepare_body,
        in_specs=[smem_spec()] * 2 + [any_spec()] * 4 + [vmem_spec()] * 2,
        out_specs=[any_spec()] * 5,
        out_shape=[pltpu.HBM(s, BF) for s in shapes],
        scratch_shapes=[pltpu.VMEM((4 * here, depth), BF)] * 2
        + [pltpu.VMEM(s, BF) for s in shapes]
        + [pltpu.SemaphoreType.DMA((7,))],
        compiler_params=params(28),
        cost_estimate=cost(4, 8),
        name="prepare",
    )(start, core, *in_hbm([own, other, cot_own, cot_other]), gain, offset)


def turn_back_body(start, core, values, held, other, double, own, sem):
    here = other.shape[0]
    double[: 2 * here, :] = values[...]
    double[2 * here :, :] = values[...]
    count = here // QB

    def step(r, carry):
        at = pl.ds(pl.multiple_of(r * QB, QB), QB)
        own[at, :] = turned([double], start[0], r).astype(BF)
        other[at, :] = turned([double], start[0], r + count).astype(BF)
        return carry

    lax.fori_loop(0, count, step, 0)
    copy = pltpu.make_async_copy(own, held.at[core[0]], sem)
    copy.start()
    copy.wait()


def place_body(core, other, held, out, sem):
    copy = pltpu.make_async_copy(other, out.at[1 - core[0]], sem)
    copy.start()
    copy.wait()


def place(core, held, other):
    return pl.pallas_call(
        place_body,
        in_specs=[smem_spec(), any_spec(), any_spec()],
        out_specs=any_spec(),
        out_shape=pltpu.HBM(held.shape, held.dtype),
        input_output_aliases={2: 0},
        scratch_shapes=[pltpu.SemaphoreType.DMA],
        compiler_params=params(4),
        cost_estimate=cost(0, 4),
        name="place",
    )(core, other, *in_hbm([held]))


def turn_back(start, core, values):
    length, depth = values.shape
    half = (length // 2, depth)
    return pl.pallas_call(
        turn_back_body,
        in_specs=[smem_spec()] * 2 + [vmem_spec()],
        out_specs=[any_spec(), vmem_spec()],
        out_shape=[pltpu.HBM((2,) + half, BF), SDS(half, BF)],
        scratch_shapes=[
            pltpu.VMEM((2 * length, depth), BF),
            pltpu.VMEM(half, BF),
            pltpu.SemaphoreType.DMA,
        ],
        compiler_params=params(16),
        cost_estimate=cost(2, 4),
        name="turn_back",
    )(start, core, values)


def arrange_body(widths, me, *refs):
    pieces, outs = refs[:4], refs[4:]
    far = me[0] // 4
    for m, piece in enumerate(pieces):
        begin = 0
        for out, width in zip(outs, widths):
            out[lax.bitwise_xor(far, m)] = piece[:, begin : begin + width]
            begin += width


def arrange(rows, me, pieces, widths):
    return pl.pallas_call(
        functools.partial(arrange_body, widths),
        in_specs=[smem_spec()] + [vmem_spec()] * 4,
        out_specs=[vmem_spec()] * len(widths),
        out_shape=[SDS((rows.far, rows.block, w), BF) for w in widths],
        compiler_params=params(8),
        cost_estimate=cost(1, 1),
        name="arrange",
    )(me, *pieces)


def project_attend_body(piece, me, normed, seg_col, seg_row, *refs):
    slabs = refs[: piece.count]
    proj_out, att, lse, weight, proj, bias, keys_m, values_t, att_t, sem, out_sem = refs[piece.count :]
    moves = [(half, 0, 384, weight.at[:, :, :, pl.ds(384 * half, 384)]) for half in range(2)]
    start_all(piece_copies(piece, me[0], slabs, moves, sem, False))
    fill_bias(bias, seg_col, seg_row)
    values_t[...] = jnp.ones_like(values_t)
    wait_bytes(weight, sem)
    length = normed.shape[0]

    for c in range(3):
        cols = slice(c * 256, c * 256 + 256)
        proj[:, cols] = nn(normed[...], flat(weight[:, :, :, cols])).astype(BF)
    proj_copy = pltpu.make_async_copy(proj, proj_out, out_sem)
    proj_copy.start()
    for half in range(2):
        flipped = proj[:, half * 384 + 256 : half * 384 + 384].T
        for h in range(4):
            values_t[half * 4 + h, 0:HD, :] = flipped[h * HD : (h + 1) * HD]

    units = [(h, i) for i in (2, 1, 0, 3) for h in range(4)]

    def step(half, carry):
        col = pl.multiple_of(half * 384, 128)
        for h in range(4):
            keys_m[h] = jnp.where(head_row(h), proj[:, pl.ds(col + 128, 128)], 0)

        def score(h, i):
            first = 768 if i == 3 else 0
            scores = nt(keys_m[h, first : (i + 1) * QB, :], proj[i * QB : (i + 1) * QB, pl.ds(col, 128)])
            edge = scores[-QB:] + bias[1 if i == 3 else 0]
            return jnp.concatenate([scores[:-QB], edge], 0) if scores.shape[0] > QB else edge

        ahead = score(*units[0])
        for k, (h, i) in enumerate(units):
            scores = ahead
            if k + 1 < len(units):
                ahead = score(*units[k + 1])
            first = 768 if i == 3 else 0
            last = (i + 1) * QB
            at = slice(i * QB, last)
            peak = jnp.max(scores, axis=0, keepdims=True) * C2
            probs = jnp.exp2(scores * C2 - peak).astype(BF)
            summed = nn(values_t[half * 4 + h, :, first:last], probs)
            total = summed[HD : HD + 1]
            att_t[pl.ds(pl.multiple_of(half * 128 + h * HD, HD), HD), at] = summed[:HD] / total
            lse[pl.ds(half * 4 + h, 1), at] = peak + jnp.log2(total)
        return carry

    lax.fori_loop(0, 2, step, 0)
    for half in range(2):
        cols = slice(half * 128, half * 128 + 128)
        att[:, cols] = att_t[cols, :].T.astype(BF)
    proj_copy.wait()


def project_attend(piece, me, normed, seg_col, seg_row, slabs):
    length, depth = normed.shape
    rows = piece.rows
    return pl.pallas_call(
        functools.partial(project_attend_body, piece),
        in_specs=[smem_spec()] + [vmem_spec()] * 3 + [any_spec()] * len(slabs),
        out_specs=[any_spec()] + [vmem_spec()] * 2,
        out_shape=[
            pltpu.HBM((length, 768), BF),
            pltpu.HBM((length, 256), BF),
            pltpu.HBM((8, length), F32),
        ],
        scratch_shapes=[
            pltpu.VMEM(rows.shape + (768,), BF),
            pltpu.VMEM((length, 768), BF),
            pltpu.VMEM((2, QB, QB), F32),
            pltpu.VMEM((4, length, 128), BF),
            pltpu.VMEM((8, HD + 16, length), BF),
            pltpu.VMEM((256, length), F32),
            pltpu.SemaphoreType.DMA,
            pltpu.SemaphoreType.DMA,
        ],
        compiler_params=params(20),
        cost_estimate=cost(8, 8),
        name="project_attend",
    )(me, *in_hbm([normed]), seg_col, seg_row, *in_hbm(slabs))


def join_heads(attended):
    return jnp.concatenate([a[:, :128] for a in attended] + [a[:, 128:] for a in attended], 1)


def out_norm_body(piece, groups, me, tokens, gain, offset, *refs):
    attended = refs[:groups]
    slabs = refs[groups : groups + piece.count]
    middle, normed, normed_t, weight, sem = refs[groups + piece.count :]
    width = weight.shape[3] // 2

    @pl.when(pl.program_id(0) == 0)
    def _():
        moves = [(half, 0, width, weight.at[:, :, :, pl.ds(width * half, width)]) for half in range(2)]
        start_all(piece_copies(piece, me[0], slabs, moves, sem, False))
        wait_bytes(weight, sem)

    value = tokens[...].astype(F32) + nt(join_heads([a[...] for a in attended]), flat(weight[...]))
    middle[...] = value
    hat, _ = norm_parts(value)
    low = (hat * gain[...] + offset[...]).astype(BF)
    normed[...] = low
    normed_t[...] = low.T


def out_norm(piece, me, tokens, gain, offset, attended, slabs):
    length, depth = tokens.shape
    return pl.pallas_call(
        functools.partial(out_norm_body, piece, len(attended)),
        grid=(length // 512,),
        in_specs=[smem_spec(), row_spec(depth), whole_spec((1, depth)), whole_spec((1, depth))]
        + [row_spec(256)] * len(attended)
        + [any_spec()] * len(slabs),
        out_specs=[row_spec(depth)] * 2 + [column_spec(depth)],
        out_shape=[
            pltpu.HBM((length, depth), F32),
            pltpu.VMEM((length, depth), BF),
            pltpu.VMEM((depth, length), BF),
        ],
        scratch_shapes=[pltpu.VMEM(piece.rows.shape + (depth,), BF), pltpu.SemaphoreType.DMA],
        compiler_params=params(28),
        cost_estimate=cost(3, 8),
        name="out_norm",
    )(me, *in_hbm([tokens]), gain, offset, *in_hbm(attended), *in_hbm(slabs))


def gelu_parts(values):
    size = jnp.abs(values)
    density = jnp.exp2(values * values * (-0.5 * LOG2E) + math.log2(1.0 / math.sqrt(2 * math.pi)))
    below = 1.0 + 0.2316419 * size
    t = pl.reciprocal(below, approx=True)
    t = t * (2.0 - below * t)
    poly = t * (
        0.319381530
        + t * (-0.356563782 + t * (1.781477937 + t * (-1.821255978 + t * 1.330274429)))
    )
    tail = density * poly
    below = jnp.where(values >= 0, 1.0 - tail, tail)
    return values * below, below + values * density


def feed_forward_body(piece, out_piece, first, final, aliased, me, normed, normed_t, cot, cot_t, *refs):
    refs = list(refs)
    held = [] if first else [refs.pop(0), refs.pop(0)]
    middle = refs.pop(0) if final else None
    slabs, refs = refs[: piece.count], refs[piece.count + aliased :]
    mixed, grad_in = refs[:2]
    outs, refs = refs[2:4], refs[4:]
    weight, staged, act, grad_hidden, mixed_acc, grad_acc, sems = refs[:7]
    mixed_low, middle_here = refs[7:] if final else (None, None)
    length, depth = normed.shape
    moves = []
    for half in range(2):
        for which in range(2):
            at = pl.ds(which * 768 + half * 384, 384)
            moves.append((half, which * 384, 384, at))
    into = [(h, c, w, weight.at[:, :, :, at]) for h, c, w, at in moves]
    outof = [(h, c, w, staged.at[:, :, :, at]) for h, c, w, at in moves]
    start_all(piece_copies(piece, me[0], slabs, into, sems.at[0], False))
    held_copies = []
    if not first:
        held_copies.append(pltpu.make_async_copy(held[0], mixed_acc, sems.at[1]))
        held_copies.append(pltpu.make_async_copy(held[1], grad_acc, sems.at[2]))
    if final:
        held_copies.append(pltpu.make_async_copy(middle, middle_here, sems.at[4]))
    start_all(held_copies)
    wait_bytes(weight, sems.at[0])
    chunks = [slice(c * 256, c * 256 + 256) for c in range(3)]

    def products(c):
        hidden = nn(normed[...], flat(weight[:, :, :, c * 256 : c * 256 + 256]))
        return hidden, nn(cot[...], flat(weight[:, :, :, 768 + c * 256 : 1024 + c * 256]))

    ahead = products(0)
    for c in range(3):
        hidden, grad_act = ahead
        if c < 2:
            ahead = products(c + 1)
        value, slope = gelu_parts(hidden)
        act[:, chunks[c]] = value.astype(BF)
        grad_hidden[:, chunks[c]] = (grad_act * slope).astype(BF)
    for copy in held_copies:
        copy.wait()
    for cols in chunks:
        mixed_part = nt(act[...], flat(weight[:, :, :, 768:1536])[cols])
        grad_part = nt(grad_hidden[...], flat(weight[:, :, :, 0:768])[cols])
        if not first:
            mixed_part = mixed_part + mixed_acc[:, cols]
            grad_part = grad_part + grad_acc[:, cols]
        if final:
            mixed_low[:, cols] = (middle_here[:, cols] + mixed_part).astype(BF)
        else:
            mixed_acc[:, cols] = mixed_part
        grad_acc[:, cols] = grad_part
    out_copies = [
        pltpu.make_async_copy(mixed_low if final else mixed_acc, mixed, sems.at[1]),
        pltpu.make_async_copy(grad_acc, grad_in, sems.at[2]),
    ]
    start_all(out_copies)
    for c in range(3):
        cols = slice(c * 256, c * 256 + 256)
        up = nn(normed_t[...], grad_hidden[:, cols]).astype(BF)
        staged[:, :, :, cols] = up.reshape(staged.shape[:3] + (256,))
        down = nn(cot_t[...], act[:, cols]).astype(BF)
        staged[:, :, :, 768 + c * 256 : 1024 + c * 256] = down.reshape(staged.shape[:3] + (256,))
    start_all(piece_copies(out_piece, me[0], outs, outof, sems.at[3], True))
    for copy in out_copies:
        copy.wait()
    wait_bytes(staged, sems.at[3])


def feed_forward(piece, out_piece, me, normed, normed_t, cot, cot_t, held, middle, slabs, onto):
    length, depth = normed.shape
    rows = piece.rows
    first, final = held is None, middle is not None
    ins = [me] + in_vmem([normed, normed_t, cot, cot_t]) + ([] if first else in_hbm(held))
    specs = [smem_spec()] + [vmem_spec()] * 4 + [any_spec()] * (0 if first else 2)
    if final:
        ins += in_hbm([middle])
        specs.append(any_spec())
    scratch = [
        pltpu.VMEM(rows.shape + (1536,), BF),
        pltpu.VMEM(rows.shape + (1536,), BF),
        pltpu.VMEM((length, 768), BF),
        pltpu.VMEM((length, 768), BF),
        pltpu.VMEM((length, depth), F32),
        pltpu.VMEM((length, depth), F32),
        pltpu.SemaphoreType.DMA((5,)),
    ]
    if final:
        scratch += [pltpu.VMEM((length, depth), BF), pltpu.VMEM((length, depth), F32)]
    got = pl.pallas_call(
        functools.partial(feed_forward_body, piece, out_piece, first, final, len(onto)),
        in_specs=specs + [any_spec()] * (piece.count + len(onto)),
        out_specs=[any_spec()] * 4,
        out_shape=[pltpu.HBM((length, depth), BF if final else F32), pltpu.HBM((length, depth), F32)]
        + [pltpu.HBM(out_piece.shape, BF)] * 2,
        input_output_aliases={len(ins) + piece.count + k: 2 + k for k in range(len(onto))},
        scratch_shapes=scratch,
        compiler_params=params(40),
        cost_estimate=cost(11, 20),
        name="feed_forward",
    )(*ins, *in_hbm(slabs), *in_hbm(onto))
    return got[0], got[1], got[2:]


def norm_pull(grad, hat, root, gain):
    scaled = grad * gain
    first = jnp.mean(scaled, axis=-1, keepdims=True)
    second = jnp.mean(scaled * hat, axis=-1, keepdims=True)
    return root * (scaled - first - hat * second)


def add_sums(sums, grad, hat):
    @pl.when(pl.program_id(0) == 0)
    def _():
        sums[...] = jnp.zeros_like(sums)

    sums[0:1, :] += jnp.sum(grad * hat, axis=0, keepdims=True)
    sums[1:2, :] += jnp.sum(grad, axis=0, keepdims=True)


def out_back_body(piece, groups, me, middle, grad_in, cot, gain, *refs):
    slabs, refs = refs[: piece.count], refs[piece.count :]
    grad_middle, branch_t, sums = refs[:3]
    grad_att = refs[3 : 3 + groups]
    weight, sem = refs[3 + groups :]
    width = weight.shape[3] // 2

    @pl.when(pl.program_id(0) == 0)
    def _():
        moves = [(half, 0, width, weight.at[:, :, :, pl.ds(width * half, width)]) for half in range(2)]
        start_all(piece_copies(piece, me[0], slabs, moves, sem, False))
        wait_bytes(weight, sem)

    hat, root = norm_parts(middle[...])
    grad = grad_in[...]
    value = cot[...].astype(F32) + norm_pull(grad, hat, root, gain[...])
    grad_middle[...] = value
    low = value.astype(BF)
    branch_t[...] = low.T
    add_sums(sums, grad, hat)
    back = nn(low, flat(weight[...])).astype(BF)
    for g in range(groups):
        grad_att[g][:, 0:128] = back[:, g * 128 : g * 128 + 128]
        grad_att[g][:, 128:256] = back[:, width + g * 128 : width + g * 128 + 128]


def out_back(piece, groups, me, middle, grad_in, cot, gain, slabs):
    length, depth = middle.shape
    got = pl.pallas_call(
        functools.partial(out_back_body, piece, groups),
        grid=(length // 512,),
        in_specs=[smem_spec()] + [row_spec(depth)] * 3 + [whole_spec((1, depth))] + [any_spec()] * len(slabs),
        out_specs=[row_spec(depth), column_spec(depth), whole_spec((8, depth))] + [row_spec(256)] * groups,
        out_shape=[pltpu.HBM((length, depth), F32), pltpu.VMEM((depth, length), BF), SDS((8, depth), F32)]
        + [pltpu.HBM((length, 256), BF)] * groups,
        scratch_shapes=[pltpu.VMEM(piece.rows.shape + (depth,), BF), pltpu.SemaphoreType.DMA],
        compiler_params=params(28),
        cost_estimate=cost(4, 16),
        name="out_back",
    )(me, *in_hbm([middle, grad_in]), *in_vmem([cot]), gain, *in_hbm(slabs))
    return got[0], got[1], got[2], got[3:]


def attend_back_body(piece, out_piece, extra, aliased, final, me, normed_t_in, proj, att, grad_att, lse, seg_col, seg_row, *refs):
    refs = list(refs)
    slabs, refs = refs[: piece.count], refs[piece.count :]
    if extra:
        branch_t = refs.pop(0)
        attended, refs = refs[:extra], refs[extra:]
    else:
        held = refs.pop(0)
    if final:
        tokens_in = refs.pop(0)
    refs = refs[aliased:]
    grad_normed, outs, refs = refs[0], refs[1:3], refs[3:]
    if final:
        sums = refs.pop(0)
    grad_proj, key_sum, value_sum = refs[:3]
    refs = refs[3:]
    bias, delta, keys_t, query_t, query_m, grad_m, staged, normed_t, total, weight, sems = refs[:11]
    copies = [pltpu.make_async_copy(normed_t_in, normed_t, sems.at[1])]
    if not extra:
        copies.append(pltpu.make_async_copy(held, total, sems.at[2]))
    if final:
        copies.append(pltpu.make_async_copy(tokens_in, refs[11], sems.at[3]))
    moves = [(half, 0, 384, weight.at[:, :, :, pl.ds(384 * half, 384)]) for half in range(2)]
    start_all(copies + piece_copies(piece, me[0], slabs, moves, sems.at[4], False))
    length = proj.shape[0]
    fill_bias(bias, seg_col, seg_row)
    if extra:
        joined = join_heads([a[...] for a in attended])
        out_grad = nn(branch_t[...], joined).astype(BF)
        staged[:, :, :, 768:] = out_grad.reshape(staged.shape[:3] + (768,))
    for half in range(2):
        cols = slice(half * 128, half * 128 + 128)
        product = (grad_att[:, cols].astype(F32) * att[:, cols].astype(F32)).T
        for h in range(4):
            delta[half * 4 + h : half * 4 + h + 1, :] = jnp.sum(
                product[h * HD : (h + 1) * HD], axis=0, keepdims=True
            )
        keys_t[cols, :] = proj[:, half * 384 + 128 : half * 384 + 256].T

    def step(half, carry):
        col = pl.multiple_of(half * 384, 128)
        out = pl.multiple_of(half * 128, 128)
        for h in range(4):
            mine = head_row(h)
            query_m[h] = jnp.where(mine, proj[:, pl.ds(col, 128)], 0)
            grad_m[h] = jnp.where(mine, grad_att[:, pl.ds(out, 128)], 0)
        key_sum[...] = jnp.zeros_like(key_sum)
        value_sum[...] = jnp.zeros_like(value_sum)
        for i in (2, 1, 0, 3):
            first = 768 if i == 3 else 0
            last = (i + 1) * QB
            here = slice(first, last)
            there = slice(i * QB, last)
            keys = proj[here, pl.ds(col + 128, 128)]
            values = proj[here, pl.ds(col + 256, 128)]

            def products(h):
                scores = nt(keys, query_m[h, there, :])
                edge = scores[-QB:] + bias[1 if i == 3 else 0]
                if last - first > QB:
                    scores = jnp.concatenate([scores[:-QB], edge], 0)
                else:
                    scores = edge
                return scores, nt(values, grad_m[h, there, :])

            all_probs, all_grads = [], []
            ahead = products(0)
            for h in range(4):
                scores, grad_probs = ahead
                if h < 3:
                    ahead = products(h + 1)
                stat = pl.ds(half * 4 + h, 1)
                lanes = pl.ds(pl.multiple_of(half * 128 + h * HD, HD), HD)
                probs = jnp.exp2(scores * C2 - lse[stat, there])
                grad_scores = (probs * (grad_probs - delta[stat, there])).astype(BF)
                all_probs.append(probs.astype(BF))
                all_grads.append(grad_scores)
                query_t[lanes, there] = nn(keys_t[lanes, here], grad_scores)
            stacked = jnp.concatenate([grad_m[h, there, :] for h in range(4)], 0)
            value_sum[here, :] += nn(jnp.concatenate(all_probs, 1), stacked)
            stacked = jnp.concatenate([query_m[h, there, :] for h in range(4)], 0)
            key_sum[here, :] += nn(jnp.concatenate(all_grads, 1), stacked)
        grad_proj[:, pl.ds(col + 128, 128)] = (key_sum[...] * SCALE).astype(BF)
        grad_proj[:, pl.ds(col + 256, 128)] = value_sum[...].astype(BF)
        return carry

    lax.fori_loop(0, 2, step, 0)
    for half in range(2):
        grad_proj[:, half * 384 : half * 384 + 128] = (
            query_t[half * 128 : half * 128 + 128, :].T * SCALE
        ).astype(BF)
    for copy in copies:
        copy.wait()
    wait_bytes(weight, sems.at[4])
    for c in range(3):
        cols = slice(c * 256, c * 256 + 256)
        part = nn(normed_t[...], grad_proj[:, cols]).astype(BF)
        staged[:, :, :, cols] = part.reshape(staged.shape[:3] + (256,))
    moves = [(half, 0, 384, staged.at[:, :, :, pl.ds(384 * half, 384)]) for half in range(2)]
    if extra:
        moves += [
            (half, -384, 384, staged.at[:, :, :, pl.ds(768 + 384 * half, 384)]) for half in range(2)
        ]
    start_all(piece_copies(out_piece, me[0], outs, moves, sems.at[0], True))
    if final:
        sums[...] = jnp.zeros_like(sums)

    total_copies = []
    for c in range(3):
        cols = slice(c * 256, c * 256 + 256)
        value = nt(grad_proj[...], flat(weight[...])[cols])
        if not extra:
            value = value + total[:, cols]
        total[:, cols] = value
        total_copies.append(
            pltpu.make_async_copy(
                total.at[:, pl.ds(c * 256, 256)], grad_normed.at[:, pl.ds(c * 256, 256)], sems.at[2]
            )
        )
        total_copies[-1].start()
    if final:

        def sum_step(r, carry):
            at = pl.ds(pl.multiple_of(r * QB, QB), QB)
            value = total[at, :]
            hat, _ = norm_parts(refs[11][at, :].astype(F32))
            sums[0:1, :] += jnp.sum(value * hat, axis=0, keepdims=True)
            sums[1:2, :] += jnp.sum(value, axis=0, keepdims=True)
            return carry

        lax.fori_loop(0, length // QB, sum_step, 0)
    wait_bytes(staged, sems.at[0])
    wait_bytes(total, sems.at[2])


def attend_back(
    piece,
    out_piece,
    me,
    normed_t,
    proj,
    att,
    grad_att,
    lse,
    seg_col,
    seg_row,
    slabs,
    branch_t,
    attended,
    held,
    tokens,
    onto,
):
    depth, length = normed_t.shape
    extra = len(attended)
    final = tokens is not None
    columns = 1536 if extra else 768
    ins = [me] + in_hbm([normed_t, proj, att, grad_att, lse]) + [seg_col, seg_row] + in_hbm(slabs)
    specs = [smem_spec(), any_spec()] + [vmem_spec()] * 6 + [any_spec()] * len(slabs)
    if extra:
        ins += in_vmem([branch_t]) + in_hbm(attended)
        specs += [vmem_spec()] * (1 + extra)
    else:
        ins += in_hbm([held])
        specs += [any_spec()]
    if final:
        ins += in_hbm([tokens])
        specs += [any_spec()]
    outs = [pltpu.HBM((length, depth), F32)] + [pltpu.HBM(out_piece.shape, BF)] * 2
    scratch = [
        pltpu.VMEM((2, QB, QB), F32),
        pltpu.VMEM((8, length), F32),
        pltpu.VMEM((256, length), BF),
        pltpu.VMEM((256, length), F32),
        pltpu.VMEM((4, length, 128), BF),
        pltpu.VMEM((4, length, 128), BF),
        pltpu.VMEM(out_piece.rows.shape + (columns,), BF),
        pltpu.VMEM((depth, length), BF),
        pltpu.VMEM((length, depth), F32),
        pltpu.VMEM(piece.rows.shape + (768,), BF),
        pltpu.SemaphoreType.DMA((5,)),
    ]
    if final:
        outs.append(SDS((8, depth), F32))
        scratch.append(pltpu.VMEM((length, depth), BF))
    got = pl.pallas_call(
        functools.partial(attend_back_body, piece, out_piece, extra, len(onto), final),
        in_specs=specs + [any_spec()] * len(onto),
        out_specs=[any_spec()] * 3 + ([vmem_spec()] if final else []),
        out_shape=outs,
        input_output_aliases={len(ins) + k: 1 + k for k in range(len(onto))},
        scratch_shapes=[
            pltpu.VMEM((length, 768), BF),
            pltpu.VMEM((length, 128), F32),
            pltpu.VMEM((length, 128), F32),
        ]
        + scratch,
        compiler_params=params(40),
        cost_estimate=cost(12, 8),
        name="attend_back",
    )(*ins, *in_hbm(onto))
    return got[0], got[1:3], got[3] if final else None


def norm_back_body(
    start, core, tokens, grad_normed, grad_middle, gain, held, other, high, low, own, sem
):
    length = high.shape[0] // 2
    r = pl.program_id(0)
    hat, root = norm_parts(tokens[...].astype(F32))
    value = grad_middle[...] + norm_pull(grad_normed[...], hat, root, gain[...])
    top = value.astype(BF)
    rest = (value - top.astype(F32)).astype(BF)
    for base in (0, length):
        at = pl.ds(pl.multiple_of(base + r * QB, QB), QB)
        high[at, :] = top
        low[at, :] = rest

    @pl.when(r == pl.num_programs(0) - 1)
    def _():
        count = own.shape[0] // QB
        for k in range(count):
            own[k * QB : k * QB + QB, :] = turned([high, low], start[0], k)
        copy = pltpu.make_async_copy(own, held.at[core[0]], sem)
        copy.start()
        for k in range(count):
            other[k * QB : k * QB + QB, :] = turned([high, low], start[0], k + count)
        copy.wait()


def norm_back(start, core, tokens, grad_normed, grad_middle, gain):
    length, depth = tokens.shape
    half = (length // 2, depth)
    return pl.pallas_call(
        norm_back_body,
        grid=(length // QB,),
        in_specs=[smem_spec()] * 2 + [row_spec(depth, QB)] * 3 + [whole_spec((1, depth))],
        out_specs=[any_spec(), whole_spec(half)],
        out_shape=[pltpu.HBM((2,) + half, F32), SDS(half, F32)],
        scratch_shapes=[
            pltpu.VMEM((2 * length, depth), BF),
            pltpu.VMEM((2 * length, depth), BF),
            pltpu.VMEM(half, F32),
            pltpu.SemaphoreType.DMA,
        ],
        compiler_params=params(24),
        cost_estimate=cost(4, 16),
        name="norm_back",
    )(start, core, *in_hbm([tokens, grad_normed, grad_middle]), gain)


def split_far_body(counts, me, *refs):
    keep, send = refs[-2:]
    far = me[0] // 4
    begin = 0
    for count in counts:
        pieces, refs = refs[:count], refs[count:]
        cols = pl.ds(begin, pieces[0].shape[-1])
        begin += pieces[0].shape[-1]
        for k, out in enumerate((keep, send)):
            for slot in range(2):
                at = lax.bitwise_xor(far, k + 2 * slot)
                total = pieces[0][at].astype(F32)
                for piece in pieces[1:]:
                    total = total + piece[at].astype(F32)
                out[slot, :, cols] = total.astype(BF)


def split_far(me, groups):
    width, specs = 0, []
    for pieces in groups:
        far, block, columns = pieces[0].shape[-3:]
        width += columns
        for piece in pieces:
            if piece.ndim == 4:
                specs.append(pl.BlockSpec((None, far, block, columns), lambda i: (0, 0, 0, 0)))
            else:
                specs.append(whole_spec(piece.shape))
    return pl.pallas_call(
        functools.partial(split_far_body, [len(pieces) for pieces in groups]),
        grid=(1,),
        in_specs=[smem_spec()] + specs,
        out_specs=[whole_spec((2, block, width))] * 2,
        out_shape=[SDS((2, block, width), BF)] * 2,
        compiler_params=params(16),
        cost_estimate=cost(1, 2),
        name="split_far",
    )(me, *[piece for pieces in groups for piece in pieces])


def put_sums(ref, base, total):
    high = total.astype(BF)
    ref[base : base + 4, :] = high
    ref[base + 4 : base + 8, :] = (total - high.astype(F32)).astype(BF)
    ref[base + 8 : base + 16, :] = jnp.zeros((8, total.shape[1]), BF)


def get_sums(ref, base):
    return ref[base : base + 4, :].astype(F32) + ref[base + 4 : base + 8, :].astype(F32)


def last_join_body(own, other, sums, sums_away, *outs):
    total = sums[...] + sums_away[...]
    rows = outs[0].shape[0] - 16
    for k, out in enumerate(outs):
        value = own[k].astype(F32) + other[k].astype(F32)
        out[:rows, :] = value.astype(BF).reshape(rows, -1)
        put_sums(out, rows, total)


def last_split_body(me, m0, m1, m2, m3, keep, send):
    far = me[0] // 4
    rows = m0.shape[0] - 16
    block = rows // 4
    for k, out in enumerate((keep, send)):
        for slot in range(2):
            at = pl.ds(pl.multiple_of(lax.bitwise_xor(far, k + 2 * slot) * block, 16), block)
            total = (m0[at, :].astype(F32) + m1[at, :].astype(F32)) + (
                m2[at, :].astype(F32) + m3[at, :].astype(F32)
            )
            out[slot * block : (slot + 1) * block, :] = total.astype(BF)
    total = (get_sums(m0, rows) + get_sums(m1, rows)) + (get_sums(m2, rows) + get_sums(m3, rows))
    put_sums(keep, 2 * block, total)
    put_sums(send, 2 * block, total)


def last_middle_body(keep, near, rest, send):
    block = (keep.shape[0] - 16) // 2
    value = keep[:block, :].astype(F32) + near[:block, :].astype(F32)
    rest[:block, :] = value.astype(BF)
    value = keep[block : 2 * block, :].astype(F32) + near[block : 2 * block, :].astype(F32)
    send[:block, :] = value.astype(BF)
    total = get_sums(keep, 2 * block) + get_sums(near, 2 * block)
    put_sums(rest, block, total)
    put_sums(send, block, total)


def last_sum_body(rest, away, first, grad_qkv, sums):
    block = rest.shape[0] - 16
    value = rest[:block, :].astype(F32) + away[:block, :].astype(F32)
    parts = [first[:, 384:], value[:, :384], value[:, 384:]]
    for which in range(3):
        cols = slice(which * 128, which * 128 + 128)
        grad_qkv[which] = jnp.concatenate([part[:, cols] for part in parts], 1)
    sums[...] = get_sums(rest, block) + get_sums(away, block)


def pack_body(part, out, up, down, packed):
    width = out.shape[1]
    packed[:, :width] = out[...]
    for s in range(up.shape[1] // part):
        cols = slice(s * part, (s + 1) * part)
        packed[:, width + 2 * s * part : width + (2 * s + 1) * part] = up[:, cols]
        packed[:, width + (2 * s + 1) * part : width + (2 * s + 2) * part] = down[:, cols]


def small_call(body, name, outs, scalars, values):
    return pl.pallas_call(
        body,
        in_specs=[smem_spec()] * len(scalars) + [vmem_spec()] * len(values),
        out_specs=[vmem_spec()] * len(outs),
        out_shape=outs,
        compiler_params=params(16),
        cost_estimate=cost(1, 3),
        name=name,
    )(*scalars, *values)


def swap(value):
    return lax.ppermute(value, "mp", [(0, 1), (1, 0)])


def tie(*values):
    return lax.optimization_barrier(values)


def hop(value, mask, count):
    return lax.ppermute(value, "dp", [(i, i ^ mask) for i in range(count)])


def hops(value, masks, count):
    return [(value, functools.partial(hop, mask=m, count=count)) for m in masks]


def far_hops(rows, values):
    return [
        (v, functools.partial(hop, mask=rows.near * m, count=rows.dp_count))
        for m, v in zip(range(1, rows.far), values)
    ]


def swaps(values):
    return [(v, swap) for v in values]


def send_all(requests):
    return [send(value) for value, send in requests]


def low_sum(values):
    total = values[0].astype(F32)
    for value in values[1:]:
        total = total + value.astype(F32)
    return total


class Flow:
    def __init__(self, me):
        self.me = me
        self.active = []

    def add(self, transfer, name, results, seeds=()):
        self.active.append([transfer, list(seeds), name, results])

    def step(self, *pivots):
        values = [v for item in self.active for v in item[1]]
        tied = list(tie(self.me, *pivots, *values))
        self.me = tied.pop(0)
        pivots, tied = tied[: len(pivots)], tied[len(pivots) :]
        going, self.active, requests = self.active, [], []
        for item in going:
            transfer, values, name, results = item
            got, tied = tied[: len(values)], tied[len(values) :]
            try:
                if callable(transfer):
                    item[0] = transfer(*got)
                    asked = next(item[0])
                else:
                    asked = transfer.send(got)
                self.active.append(item)
                requests.append(asked)
            except StopIteration as stop:
                results[name] = stop.value
        tied = list(tie(self.me, *(operand for asked in requests for operand, _ in asked)))
        self.me = tied.pop(0)
        for item, asked in zip(self.active, requests):
            item[1] = [send(operand) for (_, send), operand in zip(asked, tied)]
            tied = tied[len(asked) :]
        return pivots


def add_low(a, b):
    return (a.astype(F32) + b.astype(F32)).astype(BF)


def on_device(
    tokens, segment, ln1_gain, ln1_bias, w_qkv, w_out, ln2_gain, ln2_bias, w_up, w_down, cotangent
):
    dp_count = lax.axis_size("dp")
    core = lax.axis_index("mp")
    me = lax.axis_index("dp").astype(jnp.int32).reshape(1)
    here, depth = tokens.shape[2], tokens.shape[3]
    length = 2 * here
    rows = Rows(dp_count, depth)

    groups = w_qkv.shape[2] // 128
    part = 384
    subs = w_up.shape[1] // part
    cut = subs // 2
    qkv = [w_qkv[:, :, g * 128 : (g + 1) * 128].reshape(-1, part) for g in range(groups)]
    shards = {"q": jnp.concatenate(qkv, 1)}

    shard_a = small_call(
        functools.partial(pack_body, part),
        "pack",
        [SDS((w_up.shape[0], w_out.shape[0] + 2 * w_up.shape[1]), BF)],
        [],
        [w_out.T, w_up, w_down.T],
    )[0]

    seg = lax.dynamic_index_in_dim(segment[:, 0], core, 0, keepdims=False)
    run = length * 3 // 4
    begin = jnp.argmax(seg[: length - run + 1] == seg[run - 1 :]).astype(jnp.int32)
    start = ((begin - here * core) % length).reshape(1)
    back = (length - start) % length
    seg_tail = lax.dynamic_slice_in_dim(jnp.concatenate([seg, seg]), begin + run, length - run)
    seg_col = seg_tail.reshape(-1, 1)
    seg_row = seg_tail.reshape(1, -1)
    gain1, bias1, gain2, bias2 = (
        v.reshape(1, -1) for v in (ln1_gain, ln1_bias, ln2_gain, ln2_bias)
    )

    flow = Flow(me)
    core_place = core.astype(jnp.int32).reshape(1)
    token_halves = [tokens[:, 0], swap(tokens[:, 0])]
    cot_halves = [cotangent[:, 0], swap(cotangent[:, 0])]
    wide = 2 * part
    qkv_pieces = [Piece(rows, "slabs")] + [Piece(rows, "slabs", part * g) for g in range(groups - 1)]
    out_piece = Piece(rows, "slabs")
    feed_pieces = [Piece(rows, "slabs", part + wide * s) for s in range(cut)]
    feed_pieces += [Piece(rows, "slabs", wide * s) for s in range(subs - cut)]
    turns = [(0, 2, 1, 3), MASKS]
    feed_outs = [
        Piece(rows, "stack", wide * (s % cut), wide * cut, turns[s % cut]) for s in range(subs)
    ]
    qkv_outs = [Piece(rows, "stack", part, wide)]
    qkv_outs += [Piece(rows, "stack", part * g, part * (groups - 1)) for g in range(groups - 1)]
    far = lax.axis_index("dp") // rows.near

    def gather_whole(shard):
        return lax.all_gather(shard, "dp", axis=0, tiled=True).reshape(rows.shape + (-1,))

    def fetch_near(near):
        got = yield hops(near, MASKS[1:], dp_count)
        own = [near] + got
        return own + [swap(x) for x in own]

    def via(mask):
        return functools.partial(hop, mask=mask, count=dp_count)

    def fetch_wide(widths, shard, away):
        near, both_ways = yield [(shard, via(4)), (away, via(4))]
        a0, c0 = arrange(rows, flow.me, [shard, near, away, both_ways], widths)
        a1, a2, b0 = yield [(a0, via(1)), (a0, via(2))] + swaps([a0])
        a3, c1, b1, b2, d0 = yield [(a1, via(2)), (c0, via(1))] + swaps([a1, a2, c0])
        slabs["a"] = [a0, a1, a2, a3, b0, b1, b2, swap(a3)]
        (d1,) = yield swaps([c1])
        (c2,) = yield [(c0, via(2))]
        c3, d2 = yield [(c2, via(1))] + swaps([c2])
        return [c0, c1, c2, c3, d0, d1, d2, swap(c3)]

    def whole(shard):
        own = gather_whole(shard)
        return [own, swap(own)]

    def halve(own, other):
        (other,) = yield swaps([other])
        middle_col = own.shape[-1] // 2
        keep, send = [], []
        for cols in (slice(0, middle_col), slice(middle_col, None)):
            keep.append(low_sum([own[:2, ..., cols], other[:2, ..., cols]]).astype(BF))
            send.append(low_sum([own[2:, ..., cols], other[2:, ..., cols]]).astype(BF))
        near = yield [(v, via(m)) for v, m in zip(send, (1, 2))]
        send = [low_sum([k[1], n[1]]).astype(BF) for k, n in zip(keep, near)]
        away = yield [(v, via(m)) for v, m in zip(send, (2, 1))]
        return [list(group) for group in zip(keep, near, away)]

    def direct(mine):
        got = yield hops_of(mine, (1, 2, 3))
        return [mine[0]] + got

    def hops_of(values, masks):
        return [(values[m], via(m)) for m in masks]

    def reduce_far(groups):
        keep, send = split_far(flow.me, groups)
        (near,) = yield [(send, via(4))]
        (away,) = yield [(low_sum([keep[1], near[1]]).astype(BF), via(8))]
        return low_sum([keep[0], near[0], away])

    def reduce_all(own, other):
        groups_here = yield from halve(own, other)
        return (yield from reduce_far(sums_of["early"] + groups_here))

    def reduce_last(own, other, sums):
        other, sums_away = swap(other), swap(sums)
        mine = small_call(
            last_join_body,
            "last_join",
            [SDS((rows.far * rows.block + 16, wide), BF)] * 4,
            [],
            [own, other, sums, sums_away],
        )
        return (yield from direct(mine))

    def exchange(value):
        (got,) = yield swaps([value])
        return got

    def reduce_direct(own, other):
        (other,) = yield swaps([other])
        mine = [low_sum([own[k], other[k]]).astype(BF) for k in range(4)]
        pieces = yield from direct(mine)
        return (yield from reduce_far([pieces]))

    def plain(own, other):
        value = low_sum([own, swap(other)]).astype(BF).reshape(depth, -1)
        return lax.psum_scatter(value, "dp", scatter_dimension=0, tiled=True).astype(F32)

    def run(transfer):
        requests = next(transfer)
        while True:
            try:
                requests = transfer.send(send_all(requests))
            except StopIteration as stop:
                return stop.value

    slabs, forward = {}, []

    def project(g):
        name = "q0" if g == 0 else "q1"
        forward.append(
            project_attend(qkv_pieces[g], flow.me, normed, seg_col, seg_row, slabs[name])
        )

    if rows.split:
        shard_q = shards["q"]
        got = send_all(far_hops(rows, [shard_q] * (rows.far - 1)))
        prepared = prepare(start, core_place, *token_halves, *cot_halves, gain1, bias1)
        tied = tie(*got, *prepared, shard_a)
        got, prepared, shard_a = tied[:3], tied[3:8], tied[8]
        near_q0, near_q1 = arrange(rows, me, [shard_q] + list(got), [part, wide])
        own = [near_q0] + [hop(near_q0, m, dp_count) for m in MASKS[1:]]
        away_a = hop(shard_a, 8, dp_count)
        slabs["q0"] = own + [swap(v) for v in own]
        flow.add(fetch_near, "q1", slabs, [near_q1])
        flow.add(
            functools.partial(fetch_wide, [part + wide * cut, wide * (subs - cut)]),
            "c",
            slabs,
            [shard_a, away_a],
        )
        flow.step(own[3])
    else:
        for name, shard in (
            ("q0", shards["q"][:, :part]),
            ("q1", shards["q"][:, part:]),
            ("a", shard_a[:, : part + wide * cut]),
            ("c", shard_a[:, part + wide * cut :]),
        ):
            slabs[name] = whole(shard)
        prepared = prepare(start, core_place, *token_halves, *cot_halves, gain1, bias1)
    x, normed, normed_t, cot, cot_t = prepared
    for g in range(groups):
        project(g)
        flow.step(forward[g][2])
    atts = [f[1] for f in forward]
    middle, normed_ffn, normed_ffn_t = out_norm(
        out_piece, flow.me, x, gain2, bias2, atts, slabs["a"]
    )
    flow.step(normed_ffn)

    held = None
    sums_of = {}
    onto = []
    feed_names = ["a"] * cut + ["c"] * (subs - cut)
    for s in range(subs):
        mixed, grad_in, grads = feed_forward(
            feed_pieces[s],
            feed_outs[s],
            flow.me,
            normed_ffn,
            normed_ffn_t,
            cot,
            cot_t,
            held,
            middle if s == subs - 1 else None,
            slabs[feed_names[s]],
            onto,
        )
        held = (mixed, grad_in)
        onto = grads
        if s % cut == cut - 1:
            k = s // cut
            if rows.split and k == 0:
                flow.add(halve, "early", sums_of, grads)
            elif rows.split:
                flow.add(reduce_all, "feed", sums_of, grads)
            else:
                sums_of[k] = plain(*grads)
            onto = []
        flow.step(grad_in)
    grad_middle, branch_t, sums2, grad_atts = out_back(
        out_piece, groups, flow.me, middle, grad_in, cot, gain2, slabs["a"]
    )
    mixed, core_place, _ = flow.step(mixed, core_place, sums2)
    mixed_held, mixed_other = turn_back(back, core_place, mixed)
    flow.add(exchange, "mixed", sums_of, [mixed_other])
    grad_projs = []
    onto = []

    held = None
    qkv_slabs = [slabs["q0"]] + [slabs["q1"]] * (groups - 1)
    for g in range(groups):
        proj, att, lse = forward[g]
        held, grads, sums1 = attend_back(
            qkv_pieces[g],
            qkv_outs[g],
            flow.me,
            normed_t,
            proj,
            att,
            grad_atts[g],
            lse,
            seg_col,
            seg_row,
            qkv_slabs[g],
            branch_t,
            atts if g == 0 else [],
            held,
            x if g == groups - 1 else None,
            onto,
        )
        onto = grads
        if g == 0:
            if rows.split:
                flow.add(reduce_direct, "first", sums_of, grads)
            else:
                sums_of["first"] = plain(*grads)
            onto = []
        if g < groups - 1:
            flow.step(held)
    sums = jnp.concatenate([sums1[:2], sums2[:2]], 0)
    if rows.split:
        flow.add(reduce_last, "last", sums_of, [*grads, sums])
        (held,) = flow.step(held)
    else:
        sums_of["last"] = plain(*grads)
    start_late, _ = tie(back, flow.me)
    tokens_held, tokens_other = norm_back(start_late, core_place, x, held, grad_middle, gain1)
    tokens_held, tokens_other = flow.step(tokens_held, tokens_other)
    if rows.split:
        block = rows.block
        keep, send = small_call(
            last_split_body,
            "last_split",
            [SDS((2 * block + 16, wide), BF)] * 2,
            [flow.me],
            sums_of["last"],
        )
        near = hop(send, 4, dp_count)
        rest, send = small_call(
            last_middle_body, "last_middle", [SDS((block + 16, wide), BF)] * 2, [], [keep, near]
        )
        away = hop(send, 8, dp_count)
        while flow.active:
            flow.step()
        grad_qkv, norm_sums = small_call(
            last_sum_body,
            "last_sum",
            [SDS((3, block, part), F32), SDS((4, depth), F32)],
            [],
            [rest, away, sums_of["first"]],
        )
        grad_qkv = grad_qkv.transpose(1, 0, 2)
        grad_out = sums_of["first"][:, :part].T
        feed_sums = [sums_of["feed"]]
    else:
        early, last = sums_of["first"], sums_of["last"]
        parts = [early[:, part:], last[:, :part], last[:, part:]]
        grad_qkv = jnp.concatenate([r.reshape(-1, 3, 128) for r in parts], 2)
        grad_out = early[:, :part].T
        feed_sums = [sums_of[0], sums_of[1]]
        norm_sums = jnp.sum(lax.all_gather(sums + swap(sums), "dp", axis=0), 0)
    feed_sum = jnp.concatenate(feed_sums, 1) if len(feed_sums) > 1 else feed_sums[0]
    feed_list = [feed_sum[:, wide * s : wide * (s + 1)] for s in range(subs)]

    return (
        place(core_place, mixed_held, sums_of["mixed"])[:, None],
        place(core_place, tokens_held, swap(tokens_other))[:, None],
        norm_sums[0],
        norm_sums[1],
        grad_qkv,
        grad_out,
        norm_sums[2],
        norm_sums[3],
        jnp.concatenate([r[:, :part] for r in feed_list], 1),
        jnp.concatenate([r[:, part:] for r in feed_list], 1).T,
    )


def solution(mesh):
    in_specs = (
        P(None, "dp", "mp", None),
        P(None, "dp", None),
        P(),
        P(),
        P("dp", None, "mp"),
        P("mp", "dp"),
        P(),
        P(),
        P("dp", "mp"),
        P("mp", "dp"),
        P(None, "dp", "mp", None),
    )
    out_specs = (
        P(None, "dp", "mp", None),
        P(None, "dp", "mp", None),
        P(),
        P(),
        P("dp", None, "mp"),
        P("mp", "dp"),
        P(),
        P(),
        P("dp", "mp"),
        P("mp", "dp"),
    )
    return jax.shard_map(
        on_device, mesh=mesh, in_specs=in_specs, out_specs=out_specs, check_vma=False
    )
```

```python
import functools
import math

import jax
import jax.numpy as jnp
from jax import lax
from jax.experimental import pallas as pl
from jax.experimental.pallas import tpu as pltpu
from jax.sharding import PartitionSpec as P

HD = 32
QB = 256
EPS = 1e-05
BF = jnp.bfloat16
F32 = jnp.float32
NEG = -1e30
SCALE = 1.0 / math.sqrt(HD)
LOG2E = math.log2(math.e)
C2 = SCALE * LOG2E
MIB = 1024 * 1024
SDS = jax.ShapeDtypeStruct


def nn(a, b):
    return lax.dot_general(a, b, (((1,), (0,)), ((), ())), preferred_element_type=F32)


def nt(a, b):
    return lax.dot_general(a, b, (((1,), (1,)), ((), ())), preferred_element_type=F32)


def params(mib):
    return pltpu.CompilerParams(vmem_limit_bytes=mib * MIB)


def in_hbm(values):
    return [pltpu.with_memory_space_constraint(v, pltpu.HBM) for v in values]


def in_vmem(values):
    return [pltpu.with_memory_space_constraint(v, pltpu.VMEM) for v in values]


def cost(gflop, mbytes):
    return pl.CostEstimate(flops=int(gflop * 1e9), bytes_accessed=int(mbytes * 1e6), transcendentals=0)


def any_spec():
    return pl.BlockSpec(memory_space=pl.ANY)


def smem_spec():
    return pl.BlockSpec(memory_space=pltpu.SMEM)


def vmem_spec():
    return pl.BlockSpec(memory_space=pltpu.VMEM)


def row_spec(width, rows=512):
    return pl.BlockSpec((rows, width), lambda r: (r, 0))


def column_spec(height, rows=512):
    return pl.BlockSpec((height, rows), lambda r: (0, r))


def whole_spec(shape):
    return pl.BlockSpec(shape, lambda r: tuple(0 for _ in shape))


MASKS = (0, 1, 2, 3)


class Rows:
    def __init__(self, dp_count, depth):
        self.dp_count = dp_count
        self.depth = depth
        self.split = (depth // dp_count) % 16 == 0 and dp_count == 16
        self.near = 4 if self.split else 1
        self.far = dp_count // 4 if self.split else 1
        self.block = depth // (self.near * self.far)
        self.shape = (self.far, self.near, self.block)


class Piece:
    def __init__(self, rows, kind, start=0, width=0, masks=MASKS):
        self.rows = rows
        self.masks = masks
        self.kind = kind if rows.split else "whole"
        self.start = start
        self.count = 2 * len(MASKS) if self.kind == "slabs" else 2
        if self.kind == "stack":
            self.shape = (len(MASKS), rows.far, rows.block, width)
        else:
            self.shape = rows.shape + (width,)


def piece_copies(piece, me, refs, moves, sem, outward):
    copies = []
    each = piece.count // 2
    for half, column, width, view in moves:
        cols = pl.ds(piece.start + column, width)
        if piece.kind == "whole":
            pairs = [(refs[half].at[:, :, :, cols], view)]
        else:
            pairs = []
            for k, mask in enumerate(piece.masks):
                ref = refs[half].at[k] if piece.kind == "stack" else refs[half * each + k]
                near = lax.bitwise_xor(lax.rem(me, 4), mask)
                pairs.append((ref.at[:, :, cols], view.at[:, near]))
        for outside, inside in pairs:
            if outward:
                copies.append(pltpu.make_async_copy(inside, outside, sem))
            else:
                copies.append(pltpu.make_async_copy(outside, inside, sem))
    return copies


def start_all(copies):
    for copy in copies:
        copy.start()


def wait_bytes(ref, sem):
    pltpu.make_async_copy(ref, ref, sem).wait()


def flat(value):
    return value.reshape(-1, value.shape[-1])


def head_row(h):
    return lax.broadcasted_iota(jnp.int32, (1, 128), 1) // HD == h


def fill_bias(bias, seg_col, seg_row):
    key = lax.broadcasted_iota(jnp.int32, (QB, QB), 0)
    query = lax.broadcasted_iota(jnp.int32, (QB, QB), 1)
    bias[0] = jnp.where(query >= key, 0.0, NEG)
    bias[1] = jnp.where((query >= key) & (seg_col[...] == seg_row[...]), 0.0, NEG)


def turned(doubles, start, r):
    coarse = pl.multiple_of(start // 16 * 16 + r * QB, 16)
    fine = start % 16
    row = lax.broadcasted_iota(jnp.int32, (QB, QB + 16), 0)
    col = lax.broadcasted_iota(jnp.int32, (QB, QB + 16), 1)
    pick = jnp.where(col - row == fine, 1.0, 0.0).astype(BF)
    total = None
    for double in doubles:
        part = nn(pick, double[pl.ds(coarse, QB + 16), :])
        total = part if total is None else total + part
    return total


def norm_parts(values):
    centered = values - jnp.mean(values, axis=-1, keepdims=True)
    spread = jnp.mean(centered * centered, axis=-1, keepdims=True)
    root = lax.rsqrt(spread + EPS)
    return centered * root, root


def start_double(double, core, own, other, sem):
    here = own.shape[1]
    halves = (own, other)
    for k in range(4):
        pltpu.make_async_copy(halves[k % 2].at[core], double.at[pl.ds(k * here, here)], sem).start()


def prepare_body(start, core, own, other, gain, offset, x_out, normed_out, normed_t_out, double, x, normed, normed_t, sems):
    start_double(double, core[0], own, other, sems.at[3])
    wait_bytes(double, sems.at[3])

    def step(r, carry):
        at = pl.ds(pl.multiple_of(r * QB, QB), QB)
        value = turned([double], start[0], r)
        x[at, :] = value.astype(BF)
        hat, _ = norm_parts(value)
        low = (hat * gain[...] + offset[...]).astype(BF)
        normed[at, :] = low
        normed_t[:, at] = low.T
        return carry

    lax.fori_loop(0, x.shape[0] // QB, step, 0)
    copies = [
        pltpu.make_async_copy(normed, normed_out, sems.at[0]),
        pltpu.make_async_copy(x, x_out, sems.at[1]),
        pltpu.make_async_copy(normed_t, normed_t_out, sems.at[2]),
    ]
    start_all(copies)
    for copy in copies:
        copy.wait()


def prepare(start, core, own, other, gain, offset):
    _, here, depth = own.shape
    shape, shape_t = (2 * here, depth), (depth, 2 * here)
    shapes = [shape, shape, shape_t]
    return pl.pallas_call(
        prepare_body,
        in_specs=[smem_spec()] * 2 + [any_spec()] * 2 + [vmem_spec()] * 2,
        out_specs=[any_spec()] * 3,
        out_shape=[pltpu.HBM(s, BF) for s in shapes],
        scratch_shapes=[pltpu.VMEM((4 * here, depth), BF)]
        + [pltpu.VMEM(s, BF) for s in shapes]
        + [pltpu.SemaphoreType.DMA((4,))],
        compiler_params=params(20),
        cost_estimate=cost(4, 8),
        name="prepare",
    )(start, core, *in_hbm([own, other]), gain, offset)


def turn_body(start, core, own, other, cot_out, cot_t_out, double, cot, cot_t, sems):
    start_double(double, core[0], own, other, sems.at[2])
    wait_bytes(double, sems.at[2])

    def step(r, carry):
        at = pl.ds(pl.multiple_of(r * QB, QB), QB)
        low = turned([double], start[0], r).astype(BF)
        cot[at, :] = low
        cot_t[:, at] = low.T
        return carry

    lax.fori_loop(0, cot.shape[0] // QB, step, 0)
    copies = [
        pltpu.make_async_copy(cot, cot_out, sems.at[0]),
        pltpu.make_async_copy(cot_t, cot_t_out, sems.at[1]),
    ]
    start_all(copies)
    for copy in copies:
        copy.wait()


def turn(start, core, own, other):
    _, here, depth = own.shape
    shapes = [(2 * here, depth), (depth, 2 * here)]
    return pl.pallas_call(
        turn_body,
        in_specs=[smem_spec()] * 2 + [any_spec()] * 2,
        out_specs=[any_spec()] * 2,
        out_shape=[pltpu.HBM(s, BF) for s in shapes],
        scratch_shapes=[pltpu.VMEM((4 * here, depth), BF)]
        + [pltpu.VMEM(s, BF) for s in shapes]
        + [pltpu.SemaphoreType.DMA((3,))],
        compiler_params=params(16),
        cost_estimate=cost(4, 8),
        name="turn",
    )(start, core, *in_hbm([own, other]))


def turn_back_body(start, core, values, held, other, double, own, sem):
    here = other.shape[0]
    double[: 2 * here, :] = values[...]
    double[2 * here :, :] = values[...]
    count = here // QB

    def step(r, carry):
        at = pl.ds(pl.multiple_of(r * QB, QB), QB)
        own[at, :] = turned([double], start[0], r).astype(BF)
        other[at, :] = turned([double], start[0], r + count).astype(BF)
        return carry

    lax.fori_loop(0, count, step, 0)
    copy = pltpu.make_async_copy(own, held.at[core[0]], sem)
    copy.start()
    copy.wait()


def place_body(core, other, held, out, sem):
    copy = pltpu.make_async_copy(other, out.at[1 - core[0]], sem)
    copy.start()
    copy.wait()


def place(core, held, other):
    return pl.pallas_call(
        place_body,
        in_specs=[smem_spec(), any_spec(), any_spec()],
        out_specs=any_spec(),
        out_shape=pltpu.HBM(held.shape, held.dtype),
        input_output_aliases={2: 0},
        scratch_shapes=[pltpu.SemaphoreType.DMA],
        compiler_params=params(4),
        cost_estimate=cost(0, 4),
        name="place",
    )(core, other, *in_hbm([held]))


def turn_back(start, core, values):
    length, depth = values.shape
    half = (length // 2, depth)
    return pl.pallas_call(
        turn_back_body,
        in_specs=[smem_spec()] * 2 + [vmem_spec()],
        out_specs=[any_spec(), vmem_spec()],
        out_shape=[pltpu.HBM((2,) + half, BF), SDS(half, BF)],
        scratch_shapes=[
            pltpu.VMEM((2 * length, depth), BF),
            pltpu.VMEM(half, BF),
            pltpu.SemaphoreType.DMA,
        ],
        compiler_params=params(16),
        cost_estimate=cost(2, 4),
        name="turn_back",
    )(start, core, values)


def arrange_body(widths, me, *refs):
    pieces, outs = refs[:4], refs[4:]
    far = me[0] // 4
    for m, piece in enumerate(pieces):
        begin = 0
        for out, width in zip(outs, widths):
            out[lax.bitwise_xor(far, m)] = piece[:, begin : begin + width]
            begin += width


def arrange(rows, me, pieces, widths):
    return pl.pallas_call(
        functools.partial(arrange_body, widths),
        in_specs=[smem_spec()] + [vmem_spec()] * 4,
        out_specs=[vmem_spec()] * len(widths),
        out_shape=[SDS((rows.far, rows.block, w), BF) for w in widths],
        compiler_params=params(8),
        cost_estimate=cost(1, 1),
        name="arrange",
    )(me, *pieces)


def project_attend_body(piece, me, normed_in, seg_col, seg_row, *refs):
    slabs = refs[: piece.count]
    proj_out, att, lse, weight, proj, normed, bias, keys_m, values_t, att_t, sem, out_sem = refs[
        piece.count :
    ]
    normed_copy = pltpu.make_async_copy(normed_in, normed, out_sem)
    normed_copy.start()
    moves = [(half, 0, 384, weight.at[:, :, :, pl.ds(384 * half, 384)]) for half in range(2)]
    start_all(piece_copies(piece, me[0], slabs, moves, sem, False))
    fill_bias(bias, seg_col, seg_row)
    values_t[...] = jnp.ones_like(values_t)
    normed_copy.wait()
    wait_bytes(weight, sem)

    for c in range(3):
        cols = slice(c * 256, c * 256 + 256)
        proj[:, cols] = nn(normed[...], flat(weight[:, :, :, cols])).astype(BF)
    proj_copy = pltpu.make_async_copy(proj, proj_out, out_sem)
    proj_copy.start()
    for half in range(2):
        flipped = proj[:, half * 384 + 256 : half * 384 + 384].T
        for h in range(4):
            values_t[half * 4 + h, 0:HD, :] = flipped[h * HD : (h + 1) * HD]

    units = [(h, i) for i in (2, 1, 0, 3) for h in range(4)]

    def step(half, carry):
        col = pl.multiple_of(half * 384, 128)
        for h in range(4):
            keys_m[h] = jnp.where(head_row(h), proj[:, pl.ds(col + 128, 128)], 0)

        def score(h, i):
            first = 768 if i == 3 else 0
            scores = nt(keys_m[h, first : (i + 1) * QB, :], proj[i * QB : (i + 1) * QB, pl.ds(col, 128)])
            edge = scores[-QB:] + bias[1 if i == 3 else 0]
            return jnp.concatenate([scores[:-QB], edge], 0) if scores.shape[0] > QB else edge

        ahead = score(*units[0])
        for k, (h, i) in enumerate(units):
            scores = ahead
            if k + 1 < len(units):
                ahead = score(*units[k + 1])
            first = 768 if i == 3 else 0
            last = (i + 1) * QB
            at = slice(i * QB, last)
            peak = jnp.max(scores, axis=0, keepdims=True) * C2
            probs = jnp.exp2(scores * C2 - peak).astype(BF)
            summed = nn(values_t[half * 4 + h, :, first:last], probs)
            total = summed[HD : HD + 1]
            att_t[pl.ds(pl.multiple_of(half * 128 + h * HD, HD), HD), at] = summed[:HD] / total
            lse[pl.ds(half * 4 + h, 1), at] = peak + jnp.log2(total)
        return carry

    lax.fori_loop(0, 2, step, 0)
    for half in range(2):
        cols = slice(half * 128, half * 128 + 128)
        att[:, cols] = att_t[cols, :].T.astype(BF)
    proj_copy.wait()


def project_attend(piece, me, normed, seg_col, seg_row, slabs):
    length, depth = normed.shape
    rows = piece.rows
    return pl.pallas_call(
        functools.partial(project_attend_body, piece),
        in_specs=[smem_spec(), any_spec()] + [vmem_spec()] * 2 + [any_spec()] * len(slabs),
        out_specs=[any_spec()] + [vmem_spec()] * 2,
        out_shape=[
            pltpu.HBM((length, 768), BF),
            pltpu.HBM((length, 256), BF),
            pltpu.HBM((8, length), F32),
        ],
        scratch_shapes=[
            pltpu.VMEM(rows.shape + (768,), BF),
            pltpu.VMEM((length, 768), BF),
            pltpu.VMEM((length, depth), BF),
            pltpu.VMEM((2, QB, QB), F32),
            pltpu.VMEM((4, length, 128), BF),
            pltpu.VMEM((8, HD + 16, length), BF),
            pltpu.VMEM((256, length), F32),
            pltpu.SemaphoreType.DMA,
            pltpu.SemaphoreType.DMA,
        ],
        compiler_params=params(20),
        cost_estimate=cost(8, 8),
        name="project_attend",
    )(me, *in_hbm([normed]), seg_col, seg_row, *in_hbm(slabs))


def join_heads(attended):
    return jnp.concatenate([a[:, :128] for a in attended] + [a[:, 128:] for a in attended], 1)


def out_norm_body(piece, groups, me, tokens, gain, offset, *refs):
    attended = refs[:groups]
    slabs = refs[groups : groups + piece.count]
    middle, normed, normed_t, weight, sem = refs[groups + piece.count :]
    width = weight.shape[3] // 2

    @pl.when(pl.program_id(0) == 0)
    def _():
        moves = [(half, 0, width, weight.at[:, :, :, pl.ds(width * half, width)]) for half in range(2)]
        start_all(piece_copies(piece, me[0], slabs, moves, sem, False))
        wait_bytes(weight, sem)

    value = tokens[...].astype(F32) + nt(join_heads([a[...] for a in attended]), flat(weight[...]))
    middle[...] = value
    hat, _ = norm_parts(value)
    low = (hat * gain[...] + offset[...]).astype(BF)
    normed[...] = low
    normed_t[...] = low.T


def out_norm(piece, me, tokens, gain, offset, attended, slabs):
    length, depth = tokens.shape
    return pl.pallas_call(
        functools.partial(out_norm_body, piece, len(attended)),
        grid=(length // 512,),
        in_specs=[smem_spec(), row_spec(depth), whole_spec((1, depth)), whole_spec((1, depth))]
        + [row_spec(256)] * len(attended)
        + [any_spec()] * len(slabs),
        out_specs=[row_spec(depth)] * 2 + [column_spec(depth)],
        out_shape=[
            pltpu.HBM((length, depth), F32),
            pltpu.VMEM((length, depth), BF),
            pltpu.VMEM((depth, length), BF),
        ],
        scratch_shapes=[pltpu.VMEM(piece.rows.shape + (depth,), BF), pltpu.SemaphoreType.DMA],
        compiler_params=params(28),
        cost_estimate=cost(3, 8),
        name="out_norm",
    )(me, *in_hbm([tokens]), gain, offset, *in_hbm(attended), *in_hbm(slabs))


def gelu_parts(values):
    size = jnp.abs(values)
    density = jnp.exp2(values * values * (-0.5 * LOG2E) + math.log2(1.0 / math.sqrt(2 * math.pi)))
    below = 1.0 + 0.2316419 * size
    t = pl.reciprocal(below, approx=True)
    t = t * (2.0 - below * t)
    poly = t * (
        0.319381530
        + t * (-0.356563782 + t * (1.781477937 + t * (-1.821255978 + t * 1.330274429)))
    )
    tail = density * poly
    below = jnp.where(values >= 0, 1.0 - tail, tail)
    return values * below, below + values * density


def norm_pull(grad, hat, root, gain):
    scaled = grad * gain
    first = jnp.mean(scaled, axis=-1, keepdims=True)
    second = jnp.mean(scaled * hat, axis=-1, keepdims=True)
    return root * (scaled - first - hat * second)


def feed_forward_body(
    piece, out_piece, first, last_piece, groups, aliased, me, normed, normed_t, cot, cot_t, *refs
):
    refs = list(refs)
    final = last_piece is not None
    held = [] if first else [refs.pop(0), refs.pop(0)]
    if final:
        middle, gain = refs.pop(0), refs.pop(0)
        out_slabs, refs = refs[: last_piece.count], refs[last_piece.count :]
    slabs, refs = refs[: piece.count], refs[piece.count + aliased :]
    outs, refs = refs[:2], refs[2:]
    mixed = refs.pop(0)
    if final:
        grad_middle_out, branch_t, sums = refs[:3]
        grad_att, refs = refs[3 : 3 + groups], refs[3 + groups :]
    else:
        grad_in = refs.pop(0)
    weight, staged, act, grad_hidden, mixed_acc, grad_acc, sems = refs[:7]
    if final:
        mixed_low, middle_here, out_weight, grad_middle = refs[7:]
    length, depth = normed.shape
    moves = []
    for half in range(2):
        for which in range(2):
            at = pl.ds(which * 768 + half * 384, 384)
            moves.append((half, which * 384, 384, at))
    into = [(h, c, w, weight.at[:, :, :, at]) for h, c, w, at in moves]
    outof = [(h, c, w, staged.at[:, :, :, at]) for h, c, w, at in moves]
    start_all(piece_copies(piece, me[0], slabs, into, sems.at[0], False))
    held_copies = []
    if not first:
        held_copies.append(pltpu.make_async_copy(held[0], mixed_acc, sems.at[1]))
        held_copies.append(pltpu.make_async_copy(held[1], grad_acc, sems.at[2]))
    if final:
        held_copies.append(pltpu.make_async_copy(middle, middle_here, sems.at[4]))
    start_all(held_copies)
    if final:
        width = depth // 2
        views = [
            (half, 0, width, out_weight.at[:, :, :, pl.ds(width * half, width)]) for half in range(2)
        ]
        start_all(piece_copies(last_piece, me[0], out_slabs, views, sems.at[5], False))
    wait_bytes(weight, sems.at[0])
    chunks = [slice(c * 256, c * 256 + 256) for c in range(3)]

    def products(c):
        hidden = nn(normed[...], flat(weight[:, :, :, c * 256 : c * 256 + 256]))
        return hidden, nn(cot[...], flat(weight[:, :, :, 768 + c * 256 : 1024 + c * 256]))

    ahead = products(0)
    for c in range(3):
        hidden, grad_act = ahead
        if c < 2:
            ahead = products(c + 1)
        value, slope = gelu_parts(hidden)
        act[:, chunks[c]] = value.astype(BF)
        grad_hidden[:, chunks[c]] = (grad_act * slope).astype(BF)
    for copy in held_copies:
        copy.wait()
    for cols in chunks:
        mixed_part = nt(act[...], flat(weight[:, :, :, 768:1536])[cols])
        grad_part = nt(grad_hidden[...], flat(weight[:, :, :, 0:768])[cols])
        if not first:
            mixed_part = mixed_part + mixed_acc[:, cols]
            grad_part = grad_part + grad_acc[:, cols]
        if final:
            mixed_low[:, cols] = (middle_here[:, cols] + mixed_part).astype(BF)
        else:
            mixed_acc[:, cols] = mixed_part
        grad_acc[:, cols] = grad_part
    if final:
        out_copies = [pltpu.make_async_copy(mixed_low, mixed, sems.at[1])]
        start_all(out_copies)
        wait_bytes(out_weight, sems.at[5])
        sums[...] = jnp.zeros_like(sums)

        def back_step(r, carry):
            at = pl.ds(pl.multiple_of(r * QB, QB), QB)
            hat, root = norm_parts(middle_here[at, :])
            grad = grad_acc[at, :]
            value = cot[at, :].astype(F32) + norm_pull(grad, hat, root, gain[...])
            grad_middle[at, :] = value
            low = value.astype(BF)
            branch_t[:, at] = low.T
            sums[0:1, :] += jnp.sum(grad * hat, axis=0, keepdims=True)
            sums[1:2, :] += jnp.sum(grad, axis=0, keepdims=True)
            back = nn(low, flat(out_weight[...])).astype(BF)
            for g in range(groups):
                grad_att[g][at, 0:128] = back[:, g * 128 : g * 128 + 128]
                grad_att[g][at, 128:256] = back[:, width + g * 128 : width + g * 128 + 128]
            return carry

        lax.fori_loop(0, length // QB, back_step, 0)
        out_copies.append(pltpu.make_async_copy(grad_middle, grad_middle_out, sems.at[2]))
        out_copies[-1].start()
    else:
        out_copies = [
            pltpu.make_async_copy(mixed_acc, mixed, sems.at[1]),
            pltpu.make_async_copy(grad_acc, grad_in, sems.at[2]),
        ]
        start_all(out_copies)
    for c in range(3):
        cols = slice(c * 256, c * 256 + 256)
        up = nn(normed_t[...], grad_hidden[:, cols]).astype(BF)
        staged[:, :, :, cols] = up.reshape(staged.shape[:3] + (256,))
        down = nn(cot_t[...], act[:, cols]).astype(BF)
        staged[:, :, :, 768 + c * 256 : 1024 + c * 256] = down.reshape(staged.shape[:3] + (256,))
    start_all(piece_copies(out_piece, me[0], outs, outof, sems.at[3], True))
    for copy in out_copies:
        copy.wait()
    wait_bytes(staged, sems.at[3])


def feed_forward(
    piece, out_piece, me, normed, normed_t, cot, cot_t, held, slabs, onto, last=None
):
    length, depth = normed.shape
    rows = piece.rows
    first, final = held is None, last is not None
    ins = [me] + in_vmem([normed, normed_t, cot, cot_t]) + ([] if first else in_hbm(held))
    specs = [smem_spec()] + [vmem_spec()] * 4 + [any_spec()] * (0 if first else 2)
    scratch = [
        pltpu.VMEM(rows.shape + (1536,), BF),
        pltpu.VMEM(rows.shape + (1536,), BF),
        pltpu.VMEM((length, 768), BF),
        pltpu.VMEM((length, 768), BF),
        pltpu.VMEM((length, depth), F32),
        pltpu.VMEM((length, depth), F32),
        pltpu.SemaphoreType.DMA((6,)),
    ]
    last_piece, groups = None, 0
    outs = [pltpu.HBM(out_piece.shape, BF)] * 2 + [pltpu.HBM((length, depth), BF if final else F32)]
    out_specs = [any_spec()] * 3
    if final:
        last_piece, last_slabs, middle, gain, groups = last
        ins += in_hbm([middle]) + [gain] + in_hbm(last_slabs)
        specs += [any_spec(), vmem_spec()] + [any_spec()] * len(last_slabs)
        scratch += [
            pltpu.VMEM((length, depth), BF),
            pltpu.VMEM((length, depth), F32),
            pltpu.VMEM(rows.shape + (depth,), BF),
            pltpu.VMEM((length, depth), F32),
        ]
        outs += [pltpu.HBM((length, depth), F32), pltpu.VMEM((depth, length), BF), SDS((8, depth), F32)]
        outs += [pltpu.HBM((length, 256), BF)] * groups
        out_specs += [any_spec()] + [vmem_spec()] * (2 + groups)
    else:
        outs.append(pltpu.HBM((length, depth), F32))
        out_specs.append(any_spec())
    got = pl.pallas_call(
        functools.partial(
            feed_forward_body, piece, out_piece, first, last_piece, groups, len(onto)
        ),
        in_specs=specs + [any_spec()] * (piece.count + len(onto)),
        out_specs=out_specs,
        out_shape=outs,
        input_output_aliases={len(ins) + piece.count + k: k for k in range(len(onto))},
        scratch_shapes=scratch,
        compiler_params=params(48 if final else 32),
        cost_estimate=cost(14 if final else 11, 20),
        name="feed_forward",
    )(*ins, *in_hbm(slabs), *in_hbm(onto))
    return got[:2], got[2:]


def attend_back_body(piece, out_piece, extra, aliased, final, me, normed_t_in, proj, att, grad_att, lse, seg_col, seg_row, *refs):
    refs = list(refs)
    slabs, refs = refs[: piece.count], refs[piece.count :]
    if extra:
        branch_t = refs.pop(0)
        attended, refs = refs[:extra], refs[extra:]
    else:
        held = refs.pop(0)
    if final:
        tokens_in = refs.pop(0)
    refs = refs[aliased:]
    grad_normed, outs, refs = refs[0], refs[1:3], refs[3:]
    if final:
        sums = refs.pop(0)
    grad_proj, key_sum, value_sum = refs[:3]
    refs = refs[3:]
    bias, delta, keys_t, query_t, query_m, grad_m, staged, normed_t, total, weight, sems = refs[:11]
    copies = [pltpu.make_async_copy(normed_t_in, normed_t, sems.at[1])]
    if not extra:
        copies.append(pltpu.make_async_copy(held, total, sems.at[2]))
    if final:
        copies.append(pltpu.make_async_copy(tokens_in, refs[11], sems.at[3]))
    moves = [(half, 0, 384, weight.at[:, :, :, pl.ds(384 * half, 384)]) for half in range(2)]
    start_all(copies + piece_copies(piece, me[0], slabs, moves, sems.at[4], False))
    length = proj.shape[0]
    fill_bias(bias, seg_col, seg_row)
    if extra:
        joined = join_heads([a[...] for a in attended])
        out_grad = nn(branch_t[...], joined).astype(BF)
        staged[:, :, :, 768:] = out_grad.reshape(staged.shape[:3] + (768,))
    for half in range(2):
        cols = slice(half * 128, half * 128 + 128)
        product = (grad_att[:, cols].astype(F32) * att[:, cols].astype(F32)).T
        for h in range(4):
            delta[half * 4 + h : half * 4 + h + 1, :] = jnp.sum(
                product[h * HD : (h + 1) * HD], axis=0, keepdims=True
            )
        keys_t[cols, :] = proj[:, half * 384 + 128 : half * 384 + 256].T

    def step(half, carry):
        col = pl.multiple_of(half * 384, 128)
        out = pl.multiple_of(half * 128, 128)
        for h in range(4):
            mine = head_row(h)
            query_m[h] = jnp.where(mine, proj[:, pl.ds(col, 128)], 0)
            grad_m[h] = jnp.where(mine, grad_att[:, pl.ds(out, 128)], 0)
        key_sum[...] = jnp.zeros_like(key_sum)
        value_sum[...] = jnp.zeros_like(value_sum)
        for i in (2, 1, 0, 3):
            first = 768 if i == 3 else 0
            last = (i + 1) * QB
            here = slice(first, last)
            there = slice(i * QB, last)
            keys = proj[here, pl.ds(col + 128, 128)]
            values = proj[here, pl.ds(col + 256, 128)]

            def products(h):
                scores = nt(keys, query_m[h, there, :])
                edge = scores[-QB:] + bias[1 if i == 3 else 0]
                if last - first > QB:
                    scores = jnp.concatenate([scores[:-QB], edge], 0)
                else:
                    scores = edge
                return scores, nt(values, grad_m[h, there, :])

            all_probs, all_grads = [], []
            ahead = products(0)
            for h in range(4):
                scores, grad_probs = ahead
                if h < 3:
                    ahead = products(h + 1)
                stat = pl.ds(half * 4 + h, 1)
                lanes = pl.ds(pl.multiple_of(half * 128 + h * HD, HD), HD)
                probs = jnp.exp2(scores * C2 - lse[stat, there])
                grad_scores = (probs * (grad_probs - delta[stat, there])).astype(BF)
                all_probs.append(probs.astype(BF))
                all_grads.append(grad_scores)
                query_t[lanes, there] = nn(keys_t[lanes, here], grad_scores)
            stacked = jnp.concatenate([grad_m[h, there, :] for h in range(4)], 0)
            value_sum[here, :] += nn(jnp.concatenate(all_probs, 1), stacked)
            stacked = jnp.concatenate([query_m[h, there, :] for h in range(4)], 0)
            key_sum[here, :] += nn(jnp.concatenate(all_grads, 1), stacked)
        grad_proj[:, pl.ds(col + 128, 128)] = (key_sum[...] * SCALE).astype(BF)
        grad_proj[:, pl.ds(col + 256, 128)] = value_sum[...].astype(BF)
        return carry

    lax.fori_loop(0, 2, step, 0)
    for half in range(2):
        grad_proj[:, half * 384 : half * 384 + 128] = (
            query_t[half * 128 : half * 128 + 128, :].T * SCALE
        ).astype(BF)
    for copy in copies:
        copy.wait()
    wait_bytes(weight, sems.at[4])
    for c in range(3):
        cols = slice(c * 256, c * 256 + 256)
        part = nn(normed_t[...], grad_proj[:, cols]).astype(BF)
        staged[:, :, :, cols] = part.reshape(staged.shape[:3] + (256,))
    moves = [(half, 0, 384, staged.at[:, :, :, pl.ds(384 * half, 384)]) for half in range(2)]
    if extra:
        moves += [
            (half, -384, 384, staged.at[:, :, :, pl.ds(768 + 384 * half, 384)]) for half in range(2)
        ]
    start_all(piece_copies(out_piece, me[0], outs, moves, sems.at[0], True))
    if final:
        sums[...] = jnp.zeros_like(sums)

    total_copies = []
    for c in range(3):
        cols = slice(c * 256, c * 256 + 256)
        value = nt(grad_proj[...], flat(weight[...])[cols])
        if not extra:
            value = value + total[:, cols]
        total[:, cols] = value
        total_copies.append(
            pltpu.make_async_copy(
                total.at[:, pl.ds(c * 256, 256)], grad_normed.at[:, pl.ds(c * 256, 256)], sems.at[2]
            )
        )
        total_copies[-1].start()
    if final:

        def sum_step(r, carry):
            at = pl.ds(pl.multiple_of(r * QB, QB), QB)
            value = total[at, :]
            hat, _ = norm_parts(refs[11][at, :].astype(F32))
            sums[0:1, :] += jnp.sum(value * hat, axis=0, keepdims=True)
            sums[1:2, :] += jnp.sum(value, axis=0, keepdims=True)
            return carry

        lax.fori_loop(0, length // QB, sum_step, 0)
    wait_bytes(staged, sems.at[0])
    wait_bytes(total, sems.at[2])


def attend_back(
    piece,
    out_piece,
    me,
    normed_t,
    proj,
    att,
    grad_att,
    lse,
    seg_col,
    seg_row,
    slabs,
    branch_t,
    attended,
    held,
    tokens,
    onto,
):
    depth, length = normed_t.shape
    extra = len(attended)
    final = tokens is not None
    columns = 1536 if extra else 768
    ins = [me] + in_hbm([normed_t, proj, att, grad_att, lse]) + [seg_col, seg_row] + in_hbm(slabs)
    specs = [smem_spec(), any_spec()] + [vmem_spec()] * 6 + [any_spec()] * len(slabs)
    if extra:
        ins += in_vmem([branch_t]) + in_hbm(attended)
        specs += [vmem_spec()] * (1 + extra)
    else:
        ins += in_hbm([held])
        specs += [any_spec()]
    if final:
        ins += in_hbm([tokens])
        specs += [any_spec()]
    outs = [pltpu.HBM((length, depth), F32)] + [pltpu.HBM(out_piece.shape, BF)] * 2
    scratch = [
        pltpu.VMEM((2, QB, QB), F32),
        pltpu.VMEM((8, length), F32),
        pltpu.VMEM((256, length), BF),
        pltpu.VMEM((256, length), F32),
        pltpu.VMEM((4, length, 128), BF),
        pltpu.VMEM((4, length, 128), BF),
        pltpu.VMEM(out_piece.rows.shape + (columns,), BF),
        pltpu.VMEM((depth, length), BF),
        pltpu.VMEM((length, depth), F32),
        pltpu.VMEM(piece.rows.shape + (768,), BF),
        pltpu.SemaphoreType.DMA((5,)),
    ]
    if final:
        outs.append(SDS((8, depth), F32))
        scratch.append(pltpu.VMEM((length, depth), BF))
    got = pl.pallas_call(
        functools.partial(attend_back_body, piece, out_piece, extra, len(onto), final),
        in_specs=specs + [any_spec()] * len(onto),
        out_specs=[any_spec()] * 3 + ([vmem_spec()] if final else []),
        out_shape=outs,
        input_output_aliases={len(ins) + k: 1 + k for k in range(len(onto))},
        scratch_shapes=[
            pltpu.VMEM((length, 768), BF),
            pltpu.VMEM((length, 128), F32),
            pltpu.VMEM((length, 128), F32),
        ]
        + scratch,
        compiler_params=params(40),
        cost_estimate=cost(12, 8),
        name="attend_back",
    )(*ins, *in_hbm(onto))
    return got[0], got[1:3], got[3] if final else None


def norm_back_body(
    start, core, tokens, grad_normed, grad_middle, gain, held, other, high, low, own, sem
):
    length = high.shape[0] // 2
    r = pl.program_id(0)
    hat, root = norm_parts(tokens[...].astype(F32))
    value = grad_middle[...] + norm_pull(grad_normed[...], hat, root, gain[...])
    top = value.astype(BF)
    rest = (value - top.astype(F32)).astype(BF)
    for base in (0, length):
        at = pl.ds(pl.multiple_of(base + r * QB, QB), QB)
        high[at, :] = top
        low[at, :] = rest

    @pl.when(r == pl.num_programs(0) - 1)
    def _():
        count = own.shape[0] // QB
        for k in range(count):
            own[k * QB : k * QB + QB, :] = turned([high, low], start[0], k)
        copy = pltpu.make_async_copy(own, held.at[core[0]], sem)
        copy.start()
        for k in range(count):
            other[k * QB : k * QB + QB, :] = turned([high, low], start[0], k + count)
        copy.wait()


def norm_back(start, core, tokens, grad_normed, grad_middle, gain):
    length, depth = tokens.shape
    half = (length // 2, depth)
    return pl.pallas_call(
        norm_back_body,
        grid=(length // QB,),
        in_specs=[smem_spec()] * 2 + [row_spec(depth, QB)] * 3 + [whole_spec((1, depth))],
        out_specs=[any_spec(), whole_spec(half)],
        out_shape=[pltpu.HBM((2,) + half, F32), SDS(half, F32)],
        scratch_shapes=[
            pltpu.VMEM((2 * length, depth), BF),
            pltpu.VMEM((2 * length, depth), BF),
            pltpu.VMEM(half, F32),
            pltpu.SemaphoreType.DMA,
        ],
        compiler_params=params(24),
        cost_estimate=cost(4, 16),
        name="norm_back",
    )(start, core, *in_hbm([tokens, grad_normed, grad_middle]), gain)


def split_far_body(counts, me, *refs):
    keep, send = refs[-2:]
    far = me[0] // 4
    begin = 0
    for count in counts:
        pieces, refs = refs[:count], refs[count:]
        cols = pl.ds(begin, pieces[0].shape[-1])
        begin += pieces[0].shape[-1]
        for k, out in enumerate((keep, send)):
            for slot in range(2):
                at = lax.bitwise_xor(far, k + 2 * slot)
                total = pieces[0][at].astype(F32)
                for piece in pieces[1:]:
                    total = total + piece[at].astype(F32)
                out[slot, :, cols] = total.astype(BF)


def split_far(me, groups):
    width, specs = 0, []
    for pieces in groups:
        far, block, columns = pieces[0].shape[-3:]
        width += columns
        for piece in pieces:
            if piece.ndim == 4:
                specs.append(pl.BlockSpec((None, far, block, columns), lambda i: (0, 0, 0, 0)))
            else:
                specs.append(whole_spec(piece.shape))
    return pl.pallas_call(
        functools.partial(split_far_body, [len(pieces) for pieces in groups]),
        grid=(1,),
        in_specs=[smem_spec()] + specs,
        out_specs=[whole_spec((2, block, width))] * 2,
        out_shape=[SDS((2, block, width), BF)] * 2,
        compiler_params=params(16),
        cost_estimate=cost(1, 2),
        name="split_far",
    )(me, *[piece for pieces in groups for piece in pieces])


def put_sums(ref, base, total):
    high = total.astype(BF)
    ref[base : base + 4, :] = high
    ref[base + 4 : base + 8, :] = (total - high.astype(F32)).astype(BF)
    ref[base + 8 : base + 16, :] = jnp.zeros((8, total.shape[1]), BF)


def get_sums(ref, base):
    return ref[base : base + 4, :].astype(F32) + ref[base + 4 : base + 8, :].astype(F32)


def last_join_body(own, other, sums, sums_away, *outs):
    total = sums[...] + sums_away[...]
    rows = outs[0].shape[0] - 16
    for k, out in enumerate(outs):
        value = own[k].astype(F32) + other[k].astype(F32)
        out[:rows, :] = value.astype(BF).reshape(rows, -1)
        put_sums(out, rows, total)


def last_split_body(me, m0, m1, m2, m3, keep, send):
    far = me[0] // 4
    rows = m0.shape[0] - 16
    block = rows // 4
    for k, out in enumerate((keep, send)):
        for slot in range(2):
            at = pl.ds(pl.multiple_of(lax.bitwise_xor(far, k + 2 * slot) * block, 16), block)
            total = (m0[at, :].astype(F32) + m1[at, :].astype(F32)) + (
                m2[at, :].astype(F32) + m3[at, :].astype(F32)
            )
            out[slot * block : (slot + 1) * block, :] = total.astype(BF)
    total = (get_sums(m0, rows) + get_sums(m1, rows)) + (get_sums(m2, rows) + get_sums(m3, rows))
    put_sums(keep, 2 * block, total)
    put_sums(send, 2 * block, total)


def last_middle_body(keep, near, rest, send):
    block = (keep.shape[0] - 16) // 2
    value = keep[:block, :].astype(F32) + near[:block, :].astype(F32)
    rest[:block, :] = value.astype(BF)
    value = keep[block : 2 * block, :].astype(F32) + near[block : 2 * block, :].astype(F32)
    send[:block, :] = value.astype(BF)
    total = get_sums(keep, 2 * block) + get_sums(near, 2 * block)
    put_sums(rest, block, total)
    put_sums(send, block, total)


def last_sum_body(rest, away, first, grad_qkv, sums):
    block = rest.shape[0] - 16
    value = rest[:block, :].astype(F32) + away[:block, :].astype(F32)
    parts = [first[:, 384:], value[:, :384], value[:, 384:]]
    for which in range(3):
        cols = slice(which * 128, which * 128 + 128)
        grad_qkv[which] = jnp.concatenate([part[:, cols] for part in parts], 1)
    sums[...] = get_sums(rest, block) + get_sums(away, block)


def pack_body(part, out, up, down, packed):
    width = out.shape[1]
    packed[:, :width] = out[...]
    for s in range(up.shape[1] // part):
        cols = slice(s * part, (s + 1) * part)
        packed[:, width + 2 * s * part : width + (2 * s + 1) * part] = up[:, cols]
        packed[:, width + (2 * s + 1) * part : width + (2 * s + 2) * part] = down[:, cols]


def small_call(body, name, outs, scalars, values):
    return pl.pallas_call(
        body,
        in_specs=[smem_spec()] * len(scalars) + [vmem_spec()] * len(values),
        out_specs=[vmem_spec()] * len(outs),
        out_shape=outs,
        compiler_params=params(16),
        cost_estimate=cost(1, 3),
        name=name,
    )(*scalars, *values)


def swap(value):
    return lax.ppermute(value, "mp", [(0, 1), (1, 0)])


def tie(*values):
    return lax.optimization_barrier(values)


def hop(value, mask, count):
    return lax.ppermute(value, "dp", [(i, i ^ mask) for i in range(count)])


def hops(value, masks, count):
    return [(value, functools.partial(hop, mask=m, count=count)) for m in masks]


def far_hops(rows, values):
    return [
        (v, functools.partial(hop, mask=rows.near * m, count=rows.dp_count))
        for m, v in zip(range(1, rows.far), values)
    ]


def swaps(values):
    return [(v, swap) for v in values]


def send_all(requests):
    return [send(value) for value, send in requests]


def low_sum(values):
    total = values[0].astype(F32)
    for value in values[1:]:
        total = total + value.astype(F32)
    return total


class Flow:
    def __init__(self, me):
        self.me = me
        self.active = []

    def add(self, transfer, name, results, seeds=()):
        self.active.append([transfer, list(seeds), name, results])

    def step(self, *pivots):
        values = [v for item in self.active for v in item[1]]
        tied = list(tie(self.me, *pivots, *values))
        self.me = tied.pop(0)
        pivots, tied = tied[: len(pivots)], tied[len(pivots) :]
        going, self.active, requests = self.active, [], []
        for item in going:
            transfer, values, name, results = item
            got, tied = tied[: len(values)], tied[len(values) :]
            try:
                if callable(transfer):
                    item[0] = transfer(*got)
                    asked = next(item[0])
                else:
                    asked = transfer.send(got)
                self.active.append(item)
                requests.append(asked)
            except StopIteration as stop:
                results[name] = stop.value
        tied = list(tie(self.me, *(operand for asked in requests for operand, _ in asked)))
        self.me = tied.pop(0)
        for item, asked in zip(self.active, requests):
            item[1] = [send(operand) for (_, send), operand in zip(asked, tied)]
            tied = tied[len(asked) :]
        return pivots


def add_low(a, b):
    return (a.astype(F32) + b.astype(F32)).astype(BF)


def on_device(
    tokens, segment, ln1_gain, ln1_bias, w_qkv, w_out, ln2_gain, ln2_bias, w_up, w_down, cotangent
):
    dp_count = lax.axis_size("dp")
    core = lax.axis_index("mp")
    me = lax.axis_index("dp").astype(jnp.int32).reshape(1)
    here, depth = tokens.shape[2], tokens.shape[3]
    length = 2 * here
    rows = Rows(dp_count, depth)

    groups = w_qkv.shape[2] // 128
    part = 384
    subs = w_up.shape[1] // part
    cut = subs // 2
    qkv = [w_qkv[:, :, g * 128 : (g + 1) * 128].reshape(-1, part) for g in range(groups)]
    shards = {"q": jnp.concatenate(qkv, 1)}

    shard_a = small_call(
        functools.partial(pack_body, part),
        "pack",
        [SDS((w_up.shape[0], w_out.shape[0] + 2 * w_up.shape[1]), BF)],
        [],
        [w_out.T, w_up, w_down.T],
    )[0]

    seg = lax.dynamic_index_in_dim(segment[:, 0], core, 0, keepdims=False)
    run = length * 3 // 4
    begin = jnp.argmax(seg[: length - run + 1] == seg[run - 1 :]).astype(jnp.int32)
    start = ((begin - here * core) % length).reshape(1)
    back = (length - start) % length
    seg_tail = lax.dynamic_slice_in_dim(jnp.concatenate([seg, seg]), begin + run, length - run)
    seg_col = seg_tail.reshape(-1, 1)
    seg_row = seg_tail.reshape(1, -1)
    gain1, bias1, gain2, bias2 = (
        v.reshape(1, -1) for v in (ln1_gain, ln1_bias, ln2_gain, ln2_bias)
    )

    flow = Flow(me)
    core_place = core.astype(jnp.int32).reshape(1)
    token_halves = [tokens[:, 0], swap(tokens[:, 0])]
    cot_halves = [cotangent[:, 0], swap(cotangent[:, 0])]
    wide = 2 * part
    qkv_pieces = [Piece(rows, "slabs")] + [Piece(rows, "slabs", part * g) for g in range(groups - 1)]
    out_piece = Piece(rows, "slabs")
    feed_pieces = [Piece(rows, "slabs", part + wide * s) for s in range(cut)]
    feed_pieces += [Piece(rows, "slabs", wide * s) for s in range(subs - cut)]
    turns = [(0, 2, 1, 3), MASKS]
    feed_outs = [
        Piece(rows, "stack", wide * (s % cut), wide * cut, turns[s % cut]) for s in range(subs)
    ]
    qkv_outs = [Piece(rows, "stack", part, wide)]
    qkv_outs += [Piece(rows, "stack", part * g, part * (groups - 1)) for g in range(groups - 1)]
    far = lax.axis_index("dp") // rows.near

    def gather_whole(shard):
        return lax.all_gather(shard, "dp", axis=0, tiled=True).reshape(rows.shape + (-1,))

    def fetch_near(near):
        got = yield hops(near, MASKS[1:], dp_count)
        own = [near] + got
        return own + [swap(x) for x in own]

    def via(mask):
        return functools.partial(hop, mask=mask, count=dp_count)

    def fetch_wide(shard, away):
        near, both_ways = yield [(shard, via(4)), (away, via(4))]
        (a0,) = arrange(rows, flow.me, [shard, near, away, both_ways], [shard.shape[1]])
        a1, a2, b0, away = yield [(a0, via(1)), (a0, via(2))] + swaps([a0]) + [(shard_c, via(8))]
        a3, b1, b2, near, both_ways = yield (
            [(a1, via(2))] + swaps([a1, a2]) + [(shard_c, via(4)), (away, via(4))]
        )
        slabs["a"] = [a0, a1, a2, a3, b0, b1, b2, swap(a3)]
        (c0,) = arrange(rows, flow.me, [shard_c, near, away, both_ways], [shard_c.shape[1]])
        (d0,) = yield swaps([c0])
        c1, c2 = yield [(c0, via(1)), (c0, via(2))]
        c3, d1, d2 = yield [(c2, via(1))] + swaps([c1, c2])
        return [c0, c1, c2, c3, d0, d1, d2, swap(c3)]

    def whole(shard):
        own = gather_whole(shard)
        return [own, swap(own)]

    def halve(own, other):
        (other,) = yield swaps([other])
        middle_col = own.shape[-1] // 2
        keep, send = [], []
        for cols in (slice(0, middle_col), slice(middle_col, None)):
            keep.append(low_sum([own[:2, ..., cols], other[:2, ..., cols]]).astype(BF))
            send.append(low_sum([own[2:, ..., cols], other[2:, ..., cols]]).astype(BF))
        near = yield [(v, via(m)) for v, m in zip(send, (1, 2))]
        send = [low_sum([k[1], n[1]]).astype(BF) for k, n in zip(keep, near)]
        away = yield [(v, via(m)) for v, m in zip(send, (2, 1))]
        return [list(group) for group in zip(keep, near, away)]

    def direct(mine):
        got = yield hops_of(mine, (1, 2, 3))
        return [mine[0]] + got

    def hops_of(values, masks):
        return [(values[m], via(m)) for m in masks]

    def reduce_far(groups):
        keep, send = split_far(flow.me, groups)
        (near,) = yield [(send, via(4))]
        (away,) = yield [(low_sum([keep[1], near[1]]).astype(BF), via(8))]
        return low_sum([keep[0], near[0], away])

    def reduce_all(own, other):
        groups_here = yield from halve(own, other)
        return (yield from reduce_far(sums_of["early"] + groups_here))

    def reduce_last(own, other, sums):
        other, sums_away = swap(other), swap(sums)
        mine = small_call(
            last_join_body,
            "last_join",
            [SDS((rows.far * rows.block + 16, wide), BF)] * 4,
            [],
            [own, other, sums, sums_away],
        )
        return (yield from direct(mine))

    def exchange(value):
        (got,) = yield swaps([value])
        return got

    def reduce_direct(own, other):
        (other,) = yield swaps([other])
        mine = [low_sum([own[k], other[k]]).astype(BF) for k in range(4)]
        pieces = yield from direct(mine)
        return (yield from reduce_far([pieces]))

    def plain(own, other):
        value = low_sum([own, swap(other)]).astype(BF).reshape(depth, -1)
        return lax.psum_scatter(value, "dp", scatter_dimension=0, tiled=True).astype(F32)

    def run(transfer):
        requests = next(transfer)
        while True:
            try:
                requests = transfer.send(send_all(requests))
            except StopIteration as stop:
                return stop.value

    slabs, forward = {}, []

    def project(g):
        name = "q0" if g == 0 else "q1"
        forward.append(
            project_attend(qkv_pieces[g], flow.me, normed, seg_col, seg_row, slabs[name])
        )

    if rows.split:
        shard_q = shards["q"]
        got = send_all(far_hops(rows, [shard_q] * (rows.far - 1)))
        prepared = prepare(start, core_place, *token_halves, gain1, bias1)
        tied = tie(*got, *prepared, shard_a)
        got, prepared, shard_a = tied[:3], tied[3:6], tied[6]
        near_q0, near_q1 = arrange(rows, me, [shard_q] + list(got), [part, wide])
        own = [near_q0] + [hop(near_q0, m, dp_count) for m in MASKS[1:]]
        first_cols = part + wide * cut
        shard_c, shard_a = shard_a[:, first_cols:], shard_a[:, :first_cols]
        away_a = hop(shard_a, 8, dp_count)
        start_cot, _ = tie(start, near_q0)
        turned_cot = turn(start_cot, core_place, *cot_halves)
        tied = tie(*own, *turned_cot)
        own, turned_cot = tied[:4], tied[4:]
        slabs["q0"] = list(own) + [swap(v) for v in own]
        flow.add(fetch_near, "q1", slabs, [near_q1])
        flow.add(fetch_wide, "c", slabs, [shard_a, away_a])
        flow.step(own[3])
    else:
        for name, shard in (
            ("q0", shards["q"][:, :part]),
            ("q1", shards["q"][:, part:]),
            ("a", shard_a[:, : part + wide * cut]),
            ("c", shard_a[:, part + wide * cut :]),
        ):
            slabs[name] = whole(shard)
        prepared = prepare(start, core_place, *token_halves, gain1, bias1)
        turned_cot = turn(start, core_place, *cot_halves)
    x, normed, normed_t = prepared
    cot, cot_t = turned_cot
    for g in range(groups):
        project(g)
        flow.step(forward[g][2])
    atts = [f[1] for f in forward]
    middle, normed_ffn, normed_ffn_t = out_norm(
        out_piece, flow.me, x, gain2, bias2, atts, slabs["a"]
    )
    flow.step(normed_ffn)

    held = None
    sums_of = {}
    onto = []
    feed_names = ["a"] * cut + ["c"] * (subs - cut)
    for s in range(subs):
        final = s == subs - 1
        grads, held = feed_forward(
            feed_pieces[s],
            feed_outs[s],
            flow.me,
            normed_ffn,
            normed_ffn_t,
            cot,
            cot_t,
            held,
            slabs[feed_names[s]],
            onto,
            (out_piece, slabs["a"], middle, gain2, groups) if final else None,
        )
        onto = grads
        if s % cut == cut - 1:
            k = s // cut
            if rows.split and k == 0:
                flow.add(halve, "early", sums_of, grads)
            elif rows.split:
                flow.add(reduce_all, "feed", sums_of, grads)
            else:
                sums_of[k] = plain(*grads)
            onto = []
        if not final:
            flow.step(held[1])
    mixed, grad_middle, branch_t, sums2, *grad_atts = held
    mixed, core_place, _ = flow.step(mixed, core_place, sums2)
    mixed_held, mixed_other = turn_back(back, core_place, mixed)
    flow.add(exchange, "mixed", sums_of, [mixed_other])
    grad_projs = []
    onto = []

    held = None
    qkv_slabs = [slabs["q0"]] + [slabs["q1"]] * (groups - 1)
    for g in range(groups):
        proj, att, lse = forward[g]
        held, grads, sums1 = attend_back(
            qkv_pieces[g],
            qkv_outs[g],
            flow.me,
            normed_t,
            proj,
            att,
            grad_atts[g],
            lse,
            seg_col,
            seg_row,
            qkv_slabs[g],
            branch_t,
            atts if g == 0 else [],
            held,
            x if g == groups - 1 else None,
            onto,
        )
        onto = grads
        if g == 0:
            if rows.split:
                flow.add(reduce_direct, "first", sums_of, grads)
            else:
                sums_of["first"] = plain(*grads)
            onto = []
        if g < groups - 1:
            flow.step(held)
    sums = jnp.concatenate([sums1[:2], sums2[:2]], 0)
    if rows.split:
        flow.add(reduce_last, "last", sums_of, [*grads, sums])
        (held,) = flow.step(held)
    else:
        sums_of["last"] = plain(*grads)
    start_late, _ = tie(back, flow.me)
    tokens_held, tokens_other = norm_back(start_late, core_place, x, held, grad_middle, gain1)
    tokens_held, tokens_other = flow.step(tokens_held, tokens_other)
    if rows.split:
        block = rows.block
        keep, send = small_call(
            last_split_body,
            "last_split",
            [SDS((2 * block + 16, wide), BF)] * 2,
            [flow.me],
            sums_of["last"],
        )
        near = hop(send, 4, dp_count)
        rest, send = small_call(
            last_middle_body, "last_middle", [SDS((block + 16, wide), BF)] * 2, [], [keep, near]
        )
        away = hop(send, 8, dp_count)
        while flow.active:
            flow.step()
        grad_qkv, norm_sums = small_call(
            last_sum_body,
            "last_sum",
            [SDS((3, block, part), F32), SDS((4, depth), F32)],
            [],
            [rest, away, sums_of["first"]],
        )
        grad_qkv = grad_qkv.transpose(1, 0, 2)
        grad_out = sums_of["first"][:, :part].T
        feed_sums = [sums_of["feed"]]
    else:
        early, last = sums_of["first"], sums_of["last"]
        parts = [early[:, part:], last[:, :part], last[:, part:]]
        grad_qkv = jnp.concatenate([r.reshape(-1, 3, 128) for r in parts], 2)
        grad_out = early[:, :part].T
        feed_sums = [sums_of[0], sums_of[1]]
        norm_sums = jnp.sum(lax.all_gather(sums + swap(sums), "dp", axis=0), 0)
    feed_sum = jnp.concatenate(feed_sums, 1) if len(feed_sums) > 1 else feed_sums[0]
    feed_list = [feed_sum[:, wide * s : wide * (s + 1)] for s in range(subs)]

    return (
        place(core_place, mixed_held, sums_of["mixed"])[:, None],
        place(core_place, tokens_held, swap(tokens_other))[:, None],
        norm_sums[0],
        norm_sums[1],
        grad_qkv,
        grad_out,
        norm_sums[2],
        norm_sums[3],
        jnp.concatenate([r[:, :part] for r in feed_list], 1),
        jnp.concatenate([r[:, part:] for r in feed_list], 1).T,
    )


def solution(mesh):
    in_specs = (
        P(None, "dp", "mp", None),
        P(None, "dp", None),
        P(),
        P(),
        P("dp", None, "mp"),
        P("mp", "dp"),
        P(),
        P(),
        P("dp", "mp"),
        P("mp", "dp"),
        P(None, "dp", "mp", None),
    )
    out_specs = (
        P(None, "dp", "mp", None),
        P(None, "dp", "mp", None),
        P(),
        P(),
        P("dp", None, "mp"),
        P("mp", "dp"),
        P(),
        P(),
        P("dp", "mp"),
        P("mp", "dp"),
    )
    return jax.shard_map(
        on_device, mesh=mesh, in_specs=in_specs, out_specs=out_specs, check_vma=False
    )
```

```python
import functools
import math

import jax
import jax.numpy as jnp
from jax import lax
from jax.experimental import pallas as pl
from jax.experimental.pallas import tpu as pltpu
from jax.sharding import PartitionSpec as P

HD = 32
QB = 256
EPS = 1e-05
BF = jnp.bfloat16
F32 = jnp.float32
NEG = -1e30
SCALE = 1.0 / math.sqrt(HD)
LOG2E = math.log2(math.e)
C2 = SCALE * LOG2E
MIB = 1024 * 1024
SDS = jax.ShapeDtypeStruct


def nn(a, b):
    return lax.dot_general(a, b, (((1,), (0,)), ((), ())), preferred_element_type=F32)


def nt(a, b):
    return lax.dot_general(a, b, (((1,), (1,)), ((), ())), preferred_element_type=F32)


def params(mib):
    return pltpu.CompilerParams(vmem_limit_bytes=mib * MIB)


def in_hbm(values):
    return [pltpu.with_memory_space_constraint(v, pltpu.HBM) for v in values]


def in_vmem(values):
    return [pltpu.with_memory_space_constraint(v, pltpu.VMEM) for v in values]


def cost(gflop, mbytes):
    return pl.CostEstimate(flops=int(gflop * 1e9), bytes_accessed=int(mbytes * 1e6), transcendentals=0)


def any_spec():
    return pl.BlockSpec(memory_space=pl.ANY)


def smem_spec():
    return pl.BlockSpec(memory_space=pltpu.SMEM)


def vmem_spec():
    return pl.BlockSpec(memory_space=pltpu.VMEM)


def row_spec(width, rows=512):
    return pl.BlockSpec((rows, width), lambda r: (r, 0))


def column_spec(height, rows=512):
    return pl.BlockSpec((height, rows), lambda r: (0, r))


def whole_spec(shape):
    return pl.BlockSpec(shape, lambda r: tuple(0 for _ in shape))


MASKS = (0, 1, 2, 3)


class Rows:
    def __init__(self, dp_count, depth):
        self.dp_count = dp_count
        self.depth = depth
        self.split = (depth // dp_count) % 16 == 0 and dp_count == 16
        self.near = 4 if self.split else 1
        self.far = dp_count // 4 if self.split else 1
        self.block = depth // (self.near * self.far)
        self.shape = (self.far, self.near, self.block)


class Piece:
    def __init__(self, rows, kind, start=0, width=0, masks=MASKS):
        self.rows = rows
        self.masks = masks
        self.kind = kind if rows.split else "whole"
        self.start = start
        self.count = 2 * len(MASKS) if self.kind == "slabs" else 2
        if self.kind == "stack":
            self.shape = (len(MASKS), rows.far, rows.block, width)
        else:
            self.shape = rows.shape + (width,)


def piece_copies(piece, me, refs, moves, sem, outward):
    copies = []
    each = piece.count // 2
    for half, column, width, view in moves:
        cols = pl.ds(piece.start + column, width)
        if piece.kind == "whole":
            pairs = [(refs[half].at[:, :, :, cols], view)]
        else:
            pairs = []
            for k, mask in enumerate(piece.masks):
                ref = refs[half].at[k] if piece.kind == "stack" else refs[half * each + k]
                near = lax.bitwise_xor(lax.rem(me, 4), mask)
                pairs.append((ref.at[:, :, cols], view.at[:, near]))
        for outside, inside in pairs:
            if outward:
                copies.append(pltpu.make_async_copy(inside, outside, sem))
            else:
                copies.append(pltpu.make_async_copy(outside, inside, sem))
    return copies


def start_all(copies):
    for copy in copies:
        copy.start()


def wait_bytes(ref, sem):
    pltpu.make_async_copy(ref, ref, sem).wait()


def flat(value):
    return value.reshape(-1, value.shape[-1])


def head_row(h):
    return lax.broadcasted_iota(jnp.int32, (1, 128), 1) // HD == h


def fill_bias(bias, seg_col, seg_row):
    key = lax.broadcasted_iota(jnp.int32, (QB, QB), 0)
    query = lax.broadcasted_iota(jnp.int32, (QB, QB), 1)
    bias[0] = jnp.where(query >= key, 0.0, NEG)
    bias[1] = jnp.where((query >= key) & (seg_col[...] == seg_row[...]), 0.0, NEG)


def turned(doubles, start, r):
    coarse = pl.multiple_of(start // 16 * 16 + r * QB, 16)
    fine = start % 16
    row = lax.broadcasted_iota(jnp.int32, (QB, QB + 16), 0)
    col = lax.broadcasted_iota(jnp.int32, (QB, QB + 16), 1)
    pick = jnp.where(col - row == fine, 1.0, 0.0).astype(BF)
    total = None
    for double in doubles:
        part = nn(pick, double[pl.ds(coarse, QB + 16), :])
        total = part if total is None else total + part
    return total


def norm_parts(values):
    centered = values - jnp.mean(values, axis=-1, keepdims=True)
    spread = jnp.mean(centered * centered, axis=-1, keepdims=True)
    root = lax.rsqrt(spread + EPS)
    return centered * root, root


def start_double(double, core, own, other, sem):
    here = own.shape[1]
    halves = (own, other)
    for k in range(4):
        pltpu.make_async_copy(halves[k % 2].at[core], double.at[pl.ds(k * here, here)], sem).start()


def prepare_body(start, core, own, other, gain, offset, x_out, normed_out, normed_t_out, double, x, normed, normed_t, sems):
    start_double(double, core[0], own, other, sems.at[3])
    wait_bytes(double, sems.at[3])

    def step(r, carry):
        at = pl.ds(pl.multiple_of(r * QB, QB), QB)
        value = turned([double], start[0], r)
        x[at, :] = value.astype(BF)
        hat, _ = norm_parts(value)
        low = (hat * gain[...] + offset[...]).astype(BF)
        normed[at, :] = low
        normed_t[:, at] = low.T
        return carry

    lax.fori_loop(0, x.shape[0] // QB, step, 0)
    copies = [
        pltpu.make_async_copy(normed, normed_out, sems.at[0]),
        pltpu.make_async_copy(x, x_out, sems.at[1]),
        pltpu.make_async_copy(normed_t, normed_t_out, sems.at[2]),
    ]
    start_all(copies)
    for copy in copies:
        copy.wait()


def prepare(start, core, own, other, gain, offset):
    _, here, depth = own.shape
    shape, shape_t = (2 * here, depth), (depth, 2 * here)
    shapes = [shape, shape, shape_t]
    return pl.pallas_call(
        prepare_body,
        in_specs=[smem_spec()] * 2 + [any_spec()] * 2 + [vmem_spec()] * 2,
        out_specs=[any_spec()] * 3,
        out_shape=[pltpu.HBM(s, BF) for s in shapes],
        scratch_shapes=[pltpu.VMEM((4 * here, depth), BF)]
        + [pltpu.VMEM(s, BF) for s in shapes]
        + [pltpu.SemaphoreType.DMA((4,))],
        compiler_params=params(20),
        cost_estimate=cost(4, 8),
        name="prepare",
    )(start, core, *in_hbm([own, other]), gain, offset)


def turn_body(start, core, own, other, cot_out, cot_t_out, double, cot, cot_t, sems):
    start_double(double, core[0], own, other, sems.at[2])
    wait_bytes(double, sems.at[2])

    def step(r, carry):
        at = pl.ds(pl.multiple_of(r * QB, QB), QB)
        low = turned([double], start[0], r).astype(BF)
        cot[at, :] = low
        cot_t[:, at] = low.T
        return carry

    lax.fori_loop(0, cot.shape[0] // QB, step, 0)
    copies = [
        pltpu.make_async_copy(cot, cot_out, sems.at[0]),
        pltpu.make_async_copy(cot_t, cot_t_out, sems.at[1]),
    ]
    start_all(copies)
    for copy in copies:
        copy.wait()


def turn(start, core, own, other):
    _, here, depth = own.shape
    shapes = [(2 * here, depth), (depth, 2 * here)]
    return pl.pallas_call(
        turn_body,
        in_specs=[smem_spec()] * 2 + [any_spec()] * 2,
        out_specs=[any_spec()] * 2,
        out_shape=[pltpu.HBM(s, BF) for s in shapes],
        scratch_shapes=[pltpu.VMEM((4 * here, depth), BF)]
        + [pltpu.VMEM(s, BF) for s in shapes]
        + [pltpu.SemaphoreType.DMA((3,))],
        compiler_params=params(16),
        cost_estimate=cost(4, 8),
        name="turn",
    )(start, core, *in_hbm([own, other]))


def turn_back_body(start, core, values, held, other, double, own, sem):
    here = other.shape[0]
    double[: 2 * here, :] = values[...]
    double[2 * here :, :] = values[...]
    count = here // QB

    def step(r, carry):
        at = pl.ds(pl.multiple_of(r * QB, QB), QB)
        own[at, :] = turned([double], start[0], r).astype(BF)
        other[at, :] = turned([double], start[0], r + count).astype(BF)
        return carry

    lax.fori_loop(0, count, step, 0)
    copy = pltpu.make_async_copy(own, held.at[core[0]], sem)
    copy.start()
    copy.wait()


def place_body(core, other, held, out, sem):
    copy = pltpu.make_async_copy(other, out.at[1 - core[0]], sem)
    copy.start()
    copy.wait()


def place(core, held, other):
    return pl.pallas_call(
        place_body,
        in_specs=[smem_spec(), any_spec(), any_spec()],
        out_specs=any_spec(),
        out_shape=pltpu.HBM(held.shape, held.dtype),
        input_output_aliases={2: 0},
        scratch_shapes=[pltpu.SemaphoreType.DMA],
        compiler_params=params(4),
        cost_estimate=cost(0, 4),
        name="place",
    )(core, other, *in_hbm([held]))


def turn_back(start, core, values):
    length, depth = values.shape
    half = (length // 2, depth)
    return pl.pallas_call(
        turn_back_body,
        in_specs=[smem_spec()] * 2 + [vmem_spec()],
        out_specs=[any_spec(), vmem_spec()],
        out_shape=[pltpu.HBM((2,) + half, BF), SDS(half, BF)],
        scratch_shapes=[
            pltpu.VMEM((2 * length, depth), BF),
            pltpu.VMEM(half, BF),
            pltpu.SemaphoreType.DMA,
        ],
        compiler_params=params(16),
        cost_estimate=cost(2, 4),
        name="turn_back",
    )(start, core, values)


def arrange_body(widths, me, *refs):
    pieces, outs = refs[:4], refs[4:]
    far = me[0] // 4
    for m, piece in enumerate(pieces):
        begin = 0
        for out, width in zip(outs, widths):
            out[lax.bitwise_xor(far, m)] = piece[:, begin : begin + width]
            begin += width


def arrange(rows, me, pieces, widths):
    return pl.pallas_call(
        functools.partial(arrange_body, widths),
        in_specs=[smem_spec()] + [vmem_spec()] * 4,
        out_specs=[vmem_spec()] * len(widths),
        out_shape=[SDS((rows.far, rows.block, w), BF) for w in widths],
        compiler_params=params(8),
        cost_estimate=cost(1, 1),
        name="arrange",
    )(me, *pieces)


def project_attend_body(piece, me, normed_in, seg_col, seg_row, *refs):
    slabs = refs[: piece.count]
    proj_out, att, lse, weight, proj, normed, bias, keys_m, values_t, att_t, sem, out_sem = refs[
        piece.count :
    ]
    normed_copy = pltpu.make_async_copy(normed_in, normed, out_sem)
    normed_copy.start()
    moves = [(half, 0, 384, weight.at[:, :, :, pl.ds(384 * half, 384)]) for half in range(2)]
    start_all(piece_copies(piece, me[0], slabs, moves, sem, False))
    fill_bias(bias, seg_col, seg_row)
    values_t[...] = jnp.ones_like(values_t)
    normed_copy.wait()
    wait_bytes(weight, sem)

    for c in range(3):
        cols = slice(c * 256, c * 256 + 256)
        proj[:, cols] = nn(normed[...], flat(weight[:, :, :, cols])).astype(BF)
    proj_copy = pltpu.make_async_copy(proj, proj_out, out_sem)
    proj_copy.start()
    for half in range(2):
        flipped = proj[:, half * 384 + 256 : half * 384 + 384].T
        for h in range(4):
            values_t[half * 4 + h, 0:HD, :] = flipped[h * HD : (h + 1) * HD]

    units = [(h, i) for i in (2, 1, 0, 3) for h in range(4)]

    def step(half, carry):
        col = pl.multiple_of(half * 384, 128)
        for h in range(4):
            keys_m[h] = jnp.where(head_row(h), proj[:, pl.ds(col + 128, 128)], 0)

        def score(h, i):
            first = 768 if i == 3 else 0
            scores = nt(keys_m[h, first : (i + 1) * QB, :], proj[i * QB : (i + 1) * QB, pl.ds(col, 128)])
            edge = scores[-QB:] + bias[1 if i == 3 else 0]
            return jnp.concatenate([scores[:-QB], edge], 0) if scores.shape[0] > QB else edge

        ahead = score(*units[0])
        for k, (h, i) in enumerate(units):
            scores = ahead
            if k + 1 < len(units):
                ahead = score(*units[k + 1])
            first = 768 if i == 3 else 0
            last = (i + 1) * QB
            at = slice(i * QB, last)
            peak = jnp.max(scores, axis=0, keepdims=True) * C2
            probs = jnp.exp2(scores * C2 - peak).astype(BF)
            summed = nn(values_t[half * 4 + h, :, first:last], probs)
            total = summed[HD : HD + 1]
            att_t[pl.ds(pl.multiple_of(half * 128 + h * HD, HD), HD), at] = summed[:HD] / total
            lse[pl.ds(half * 4 + h, 1), at] = peak + jnp.log2(total)
        return carry

    lax.fori_loop(0, 2, step, 0)
    for half in range(2):
        cols = slice(half * 128, half * 128 + 128)
        att[:, cols] = att_t[cols, :].T.astype(BF)
    proj_copy.wait()


def project_attend(piece, me, normed, seg_col, seg_row, slabs):
    length, depth = normed.shape
    rows = piece.rows
    return pl.pallas_call(
        functools.partial(project_attend_body, piece),
        in_specs=[smem_spec(), any_spec()] + [vmem_spec()] * 2 + [any_spec()] * len(slabs),
        out_specs=[any_spec()] + [vmem_spec()] * 2,
        out_shape=[
            pltpu.HBM((length, 768), BF),
            pltpu.HBM((length, 256), BF),
            pltpu.HBM((8, length), F32),
        ],
        scratch_shapes=[
            pltpu.VMEM(rows.shape + (768,), BF),
            pltpu.VMEM((length, 768), BF),
            pltpu.VMEM((length, depth), BF),
            pltpu.VMEM((2, QB, QB), F32),
            pltpu.VMEM((4, length, 128), BF),
            pltpu.VMEM((8, HD + 16, length), BF),
            pltpu.VMEM((256, length), F32),
            pltpu.SemaphoreType.DMA,
            pltpu.SemaphoreType.DMA,
        ],
        compiler_params=params(20),
        cost_estimate=cost(8, 8),
        name="project_attend",
    )(me, *in_hbm([normed]), seg_col, seg_row, *in_hbm(slabs))


def join_heads(attended):
    return jnp.concatenate([a[:, :128] for a in attended] + [a[:, 128:] for a in attended], 1)


def out_norm_body(piece, groups, me, tokens, gain, offset, *refs):
    attended = refs[:groups]
    slabs = refs[groups : groups + piece.count]
    middle, normed, normed_t, weight, sem = refs[groups + piece.count :]
    width = weight.shape[3] // 2

    @pl.when(pl.program_id(0) == 0)
    def _():
        moves = [(half, 0, width, weight.at[:, :, :, pl.ds(width * half, width)]) for half in range(2)]
        start_all(piece_copies(piece, me[0], slabs, moves, sem, False))
        wait_bytes(weight, sem)

    value = tokens[...].astype(F32) + nt(join_heads([a[...] for a in attended]), flat(weight[...]))
    middle[...] = value
    hat, _ = norm_parts(value)
    low = (hat * gain[...] + offset[...]).astype(BF)
    normed[...] = low
    normed_t[...] = low.T


def out_norm(piece, me, tokens, gain, offset, attended, slabs):
    length, depth = tokens.shape
    return pl.pallas_call(
        functools.partial(out_norm_body, piece, len(attended)),
        grid=(length // 512,),
        in_specs=[smem_spec(), row_spec(depth), whole_spec((1, depth)), whole_spec((1, depth))]
        + [row_spec(256)] * len(attended)
        + [any_spec()] * len(slabs),
        out_specs=[row_spec(depth)] * 2 + [column_spec(depth)],
        out_shape=[
            pltpu.HBM((length, depth), F32),
            pltpu.VMEM((length, depth), BF),
            pltpu.VMEM((depth, length), BF),
        ],
        scratch_shapes=[pltpu.VMEM(piece.rows.shape + (depth,), BF), pltpu.SemaphoreType.DMA],
        compiler_params=params(28),
        cost_estimate=cost(3, 8),
        name="out_norm",
    )(me, *in_hbm([tokens]), gain, offset, *in_hbm(attended), *in_hbm(slabs))


def gelu_parts(values):
    size = jnp.abs(values)
    density = jnp.exp2(values * values * (-0.5 * LOG2E) + math.log2(1.0 / math.sqrt(2 * math.pi)))
    below = 1.0 + 0.2316419 * size
    t = pl.reciprocal(below, approx=True)
    t = t * (2.0 - below * t)
    poly = t * (
        0.319381530
        + t * (-0.356563782 + t * (1.781477937 + t * (-1.821255978 + t * 1.330274429)))
    )
    tail = density * poly
    below = jnp.where(values >= 0, 1.0 - tail, tail)
    return values * below, below + values * density


def norm_pull(grad, hat, root, gain):
    scaled = grad * gain
    first = jnp.mean(scaled, axis=-1, keepdims=True)
    second = jnp.mean(scaled * hat, axis=-1, keepdims=True)
    return root * (scaled - first - hat * second)


def feed_forward_body(
    piece, out_piece, first, last_piece, groups, aliased, me, normed, normed_t, cot, cot_t, *refs
):
    refs = list(refs)
    final = last_piece is not None
    held = [] if first else [refs.pop(0), refs.pop(0)]
    if final:
        middle, gain = refs.pop(0), refs.pop(0)
        out_slabs, refs = refs[: last_piece.count], refs[last_piece.count :]
    slabs, refs = refs[: piece.count], refs[piece.count + aliased :]
    outs, refs = refs[:2], refs[2:]
    mixed = refs.pop(0)
    if final:
        grad_middle_out, branch_t, sums = refs[:3]
        grad_att, refs = refs[3 : 3 + groups], refs[3 + groups :]
    else:
        grad_in = refs.pop(0)
    weight, staged, act, grad_hidden, mixed_acc, grad_acc, sems = refs[:7]
    if final:
        mixed_low, middle_here, out_weight, grad_middle = refs[7:]
    length, depth = normed.shape
    moves = []
    for half in range(2):
        for which in range(2):
            at = pl.ds(which * 768 + half * 384, 384)
            moves.append((half, which * 384, 384, at))
    into = [(h, c, w, weight.at[:, :, :, at]) for h, c, w, at in moves]
    outof = [(h, c, w, staged.at[:, :, :, at]) for h, c, w, at in moves]
    start_all(piece_copies(piece, me[0], slabs, into, sems.at[0], False))
    held_copies = []
    if not first:
        held_copies.append(pltpu.make_async_copy(held[0], mixed_acc, sems.at[1]))
        held_copies.append(pltpu.make_async_copy(held[1], grad_acc, sems.at[2]))
    if final:
        held_copies.append(pltpu.make_async_copy(middle, middle_here, sems.at[4]))
    start_all(held_copies)
    if final:
        width = depth // 2
        views = [
            (half, 0, width, out_weight.at[:, :, :, pl.ds(width * half, width)]) for half in range(2)
        ]
        start_all(piece_copies(last_piece, me[0], out_slabs, views, sems.at[5], False))
    wait_bytes(weight, sems.at[0])
    chunks = [slice(c * 256, c * 256 + 256) for c in range(3)]

    def products(c):
        hidden = nn(normed[...], flat(weight[:, :, :, c * 256 : c * 256 + 256]))
        return hidden, nn(cot[...], flat(weight[:, :, :, 768 + c * 256 : 1024 + c * 256]))

    ahead = products(0)
    for c in range(3):
        hidden, grad_act = ahead
        if c < 2:
            ahead = products(c + 1)
        value, slope = gelu_parts(hidden)
        act[:, chunks[c]] = value.astype(BF)
        grad_hidden[:, chunks[c]] = (grad_act * slope).astype(BF)
    for copy in held_copies:
        copy.wait()
    for cols in chunks:
        mixed_part = nt(act[...], flat(weight[:, :, :, 768:1536])[cols])
        grad_part = nt(grad_hidden[...], flat(weight[:, :, :, 0:768])[cols])
        if not first:
            mixed_part = mixed_part + mixed_acc[:, cols]
            grad_part = grad_part + grad_acc[:, cols]
        if final:
            mixed_low[:, cols] = (middle_here[:, cols] + mixed_part).astype(BF)
        else:
            mixed_acc[:, cols] = mixed_part
        grad_acc[:, cols] = grad_part
    if final:
        out_copies = [pltpu.make_async_copy(mixed_low, mixed, sems.at[1])]
        start_all(out_copies)
        wait_bytes(out_weight, sems.at[5])
        sums[...] = jnp.zeros_like(sums)

        def back_step(r, carry):
            at = pl.ds(pl.multiple_of(r * 512, 512), 512)
            hat, root = norm_parts(middle_here[at, :])
            grad = grad_acc[at, :]
            value = cot[at, :].astype(F32) + norm_pull(grad, hat, root, gain[...])
            grad_middle[at, :] = value
            low = value.astype(BF)
            branch_t[:, at] = low.T
            sums[0:1, :] += jnp.sum(grad * hat, axis=0, keepdims=True)
            sums[1:2, :] += jnp.sum(grad, axis=0, keepdims=True)
            back = nn(low, flat(out_weight[...])).astype(BF)
            for g in range(groups):
                grad_att[g][at, 0:128] = back[:, g * 128 : g * 128 + 128]
                grad_att[g][at, 128:256] = back[:, width + g * 128 : width + g * 128 + 128]
            return carry

        lax.fori_loop(0, length // 512, back_step, 0)
        out_copies.append(pltpu.make_async_copy(grad_middle, grad_middle_out, sems.at[2]))
        out_copies[-1].start()
    else:
        out_copies = [
            pltpu.make_async_copy(mixed_acc, mixed, sems.at[1]),
            pltpu.make_async_copy(grad_acc, grad_in, sems.at[2]),
        ]
        start_all(out_copies)
    for c in range(3):
        cols = slice(c * 256, c * 256 + 256)
        up = nn(normed_t[...], grad_hidden[:, cols]).astype(BF)
        staged[:, :, :, cols] = up.reshape(staged.shape[:3] + (256,))
        down = nn(cot_t[...], act[:, cols]).astype(BF)
        staged[:, :, :, 768 + c * 256 : 1024 + c * 256] = down.reshape(staged.shape[:3] + (256,))
    start_all(piece_copies(out_piece, me[0], outs, outof, sems.at[3], True))
    for copy in out_copies:
        copy.wait()
    wait_bytes(staged, sems.at[3])


def feed_forward(
    piece, out_piece, me, normed, normed_t, cot, cot_t, held, slabs, onto, last=None
):
    length, depth = normed.shape
    rows = piece.rows
    first, final = held is None, last is not None
    ins = [me] + in_vmem([normed, normed_t, cot, cot_t]) + ([] if first else in_hbm(held))
    specs = [smem_spec()] + [vmem_spec()] * 4 + [any_spec()] * (0 if first else 2)
    scratch = [
        pltpu.VMEM(rows.shape + (1536,), BF),
        pltpu.VMEM(rows.shape + (1536,), BF),
        pltpu.VMEM((length, 768), BF),
        pltpu.VMEM((length, 768), BF),
        pltpu.VMEM((length, depth), F32),
        pltpu.VMEM((length, depth), F32),
        pltpu.SemaphoreType.DMA((6,)),
    ]
    last_piece, groups = None, 0
    outs = [pltpu.HBM(out_piece.shape, BF)] * 2 + [pltpu.HBM((length, depth), BF if final else F32)]
    out_specs = [any_spec()] * 3
    if final:
        last_piece, last_slabs, middle, gain, groups = last
        ins += in_hbm([middle]) + [gain] + in_hbm(last_slabs)
        specs += [any_spec(), vmem_spec()] + [any_spec()] * len(last_slabs)
        scratch += [
            pltpu.VMEM((length, depth), BF),
            pltpu.VMEM((length, depth), F32),
            pltpu.VMEM(rows.shape + (depth,), BF),
            pltpu.VMEM((length, depth), F32),
        ]
        outs += [pltpu.HBM((length, depth), F32), pltpu.VMEM((depth, length), BF), SDS((8, depth), F32)]
        outs += [pltpu.HBM((length, 256), BF)] * groups
        out_specs += [any_spec()] + [vmem_spec()] * (2 + groups)
    else:
        outs.append(pltpu.HBM((length, depth), F32))
        out_specs.append(any_spec())
    got = pl.pallas_call(
        functools.partial(
            feed_forward_body, piece, out_piece, first, last_piece, groups, len(onto)
        ),
        in_specs=specs + [any_spec()] * (piece.count + len(onto)),
        out_specs=out_specs,
        out_shape=outs,
        input_output_aliases={len(ins) + piece.count + k: k for k in range(len(onto))},
        scratch_shapes=scratch,
        compiler_params=params(48 if final else 32),
        cost_estimate=cost(14 if final else 11, 20),
        name="feed_forward",
    )(*ins, *in_hbm(slabs), *in_hbm(onto))
    return got[:2], got[2:]


def attend_back_body(piece, out_piece, extra, aliased, final, me, normed_t_in, proj, att, grad_att, lse, seg_col, seg_row, *refs):
    refs = list(refs)
    slabs, refs = refs[: piece.count], refs[piece.count :]
    if extra:
        branch_t = refs.pop(0)
        attended, refs = refs[:extra], refs[extra:]
    else:
        held = refs.pop(0)
    if final:
        tokens_in = refs.pop(0)
    refs = refs[aliased:]
    grad_normed, outs, refs = refs[0], refs[1:3], refs[3:]
    if final:
        sums = refs.pop(0)
    grad_proj, key_sum, value_sum = refs[:3]
    refs = refs[3:]
    bias, delta, keys_t, query_t, query_m, grad_m, staged, normed_t, total, weight, sems = refs[:11]
    copies = [pltpu.make_async_copy(normed_t_in, normed_t, sems.at[1])]
    if not extra:
        copies.append(pltpu.make_async_copy(held, total, sems.at[2]))
    if final:
        copies.append(pltpu.make_async_copy(tokens_in, refs[11], sems.at[3]))
    moves = [(half, 0, 384, weight.at[:, :, :, pl.ds(384 * half, 384)]) for half in range(2)]
    start_all(copies + piece_copies(piece, me[0], slabs, moves, sems.at[4], False))
    length = proj.shape[0]
    fill_bias(bias, seg_col, seg_row)
    if extra:
        joined = join_heads([a[...] for a in attended])
        out_grad = nn(branch_t[...], joined).astype(BF)
        staged[:, :, :, 768:] = out_grad.reshape(staged.shape[:3] + (768,))
    for half in range(2):
        cols = slice(half * 128, half * 128 + 128)
        product = (grad_att[:, cols].astype(F32) * att[:, cols].astype(F32)).T
        for h in range(4):
            delta[half * 4 + h : half * 4 + h + 1, :] = jnp.sum(
                product[h * HD : (h + 1) * HD], axis=0, keepdims=True
            )
        keys_t[cols, :] = proj[:, half * 384 + 128 : half * 384 + 256].T

    def step(half, carry):
        col = pl.multiple_of(half * 384, 128)
        out = pl.multiple_of(half * 128, 128)
        for h in range(4):
            mine = head_row(h)
            query_m[h] = jnp.where(mine, proj[:, pl.ds(col, 128)], 0)
            grad_m[h] = jnp.where(mine, grad_att[:, pl.ds(out, 128)], 0)
        key_sum[...] = jnp.zeros_like(key_sum)
        value_sum[...] = jnp.zeros_like(value_sum)
        for i in (2, 1, 0, 3):
            first = 768 if i == 3 else 0
            last = (i + 1) * QB
            here = slice(first, last)
            there = slice(i * QB, last)
            keys = proj[here, pl.ds(col + 128, 128)]
            values = proj[here, pl.ds(col + 256, 128)]

            def products(h):
                scores = nt(keys, query_m[h, there, :])
                edge = scores[-QB:] + bias[1 if i == 3 else 0]
                if last - first > QB:
                    scores = jnp.concatenate([scores[:-QB], edge], 0)
                else:
                    scores = edge
                return scores, nt(values, grad_m[h, there, :])

            all_probs, all_grads = [], []
            ahead = products(0)
            for h in range(4):
                scores, grad_probs = ahead
                if h < 3:
                    ahead = products(h + 1)
                stat = pl.ds(half * 4 + h, 1)
                lanes = pl.ds(pl.multiple_of(half * 128 + h * HD, HD), HD)
                probs = jnp.exp2(scores * C2 - lse[stat, there])
                grad_scores = (probs * (grad_probs - delta[stat, there])).astype(BF)
                all_probs.append(probs.astype(BF))
                all_grads.append(grad_scores)
                query_t[lanes, there] = nn(keys_t[lanes, here], grad_scores)
            stacked = jnp.concatenate([grad_m[h, there, :] for h in range(4)], 0)
            value_sum[here, :] += nn(jnp.concatenate(all_probs, 1), stacked)
            stacked = jnp.concatenate([query_m[h, there, :] for h in range(4)], 0)
            key_sum[here, :] += nn(jnp.concatenate(all_grads, 1), stacked)
        grad_proj[:, pl.ds(col + 128, 128)] = (key_sum[...] * SCALE).astype(BF)
        grad_proj[:, pl.ds(col + 256, 128)] = value_sum[...].astype(BF)
        return carry

    lax.fori_loop(0, 2, step, 0)
    for half in range(2):
        grad_proj[:, half * 384 : half * 384 + 128] = (
            query_t[half * 128 : half * 128 + 128, :].T * SCALE
        ).astype(BF)
    for copy in copies:
        copy.wait()
    wait_bytes(weight, sems.at[4])
    for c in range(3):
        cols = slice(c * 256, c * 256 + 256)
        part = nn(normed_t[...], grad_proj[:, cols]).astype(BF)
        staged[:, :, :, cols] = part.reshape(staged.shape[:3] + (256,))
    moves = [(half, 0, 384, staged.at[:, :, :, pl.ds(384 * half, 384)]) for half in range(2)]
    if extra:
        moves += [
            (half, -384, 384, staged.at[:, :, :, pl.ds(768 + 384 * half, 384)]) for half in range(2)
        ]
    start_all(piece_copies(out_piece, me[0], outs, moves, sems.at[0], True))
    if final:
        sums[...] = jnp.zeros_like(sums)

    total_copies = []
    for c in range(3):
        cols = slice(c * 256, c * 256 + 256)
        value = nt(grad_proj[...], flat(weight[...])[cols])
        if not extra:
            value = value + total[:, cols]
        total[:, cols] = value
        total_copies.append(
            pltpu.make_async_copy(
                total.at[:, pl.ds(c * 256, 256)], grad_normed.at[:, pl.ds(c * 256, 256)], sems.at[2]
            )
        )
        total_copies[-1].start()
    if final:

        def sum_step(r, carry):
            at = pl.ds(pl.multiple_of(r * QB, QB), QB)
            value = total[at, :]
            hat, _ = norm_parts(refs[11][at, :].astype(F32))
            sums[0:1, :] += jnp.sum(value * hat, axis=0, keepdims=True)
            sums[1:2, :] += jnp.sum(value, axis=0, keepdims=True)
            return carry

        lax.fori_loop(0, length // QB, sum_step, 0)
    wait_bytes(staged, sems.at[0])
    wait_bytes(total, sems.at[2])


def attend_back(
    piece,
    out_piece,
    me,
    normed_t,
    proj,
    att,
    grad_att,
    lse,
    seg_col,
    seg_row,
    slabs,
    branch_t,
    attended,
    held,
    tokens,
    onto,
):
    depth, length = normed_t.shape
    extra = len(attended)
    final = tokens is not None
    columns = 1536 if extra else 768
    ins = [me] + in_hbm([normed_t, proj, att, grad_att, lse]) + [seg_col, seg_row] + in_hbm(slabs)
    specs = [smem_spec(), any_spec()] + [vmem_spec()] * 6 + [any_spec()] * len(slabs)
    if extra:
        ins += in_vmem([branch_t]) + in_hbm(attended)
        specs += [vmem_spec()] * (1 + extra)
    else:
        ins += in_hbm([held])
        specs += [any_spec()]
    if final:
        ins += in_hbm([tokens])
        specs += [any_spec()]
    outs = [pltpu.HBM((length, depth), F32)] + [pltpu.HBM(out_piece.shape, BF)] * 2
    scratch = [
        pltpu.VMEM((2, QB, QB), F32),
        pltpu.VMEM((8, length), F32),
        pltpu.VMEM((256, length), BF),
        pltpu.VMEM((256, length), F32),
        pltpu.VMEM((4, length, 128), BF),
        pltpu.VMEM((4, length, 128), BF),
        pltpu.VMEM(out_piece.rows.shape + (columns,), BF),
        pltpu.VMEM((depth, length), BF),
        pltpu.VMEM((length, depth), F32),
        pltpu.VMEM(piece.rows.shape + (768,), BF),
        pltpu.SemaphoreType.DMA((5,)),
    ]
    if final:
        outs.append(SDS((8, depth), F32))
        scratch.append(pltpu.VMEM((length, depth), BF))
    got = pl.pallas_call(
        functools.partial(attend_back_body, piece, out_piece, extra, len(onto), final),
        in_specs=specs + [any_spec()] * len(onto),
        out_specs=[any_spec()] * 3 + ([vmem_spec()] if final else []),
        out_shape=outs,
        input_output_aliases={len(ins) + k: 1 + k for k in range(len(onto))},
        scratch_shapes=[
            pltpu.VMEM((length, 768), BF),
            pltpu.VMEM((length, 128), F32),
            pltpu.VMEM((length, 128), F32),
        ]
        + scratch,
        compiler_params=params(40),
        cost_estimate=cost(12, 8),
        name="attend_back",
    )(*ins, *in_hbm(onto))
    return got[0], got[1:3], got[3] if final else None


def norm_back_body(
    start, core, tokens, grad_normed, grad_middle, gain, held, other, high, low, own, sem
):
    length = high.shape[0] // 2
    r = pl.program_id(0)
    hat, root = norm_parts(tokens[...].astype(F32))
    value = grad_middle[...] + norm_pull(grad_normed[...], hat, root, gain[...])
    top = value.astype(BF)
    rest = (value - top.astype(F32)).astype(BF)
    for base in (0, length):
        at = pl.ds(pl.multiple_of(base + r * QB, QB), QB)
        high[at, :] = top
        low[at, :] = rest

    @pl.when(r == pl.num_programs(0) - 1)
    def _():
        count = own.shape[0] // QB
        for k in range(count):
            own[k * QB : k * QB + QB, :] = turned([high, low], start[0], k)
        copy = pltpu.make_async_copy(own, held.at[core[0]], sem)
        copy.start()
        for k in range(count):
            other[k * QB : k * QB + QB, :] = turned([high, low], start[0], k + count)
        copy.wait()


def norm_back(start, core, tokens, grad_normed, grad_middle, gain):
    length, depth = tokens.shape
    half = (length // 2, depth)
    return pl.pallas_call(
        norm_back_body,
        grid=(length // QB,),
        in_specs=[smem_spec()] * 2 + [row_spec(depth, QB)] * 3 + [whole_spec((1, depth))],
        out_specs=[any_spec(), whole_spec(half)],
        out_shape=[pltpu.HBM((2,) + half, F32), SDS(half, F32)],
        scratch_shapes=[
            pltpu.VMEM((2 * length, depth), BF),
            pltpu.VMEM((2 * length, depth), BF),
            pltpu.VMEM(half, F32),
            pltpu.SemaphoreType.DMA,
        ],
        compiler_params=params(24),
        cost_estimate=cost(4, 16),
        name="norm_back",
    )(start, core, *in_hbm([tokens, grad_normed, grad_middle]), gain)


def split_far_body(counts, me, *refs):
    keep, send = refs[-2:]
    far = me[0] // 4
    begin = 0
    for count in counts:
        pieces, refs = refs[:count], refs[count:]
        cols = pl.ds(begin, pieces[0].shape[-1])
        begin += pieces[0].shape[-1]
        for k, out in enumerate((keep, send)):
            for slot in range(2):
                at = lax.bitwise_xor(far, k + 2 * slot)
                total = pieces[0][at].astype(F32)
                for piece in pieces[1:]:
                    total = total + piece[at].astype(F32)
                out[slot, :, cols] = total.astype(BF)


def split_far(me, groups):
    width, specs = 0, []
    for pieces in groups:
        far, block, columns = pieces[0].shape[-3:]
        width += columns
        for piece in pieces:
            if piece.ndim == 4:
                specs.append(pl.BlockSpec((None, far, block, columns), lambda i: (0, 0, 0, 0)))
            else:
                specs.append(whole_spec(piece.shape))
    return pl.pallas_call(
        functools.partial(split_far_body, [len(pieces) for pieces in groups]),
        grid=(1,),
        in_specs=[smem_spec()] + specs,
        out_specs=[whole_spec((2, block, width))] * 2,
        out_shape=[SDS((2, block, width), BF)] * 2,
        compiler_params=params(16),
        cost_estimate=cost(1, 2),
        name="split_far",
    )(me, *[piece for pieces in groups for piece in pieces])


def put_sums(ref, base, total):
    high = total.astype(BF)
    ref[base : base + 4, :] = high
    ref[base + 4 : base + 8, :] = (total - high.astype(F32)).astype(BF)
    ref[base + 8 : base + 16, :] = jnp.zeros((8, total.shape[1]), BF)


def get_sums(ref, base):
    return ref[base : base + 4, :].astype(F32) + ref[base + 4 : base + 8, :].astype(F32)


def last_join_body(own, other, sums, sums_away, *outs):
    total = sums[...] + sums_away[...]
    rows = outs[0].shape[0] - 16
    for k, out in enumerate(outs):
        value = own[k].astype(F32) + other[k].astype(F32)
        out[:rows, :] = value.astype(BF).reshape(rows, -1)
        put_sums(out, rows, total)


def last_split_body(me, m0, m1, m2, m3, keep, send):
    far = me[0] // 4
    rows = m0.shape[0] - 16
    block = rows // 4
    for k, out in enumerate((keep, send)):
        for slot in range(2):
            at = pl.ds(pl.multiple_of(lax.bitwise_xor(far, k + 2 * slot) * block, 16), block)
            total = (m0[at, :].astype(F32) + m1[at, :].astype(F32)) + (
                m2[at, :].astype(F32) + m3[at, :].astype(F32)
            )
            out[slot * block : (slot + 1) * block, :] = total.astype(BF)
    total = (get_sums(m0, rows) + get_sums(m1, rows)) + (get_sums(m2, rows) + get_sums(m3, rows))
    put_sums(keep, 2 * block, total)
    put_sums(send, 2 * block, total)


def last_middle_body(keep, near, rest, send):
    block = (keep.shape[0] - 16) // 2
    value = keep[:block, :].astype(F32) + near[:block, :].astype(F32)
    rest[:block, :] = value.astype(BF)
    value = keep[block : 2 * block, :].astype(F32) + near[block : 2 * block, :].astype(F32)
    send[:block, :] = value.astype(BF)
    total = get_sums(keep, 2 * block) + get_sums(near, 2 * block)
    put_sums(rest, block, total)
    put_sums(send, block, total)


def last_sum_body(rest, away, first, grad_qkv, sums):
    block = rest.shape[0] - 16
    value = rest[:block, :].astype(F32) + away[:block, :].astype(F32)
    parts = [first[:, 384:], value[:, :384], value[:, 384:]]
    for which in range(3):
        cols = slice(which * 128, which * 128 + 128)
        grad_qkv[which] = jnp.concatenate([part[:, cols] for part in parts], 1)
    sums[...] = get_sums(rest, block) + get_sums(away, block)


def pack_body(part, out, up, down, packed):
    width = out.shape[1]
    packed[:, :width] = out[...]
    for s in range(up.shape[1] // part):
        cols = slice(s * part, (s + 1) * part)
        packed[:, width + 2 * s * part : width + (2 * s + 1) * part] = up[:, cols]
        packed[:, width + (2 * s + 1) * part : width + (2 * s + 2) * part] = down[:, cols]


def small_call(body, name, outs, scalars, values):
    return pl.pallas_call(
        body,
        in_specs=[smem_spec()] * len(scalars) + [vmem_spec()] * len(values),
        out_specs=[vmem_spec()] * len(outs),
        out_shape=outs,
        compiler_params=params(16),
        cost_estimate=cost(1, 3),
        name=name,
    )(*scalars, *values)


def swap(value):
    return lax.ppermute(value, "mp", [(0, 1), (1, 0)])


def tie(*values):
    return lax.optimization_barrier(values)


def hop(value, mask, count):
    return lax.ppermute(value, "dp", [(i, i ^ mask) for i in range(count)])


def hops(value, masks, count):
    return [(value, functools.partial(hop, mask=m, count=count)) for m in masks]


def far_hops(rows, values):
    return [
        (v, functools.partial(hop, mask=rows.near * m, count=rows.dp_count))
        for m, v in zip(range(1, rows.far), values)
    ]


def swaps(values):
    return [(v, swap) for v in values]


def send_all(requests):
    return [send(value) for value, send in requests]


def low_sum(values):
    total = values[0].astype(F32)
    for value in values[1:]:
        total = total + value.astype(F32)
    return total


class Flow:
    def __init__(self, me):
        self.me = me
        self.active = []

    def add(self, transfer, name, results, seeds=()):
        self.active.append([transfer, list(seeds), name, results])

    def step(self, *pivots, gate=None):
        values = [v for item in self.active for v in item[1]]
        tied = list(tie(self.me, *pivots, *values))
        self.me = tied.pop(0)
        pivots, tied = tied[: len(pivots)], tied[len(pivots) :]
        going, self.active, requests = self.active, [], []
        for item in going:
            transfer, values, name, results = item
            got, tied = tied[: len(values)], tied[len(values) :]
            try:
                if callable(transfer):
                    item[0] = transfer(*got)
                    asked = next(item[0])
                else:
                    asked = transfer.send(got)
                self.active.append(item)
                requests.append(asked)
            except StopIteration as stop:
                results[name] = stop.value
        gates = gate() if gate else []
        operands = [operand for asked in requests for operand, _ in asked]
        tied = list(tie(self.me, *gates, *operands))
        self.me = tied[0]
        tied = tied[1 + len(gates) :]
        for item, asked in zip(self.active, requests):
            item[1] = [send(operand) for (_, send), operand in zip(asked, tied)]
            tied = tied[len(asked) :]
        return pivots


def add_low(a, b):
    return (a.astype(F32) + b.astype(F32)).astype(BF)


def on_device(
    tokens, segment, ln1_gain, ln1_bias, w_qkv, w_out, ln2_gain, ln2_bias, w_up, w_down, cotangent
):
    dp_count = lax.axis_size("dp")
    core = lax.axis_index("mp")
    me = lax.axis_index("dp").astype(jnp.int32).reshape(1)
    here, depth = tokens.shape[2], tokens.shape[3]
    length = 2 * here
    rows = Rows(dp_count, depth)

    groups = w_qkv.shape[2] // 128
    part = 384
    subs = w_up.shape[1] // part
    cut = subs // 2
    qkv = [w_qkv[:, :, g * 128 : (g + 1) * 128].reshape(-1, part) for g in range(groups)]
    shards = {"q": jnp.concatenate(qkv, 1)}

    shard_a = small_call(
        functools.partial(pack_body, part),
        "pack",
        [SDS((w_up.shape[0], w_out.shape[0] + 2 * w_up.shape[1]), BF)],
        [],
        [w_out.T, w_up, w_down.T],
    )[0]

    seg = lax.dynamic_index_in_dim(segment[:, 0], core, 0, keepdims=False)
    run = length * 3 // 4
    begin = jnp.argmax(seg[: length - run + 1] == seg[run - 1 :]).astype(jnp.int32)
    start = ((begin - here * core) % length).reshape(1)
    back = (length - start) % length
    seg_tail = lax.dynamic_slice_in_dim(jnp.concatenate([seg, seg]), begin + run, length - run)
    seg_col = seg_tail.reshape(-1, 1)
    seg_row = seg_tail.reshape(1, -1)
    gain1, bias1, gain2, bias2 = (
        v.reshape(1, -1) for v in (ln1_gain, ln1_bias, ln2_gain, ln2_bias)
    )

    flow = Flow(me)
    core_place = core.astype(jnp.int32).reshape(1)
    token_halves = [tokens[:, 0], swap(tokens[:, 0])]
    cot_halves = [cotangent[:, 0], swap(cotangent[:, 0])]
    wide = 2 * part
    qkv_pieces = [Piece(rows, "slabs")] + [Piece(rows, "slabs", part * g) for g in range(groups - 1)]
    out_piece = Piece(rows, "slabs")
    feed_pieces = [Piece(rows, "slabs", part + wide * s) for s in range(cut)]
    feed_pieces += [Piece(rows, "slabs", wide * s) for s in range(subs - cut)]
    turns = [(0, 2, 1, 3), MASKS]
    feed_outs = [
        Piece(rows, "stack", 0, wide, turns[s % 2]) for s in range(subs)
    ]
    qkv_outs = [Piece(rows, "stack", part, wide)]
    qkv_outs += [Piece(rows, "stack", part * g, part * (groups - 1)) for g in range(groups - 1)]
    far = lax.axis_index("dp") // rows.near

    def gather_whole(shard):
        return lax.all_gather(shard, "dp", axis=0, tiled=True).reshape(rows.shape + (-1,))

    def fetch_near(near):
        got = yield hops(near, MASKS[1:], dp_count)
        own = [near] + got
        return own + [swap(x) for x in own]

    def via(mask):
        return functools.partial(hop, mask=mask, count=dp_count)

    def fetch_wide(shard, away):
        near, both_ways = yield [(shard, via(4)), (away, via(4))]
        (a0,) = arrange(rows, flow.me, [shard, near, away, both_ways], [shard.shape[1]])
        a1, a2, b0, away = yield [(a0, via(1)), (a0, via(2))] + swaps([a0]) + [(shard_c, via(8))]
        a3, b1, b2, near, both_ways = yield (
            [(a1, via(2))] + swaps([a1, a2]) + [(shard_c, via(4)), (away, via(4))]
        )
        slabs["a"] = [a0, a1, a2, a3, b0, b1, b2, swap(a3)]
        (c0,) = arrange(rows, flow.me, [shard_c, near, away, both_ways], [shard_c.shape[1]])
        (d0,) = yield swaps([c0])
        c1, c2 = yield [(c0, via(1)), (c0, via(2))]
        c3, d1, d2 = yield [(c2, via(1))] + swaps([c1, c2])
        return [c0, c1, c2, c3, d0, d1, d2, swap(c3)]

    def whole(shard):
        own = gather_whole(shard)
        return [own, swap(own)]

    def halve(first, hurry, own, other):
        if hurry:
            other = swap(other)
        else:
            (other,) = yield swaps([other])
        keep, send = (low_sum([own[k : k + 2], other[k : k + 2]]).astype(BF) for k in (0, 2))
        (near,) = yield [(send, via(first))]
        (away,) = yield [(low_sum([keep[1], near[1]]).astype(BF), via(3 - first))]
        return [keep, near, away]

    def direct(mine):
        got = yield hops_of(mine, (1, 2, 3))
        return [mine[0]] + got

    def hops_of(values, masks):
        return [(values[m], via(m)) for m in masks]

    def reduce_far(groups):
        keep, send = split_far(flow.me, groups)
        (near,) = yield [(send, via(4))]
        (away,) = yield [(low_sum([keep[1], near[1]]).astype(BF), via(8))]
        return low_sum([keep[0], near[0], away])

    def reduce_all(first, own, other):
        group = yield from halve(first, True, own, other)
        return (yield from reduce_far([sums_of[s] for s in range(subs - 1)] + [group]))

    def reduce_last(own, other, sums):
        other, sums_away = swap(other), swap(sums)
        mine = small_call(
            last_join_body,
            "last_join",
            [SDS((rows.far * rows.block + 16, wide), BF)] * 4,
            [],
            [own, other, sums, sums_away],
        )
        return (yield from direct(mine))

    def exchange(value):
        (got,) = yield swaps([value])
        return got

    def reduce_direct(own, other):
        (other,) = yield swaps([other])
        mine = [low_sum([own[k], other[k]]).astype(BF) for k in range(4)]
        pieces = yield from direct(mine)
        return (yield from reduce_far([pieces]))

    def plain(own, other):
        value = low_sum([own, swap(other)]).astype(BF).reshape(depth, -1)
        return lax.psum_scatter(value, "dp", scatter_dimension=0, tiled=True).astype(F32)

    def run(transfer):
        requests = next(transfer)
        while True:
            try:
                requests = transfer.send(send_all(requests))
            except StopIteration as stop:
                return stop.value

    slabs, forward = {}, []

    def project(g):
        name = "q0" if g == 0 else "q1"
        forward.append(
            project_attend(qkv_pieces[g], flow.me, normed, seg_col, seg_row, slabs[name])
        )

    if rows.split:
        shard_q = shards["q"]
        got = send_all(far_hops(rows, [shard_q] * (rows.far - 1)))
        prepared = prepare(start, core_place, *token_halves, gain1, bias1)
        tied = tie(*got, *prepared, shard_a)
        got, prepared, shard_a = tied[:3], tied[3:6], tied[6]
        near_q0, near_q1 = arrange(rows, me, [shard_q] + list(got), [part, wide])
        own = [near_q0] + [hop(near_q0, m, dp_count) for m in MASKS[1:]]
        first_cols = part + wide * cut
        shard_c, shard_a = shard_a[:, first_cols:], shard_a[:, :first_cols]
        away_a = hop(shard_a, 8, dp_count)
        start_cot, _ = tie(start, near_q0)
        turned_cot = turn(start_cot, core_place, *cot_halves)
        tied = tie(*own, *turned_cot)
        own, turned_cot = tied[:4], tied[4:]
        slabs["q0"] = list(own) + [swap(v) for v in own]
        flow.add(fetch_near, "q1", slabs, [near_q1])
        flow.add(fetch_wide, "c", slabs, [shard_a, away_a])
        flow.step(own[3])
    else:
        for name, shard in (
            ("q0", shards["q"][:, :part]),
            ("q1", shards["q"][:, part:]),
            ("a", shard_a[:, : part + wide * cut]),
            ("c", shard_a[:, part + wide * cut :]),
        ):
            slabs[name] = whole(shard)
        prepared = prepare(start, core_place, *token_halves, gain1, bias1)
        turned_cot = turn(start, core_place, *cot_halves)
    x, normed, normed_t = prepared
    cot, cot_t = turned_cot
    for g in range(groups):
        project(g)
        flow.step(forward[g][2])
    atts = [f[1] for f in forward]
    middle, normed_ffn, normed_ffn_t = out_norm(
        out_piece, flow.me, x, gain2, bias2, atts, slabs["a"]
    )
    flow.step(normed_ffn)

    held = None
    sums_of = {}
    onto = []
    feed_names = ["a"] * cut + ["c"] * (subs - cut)
    for s in range(subs):
        final = s == subs - 1
        grads, held = feed_forward(
            feed_pieces[s],
            feed_outs[s],
            flow.me,
            normed_ffn,
            normed_ffn_t,
            cot,
            cot_t,
            held,
            slabs[feed_names[s]],
            [],
            (out_piece, slabs["a"], middle, gain2, groups) if final else None,
        )
        first = 1 + s % 2
        if not rows.split:
            sums_of[s] = plain(*grads)
        elif final:
            flow.add(functools.partial(reduce_all, first), "feed", sums_of, grads)
        else:
            flow.add(functools.partial(halve, first, False), s, sums_of, grads)
        if s == 1 and rows.split:
            flow.step(held[1], gate=lambda: slabs["c"][-1:])
        elif not final:
            flow.step(held[1])
    mixed, grad_middle, branch_t, sums2, *grad_atts = held
    mixed, core_place, _ = flow.step(mixed, core_place, sums2)
    mixed_held, mixed_other = turn_back(back, core_place, mixed)
    flow.add(exchange, "mixed", sums_of, [mixed_other])
    grad_projs = []
    onto = []

    held = None
    qkv_slabs = [slabs["q0"]] + [slabs["q1"]] * (groups - 1)
    for g in range(groups):
        proj, att, lse = forward[g]
        held, grads, sums1 = attend_back(
            qkv_pieces[g],
            qkv_outs[g],
            flow.me,
            normed_t,
            proj,
            att,
            grad_atts[g],
            lse,
            seg_col,
            seg_row,
            qkv_slabs[g],
            branch_t,
            atts if g == 0 else [],
            held,
            x if g == groups - 1 else None,
            onto,
        )
        onto = grads
        if g == 0:
            if rows.split:
                flow.add(reduce_direct, "first", sums_of, grads)
            else:
                sums_of["first"] = plain(*grads)
            onto = []
        if g < groups - 1:
            flow.step(held)
    sums = jnp.concatenate([sums1[:2], sums2[:2]], 0)
    if rows.split:
        flow.add(reduce_last, "last", sums_of, [*grads, sums])
        (held,) = flow.step(held)
    else:
        sums_of["last"] = plain(*grads)
    start_late, _ = tie(back, flow.me)
    tokens_held, tokens_other = norm_back(start_late, core_place, x, held, grad_middle, gain1)
    tokens_held, tokens_other = flow.step(tokens_held, tokens_other)
    if rows.split:
        block = rows.block
        keep, send = small_call(
            last_split_body,
            "last_split",
            [SDS((2 * block + 16, wide), BF)] * 2,
            [flow.me],
            sums_of["last"],
        )
        near = hop(send, 4, dp_count)
        rest, send = small_call(
            last_middle_body, "last_middle", [SDS((block + 16, wide), BF)] * 2, [], [keep, near]
        )
        away = hop(send, 8, dp_count)
        while flow.active:
            flow.step()
        grad_qkv, norm_sums = small_call(
            last_sum_body,
            "last_sum",
            [SDS((3, block, part), F32), SDS((4, depth), F32)],
            [],
            [rest, away, sums_of["first"]],
        )
        grad_qkv = grad_qkv.transpose(1, 0, 2)
        grad_out = sums_of["first"][:, :part].T
        feed_sums = [sums_of["feed"]]
    else:
        early, last = sums_of["first"], sums_of["last"]
        parts = [early[:, part:], last[:, :part], last[:, part:]]
        grad_qkv = jnp.concatenate([r.reshape(-1, 3, 128) for r in parts], 2)
        grad_out = early[:, :part].T
        feed_sums = [sums_of[s] for s in range(subs)]
        norm_sums = jnp.sum(lax.all_gather(sums + swap(sums), "dp", axis=0), 0)
    feed_sum = jnp.concatenate(feed_sums, 1) if len(feed_sums) > 1 else feed_sums[0]
    feed_list = [feed_sum[:, wide * s : wide * (s + 1)] for s in range(subs)]

    return (
        place(core_place, mixed_held, sums_of["mixed"])[:, None],
        place(core_place, tokens_held, swap(tokens_other))[:, None],
        norm_sums[0],
        norm_sums[1],
        grad_qkv,
        grad_out,
        norm_sums[2],
        norm_sums[3],
        jnp.concatenate([r[:, :part] for r in feed_list], 1),
        jnp.concatenate([r[:, part:] for r in feed_list], 1).T,
    )


def solution(mesh):
    in_specs = (
        P(None, "dp", "mp", None),
        P(None, "dp", None),
        P(),
        P(),
        P("dp", None, "mp"),
        P("mp", "dp"),
        P(),
        P(),
        P("dp", "mp"),
        P("mp", "dp"),
        P(None, "dp", "mp", None),
    )
    out_specs = (
        P(None, "dp", "mp", None),
        P(None, "dp", "mp", None),
        P(),
        P(),
        P("dp", None, "mp"),
        P("mp", "dp"),
        P(),
        P(),
        P("dp", "mp"),
        P("mp", "dp"),
    )
    return jax.shard_map(
        on_device, mesh=mesh, in_specs=in_specs, out_specs=out_specs, check_vma=False
    )
```

```python
import functools
import math

import jax
import jax.numpy as jnp
from jax import lax
from jax.experimental import pallas as pl
from jax.experimental.pallas import tpu as pltpu
from jax.sharding import PartitionSpec as P

HD = 32
QB = 256
EPS = 1e-05
BF = jnp.bfloat16
F32 = jnp.float32
NEG = -1e30
SCALE = 1.0 / math.sqrt(HD)
LOG2E = math.log2(math.e)
C2 = SCALE * LOG2E
MIB = 1024 * 1024
SDS = jax.ShapeDtypeStruct


def nn(a, b):
    return lax.dot_general(a, b, (((1,), (0,)), ((), ())), preferred_element_type=F32)


def nt(a, b):
    return lax.dot_general(a, b, (((1,), (1,)), ((), ())), preferred_element_type=F32)


def params(mib):
    return pltpu.CompilerParams(vmem_limit_bytes=mib * MIB)


def in_hbm(values):
    return [pltpu.with_memory_space_constraint(v, pltpu.HBM) for v in values]


def in_vmem(values):
    return [pltpu.with_memory_space_constraint(v, pltpu.VMEM) for v in values]


def cost(gflop, mbytes):
    return pl.CostEstimate(flops=int(gflop * 1e9), bytes_accessed=int(mbytes * 1e6), transcendentals=0)


def any_spec():
    return pl.BlockSpec(memory_space=pl.ANY)


def smem_spec():
    return pl.BlockSpec(memory_space=pltpu.SMEM)


def vmem_spec():
    return pl.BlockSpec(memory_space=pltpu.VMEM)


def row_spec(width, rows=512):
    return pl.BlockSpec((rows, width), lambda r: (r, 0))


def column_spec(height, rows=512):
    return pl.BlockSpec((height, rows), lambda r: (0, r))


def whole_spec(shape):
    return pl.BlockSpec(shape, lambda r: tuple(0 for _ in shape))


MASKS = (0, 1, 2, 3)


class Rows:
    def __init__(self, dp_count, depth):
        self.dp_count = dp_count
        self.depth = depth
        self.split = (depth // dp_count) % 16 == 0 and dp_count == 16
        self.near = 4 if self.split else 1
        self.far = dp_count // 4 if self.split else 1
        self.block = depth // (self.near * self.far)
        self.shape = (self.far, self.near, self.block)


class Piece:
    def __init__(self, rows, kind, start=0, width=0, masks=MASKS):
        self.rows = rows
        self.masks = masks
        self.kind = kind if rows.split else "whole"
        self.start = start
        self.count = 2 * len(MASKS) if self.kind == "slabs" else 2
        if self.kind == "stack":
            self.shape = (len(MASKS), rows.far, rows.block, width)
        else:
            self.shape = rows.shape + (width,)


def piece_copies(piece, me, refs, moves, sem, outward):
    copies = []
    each = piece.count // 2
    for half, column, width, view in moves:
        cols = pl.ds(piece.start + column, width)
        if piece.kind == "whole":
            pairs = [(refs[half].at[:, :, :, cols], view)]
        else:
            pairs = []
            for k, mask in enumerate(piece.masks):
                ref = refs[half].at[k] if piece.kind == "stack" else refs[half * each + k]
                near = lax.bitwise_xor(lax.rem(me, 4), mask)
                pairs.append((ref.at[:, :, cols], view.at[:, near]))
        for outside, inside in pairs:
            if outward:
                copies.append(pltpu.make_async_copy(inside, outside, sem))
            else:
                copies.append(pltpu.make_async_copy(outside, inside, sem))
    return copies


def start_all(copies):
    for copy in copies:
        copy.start()


def wait_bytes(ref, sem):
    pltpu.make_async_copy(ref, ref, sem).wait()


def flat(value):
    return value.reshape(-1, value.shape[-1])


def head_row(h):
    return lax.broadcasted_iota(jnp.int32, (1, 128), 1) // HD == h


def fill_bias(bias, seg_col, seg_row):
    key = lax.broadcasted_iota(jnp.int32, (QB, QB), 0)
    query = lax.broadcasted_iota(jnp.int32, (QB, QB), 1)
    bias[0] = jnp.where(query >= key, 0.0, NEG)
    bias[1] = jnp.where((query >= key) & (seg_col[...] == seg_row[...]), 0.0, NEG)


def turned(doubles, start, r):
    coarse = pl.multiple_of(start // 16 * 16 + r * QB, 16)
    fine = start % 16
    row = lax.broadcasted_iota(jnp.int32, (QB, QB + 16), 0)
    col = lax.broadcasted_iota(jnp.int32, (QB, QB + 16), 1)
    pick = jnp.where(col - row == fine, 1.0, 0.0).astype(BF)
    total = None
    for double in doubles:
        part = nn(pick, double[pl.ds(coarse, QB + 16), :])
        total = part if total is None else total + part
    return total


def norm_parts(values):
    centered = values - jnp.mean(values, axis=-1, keepdims=True)
    spread = jnp.mean(centered * centered, axis=-1, keepdims=True)
    root = lax.rsqrt(spread + EPS)
    return centered * root, root


def start_double(double, core, own, other, sem):
    here = own.shape[1]
    halves = (own, other)
    for k in range(4):
        pltpu.make_async_copy(halves[k % 2].at[core], double.at[pl.ds(k * here, here)], sem).start()


def prepare_body(start, core, own, other, gain, offset, x_out, normed_out, normed_t_out, double, x, normed, normed_t, sems):
    start_double(double, core[0], own, other, sems.at[3])
    wait_bytes(double, sems.at[3])

    def step(r, carry):
        at = pl.ds(pl.multiple_of(r * QB, QB), QB)
        value = turned([double], start[0], r)
        x[at, :] = value.astype(BF)
        hat, _ = norm_parts(value)
        low = (hat * gain[...] + offset[...]).astype(BF)
        normed[at, :] = low
        normed_t[:, at] = low.T
        return carry

    lax.fori_loop(0, x.shape[0] // QB, step, 0)
    copies = [
        pltpu.make_async_copy(normed, normed_out, sems.at[0]),
        pltpu.make_async_copy(x, x_out, sems.at[1]),
        pltpu.make_async_copy(normed_t, normed_t_out, sems.at[2]),
    ]
    start_all(copies)
    for copy in copies:
        copy.wait()


def prepare(start, core, own, other, gain, offset):
    _, here, depth = own.shape
    shape, shape_t = (2 * here, depth), (depth, 2 * here)
    shapes = [shape, shape, shape_t]
    return pl.pallas_call(
        prepare_body,
        in_specs=[smem_spec()] * 2 + [any_spec()] * 2 + [vmem_spec()] * 2,
        out_specs=[any_spec()] * 3,
        out_shape=[pltpu.HBM(s, BF) for s in shapes],
        scratch_shapes=[pltpu.VMEM((4 * here, depth), BF)]
        + [pltpu.VMEM(s, BF) for s in shapes]
        + [pltpu.SemaphoreType.DMA((4,))],
        compiler_params=params(20),
        cost_estimate=cost(4, 8),
        name="prepare",
    )(start, core, *in_hbm([own, other]), gain, offset)


def turn_body(start, core, own, other, cot_out, cot_t_out, double, cot, cot_t, sems):
    start_double(double, core[0], own, other, sems.at[2])
    wait_bytes(double, sems.at[2])

    def step(r, carry):
        at = pl.ds(pl.multiple_of(r * QB, QB), QB)
        low = turned([double], start[0], r).astype(BF)
        cot[at, :] = low
        cot_t[:, at] = low.T
        return carry

    lax.fori_loop(0, cot.shape[0] // QB, step, 0)
    copies = [
        pltpu.make_async_copy(cot, cot_out, sems.at[0]),
        pltpu.make_async_copy(cot_t, cot_t_out, sems.at[1]),
    ]
    start_all(copies)
    for copy in copies:
        copy.wait()


def turn(start, core, own, other):
    _, here, depth = own.shape
    shapes = [(2 * here, depth), (depth, 2 * here)]
    return pl.pallas_call(
        turn_body,
        in_specs=[smem_spec()] * 2 + [any_spec()] * 2,
        out_specs=[any_spec()] * 2,
        out_shape=[pltpu.HBM(s, BF) for s in shapes],
        scratch_shapes=[pltpu.VMEM((4 * here, depth), BF)]
        + [pltpu.VMEM(s, BF) for s in shapes]
        + [pltpu.SemaphoreType.DMA((3,))],
        compiler_params=params(16),
        cost_estimate=cost(4, 8),
        name="turn",
    )(start, core, *in_hbm([own, other]))


def turn_back_body(start, core, values, held, other, double, own, sem):
    here = other.shape[0]
    double[: 2 * here, :] = values[...]
    double[2 * here :, :] = values[...]
    count = here // QB

    def step(r, carry):
        at = pl.ds(pl.multiple_of(r * QB, QB), QB)
        own[at, :] = turned([double], start[0], r).astype(BF)
        other[at, :] = turned([double], start[0], r + count).astype(BF)
        return carry

    lax.fori_loop(0, count, step, 0)
    copy = pltpu.make_async_copy(own, held.at[core[0]], sem)
    copy.start()
    copy.wait()


def place_body(core, other, held, out, sem):
    copy = pltpu.make_async_copy(other, out.at[1 - core[0]], sem)
    copy.start()
    copy.wait()


def place(core, held, other):
    return pl.pallas_call(
        place_body,
        in_specs=[smem_spec(), any_spec(), any_spec()],
        out_specs=any_spec(),
        out_shape=pltpu.HBM(held.shape, held.dtype),
        input_output_aliases={2: 0},
        scratch_shapes=[pltpu.SemaphoreType.DMA],
        compiler_params=params(4),
        cost_estimate=cost(0, 4),
        name="place",
    )(core, other, *in_hbm([held]))


def turn_back(start, core, values):
    length, depth = values.shape
    half = (length // 2, depth)
    return pl.pallas_call(
        turn_back_body,
        in_specs=[smem_spec()] * 2 + [vmem_spec()],
        out_specs=[any_spec(), vmem_spec()],
        out_shape=[pltpu.HBM((2,) + half, BF), SDS(half, BF)],
        scratch_shapes=[
            pltpu.VMEM((2 * length, depth), BF),
            pltpu.VMEM(half, BF),
            pltpu.SemaphoreType.DMA,
        ],
        compiler_params=params(16),
        cost_estimate=cost(2, 4),
        name="turn_back",
    )(start, core, values)


def arrange_body(widths, me, *refs):
    pieces, outs = refs[:4], refs[4:]
    far = me[0] // 4
    for m, piece in enumerate(pieces):
        begin = 0
        for out, width in zip(outs, widths):
            out[lax.bitwise_xor(far, m)] = piece[:, begin : begin + width]
            begin += width


def arrange(rows, me, pieces, widths):
    return pl.pallas_call(
        functools.partial(arrange_body, widths),
        in_specs=[smem_spec()] + [vmem_spec()] * 4,
        out_specs=[vmem_spec()] * len(widths),
        out_shape=[SDS((rows.far, rows.block, w), BF) for w in widths],
        compiler_params=params(8),
        cost_estimate=cost(1, 1),
        name="arrange",
    )(me, *pieces)


KEPT = (0, 256, 768, 1536)


def project_attend_body(piece, me, normed_in, seg_col, seg_row, *refs):
    slabs = refs[: piece.count]
    proj_out, att, inverse, kept_out, weight, proj, normed, bias = refs[piece.count : piece.count + 8]
    keys_m, values_t, att_t, kept, sem, out_sem, kept_sem = refs[piece.count + 8 :]
    normed_copy = pltpu.make_async_copy(normed_in, normed, out_sem)
    normed_copy.start()
    moves = [(half, 0, 384, weight.at[:, :, :, pl.ds(384 * half, 384)]) for half in range(2)]
    start_all(piece_copies(piece, me[0], slabs, moves, sem, False))
    fill_bias(bias, seg_col, seg_row)
    values_t[...] = jnp.ones_like(values_t)
    normed_copy.wait()
    wait_bytes(weight, sem)

    for c in range(3):
        cols = slice(c * 256, c * 256 + 256)
        proj[:, cols] = nn(normed[...], flat(weight[:, :, :, cols])).astype(BF)
    proj_copy = pltpu.make_async_copy(proj, proj_out, out_sem)
    proj_copy.start()
    for half in range(2):
        flipped = proj[:, half * 384 + 256 : half * 384 + 384].T
        for h in range(4):
            values_t[half * 4 + h, 0:HD, :] = flipped[h * HD : (h + 1) * HD]

    units = [(h, i) for i in (2, 1, 0, 3) for h in range(4)]

    def step(half, carry):
        col = pl.multiple_of(half * 384, 128)
        for h in range(4):
            keys_m[h] = jnp.where(head_row(h), proj[:, pl.ds(col + 128, 128)], 0)

        def score(h, i):
            first = 768 if i == 3 else 0
            scores = nt(keys_m[h, first : (i + 1) * QB, :], proj[i * QB : (i + 1) * QB, pl.ds(col, 128)])
            edge = scores[-QB:] + bias[1 if i == 3 else 0]
            return jnp.concatenate([scores[:-QB], edge], 0) if scores.shape[0] > QB else edge

        ahead = score(*units[0])
        for k, (h, i) in enumerate(units):
            scores = ahead
            if k + 1 < len(units):
                ahead = score(*units[k + 1])
            first = 768 if i == 3 else 0
            last = (i + 1) * QB
            at = slice(i * QB, last)
            peak = jnp.max(scores, axis=0, keepdims=True) * C2
            probs = jnp.exp2(scores * C2 - peak).astype(BF)
            kept[half * 4 + h, KEPT[i] : KEPT[i] + last - first, :] = probs
            summed = nn(values_t[half * 4 + h, :, first:last], probs)
            share = 1.0 / summed[HD : HD + 1]
            att_t[pl.ds(pl.multiple_of(half * 128 + h * HD, HD), HD), at] = summed[:HD] * share
            inverse[pl.ds(half * 4 + h, 1), at] = share
            if h == 3:
                part = (pl.ds(half * 4, 4), pl.ds(KEPT[i], last - first))
                pltpu.make_async_copy(kept.at[part], kept_out.at[part], kept_sem).start()
        return carry

    lax.fori_loop(0, 2, step, 0)
    for half in range(2):
        cols = slice(half * 128, half * 128 + 128)
        att[:, cols] = att_t[cols, :].T.astype(BF)
    proj_copy.wait()
    wait_bytes(kept, kept_sem)


def project_attend(piece, me, normed, seg_col, seg_row, slabs):
    length, depth = normed.shape
    rows = piece.rows
    return pl.pallas_call(
        functools.partial(project_attend_body, piece),
        in_specs=[smem_spec(), any_spec()] + [vmem_spec()] * 2 + [any_spec()] * len(slabs),
        out_specs=[any_spec()] + [vmem_spec()] * 2 + [any_spec()],
        out_shape=[
            pltpu.HBM((length, 768), BF),
            pltpu.HBM((length, 256), BF),
            pltpu.HBM((8, length), F32),
            pltpu.HBM((8, 1792, QB), BF),
        ],
        scratch_shapes=[
            pltpu.VMEM(rows.shape + (768,), BF),
            pltpu.VMEM((length, 768), BF),
            pltpu.VMEM((length, depth), BF),
            pltpu.VMEM((2, QB, QB), F32),
            pltpu.VMEM((4, length, 128), BF),
            pltpu.VMEM((8, HD + 16, length), BF),
            pltpu.VMEM((256, length), F32),
            pltpu.VMEM((8, 1792, QB), BF),
            pltpu.SemaphoreType.DMA,
            pltpu.SemaphoreType.DMA,
            pltpu.SemaphoreType.DMA,
        ],
        compiler_params=params(32),
        cost_estimate=cost(8, 8),
        name="project_attend",
    )(me, *in_hbm([normed]), seg_col, seg_row, *in_hbm(slabs))


def join_heads(attended):
    return jnp.concatenate([a[:, :128] for a in attended] + [a[:, 128:] for a in attended], 1)


def out_norm_body(piece, groups, me, tokens, gain, offset, *refs):
    attended = refs[:groups]
    slabs = refs[groups : groups + piece.count]
    middle, normed, normed_t, weight, sem = refs[groups + piece.count :]
    width = weight.shape[3] // 2

    @pl.when(pl.program_id(0) == 0)
    def _():
        moves = [(half, 0, width, weight.at[:, :, :, pl.ds(width * half, width)]) for half in range(2)]
        start_all(piece_copies(piece, me[0], slabs, moves, sem, False))
        wait_bytes(weight, sem)

    value = tokens[...].astype(F32) + nt(join_heads([a[...] for a in attended]), flat(weight[...]))
    middle[...] = value
    hat, _ = norm_parts(value)
    low = (hat * gain[...] + offset[...]).astype(BF)
    normed[...] = low
    normed_t[...] = low.T


def out_norm(piece, me, tokens, gain, offset, attended, slabs):
    length, depth = tokens.shape
    return pl.pallas_call(
        functools.partial(out_norm_body, piece, len(attended)),
        grid=(length // 512,),
        in_specs=[smem_spec(), row_spec(depth), whole_spec((1, depth)), whole_spec((1, depth))]
        + [row_spec(256)] * len(attended)
        + [any_spec()] * len(slabs),
        out_specs=[row_spec(depth)] * 2 + [column_spec(depth)],
        out_shape=[
            pltpu.HBM((length, depth), F32),
            pltpu.VMEM((length, depth), BF),
            pltpu.VMEM((depth, length), BF),
        ],
        scratch_shapes=[pltpu.VMEM(piece.rows.shape + (depth,), BF), pltpu.SemaphoreType.DMA],
        compiler_params=params(28),
        cost_estimate=cost(3, 8),
        name="out_norm",
    )(me, *in_hbm([tokens]), gain, offset, *in_hbm(attended), *in_hbm(slabs))


def gelu_parts(values):
    size = jnp.abs(values)
    density = jnp.exp2(values * values * (-0.5 * LOG2E) + math.log2(1.0 / math.sqrt(2 * math.pi)))
    below = 1.0 + 0.2316419 * size
    t = pl.reciprocal(below, approx=True)
    t = t * (2.0 - below * t)
    poly = t * (
        0.319381530
        + t * (-0.356563782 + t * (1.781477937 + t * (-1.821255978 + t * 1.330274429)))
    )
    tail = density * poly
    below = jnp.where(values >= 0, 1.0 - tail, tail)
    return values * below, below + values * density


def norm_pull(grad, hat, root, gain):
    scaled = grad * gain
    first = jnp.mean(scaled, axis=-1, keepdims=True)
    second = jnp.mean(scaled * hat, axis=-1, keepdims=True)
    return root * (scaled - first - hat * second)


def feed_forward_body(
    piece, out_piece, first, last_piece, groups, aliased, me, normed, normed_t, cot, cot_t, *refs
):
    refs = list(refs)
    final = last_piece is not None
    held = [] if first else [refs.pop(0), refs.pop(0)]
    if final:
        middle, gain = refs.pop(0), refs.pop(0)
        out_slabs, refs = refs[: last_piece.count], refs[last_piece.count :]
    slabs, refs = refs[: piece.count], refs[piece.count + aliased :]
    outs, refs = refs[:2], refs[2:]
    mixed = refs.pop(0)
    if final:
        grad_middle_out, branch_t, sums = refs[:3]
        grad_att, refs = refs[3 : 3 + groups], refs[3 + groups :]
    else:
        grad_in = refs.pop(0)
    weight, staged, act, grad_hidden, mixed_acc, grad_acc, sems = refs[:7]
    if final:
        mixed_low, middle_here, out_weight, grad_middle = refs[7:]
    length, depth = normed.shape
    moves = []
    for half in range(2):
        for which in range(2):
            at = pl.ds(which * 768 + half * 384, 384)
            moves.append((half, which * 384, 384, at))
    into = [(h, c, w, weight.at[:, :, :, at]) for h, c, w, at in moves]
    outof = [(h, c, w, staged.at[:, :, :, at]) for h, c, w, at in moves]
    start_all(piece_copies(piece, me[0], slabs, into, sems.at[0], False))
    held_copies = []
    if not first:
        held_copies.append(pltpu.make_async_copy(held[0], mixed_acc, sems.at[1]))
        held_copies.append(pltpu.make_async_copy(held[1], grad_acc, sems.at[2]))
    if final:
        held_copies.append(pltpu.make_async_copy(middle, middle_here, sems.at[4]))
    start_all(held_copies)
    if final:
        width = depth // 2
        views = [
            (half, 0, width, out_weight.at[:, :, :, pl.ds(width * half, width)]) for half in range(2)
        ]
        start_all(piece_copies(last_piece, me[0], out_slabs, views, sems.at[5], False))
    wait_bytes(weight, sems.at[0])
    chunks = [slice(c * 256, c * 256 + 256) for c in range(3)]

    def products(c):
        hidden = nn(normed[...], flat(weight[:, :, :, c * 256 : c * 256 + 256]))
        return hidden, nn(cot[...], flat(weight[:, :, :, 768 + c * 256 : 1024 + c * 256]))

    ahead = products(0)
    for c in range(3):
        hidden, grad_act = ahead
        if c < 2:
            ahead = products(c + 1)
        value, slope = gelu_parts(hidden)
        act[:, chunks[c]] = value.astype(BF)
        grad_hidden[:, chunks[c]] = (grad_act * slope).astype(BF)
    for copy in held_copies:
        copy.wait()
    for cols in chunks:
        mixed_part = nt(act[...], flat(weight[:, :, :, 768:1536])[cols])
        grad_part = nt(grad_hidden[...], flat(weight[:, :, :, 0:768])[cols])
        if not first:
            mixed_part = mixed_part + mixed_acc[:, cols]
            grad_part = grad_part + grad_acc[:, cols]
        if final:
            mixed_low[:, cols] = (middle_here[:, cols] + mixed_part).astype(BF)
        else:
            mixed_acc[:, cols] = mixed_part
        grad_acc[:, cols] = grad_part
    if final:
        out_copies = [pltpu.make_async_copy(mixed_low, mixed, sems.at[1])]
        start_all(out_copies)
        wait_bytes(out_weight, sems.at[5])
        sums[...] = jnp.zeros_like(sums)

        def back_step(r, carry):
            at = pl.ds(pl.multiple_of(r * 512, 512), 512)
            hat, root = norm_parts(middle_here[at, :])
            grad = grad_acc[at, :]
            value = cot[at, :].astype(F32) + norm_pull(grad, hat, root, gain[...])
            grad_middle[at, :] = value
            low = value.astype(BF)
            branch_t[:, at] = low.T
            sums[0:1, :] += jnp.sum(grad * hat, axis=0, keepdims=True)
            sums[1:2, :] += jnp.sum(grad, axis=0, keepdims=True)
            back = nn(low, flat(out_weight[...])).astype(BF)
            for g in range(groups):
                grad_att[g][at, 0:128] = back[:, g * 128 : g * 128 + 128]
                grad_att[g][at, 128:256] = back[:, width + g * 128 : width + g * 128 + 128]
            return carry

        lax.fori_loop(0, length // 512, back_step, 0)
        out_copies.append(pltpu.make_async_copy(grad_middle, grad_middle_out, sems.at[2]))
        out_copies[-1].start()
    else:
        out_copies = [
            pltpu.make_async_copy(mixed_acc, mixed, sems.at[1]),
            pltpu.make_async_copy(grad_acc, grad_in, sems.at[2]),
        ]
        start_all(out_copies)
    for c in range(3):
        cols = slice(c * 256, c * 256 + 256)
        up = nn(normed_t[...], grad_hidden[:, cols]).astype(BF)
        staged[:, :, :, cols] = up.reshape(staged.shape[:3] + (256,))
        down = nn(cot_t[...], act[:, cols]).astype(BF)
        staged[:, :, :, 768 + c * 256 : 1024 + c * 256] = down.reshape(staged.shape[:3] + (256,))
    start_all(piece_copies(out_piece, me[0], outs, outof, sems.at[3], True))
    for copy in out_copies:
        copy.wait()
    wait_bytes(staged, sems.at[3])


def feed_forward(
    piece, out_piece, me, normed, normed_t, cot, cot_t, held, slabs, onto, last=None
):
    length, depth = normed.shape
    rows = piece.rows
    first, final = held is None, last is not None
    ins = [me] + in_vmem([normed, normed_t, cot, cot_t]) + ([] if first else in_hbm(held))
    specs = [smem_spec()] + [vmem_spec()] * 4 + [any_spec()] * (0 if first else 2)
    scratch = [
        pltpu.VMEM(rows.shape + (1536,), BF),
        pltpu.VMEM(rows.shape + (1536,), BF),
        pltpu.VMEM((length, 768), BF),
        pltpu.VMEM((length, 768), BF),
        pltpu.VMEM((length, depth), F32),
        pltpu.VMEM((length, depth), F32),
        pltpu.SemaphoreType.DMA((6,)),
    ]
    last_piece, groups = None, 0
    outs = [SDS(out_piece.shape, BF)] * 2 + [pltpu.HBM((length, depth), BF if final else F32)]
    out_specs = [any_spec()] * 3
    if final:
        last_piece, last_slabs, middle, gain, groups = last
        ins += in_hbm([middle]) + [gain] + in_hbm(last_slabs)
        specs += [any_spec(), vmem_spec()] + [any_spec()] * len(last_slabs)
        scratch += [
            pltpu.VMEM((length, depth), BF),
            pltpu.VMEM((length, depth), F32),
            pltpu.VMEM(rows.shape + (depth,), BF),
            pltpu.VMEM((length, depth), F32),
        ]
        outs += [pltpu.HBM((length, depth), F32), pltpu.VMEM((depth, length), BF), SDS((8, depth), F32)]
        outs += [pltpu.HBM((length, 256), BF)] * groups
        out_specs += [any_spec()] + [vmem_spec()] * (2 + groups)
    else:
        outs.append(pltpu.HBM((length, depth), F32))
        out_specs.append(any_spec())
    got = pl.pallas_call(
        functools.partial(
            feed_forward_body, piece, out_piece, first, last_piece, groups, len(onto)
        ),
        in_specs=specs + [any_spec()] * (piece.count + len(onto)),
        out_specs=out_specs,
        out_shape=outs,
        input_output_aliases={len(ins) + piece.count + k: k for k in range(len(onto))},
        scratch_shapes=scratch,
        compiler_params=params(48 if final else 32),
        cost_estimate=cost(14 if final else 11, 20),
        name="feed_forward",
    )(*ins, *in_hbm(slabs), *in_hbm(onto))
    return got[:2], got[2:]


def attend_back_body(piece, out_piece, extra, aliased, final, me, normed_t_in, proj, att, grad_att, inverse, kept_in, *refs):
    refs = list(refs)
    slabs, refs = refs[: piece.count], refs[piece.count :]
    if extra:
        branch_t = refs.pop(0)
        attended, refs = refs[:extra], refs[extra:]
    else:
        held = refs.pop(0)
    if final:
        tokens_in = refs.pop(0)
    refs = refs[aliased:]
    grad_normed, outs, refs = refs[0], refs[1:3], refs[3:]
    if final:
        sums = refs.pop(0)
    grad_proj, key_sum, value_sum = refs[:3]
    refs = refs[3:]
    kept, delta, keys_t, query_t, query_m, grad_m, staged, normed_t, total, weight, sems = refs[:11]
    for half in range(2):
        part = pl.ds(half * 4, 4)
        pltpu.make_async_copy(kept_in.at[part], kept.at[part], sems.at[5 + half]).start()
    copies = [pltpu.make_async_copy(normed_t_in, normed_t, sems.at[1])]
    if not extra:
        copies.append(pltpu.make_async_copy(held, total, sems.at[2]))
    if final:
        copies.append(pltpu.make_async_copy(tokens_in, refs[11], sems.at[3]))
    moves = [(half, 0, 384, weight.at[:, :, :, pl.ds(384 * half, 384)]) for half in range(2)]
    start_all(copies + piece_copies(piece, me[0], slabs, moves, sems.at[4], False))
    length = proj.shape[0]
    if extra:
        joined = join_heads([a[...] for a in attended])
        out_grad = nn(branch_t[...], joined).astype(BF)
        staged[:, :, :, 768:] = out_grad.reshape(staged.shape[:3] + (768,))
    for half in range(2):
        cols = slice(half * 128, half * 128 + 128)
        product = (grad_att[:, cols].astype(F32) * att[:, cols].astype(F32)).T
        for h in range(4):
            stat = slice(half * 4 + h, half * 4 + h + 1)
            total_here = jnp.sum(product[h * HD : (h + 1) * HD], axis=0, keepdims=True)
            delta[stat, :] = total_here * inverse[stat, :]
        keys_t[cols, :] = proj[:, half * 384 + 128 : half * 384 + 256].T

    def step(half, carry):
        col = pl.multiple_of(half * 384, 128)
        out = pl.multiple_of(half * 128, 128)
        share = jnp.concatenate(
            [jnp.broadcast_to(inverse[pl.ds(half * 4 + h, 1), :], (HD, length)) for h in range(4)], 0
        ).T
        grads = (grad_att[:, pl.ds(out, 128)].astype(F32) * share).astype(BF)
        for h in range(4):
            mine = head_row(h)
            query_m[h] = jnp.where(mine, proj[:, pl.ds(col, 128)], 0)
            grad_m[h] = jnp.where(mine, grads, 0)
        wait_bytes(kept.at[pl.ds(half * 4, 4)], sems.at[5 + half])
        key_sum[...] = jnp.zeros_like(key_sum)
        value_sum[...] = jnp.zeros_like(value_sum)
        for i in (2, 1, 0, 3):
            first = 768 if i == 3 else 0
            last = (i + 1) * QB
            here = slice(first, last)
            there = slice(i * QB, last)
            values = proj[here, pl.ds(col + 256, 128)]
            rows_here = slice(KEPT[i], KEPT[i] + last - first)
            all_probs, all_grads = [], []
            ahead = nt(values, grad_m[0, there, :])
            for h in range(4):
                grad_probs = ahead
                if h < 3:
                    ahead = nt(values, grad_m[h + 1, there, :])
                stat = pl.ds(half * 4 + h, 1)
                lanes = pl.ds(pl.multiple_of(half * 128 + h * HD, HD), HD)
                probs = kept[half * 4 + h, rows_here, :]
                grad_scores = (probs.astype(F32) * (grad_probs - delta[stat, there])).astype(BF)
                all_probs.append(probs)
                all_grads.append(grad_scores)
                query_t[lanes, there] = nn(keys_t[lanes, here], grad_scores)
            stacked = jnp.concatenate([grad_m[h, there, :] for h in range(4)], 0)
            value_sum[here, :] += nn(jnp.concatenate(all_probs, 1), stacked)
            stacked = jnp.concatenate([query_m[h, there, :] for h in range(4)], 0)
            key_sum[here, :] += nn(jnp.concatenate(all_grads, 1), stacked)
        grad_proj[:, pl.ds(col + 128, 128)] = (key_sum[...] * SCALE).astype(BF)
        grad_proj[:, pl.ds(col + 256, 128)] = value_sum[...].astype(BF)
        return carry

    lax.fori_loop(0, 2, step, 0)
    for half in range(2):
        grad_proj[:, half * 384 : half * 384 + 128] = (
            query_t[half * 128 : half * 128 + 128, :].T * SCALE
        ).astype(BF)
    for copy in copies:
        copy.wait()
    wait_bytes(weight, sems.at[4])
    for c in range(3):
        cols = slice(c * 256, c * 256 + 256)
        part = nn(normed_t[...], grad_proj[:, cols]).astype(BF)
        staged[:, :, :, cols] = part.reshape(staged.shape[:3] + (256,))
    moves = [(half, 0, 384, staged.at[:, :, :, pl.ds(384 * half, 384)]) for half in range(2)]
    if extra:
        moves += [
            (half, -384, 384, staged.at[:, :, :, pl.ds(768 + 384 * half, 384)]) for half in range(2)
        ]
    start_all(piece_copies(out_piece, me[0], outs, moves, sems.at[0], True))
    if final:
        sums[...] = jnp.zeros_like(sums)

    total_copies = []
    for c in range(3):
        cols = slice(c * 256, c * 256 + 256)
        value = nt(grad_proj[...], flat(weight[...])[cols])
        if not extra:
            value = value + total[:, cols]
        total[:, cols] = value
        total_copies.append(
            pltpu.make_async_copy(
                total.at[:, pl.ds(c * 256, 256)], grad_normed.at[:, pl.ds(c * 256, 256)], sems.at[2]
            )
        )
        total_copies[-1].start()
    if final:

        def sum_step(r, carry):
            at = pl.ds(pl.multiple_of(r * QB, QB), QB)
            value = total[at, :]
            hat, _ = norm_parts(refs[11][at, :].astype(F32))
            sums[0:1, :] += jnp.sum(value * hat, axis=0, keepdims=True)
            sums[1:2, :] += jnp.sum(value, axis=0, keepdims=True)
            return carry

        lax.fori_loop(0, length // QB, sum_step, 0)
    wait_bytes(staged, sems.at[0])
    wait_bytes(total, sems.at[2])


def attend_back(
    piece,
    out_piece,
    me,
    normed_t,
    proj,
    att,
    grad_att,
    inverse,
    kept,
    slabs,
    branch_t,
    attended,
    held,
    tokens,
    onto,
):
    depth, length = normed_t.shape
    extra = len(attended)
    final = tokens is not None
    columns = 1536 if extra else 768
    ins = [me] + in_hbm([normed_t, proj, att, grad_att, inverse, kept]) + in_hbm(slabs)
    specs = [smem_spec(), any_spec()] + [vmem_spec()] * 4 + [any_spec()] * (1 + len(slabs))
    if extra:
        ins += in_vmem([branch_t]) + in_hbm(attended)
        specs += [vmem_spec()] * (1 + extra)
    else:
        ins += in_hbm([held])
        specs += [any_spec()]
    if final:
        ins += in_hbm([tokens])
        specs += [any_spec()]
    outs = [pltpu.HBM((length, depth), F32)] + [SDS(out_piece.shape, BF)] * 2
    scratch = [
        pltpu.VMEM((8, 1792, QB), BF),
        pltpu.VMEM((8, length), F32),
        pltpu.VMEM((256, length), BF),
        pltpu.VMEM((256, length), F32),
        pltpu.VMEM((4, length, 128), BF),
        pltpu.VMEM((4, length, 128), BF),
        pltpu.VMEM(out_piece.rows.shape + (columns,), BF),
        pltpu.VMEM((depth, length), BF),
        pltpu.VMEM((length, depth), F32),
        pltpu.VMEM(piece.rows.shape + (768,), BF),
        pltpu.SemaphoreType.DMA((7,)),
    ]
    if final:
        outs.append(SDS((8, depth), F32))
        scratch.append(pltpu.VMEM((length, depth), BF))
    got = pl.pallas_call(
        functools.partial(attend_back_body, piece, out_piece, extra, len(onto), final),
        in_specs=specs + [any_spec()] * len(onto),
        out_specs=[any_spec()] * 3 + ([vmem_spec()] if final else []),
        out_shape=outs,
        input_output_aliases={len(ins) + k: 1 + k for k in range(len(onto))},
        scratch_shapes=[
            pltpu.VMEM((length, 768), BF),
            pltpu.VMEM((length, 128), F32),
            pltpu.VMEM((length, 128), F32),
        ]
        + scratch,
        compiler_params=params(40),
        cost_estimate=cost(12, 8),
        name="attend_back",
    )(*ins, *onto)
    return got[0], got[1:3], got[3] if final else None


def norm_back_body(
    start, core, tokens, grad_normed, grad_middle, gain, held, other, high, low, own, sem
):
    length = high.shape[0] // 2
    r = pl.program_id(0)
    hat, root = norm_parts(tokens[...].astype(F32))
    value = grad_middle[...] + norm_pull(grad_normed[...], hat, root, gain[...])
    top = value.astype(BF)
    rest = (value - top.astype(F32)).astype(BF)
    for base in (0, length):
        at = pl.ds(pl.multiple_of(base + r * QB, QB), QB)
        high[at, :] = top
        low[at, :] = rest

    @pl.when(r == pl.num_programs(0) - 1)
    def _():
        count = own.shape[0] // QB
        for k in range(count):
            own[k * QB : k * QB + QB, :] = turned([high, low], start[0], k)
        copy = pltpu.make_async_copy(own, held.at[core[0]], sem)
        copy.start()
        for k in range(count):
            other[k * QB : k * QB + QB, :] = turned([high, low], start[0], k + count)
        copy.wait()


def norm_back(start, core, tokens, grad_normed, grad_middle, gain):
    length, depth = tokens.shape
    half = (length // 2, depth)
    return pl.pallas_call(
        norm_back_body,
        grid=(length // QB,),
        in_specs=[smem_spec()] * 2 + [row_spec(depth, QB)] * 3 + [whole_spec((1, depth))],
        out_specs=[any_spec(), whole_spec(half)],
        out_shape=[pltpu.HBM((2,) + half, F32), SDS(half, F32)],
        scratch_shapes=[
            pltpu.VMEM((2 * length, depth), BF),
            pltpu.VMEM((2 * length, depth), BF),
            pltpu.VMEM(half, F32),
            pltpu.SemaphoreType.DMA,
        ],
        compiler_params=params(24),
        cost_estimate=cost(4, 16),
        name="norm_back",
    )(start, core, *in_hbm([tokens, grad_normed, grad_middle]), gain)


def split_far_body(counts, me, *refs):
    keep, send = refs[-2:]
    far = me[0] // 4
    begin = 0
    for count in counts:
        pieces, refs = refs[:count], refs[count:]
        cols = pl.ds(begin, pieces[0].shape[-1])
        begin += pieces[0].shape[-1]
        for k, out in enumerate((keep, send)):
            for slot in range(2):
                at = lax.bitwise_xor(far, k + 2 * slot)
                total = pieces[0][at].astype(F32)
                for piece in pieces[1:]:
                    total = total + piece[at].astype(F32)
                out[slot, :, cols] = total.astype(BF)


def split_far(me, groups):
    width, specs = 0, []
    for pieces in groups:
        far, block, columns = pieces[0].shape[-3:]
        width += columns
        for piece in pieces:
            if piece.ndim == 4:
                specs.append(pl.BlockSpec((None, far, block, columns), lambda i: (0, 0, 0, 0)))
            else:
                specs.append(whole_spec(piece.shape))
    return pl.pallas_call(
        functools.partial(split_far_body, [len(pieces) for pieces in groups]),
        grid=(1,),
        in_specs=[smem_spec()] + specs,
        out_specs=[whole_spec((2, block, width))] * 2,
        out_shape=[SDS((2, block, width), BF)] * 2,
        compiler_params=params(16),
        cost_estimate=cost(1, 2),
        name="split_far",
    )(me, *[piece for pieces in groups for piece in pieces])


def put_sums(ref, base, total):
    high = total.astype(BF)
    ref[base : base + 4, :] = high
    ref[base + 4 : base + 8, :] = (total - high.astype(F32)).astype(BF)
    ref[base + 8 : base + 16, :] = jnp.zeros((8, total.shape[1]), BF)


def get_sums(ref, base):
    return ref[base : base + 4, :].astype(F32) + ref[base + 4 : base + 8, :].astype(F32)


def last_join_body(own, other, sums, sums_away, *outs):
    total = sums[...] + sums_away[...]
    rows = outs[0].shape[0] - 16
    for k, out in enumerate(outs):
        value = own[k].astype(F32) + other[k].astype(F32)
        out[:rows, :] = value.astype(BF).reshape(rows, -1)
        put_sums(out, rows, total)


def last_split_body(me, m0, m1, m2, m3, keep, send):
    far = me[0] // 4
    rows = m0.shape[0] - 16
    block = rows // 4
    for k, out in enumerate((keep, send)):
        for slot in range(2):
            at = pl.ds(pl.multiple_of(lax.bitwise_xor(far, k + 2 * slot) * block, 16), block)
            total = (m0[at, :].astype(F32) + m1[at, :].astype(F32)) + (
                m2[at, :].astype(F32) + m3[at, :].astype(F32)
            )
            out[slot * block : (slot + 1) * block, :] = total.astype(BF)
    total = (get_sums(m0, rows) + get_sums(m1, rows)) + (get_sums(m2, rows) + get_sums(m3, rows))
    put_sums(keep, 2 * block, total)
    put_sums(send, 2 * block, total)


def last_middle_body(keep, near, rest, send):
    block = (keep.shape[0] - 16) // 2
    value = keep[:block, :].astype(F32) + near[:block, :].astype(F32)
    rest[:block, :] = value.astype(BF)
    value = keep[block : 2 * block, :].astype(F32) + near[block : 2 * block, :].astype(F32)
    send[:block, :] = value.astype(BF)
    total = get_sums(keep, 2 * block) + get_sums(near, 2 * block)
    put_sums(rest, block, total)
    put_sums(send, block, total)


def last_sum_body(rest, away, first, grad_qkv, sums):
    block = rest.shape[0] - 16
    value = rest[:block, :].astype(F32) + away[:block, :].astype(F32)
    parts = [first[:, 384:], value[:, :384], value[:, 384:]]
    for which in range(3):
        cols = slice(which * 128, which * 128 + 128)
        grad_qkv[which] = jnp.concatenate([part[:, cols] for part in parts], 1)
    sums[...] = get_sums(rest, block) + get_sums(away, block)


def pack_body(part, out, up, down, packed):
    width = out.shape[1]
    packed[:, :width] = out[...]
    for s in range(up.shape[1] // part):
        cols = slice(s * part, (s + 1) * part)
        packed[:, width + 2 * s * part : width + (2 * s + 1) * part] = up[:, cols]
        packed[:, width + (2 * s + 1) * part : width + (2 * s + 2) * part] = down[:, cols]


def small_call(body, name, outs, scalars, values):
    return pl.pallas_call(
        body,
        in_specs=[smem_spec()] * len(scalars) + [vmem_spec()] * len(values),
        out_specs=[vmem_spec()] * len(outs),
        out_shape=outs,
        compiler_params=params(16),
        cost_estimate=cost(1, 3),
        name=name,
    )(*scalars, *values)


def swap(value):
    return lax.ppermute(value, "mp", [(0, 1), (1, 0)])


def tie(*values):
    return lax.optimization_barrier(values)


def hop(value, mask, count):
    return lax.ppermute(value, "dp", [(i, i ^ mask) for i in range(count)])


def hops(value, masks, count):
    return [(value, functools.partial(hop, mask=m, count=count)) for m in masks]


def far_hops(rows, values):
    return [
        (v, functools.partial(hop, mask=rows.near * m, count=rows.dp_count))
        for m, v in zip(range(1, rows.far), values)
    ]


def swaps(values):
    return [(v, swap) for v in values]


def send_all(requests):
    return [send(value) for value, send in requests]


def low_sum(values):
    total = values[0].astype(F32)
    for value in values[1:]:
        total = total + value.astype(F32)
    return total


class Flow:
    def __init__(self, me):
        self.me = me
        self.active = []

    def add(self, transfer, name, results, seeds=()):
        self.active.append([transfer, list(seeds), name, results])

    def step(self, *pivots, gate=None):
        values = [v for item in self.active for v in item[1]]
        tied = list(tie(self.me, *pivots, *values))
        self.me = tied.pop(0)
        pivots, tied = tied[: len(pivots)], tied[len(pivots) :]
        going, self.active, requests = self.active, [], []
        for item in going:
            transfer, values, name, results = item
            got, tied = tied[: len(values)], tied[len(values) :]
            try:
                if callable(transfer):
                    item[0] = transfer(*got)
                    asked = next(item[0])
                else:
                    asked = transfer.send(got)
                self.active.append(item)
                requests.append(asked)
            except StopIteration as stop:
                results[name] = stop.value
        gates = gate() if gate else []
        operands = [operand for asked in requests for operand, _ in asked]
        tied = list(tie(self.me, *gates, *operands))
        self.me = tied[0]
        tied = tied[1 + len(gates) :]
        for item, asked in zip(self.active, requests):
            item[1] = [send(operand) for (_, send), operand in zip(asked, tied)]
            tied = tied[len(asked) :]
        return pivots


def add_low(a, b):
    return (a.astype(F32) + b.astype(F32)).astype(BF)


def on_device(
    tokens, segment, ln1_gain, ln1_bias, w_qkv, w_out, ln2_gain, ln2_bias, w_up, w_down, cotangent
):
    dp_count = lax.axis_size("dp")
    core = lax.axis_index("mp")
    me = lax.axis_index("dp").astype(jnp.int32).reshape(1)
    here, depth = tokens.shape[2], tokens.shape[3]
    length = 2 * here
    rows = Rows(dp_count, depth)

    groups = w_qkv.shape[2] // 128
    part = 384
    subs = w_up.shape[1] // part
    cut = subs // 2
    qkv = [w_qkv[:, :, g * 128 : (g + 1) * 128].reshape(-1, part) for g in range(groups)]
    shards = {"q": jnp.concatenate(qkv, 1)}

    shard_a = small_call(
        functools.partial(pack_body, part),
        "pack",
        [SDS((w_up.shape[0], w_out.shape[0] + 2 * w_up.shape[1]), BF)],
        [],
        [w_out.T, w_up, w_down.T],
    )[0]

    seg = lax.dynamic_index_in_dim(segment[:, 0], core, 0, keepdims=False)
    run = length * 3 // 4
    begin = jnp.argmax(seg[: length - run + 1] == seg[run - 1 :]).astype(jnp.int32)
    start = ((begin - here * core) % length).reshape(1)
    back = (length - start) % length
    seg_tail = lax.dynamic_slice_in_dim(jnp.concatenate([seg, seg]), begin + run, length - run)
    seg_col = seg_tail.reshape(-1, 1)
    seg_row = seg_tail.reshape(1, -1)
    gain1, bias1, gain2, bias2 = (
        v.reshape(1, -1) for v in (ln1_gain, ln1_bias, ln2_gain, ln2_bias)
    )

    flow = Flow(me)
    core_place = core.astype(jnp.int32).reshape(1)
    token_halves = [tokens[:, 0], swap(tokens[:, 0])]
    cot_halves = [cotangent[:, 0], swap(cotangent[:, 0])]
    wide = 2 * part
    qkv_pieces = [Piece(rows, "slabs")] + [Piece(rows, "slabs", part * g) for g in range(groups - 1)]
    out_piece = Piece(rows, "slabs")
    feed_pieces = [Piece(rows, "slabs", part + wide * s) for s in range(cut)]
    feed_pieces += [Piece(rows, "slabs", wide * s) for s in range(subs - cut)]
    turns = [(0, 2, 1, 3), MASKS]
    feed_outs = [
        Piece(rows, "stack", 0, wide, turns[s % 2]) for s in range(subs)
    ]
    qkv_outs = [Piece(rows, "stack", part, wide)]
    qkv_outs += [Piece(rows, "stack", part * g, part * (groups - 1)) for g in range(groups - 1)]
    far = lax.axis_index("dp") // rows.near

    def gather_whole(shard):
        return lax.all_gather(shard, "dp", axis=0, tiled=True).reshape(rows.shape + (-1,))

    def fetch_near(near):
        got = yield hops(near, MASKS[1:], dp_count)
        own = [near] + got
        return own + [swap(x) for x in own]

    def via(mask):
        return functools.partial(hop, mask=mask, count=dp_count)

    def fetch_wide(shard, away):
        near, both_ways = yield [(shard, via(4)), (away, via(4))]
        (a0,) = arrange(rows, flow.me, [shard, near, away, both_ways], [shard.shape[1]])
        a1, a2, b0, away = yield [(a0, via(1)), (a0, via(2))] + swaps([a0]) + [(shard_c, via(8))]
        a3, b1, b2, near, both_ways = yield (
            [(a1, via(2))] + swaps([a1, a2]) + [(shard_c, via(4)), (away, via(4))]
        )
        slabs["a"] = [a0, a1, a2, a3, b0, b1, b2, swap(a3)]
        (c0,) = arrange(rows, flow.me, [shard_c, near, away, both_ways], [shard_c.shape[1]])
        (d0,) = yield swaps([c0])
        c1, c2 = yield [(c0, via(1)), (c0, via(2))]
        c3, d1, d2 = yield [(c2, via(1))] + swaps([c1, c2])
        return [c0, c1, c2, c3, d0, d1, d2, swap(c3)]

    def whole(shard):
        own = gather_whole(shard)
        return [own, swap(own)]

    def halve(first, hurry, own, other):
        if hurry:
            other = swap(other)
        else:
            (other,) = yield swaps([other])
        keep, send = (low_sum([own[k : k + 2], other[k : k + 2]]).astype(BF) for k in (0, 2))
        (near,) = yield [(send, via(first))]
        (away,) = yield [(low_sum([keep[1], near[1]]).astype(BF), via(3 - first))]
        return [keep, near, away]

    def direct(mine):
        got = yield hops_of(mine, (1, 2, 3))
        return [mine[0]] + got

    def hops_of(values, masks):
        return [(values[m], via(m)) for m in masks]

    def reduce_far(groups):
        keep, send = split_far(flow.me, groups)
        (near,) = yield [(send, via(4))]
        (away,) = yield [(low_sum([keep[1], near[1]]).astype(BF), via(8))]
        return low_sum([keep[0], near[0], away])

    def reduce_all(first, own, other):
        group = yield from halve(first, True, own, other)
        return (yield from reduce_far([sums_of[s] for s in range(subs - 1)] + [group]))

    def reduce_last(own, other, sums):
        other, sums_away = swap(other), swap(sums)
        mine = small_call(
            last_join_body,
            "last_join",
            [SDS((rows.far * rows.block + 16, wide), BF)] * 4,
            [],
            [own, other, sums, sums_away],
        )
        return (yield from direct(mine))

    def exchange(value):
        (got,) = yield swaps([value])
        return got

    def reduce_direct(own, other):
        (other,) = yield swaps([other])
        mine = [low_sum([own[k], other[k]]).astype(BF) for k in range(4)]
        pieces = yield from direct(mine)
        return (yield from reduce_far([pieces]))

    def plain(own, other):
        value = low_sum([own, swap(other)]).astype(BF).reshape(depth, -1)
        return lax.psum_scatter(value, "dp", scatter_dimension=0, tiled=True).astype(F32)

    def run(transfer):
        requests = next(transfer)
        while True:
            try:
                requests = transfer.send(send_all(requests))
            except StopIteration as stop:
                return stop.value

    slabs, forward = {}, []

    def project(g):
        name = "q0" if g == 0 else "q1"
        forward.append(
            project_attend(qkv_pieces[g], flow.me, normed, seg_col, seg_row, slabs[name])
        )

    if rows.split:
        shard_q = shards["q"]
        got = send_all(far_hops(rows, [shard_q] * (rows.far - 1)))
        prepared = prepare(start, core_place, *token_halves, gain1, bias1)
        tied = tie(*got, *prepared, shard_a)
        got, prepared, shard_a = tied[:3], tied[3:6], tied[6]
        near_q0, near_q1 = arrange(rows, me, [shard_q] + list(got), [part, wide])
        own = [near_q0] + [hop(near_q0, m, dp_count) for m in MASKS[1:]]
        first_cols = part + wide * cut
        shard_c, shard_a = shard_a[:, first_cols:], shard_a[:, :first_cols]
        away_a = hop(shard_a, 8, dp_count)
        start_cot, _ = tie(start, near_q0)
        turned_cot = turn(start_cot, core_place, *cot_halves)
        tied = tie(*own, *turned_cot)
        own, turned_cot = tied[:4], tied[4:]
        slabs["q0"] = list(own) + [swap(v) for v in own]
        flow.add(fetch_near, "q1", slabs, [near_q1])
        flow.add(fetch_wide, "c", slabs, [shard_a, away_a])
        flow.step(own[3])
    else:
        for name, shard in (
            ("q0", shards["q"][:, :part]),
            ("q1", shards["q"][:, part:]),
            ("a", shard_a[:, : part + wide * cut]),
            ("c", shard_a[:, part + wide * cut :]),
        ):
            slabs[name] = whole(shard)
        prepared = prepare(start, core_place, *token_halves, gain1, bias1)
        turned_cot = turn(start, core_place, *cot_halves)
    x, normed, normed_t = prepared
    cot, cot_t = turned_cot
    for g in range(groups):
        project(g)
        flow.step(forward[g][2])
    atts = [f[1] for f in forward]
    middle, normed_ffn, normed_ffn_t = out_norm(
        out_piece, flow.me, x, gain2, bias2, atts, slabs["a"]
    )
    flow.step(normed_ffn)

    held = None
    sums_of = {}
    onto = []
    feed_names = ["a"] * cut + ["c"] * (subs - cut)
    for s in range(subs):
        final = s == subs - 1
        grads, held = feed_forward(
            feed_pieces[s],
            feed_outs[s],
            flow.me,
            normed_ffn,
            normed_ffn_t,
            cot,
            cot_t,
            held,
            slabs[feed_names[s]],
            [],
            (out_piece, slabs["a"], middle, gain2, groups) if final else None,
        )
        first = 1 + s % 2
        if not rows.split:
            sums_of[s] = plain(*grads)
        elif final:
            flow.add(functools.partial(reduce_all, first), "feed", sums_of, grads)
        else:
            flow.add(functools.partial(halve, first, False), s, sums_of, grads)
        if s == 1 and rows.split:
            flow.step(held[1], gate=lambda: slabs["c"][-1:])
        elif not final:
            flow.step(held[1])
    mixed, grad_middle, branch_t, sums2, *grad_atts = held
    mixed, core_place, _ = flow.step(mixed, core_place, sums2)
    mixed_held, mixed_other = turn_back(back, core_place, mixed)
    flow.add(exchange, "mixed", sums_of, [mixed_other])
    grad_projs = []
    onto = []

    held = None
    qkv_slabs = [slabs["q0"]] + [slabs["q1"]] * (groups - 1)
    for g in range(groups):
        proj, att, inverse, kept = forward[g]
        held, grads, sums1 = attend_back(
            qkv_pieces[g],
            qkv_outs[g],
            flow.me,
            normed_t,
            proj,
            att,
            grad_atts[g],
            inverse,
            kept,
            qkv_slabs[g],
            branch_t,
            atts if g == 0 else [],
            held,
            x if g == groups - 1 else None,
            onto,
        )
        onto = grads
        if g == 0:
            if rows.split:
                flow.add(reduce_direct, "first", sums_of, grads)
            else:
                sums_of["first"] = plain(*grads)
            onto = []
        if g < groups - 1:
            flow.step(held)
    sums = jnp.concatenate([sums1[:2], sums2[:2]], 0)
    if rows.split:
        flow.add(reduce_last, "last", sums_of, [*grads, sums])
        (held,) = flow.step(held)
    else:
        sums_of["last"] = plain(*grads)
    start_late, _ = tie(back, flow.me)
    tokens_held, tokens_other = norm_back(start_late, core_place, x, held, grad_middle, gain1)
    tokens_held, tokens_other = flow.step(tokens_held, tokens_other)
    if rows.split:
        block = rows.block
        keep, send = small_call(
            last_split_body,
            "last_split",
            [SDS((2 * block + 16, wide), BF)] * 2,
            [flow.me],
            sums_of["last"],
        )
        near = hop(send, 4, dp_count)
        rest, send = small_call(
            last_middle_body, "last_middle", [SDS((block + 16, wide), BF)] * 2, [], [keep, near]
        )
        away = hop(send, 8, dp_count)
        while flow.active:
            flow.step()
        grad_qkv, norm_sums = small_call(
            last_sum_body,
            "last_sum",
            [SDS((3, block, part), F32), SDS((4, depth), F32)],
            [],
            [rest, away, sums_of["first"]],
        )
        grad_qkv = grad_qkv.transpose(1, 0, 2)
        grad_out = sums_of["first"][:, :part].T
        feed_sums = [sums_of["feed"]]
    else:
        early, last = sums_of["first"], sums_of["last"]
        parts = [early[:, part:], last[:, :part], last[:, part:]]
        grad_qkv = jnp.concatenate([r.reshape(-1, 3, 128) for r in parts], 2)
        grad_out = early[:, :part].T
        feed_sums = [sums_of[s] for s in range(subs)]
        norm_sums = jnp.sum(lax.all_gather(sums + swap(sums), "dp", axis=0), 0)
    feed_sum = jnp.concatenate(feed_sums, 1) if len(feed_sums) > 1 else feed_sums[0]
    feed_list = [feed_sum[:, wide * s : wide * (s + 1)] for s in range(subs)]

    return (
        place(core_place, mixed_held, sums_of["mixed"])[:, None],
        place(core_place, tokens_held, swap(tokens_other))[:, None],
        norm_sums[0],
        norm_sums[1],
        grad_qkv,
        grad_out,
        norm_sums[2],
        norm_sums[3],
        jnp.concatenate([r[:, :part] for r in feed_list], 1),
        jnp.concatenate([r[:, part:] for r in feed_list], 1).T,
    )


def solution(mesh):
    in_specs = (
        P(None, "dp", "mp", None),
        P(None, "dp", None),
        P(),
        P(),
        P("dp", None, "mp"),
        P("mp", "dp"),
        P(),
        P(),
        P("dp", "mp"),
        P("mp", "dp"),
        P(None, "dp", "mp", None),
    )
    out_specs = (
        P(None, "dp", "mp", None),
        P(None, "dp", "mp", None),
        P(),
        P(),
        P("dp", None, "mp"),
        P("mp", "dp"),
        P(),
        P(),
        P("dp", "mp"),
        P("mp", "dp"),
    )
    return jax.shard_map(
        on_device, mesh=mesh, in_specs=in_specs, out_specs=out_specs, check_vma=False
    )
```

```python
import functools
import math

import jax
import jax.numpy as jnp
from jax import lax
from jax.experimental import pallas as pl
from jax.experimental.pallas import tpu as pltpu
from jax.sharding import PartitionSpec as P

HD = 32
QB = 256
EPS = 1e-05
BF = jnp.bfloat16
F32 = jnp.float32
NEG = -1e30
SCALE = 1.0 / math.sqrt(HD)
LOG2E = math.log2(math.e)
C2 = SCALE * LOG2E
MIB = 1024 * 1024
SDS = jax.ShapeDtypeStruct


def nn(a, b):
    return lax.dot_general(a, b, (((1,), (0,)), ((), ())), preferred_element_type=F32)


def nt(a, b):
    return lax.dot_general(a, b, (((1,), (1,)), ((), ())), preferred_element_type=F32)


def params(mib):
    return pltpu.CompilerParams(vmem_limit_bytes=mib * MIB)


def in_hbm(values):
    return [pltpu.with_memory_space_constraint(v, pltpu.HBM) for v in values]


def in_vmem(values):
    return [pltpu.with_memory_space_constraint(v, pltpu.VMEM) for v in values]


def cost(gflop, mbytes):
    return pl.CostEstimate(flops=int(gflop * 1e9), bytes_accessed=int(mbytes * 1e6), transcendentals=0)


def any_spec():
    return pl.BlockSpec(memory_space=pl.ANY)


def smem_spec():
    return pl.BlockSpec(memory_space=pltpu.SMEM)


def vmem_spec():
    return pl.BlockSpec(memory_space=pltpu.VMEM)


def row_spec(width, rows=512):
    return pl.BlockSpec((rows, width), lambda r: (r, 0))


def column_spec(height, rows=512):
    return pl.BlockSpec((height, rows), lambda r: (0, r))


def whole_spec(shape):
    return pl.BlockSpec(shape, lambda r: tuple(0 for _ in shape))


MASKS = (0, 1, 2, 3)


class Rows:
    def __init__(self, dp_count, depth):
        self.dp_count = dp_count
        self.depth = depth
        self.split = (depth // dp_count) % 16 == 0 and dp_count == 16
        self.near = 4 if self.split else 1
        self.far = dp_count // 4 if self.split else 1
        self.block = depth // (self.near * self.far)
        self.shape = (self.far, self.near, self.block)


class Piece:
    def __init__(self, rows, kind, start=0, width=0, masks=MASKS):
        self.rows = rows
        self.masks = masks
        self.kind = kind if rows.split else "whole"
        self.start = start
        self.count = 2 * len(MASKS) if self.kind == "slabs" else 2
        if self.kind == "stack":
            self.shape = (len(MASKS), rows.far, rows.block, width)
        else:
            self.shape = rows.shape + (width,)


def piece_copies(piece, me, refs, moves, sem, outward):
    copies = []
    each = piece.count // 2
    for half, column, width, view in moves:
        cols = pl.ds(piece.start + column, width)
        if piece.kind == "whole":
            pairs = [(refs[half].at[:, :, :, cols], view)]
        else:
            pairs = []
            for k, mask in enumerate(piece.masks):
                ref = refs[half].at[k] if piece.kind == "stack" else refs[half * each + k]
                near = lax.bitwise_xor(lax.rem(me, 4), mask)
                pairs.append((ref.at[:, :, cols], view.at[:, near]))
        for outside, inside in pairs:
            if outward:
                copies.append(pltpu.make_async_copy(inside, outside, sem))
            else:
                copies.append(pltpu.make_async_copy(outside, inside, sem))
    return copies


def start_all(copies):
    for copy in copies:
        copy.start()


def wait_bytes(ref, sem):
    pltpu.make_async_copy(ref, ref, sem).wait()


def flat(value):
    return value.reshape(-1, value.shape[-1])


def head_row(h):
    return lax.broadcasted_iota(jnp.int32, (1, 128), 1) // HD == h


def fill_bias(bias, seg_col, seg_row):
    key = lax.broadcasted_iota(jnp.int32, (QB, QB), 0)
    query = lax.broadcasted_iota(jnp.int32, (QB, QB), 1)
    bias[0] = jnp.where(query >= key, 0.0, NEG)
    bias[1] = jnp.where((query >= key) & (seg_col[...] == seg_row[...]), 0.0, NEG)


def turned(doubles, start, r):
    coarse = pl.multiple_of(start // 16 * 16 + r * QB, 16)
    fine = start % 16
    row = lax.broadcasted_iota(jnp.int32, (QB, QB + 16), 0)
    col = lax.broadcasted_iota(jnp.int32, (QB, QB + 16), 1)
    pick = jnp.where(col - row == fine, 1.0, 0.0).astype(BF)
    total = None
    for double in doubles:
        part = nn(pick, double[pl.ds(coarse, QB + 16), :])
        total = part if total is None else total + part
    return total


def norm_parts(values):
    centered = values - jnp.mean(values, axis=-1, keepdims=True)
    spread = jnp.mean(centered * centered, axis=-1, keepdims=True)
    root = lax.rsqrt(spread + EPS)
    return centered * root, root


def fill_double(double, core, own, other, sem):
    here = own.shape[1]
    for k, half in enumerate((own, other)):
        pltpu.make_async_copy(half.at[core], double.at[pl.ds(k * here, here)], sem).start()
    wait_bytes(double.at[pl.ds(0, 2 * here)], sem)
    double[2 * here :, :] = double[: 2 * here, :]


def prepare_body(start, core, own, other, gain, offset, x_out, normed_out, normed_t_out, double, x, normed, normed_t, sems):
    fill_double(double, core[0], own, other, sems.at[3])

    def step(r, carry):
        at = pl.ds(pl.multiple_of(r * QB, QB), QB)
        value = turned([double], start[0], r)
        x[at, :] = value.astype(BF)
        hat, _ = norm_parts(value)
        low = (hat * gain[...] + offset[...]).astype(BF)
        normed[at, :] = low
        normed_t[:, at] = low.T
        return carry

    lax.fori_loop(0, x.shape[0] // QB, step, 0)
    copies = [
        pltpu.make_async_copy(normed, normed_out, sems.at[0]),
        pltpu.make_async_copy(x, x_out, sems.at[1]),
        pltpu.make_async_copy(normed_t, normed_t_out, sems.at[2]),
    ]
    start_all(copies)
    for copy in copies:
        copy.wait()


def prepare(start, core, own, other, gain, offset):
    _, here, depth = own.shape
    shape, shape_t = (2 * here, depth), (depth, 2 * here)
    shapes = [shape, shape, shape_t]
    return pl.pallas_call(
        prepare_body,
        in_specs=[smem_spec()] * 2 + [any_spec()] * 2 + [vmem_spec()] * 2,
        out_specs=[any_spec()] * 3,
        out_shape=[pltpu.HBM(s, BF) for s in shapes],
        scratch_shapes=[pltpu.VMEM((4 * here, depth), BF)]
        + [pltpu.VMEM(s, BF) for s in shapes]
        + [pltpu.SemaphoreType.DMA((4,))],
        compiler_params=params(20),
        cost_estimate=cost(4, 8),
        name="prepare",
    )(start, core, *in_hbm([own, other]), gain, offset)


def turn_body(start, core, own, other, cot_out, cot_t_out, double, cot, cot_t, sems):
    fill_double(double, core[0], own, other, sems.at[2])

    def step(r, carry):
        at = pl.ds(pl.multiple_of(r * QB, QB), QB)
        low = turned([double], start[0], r).astype(BF)
        cot[at, :] = low
        cot_t[:, at] = low.T
        return carry

    lax.fori_loop(0, cot.shape[0] // QB, step, 0)
    copies = [
        pltpu.make_async_copy(cot, cot_out, sems.at[0]),
        pltpu.make_async_copy(cot_t, cot_t_out, sems.at[1]),
    ]
    start_all(copies)
    for copy in copies:
        copy.wait()


def turn(start, core, own, other):
    _, here, depth = own.shape
    shapes = [(2 * here, depth), (depth, 2 * here)]
    return pl.pallas_call(
        turn_body,
        in_specs=[smem_spec()] * 2 + [any_spec()] * 2,
        out_specs=[any_spec()] * 2,
        out_shape=[pltpu.HBM(s, BF) for s in shapes],
        scratch_shapes=[pltpu.VMEM((4 * here, depth), BF)]
        + [pltpu.VMEM(s, BF) for s in shapes]
        + [pltpu.SemaphoreType.DMA((3,))],
        compiler_params=params(16),
        cost_estimate=cost(4, 8),
        name="turn",
    )(start, core, *in_hbm([own, other]))


def turn_back_body(start, core, values, held, other, double, own, sem):
    here = other.shape[0]
    double[: 2 * here, :] = values[...]
    double[2 * here :, :] = values[...]
    count = here // QB

    def step(r, carry):
        at = pl.ds(pl.multiple_of(r * QB, QB), QB)
        own[at, :] = turned([double], start[0], r).astype(BF)
        other[at, :] = turned([double], start[0], r + count).astype(BF)
        return carry

    lax.fori_loop(0, count, step, 0)
    copy = pltpu.make_async_copy(own, held.at[core[0]], sem)
    copy.start()
    copy.wait()


def place_body(core, other, held, out, sem):
    copy = pltpu.make_async_copy(other, out.at[1 - core[0]], sem)
    copy.start()
    copy.wait()


def place(core, held, other):
    return pl.pallas_call(
        place_body,
        in_specs=[smem_spec(), any_spec(), any_spec()],
        out_specs=any_spec(),
        out_shape=pltpu.HBM(held.shape, held.dtype),
        input_output_aliases={2: 0},
        scratch_shapes=[pltpu.SemaphoreType.DMA],
        compiler_params=params(4),
        cost_estimate=cost(0, 4),
        name="place",
    )(core, other, *in_hbm([held]))


def turn_back(start, core, values):
    length, depth = values.shape
    half = (length // 2, depth)
    return pl.pallas_call(
        turn_back_body,
        in_specs=[smem_spec()] * 2 + [vmem_spec()],
        out_specs=[any_spec(), vmem_spec()],
        out_shape=[pltpu.HBM((2,) + half, BF), SDS(half, BF)],
        scratch_shapes=[
            pltpu.VMEM((2 * length, depth), BF),
            pltpu.VMEM(half, BF),
            pltpu.SemaphoreType.DMA,
        ],
        compiler_params=params(16),
        cost_estimate=cost(2, 4),
        name="turn_back",
    )(start, core, values)


def arrange_body(widths, me, *refs):
    pieces, outs = refs[:4], refs[4:]
    far = me[0] // 4
    for m, piece in enumerate(pieces):
        begin = 0
        for out, width in zip(outs, widths):
            out[lax.bitwise_xor(far, m)] = piece[:, begin : begin + width]
            begin += width


def arrange(rows, me, pieces, widths):
    return pl.pallas_call(
        functools.partial(arrange_body, widths),
        in_specs=[smem_spec()] + [vmem_spec()] * 4,
        out_specs=[vmem_spec()] * len(widths),
        out_shape=[SDS((rows.far, rows.block, w), BF) for w in widths],
        compiler_params=params(8),
        cost_estimate=cost(1, 1),
        name="arrange",
    )(me, *pieces)


KEPT = (0, 256, 768, 1536)
KEPT_ROWS = (256, 512, 768, 256)
ORDER = (2, 1, 0, 3)


def project_attend_body(piece, me, normed_in, seg_col, seg_row, *refs):
    slabs = refs[: piece.count]
    proj_out, att, inverse, kept_out, weight, proj, normed, bias = refs[piece.count : piece.count + 8]
    keys_m, values_t, att_t, kept, sem, out_sem, kept_sem = refs[piece.count + 8 :]
    normed_copy = pltpu.make_async_copy(normed_in, normed, out_sem)
    normed_copy.start()
    moves = [(half, 0, 384, weight.at[:, :, :, pl.ds(384 * half, 384)]) for half in range(2)]
    start_all(piece_copies(piece, me[0], slabs, moves, sem, False))
    fill_bias(bias, seg_col, seg_row)
    values_t[...] = jnp.ones_like(values_t)
    normed_copy.wait()
    wait_bytes(weight, sem)

    for c in range(3):
        cols = slice(c * 256, c * 256 + 256)
        proj[:, cols] = nn(normed[...], flat(weight[:, :, :, cols])).astype(BF)
    proj_copy = pltpu.make_async_copy(proj, proj_out, out_sem)
    proj_copy.start()
    for half in range(2):
        flipped = proj[:, half * 384 + 256 : half * 384 + 384].T
        for h in range(4):
            values_t[half * 4 + h, 0:HD, :] = flipped[h * HD : (h + 1) * HD]

    units = [(h, i) for i in (2, 1, 0, 3) for h in range(4)]

    def step(half, carry):
        col = pl.multiple_of(half * 384, 128)
        for h in range(4):
            keys_m[h] = jnp.where(head_row(h), proj[:, pl.ds(col + 128, 128)], 0)

        def score(h, i):
            first = 768 if i == 3 else 0
            scores = nt(keys_m[h, first : (i + 1) * QB, :], proj[i * QB : (i + 1) * QB, pl.ds(col, 128)])
            edge = scores[-QB:] + bias[1 if i == 3 else 0]
            return jnp.concatenate([scores[:-QB], edge], 0) if scores.shape[0] > QB else edge

        ahead = score(*units[0])
        for k, (h, i) in enumerate(units):
            scores = ahead
            if k + 1 < len(units):
                ahead = score(*units[k + 1])
            first = 768 if i == 3 else 0
            last = (i + 1) * QB
            at = slice(i * QB, last)
            peak = jnp.max(scores, axis=0, keepdims=True) * C2
            probs = jnp.exp2(scores * C2 - peak).astype(BF)
            kept[half * 4 + h, KEPT[i] : KEPT[i] + last - first, :] = probs
            summed = nn(values_t[half * 4 + h, :, first:last], probs)
            share = 1.0 / summed[HD : HD + 1]
            att_t[pl.ds(pl.multiple_of(half * 128 + h * HD, HD), HD), at] = summed[:HD] * share
            inverse[pl.ds(half * 4 + h, 1), at] = share
            if h == 3:
                part = (pl.ds(half * 4, 4), pl.ds(KEPT[i], last - first))
                pltpu.make_async_copy(kept.at[part], kept_out.at[part], kept_sem).start()
        return carry

    lax.fori_loop(0, 2, step, 0)
    for half in range(2):
        cols = slice(half * 128, half * 128 + 128)
        att[:, cols] = att_t[cols, :].T.astype(BF)
    proj_copy.wait()
    wait_bytes(kept, kept_sem)


def project_attend(piece, me, normed, seg_col, seg_row, slabs):
    length, depth = normed.shape
    rows = piece.rows
    return pl.pallas_call(
        functools.partial(project_attend_body, piece),
        in_specs=[smem_spec(), any_spec()] + [vmem_spec()] * 2 + [any_spec()] * len(slabs),
        out_specs=[any_spec()] + [vmem_spec()] * 2 + [any_spec()],
        out_shape=[
            pltpu.HBM((length, 768), BF),
            pltpu.HBM((length, 256), BF),
            pltpu.HBM((8, length), F32),
            pltpu.HBM((8, 1792, QB), BF),
        ],
        scratch_shapes=[
            pltpu.VMEM(rows.shape + (768,), BF),
            pltpu.VMEM((length, 768), BF),
            pltpu.VMEM((length, depth), BF),
            pltpu.VMEM((2, QB, QB), F32),
            pltpu.VMEM((4, length, 128), BF),
            pltpu.VMEM((8, HD + 16, length), BF),
            pltpu.VMEM((256, length), F32),
            pltpu.VMEM((8, 1792, QB), BF),
            pltpu.SemaphoreType.DMA,
            pltpu.SemaphoreType.DMA,
            pltpu.SemaphoreType.DMA,
        ],
        compiler_params=params(32),
        cost_estimate=cost(8, 8),
        name="project_attend",
    )(me, *in_hbm([normed]), seg_col, seg_row, *in_hbm(slabs))


def join_heads(attended):
    return jnp.concatenate([a[:, :128] for a in attended] + [a[:, 128:] for a in attended], 1)


def out_norm_body(piece, groups, me, tokens, gain, offset, *refs):
    attended = refs[:groups]
    slabs = refs[groups : groups + piece.count]
    middle, normed, normed_t, weight, sem = refs[groups + piece.count :]
    width = weight.shape[3] // 2

    @pl.when(pl.program_id(0) == 0)
    def _():
        moves = [(half, 0, width, weight.at[:, :, :, pl.ds(width * half, width)]) for half in range(2)]
        start_all(piece_copies(piece, me[0], slabs, moves, sem, False))
        wait_bytes(weight, sem)

    value = tokens[...].astype(F32) + nt(join_heads([a[...] for a in attended]), flat(weight[...]))
    middle[...] = value
    hat, _ = norm_parts(value)
    low = (hat * gain[...] + offset[...]).astype(BF)
    normed[...] = low
    normed_t[...] = low.T


def out_norm(piece, me, tokens, gain, offset, attended, slabs):
    length, depth = tokens.shape
    return pl.pallas_call(
        functools.partial(out_norm_body, piece, len(attended)),
        grid=(length // 512,),
        in_specs=[smem_spec(), row_spec(depth), whole_spec((1, depth)), whole_spec((1, depth))]
        + [row_spec(256)] * len(attended)
        + [any_spec()] * len(slabs),
        out_specs=[row_spec(depth)] * 2 + [column_spec(depth)],
        out_shape=[
            pltpu.HBM((length, depth), F32),
            pltpu.VMEM((length, depth), BF),
            pltpu.VMEM((depth, length), BF),
        ],
        scratch_shapes=[pltpu.VMEM(piece.rows.shape + (depth,), BF), pltpu.SemaphoreType.DMA],
        compiler_params=params(28),
        cost_estimate=cost(3, 8),
        name="out_norm",
    )(me, *in_hbm([tokens]), gain, offset, *in_hbm(attended), *in_hbm(slabs))


def gelu_parts(values):
    size = jnp.abs(values)
    density = jnp.exp2(values * values * (-0.5 * LOG2E) + math.log2(1.0 / math.sqrt(2 * math.pi)))
    below = 1.0 + 0.2316419 * size
    t = pl.reciprocal(below, approx=True)
    t = t * (2.0 - below * t)
    poly = t * (
        0.319381530
        + t * (-0.356563782 + t * (1.781477937 + t * (-1.821255978 + t * 1.330274429)))
    )
    tail = density * poly
    below = jnp.where(values >= 0, 1.0 - tail, tail)
    return values * below, below + values * density


def norm_pull(grad, hat, root, gain):
    scaled = grad * gain
    first = jnp.mean(scaled, axis=-1, keepdims=True)
    second = jnp.mean(scaled * hat, axis=-1, keepdims=True)
    return root * (scaled - first - hat * second)


def feed_forward_body(
    piece, out_piece, first, last_piece, groups, aliased, me, normed, normed_t, cot, cot_t, *refs
):
    refs = list(refs)
    final = last_piece is not None
    held = [] if first else [refs.pop(0), refs.pop(0)]
    if final:
        middle, gain = refs.pop(0), refs.pop(0)
        out_slabs, refs = refs[: last_piece.count], refs[last_piece.count :]
    slabs, refs = refs[: piece.count], refs[piece.count + aliased :]
    outs, refs = refs[:2], refs[2:]
    mixed_acc, grad_acc, refs = refs[0], refs[1], refs[2:]
    if final:
        mixed, grad_middle_out, branch_t, sums = refs[:4]
        grad_att, refs = refs[4 : 4 + groups], refs[4 + groups :]
    weight, staged, act, grad_hidden, sems = refs[:5]
    if final:
        mixed_low, middle_here, out_weight, grad_middle = refs[5:]
    length, depth = normed.shape
    moves = []
    for half in range(2):
        for which in range(2):
            at = pl.ds(which * 768 + half * 384, 384)
            moves.append((half, which * 384, 384, at))
    into = [(h, c, w, weight.at[:, :, :, at]) for h, c, w, at in moves]
    outof = [(h, c, w, staged.at[:, :, :, at]) for h, c, w, at in moves]
    start_all(piece_copies(piece, me[0], slabs, into, sems.at[0], False))
    if final:
        middle_copy = pltpu.make_async_copy(middle, middle_here, sems.at[4])
        middle_copy.start()
        width = depth // 2
        views = [
            (half, 0, width, out_weight.at[:, :, :, pl.ds(width * half, width)]) for half in range(2)
        ]
        start_all(piece_copies(last_piece, me[0], out_slabs, views, sems.at[5], False))
    wait_bytes(weight, sems.at[0])
    chunks = [slice(c * 256, c * 256 + 256) for c in range(3)]

    def products(c):
        hidden = nn(normed[...], flat(weight[:, :, :, c * 256 : c * 256 + 256]))
        return hidden, nn(cot[...], flat(weight[:, :, :, 768 + c * 256 : 1024 + c * 256]))

    ahead = products(0)
    for c in range(3):
        hidden, grad_act = ahead
        if c < 2:
            ahead = products(c + 1)
        value, slope = gelu_parts(hidden)
        act[:, chunks[c]] = value.astype(BF)
        grad_hidden[:, chunks[c]] = (grad_act * slope).astype(BF)
    if final:
        middle_copy.wait()
    for cols in chunks:
        mixed_part = nt(act[...], flat(weight[:, :, :, 768:1536])[cols])
        grad_part = nt(grad_hidden[...], flat(weight[:, :, :, 0:768])[cols])
        if not first:
            mixed_part = mixed_part + held[0][:, cols]
            grad_part = grad_part + held[1][:, cols]
        if final:
            mixed_low[:, cols] = (middle_here[:, cols] + mixed_part).astype(BF)
        else:
            mixed_acc[:, cols] = mixed_part
        grad_acc[:, cols] = grad_part
    if final:
        out_copies = [pltpu.make_async_copy(mixed_low, mixed, sems.at[1])]
        start_all(out_copies)
        wait_bytes(out_weight, sems.at[5])
        sums[...] = jnp.zeros_like(sums)

        def back_step(r, carry):
            at = pl.ds(pl.multiple_of(r * 512, 512), 512)
            hat, root = norm_parts(middle_here[at, :])
            grad = grad_acc[at, :]
            value = cot[at, :].astype(F32) + norm_pull(grad, hat, root, gain[...])
            grad_middle[at, :] = value
            low = value.astype(BF)
            branch_t[:, at] = low.T
            sums[0:1, :] += jnp.sum(grad * hat, axis=0, keepdims=True)
            sums[1:2, :] += jnp.sum(grad, axis=0, keepdims=True)
            back = nn(low, flat(out_weight[...])).astype(BF)
            for g in range(groups):
                grad_att[g][at, 0:128] = back[:, g * 128 : g * 128 + 128]
                grad_att[g][at, 128:256] = back[:, width + g * 128 : width + g * 128 + 128]
            return carry

        lax.fori_loop(0, length // 512, back_step, 0)
        out_copies.append(pltpu.make_async_copy(grad_middle, grad_middle_out, sems.at[2]))
        out_copies[-1].start()
    else:
        out_copies = []
    for c in range(3):
        cols = slice(c * 256, c * 256 + 256)
        up = nn(normed_t[...], grad_hidden[:, cols]).astype(BF)
        staged[:, :, :, cols] = up.reshape(staged.shape[:3] + (256,))
        down = nn(cot_t[...], act[:, cols]).astype(BF)
        staged[:, :, :, 768 + c * 256 : 1024 + c * 256] = down.reshape(staged.shape[:3] + (256,))
    start_all(piece_copies(out_piece, me[0], outs, outof, sems.at[3], True))
    for copy in out_copies:
        copy.wait()
    wait_bytes(staged, sems.at[3])


def feed_forward(
    piece, out_piece, me, normed, normed_t, cot, cot_t, held, slabs, onto, last=None
):
    length, depth = normed.shape
    rows = piece.rows
    first, final = held is None, last is not None
    ins = [me] + in_vmem([normed, normed_t, cot, cot_t]) + ([] if first else in_vmem(held))
    specs = [smem_spec()] + [vmem_spec()] * (len(ins) - 1)
    aliases = {} if first else {5: 2, 6: 3}
    scratch = [
        pltpu.VMEM(rows.shape + (1536,), BF),
        pltpu.VMEM(rows.shape + (1536,), BF),
        pltpu.VMEM((length, 768), BF),
        pltpu.VMEM((length, 768), BF),
        pltpu.SemaphoreType.DMA((6,)),
    ]
    last_piece, groups = None, 0
    outs = [SDS(out_piece.shape, BF)] * 2 + [pltpu.VMEM((length, depth), F32)] * 2
    out_specs = [any_spec()] * 2 + [vmem_spec()] * 2
    if final:
        last_piece, last_slabs, middle, gain, groups = last
        ins += in_hbm([middle]) + [gain] + in_hbm(last_slabs)
        specs += [any_spec(), vmem_spec()] + [any_spec()] * len(last_slabs)
        scratch += [
            pltpu.VMEM((length, depth), BF),
            pltpu.VMEM((length, depth), F32),
            pltpu.VMEM(rows.shape + (depth,), BF),
            pltpu.VMEM((length, depth), F32),
        ]
        outs += [pltpu.HBM((length, depth), BF), pltpu.HBM((length, depth), F32)]
        outs += [pltpu.VMEM((depth, length), BF), SDS((8, depth), F32)]
        outs += [pltpu.HBM((length, 256), BF)] * groups
        out_specs += [any_spec()] * 2 + [vmem_spec()] * (2 + groups)
    aliases |= {len(ins) + piece.count + k: k for k in range(len(onto))}
    got = pl.pallas_call(
        functools.partial(
            feed_forward_body, piece, out_piece, first, last_piece, groups, len(onto)
        ),
        in_specs=specs + [any_spec()] * (piece.count + len(onto)),
        out_specs=out_specs,
        out_shape=outs,
        input_output_aliases=aliases,
        scratch_shapes=scratch,
        compiler_params=params(40 if final else 24),
        cost_estimate=cost(14 if final else 11, 20),
        name="feed_forward",
    )(*ins, *in_hbm(slabs), *in_hbm(onto))
    return got[:2], got[2:4], got[4:]


def attend_back_body(piece, out_piece, extra, aliased, final, me, normed_t_in, proj, att, grad_att, inverse, kept_in, *refs):
    refs = list(refs)
    slabs, refs = refs[: piece.count], refs[piece.count :]
    if extra:
        branch_t = refs.pop(0)
        attended, refs = refs[:extra], refs[extra:]
    else:
        held = refs.pop(0)
    if final:
        tokens_in = refs.pop(0)
    refs = refs[aliased:]
    total, outs, refs = refs[0], refs[1:3], refs[3:]
    if final:
        sums = refs.pop(0)
    grad_proj, key_sum, value_sum = refs[:3]
    refs = refs[3:]
    kept, delta, keys_t, query_t, query_m, grad_m, staged, normed_t, weight, sems = refs[:10]
    for half in range(2):
        for i in ORDER:
            part = (pl.ds(half * 4, 4), pl.ds(KEPT[i], KEPT_ROWS[i]))
            sem = sems.at[5 + 4 * half + i]
            pltpu.make_async_copy(kept_in.at[part], kept.at[part], sem).start()
    copies = [pltpu.make_async_copy(normed_t_in, normed_t, sems.at[1])]
    if final:
        copies.append(pltpu.make_async_copy(tokens_in, refs[10], sems.at[3]))
    moves = [(half, 0, 384, weight.at[:, :, :, pl.ds(384 * half, 384)]) for half in range(2)]
    start_all(copies + piece_copies(piece, me[0], slabs, moves, sems.at[4], False))
    length = proj.shape[0]
    if extra:
        joined = join_heads([a[...] for a in attended])
        out_grad = nn(branch_t[...], joined).astype(BF)
        staged[:, :, :, 768:] = out_grad.reshape(staged.shape[:3] + (768,))
    for half in range(2):
        cols = slice(half * 128, half * 128 + 128)
        product = (grad_att[:, cols].astype(F32) * att[:, cols].astype(F32)).T
        for h in range(4):
            stat = slice(half * 4 + h, half * 4 + h + 1)
            total_here = jnp.sum(product[h * HD : (h + 1) * HD], axis=0, keepdims=True)
            delta[stat, :] = total_here * inverse[stat, :]
        keys_t[cols, :] = proj[:, half * 384 + 128 : half * 384 + 256].T

    def step(half, carry):
        col = pl.multiple_of(half * 384, 128)
        out = pl.multiple_of(half * 128, 128)
        share = jnp.concatenate(
            [jnp.broadcast_to(inverse[pl.ds(half * 4 + h, 1), :], (HD, length)) for h in range(4)], 0
        ).T
        grads = (grad_att[:, pl.ds(out, 128)].astype(F32) * share).astype(BF)
        for h in range(4):
            mine = head_row(h)
            query_m[h] = jnp.where(mine, proj[:, pl.ds(col, 128)], 0)
            grad_m[h] = jnp.where(mine, grads, 0)
        key_sum[...] = jnp.zeros_like(key_sum)
        value_sum[...] = jnp.zeros_like(value_sum)
        for i in (2, 1, 0, 3):
            first = 768 if i == 3 else 0
            last = (i + 1) * QB
            here = slice(first, last)
            there = slice(i * QB, last)
            values = proj[here, pl.ds(col + 256, 128)]
            rows_here = slice(KEPT[i], KEPT[i] + last - first)
            wait_bytes(
                kept.at[pl.ds(half * 4, 4), pl.ds(KEPT[i], KEPT_ROWS[i])], sems.at[5 + 4 * half + i]
            )
            all_probs, all_grads = [], []
            ahead = nt(values, grad_m[0, there, :])
            for h in range(4):
                grad_probs = ahead
                if h < 3:
                    ahead = nt(values, grad_m[h + 1, there, :])
                stat = pl.ds(half * 4 + h, 1)
                lanes = pl.ds(pl.multiple_of(half * 128 + h * HD, HD), HD)
                probs = kept[half * 4 + h, rows_here, :]
                grad_scores = (probs.astype(F32) * (grad_probs - delta[stat, there])).astype(BF)
                all_probs.append(probs)
                all_grads.append(grad_scores)
                query_t[lanes, there] = nn(keys_t[lanes, here], grad_scores)
            stacked = jnp.concatenate([grad_m[h, there, :] for h in range(4)], 0)
            value_sum[here, :] += nn(jnp.concatenate(all_probs, 1), stacked)
            stacked = jnp.concatenate([query_m[h, there, :] for h in range(4)], 0)
            key_sum[here, :] += nn(jnp.concatenate(all_grads, 1), stacked)
        grad_proj[:, pl.ds(col + 128, 128)] = (key_sum[...] * SCALE).astype(BF)
        grad_proj[:, pl.ds(col + 256, 128)] = value_sum[...].astype(BF)
        return carry

    lax.fori_loop(0, 2, step, 0)
    for half in range(2):
        grad_proj[:, half * 384 : half * 384 + 128] = (
            query_t[half * 128 : half * 128 + 128, :].T * SCALE
        ).astype(BF)
    for copy in copies:
        copy.wait()
    wait_bytes(weight, sems.at[4])
    for c in range(3):
        cols = slice(c * 256, c * 256 + 256)
        part = nn(normed_t[...], grad_proj[:, cols]).astype(BF)
        staged[:, :, :, cols] = part.reshape(staged.shape[:3] + (256,))
    moves = [(half, 0, 384, staged.at[:, :, :, pl.ds(384 * half, 384)]) for half in range(2)]
    if extra:
        moves += [
            (half, -384, 384, staged.at[:, :, :, pl.ds(768 + 384 * half, 384)]) for half in range(2)
        ]
    start_all(piece_copies(out_piece, me[0], outs, moves, sems.at[0], True))
    if final:
        sums[...] = jnp.zeros_like(sums)

    for c in range(3):
        cols = slice(c * 256, c * 256 + 256)
        value = nt(grad_proj[...], flat(weight[...])[cols])
        total[:, cols] = value if extra else value + held[:, cols]
    if final:

        def sum_step(r, carry):
            at = pl.ds(pl.multiple_of(r * QB, QB), QB)
            value = total[at, :]
            hat, _ = norm_parts(refs[10][at, :].astype(F32))
            sums[0:1, :] += jnp.sum(value * hat, axis=0, keepdims=True)
            sums[1:2, :] += jnp.sum(value, axis=0, keepdims=True)
            return carry

        lax.fori_loop(0, length // QB, sum_step, 0)
    wait_bytes(staged, sems.at[0])


def attend_back(
    piece,
    out_piece,
    me,
    normed_t,
    proj,
    att,
    grad_att,
    inverse,
    kept,
    slabs,
    branch_t,
    attended,
    held,
    tokens,
    onto,
):
    depth, length = normed_t.shape
    extra = len(attended)
    final = tokens is not None
    columns = 1536 if extra else 768
    ins = [me] + in_hbm([normed_t, proj, att, grad_att, inverse, kept]) + in_hbm(slabs)
    specs = [smem_spec(), any_spec()] + [vmem_spec()] * 4 + [any_spec()] * (1 + len(slabs))
    aliases = {}
    if extra:
        ins += in_vmem([branch_t]) + in_hbm(attended)
        specs += [vmem_spec()] * (1 + extra)
    else:
        aliases = {len(ins): 0}
        ins += in_vmem([held])
        specs += [vmem_spec()]
    if final:
        ins += in_hbm([tokens])
        specs += [any_spec()]
    outs = [pltpu.VMEM((length, depth), F32)] + [SDS(out_piece.shape, BF)] * 2
    scratch = [
        pltpu.VMEM((8, 1792, QB), BF),
        pltpu.VMEM((8, length), F32),
        pltpu.VMEM((256, length), BF),
        pltpu.VMEM((256, length), F32),
        pltpu.VMEM((4, length, 128), BF),
        pltpu.VMEM((4, length, 128), BF),
        pltpu.VMEM(out_piece.rows.shape + (columns,), BF),
        pltpu.VMEM((depth, length), BF),
        pltpu.VMEM(piece.rows.shape + (768,), BF),
        pltpu.SemaphoreType.DMA((13,)),
    ]
    if final:
        outs.append(SDS((8, depth), F32))
        scratch.append(pltpu.VMEM((length, depth), BF))
    got = pl.pallas_call(
        functools.partial(attend_back_body, piece, out_piece, extra, len(onto), final),
        in_specs=specs + [any_spec()] * len(onto),
        out_specs=[vmem_spec()] + [any_spec()] * 2 + ([vmem_spec()] if final else []),
        out_shape=outs,
        input_output_aliases=aliases | {len(ins) + k: 1 + k for k in range(len(onto))},
        scratch_shapes=[
            pltpu.VMEM((length, 768), BF),
            pltpu.VMEM((length, 128), F32),
            pltpu.VMEM((length, 128), F32),
        ]
        + scratch,
        compiler_params=params(40),
        cost_estimate=cost(12, 8),
        name="attend_back",
    )(*ins, *onto)
    return got[0], got[1:3], got[3] if final else None


def norm_back_body(
    start, core, tokens, grad_normed, grad_middle, gain, held, other, high, low, own, sem
):
    length = high.shape[0] // 2
    r = pl.program_id(0)
    hat, root = norm_parts(tokens[...].astype(F32))
    value = grad_middle[...] + norm_pull(grad_normed[...], hat, root, gain[...])
    top = value.astype(BF)
    rest = (value - top.astype(F32)).astype(BF)
    for base in (0, length):
        at = pl.ds(pl.multiple_of(base + r * QB, QB), QB)
        high[at, :] = top
        low[at, :] = rest

    @pl.when(r == pl.num_programs(0) - 1)
    def _():
        count = own.shape[0] // QB
        for k in range(count):
            own[k * QB : k * QB + QB, :] = turned([high, low], start[0], k)
        copy = pltpu.make_async_copy(own, held.at[core[0]], sem)
        copy.start()
        for k in range(count):
            other[k * QB : k * QB + QB, :] = turned([high, low], start[0], k + count)
        copy.wait()


def norm_back(start, core, tokens, grad_normed, grad_middle, gain):
    length, depth = tokens.shape
    half = (length // 2, depth)
    return pl.pallas_call(
        norm_back_body,
        grid=(length // QB,),
        in_specs=[smem_spec()] * 2 + [row_spec(depth, QB)] * 3 + [whole_spec((1, depth))],
        out_specs=[any_spec(), whole_spec(half)],
        out_shape=[pltpu.HBM((2,) + half, F32), SDS(half, F32)],
        scratch_shapes=[
            pltpu.VMEM((2 * length, depth), BF),
            pltpu.VMEM((2 * length, depth), BF),
            pltpu.VMEM(half, F32),
            pltpu.SemaphoreType.DMA,
        ],
        compiler_params=params(24),
        cost_estimate=cost(4, 16),
        name="norm_back",
    )(start, core, *in_hbm([tokens]), *in_vmem([grad_normed]), *in_hbm([grad_middle]), gain)


def split_far_body(counts, me, *refs):
    keep, send = refs[-2:]
    far = me[0] // 4
    begin = 0
    for count in counts:
        pieces, refs = refs[:count], refs[count:]
        cols = pl.ds(begin, pieces[0].shape[-1])
        begin += pieces[0].shape[-1]
        for k, out in enumerate((keep, send)):
            for slot in range(2):
                at = lax.bitwise_xor(far, k + 2 * slot)
                total = pieces[0][at].astype(F32)
                for piece in pieces[1:]:
                    total = total + piece[at].astype(F32)
                out[slot, :, cols] = total.astype(BF)


def split_far(me, groups):
    width, specs = 0, []
    for pieces in groups:
        far, block, columns = pieces[0].shape[-3:]
        width += columns
        for piece in pieces:
            if piece.ndim == 4:
                specs.append(pl.BlockSpec((None, far, block, columns), lambda i: (0, 0, 0, 0)))
            else:
                specs.append(whole_spec(piece.shape))
    return pl.pallas_call(
        functools.partial(split_far_body, [len(pieces) for pieces in groups]),
        grid=(1,),
        in_specs=[smem_spec()] + specs,
        out_specs=[whole_spec((2, block, width))] * 2,
        out_shape=[SDS((2, block, width), BF)] * 2,
        compiler_params=params(16),
        cost_estimate=cost(1, 2),
        name="split_far",
    )(me, *[piece for pieces in groups for piece in pieces])


def put_sums(ref, base, total):
    high = total.astype(BF)
    ref[base : base + 4, :] = high
    ref[base + 4 : base + 8, :] = (total - high.astype(F32)).astype(BF)
    ref[base + 8 : base + 16, :] = jnp.zeros((8, total.shape[1]), BF)


def get_sums(ref, base):
    return ref[base : base + 4, :].astype(F32) + ref[base + 4 : base + 8, :].astype(F32)


def last_join_body(own, other, sums, sums_away, *outs):
    total = sums[...] + sums_away[...]
    rows = outs[0].shape[0] - 16
    for k, out in enumerate(outs):
        value = own[k].astype(F32) + other[k].astype(F32)
        out[:rows, :] = value.astype(BF).reshape(rows, -1)
        put_sums(out, rows, total)


def last_split_body(me, m0, m1, m2, m3, keep, send):
    far = me[0] // 4
    rows = m0.shape[0] - 16
    block = rows // 4
    for k, out in enumerate((keep, send)):
        for slot in range(2):
            at = pl.ds(pl.multiple_of(lax.bitwise_xor(far, k + 2 * slot) * block, 16), block)
            total = (m0[at, :].astype(F32) + m1[at, :].astype(F32)) + (
                m2[at, :].astype(F32) + m3[at, :].astype(F32)
            )
            out[slot * block : (slot + 1) * block, :] = total.astype(BF)
    total = (get_sums(m0, rows) + get_sums(m1, rows)) + (get_sums(m2, rows) + get_sums(m3, rows))
    put_sums(keep, 2 * block, total)
    put_sums(send, 2 * block, total)


def last_middle_body(keep, near, rest, send):
    block = (keep.shape[0] - 16) // 2
    value = keep[:block, :].astype(F32) + near[:block, :].astype(F32)
    rest[:block, :] = value.astype(BF)
    value = keep[block : 2 * block, :].astype(F32) + near[block : 2 * block, :].astype(F32)
    send[:block, :] = value.astype(BF)
    total = get_sums(keep, 2 * block) + get_sums(near, 2 * block)
    put_sums(rest, block, total)
    put_sums(send, block, total)


def last_sum_body(rest, away, first, grad_qkv, sums):
    block = rest.shape[0] - 16
    value = rest[:block, :].astype(F32) + away[:block, :].astype(F32)
    parts = [first[:, 384:], value[:, :384], value[:, 384:]]
    for which in range(3):
        cols = slice(which * 128, which * 128 + 128)
        grad_qkv[which] = jnp.concatenate([part[:, cols] for part in parts], 1)
    sums[...] = get_sums(rest, block) + get_sums(away, block)


def pack_body(part, out, up, down, packed):
    width = out.shape[1]
    packed[:, :width] = out[...]
    for s in range(up.shape[1] // part):
        cols = slice(s * part, (s + 1) * part)
        packed[:, width + 2 * s * part : width + (2 * s + 1) * part] = up[:, cols]
        packed[:, width + (2 * s + 1) * part : width + (2 * s + 2) * part] = down[:, cols]


def small_call(body, name, outs, scalars, values):
    return pl.pallas_call(
        body,
        in_specs=[smem_spec()] * len(scalars) + [vmem_spec()] * len(values),
        out_specs=[vmem_spec()] * len(outs),
        out_shape=outs,
        compiler_params=params(16),
        cost_estimate=cost(1, 3),
        name=name,
    )(*scalars, *values)


def swap(value):
    return lax.ppermute(value, "mp", [(0, 1), (1, 0)])


def tie(*values):
    return lax.optimization_barrier(values)


def hop(value, mask, count):
    return lax.ppermute(value, "dp", [(i, i ^ mask) for i in range(count)])


def hops(value, masks, count):
    return [(value, functools.partial(hop, mask=m, count=count)) for m in masks]


def far_hops(rows, values):
    return [
        (v, functools.partial(hop, mask=rows.near * m, count=rows.dp_count))
        for m, v in zip(range(1, rows.far), values)
    ]


def swaps(values):
    return [(v, swap) for v in values]


def send_all(requests):
    return [send(value) for value, send in requests]


def low_sum(values):
    total = values[0].astype(F32)
    for value in values[1:]:
        total = total + value.astype(F32)
    return total


class Flow:
    def __init__(self, me):
        self.me = me
        self.active = []

    def add(self, transfer, name, results, seeds=()):
        self.active.append([transfer, list(seeds), name, results])

    def step(self, *pivots, gate=None):
        values = [v for item in self.active for v in item[1]]
        tied = list(tie(self.me, *pivots, *values))
        self.me = tied.pop(0)
        pivots, tied = tied[: len(pivots)], tied[len(pivots) :]
        going, self.active, requests = self.active, [], []
        for item in going:
            transfer, values, name, results = item
            got, tied = tied[: len(values)], tied[len(values) :]
            try:
                if callable(transfer):
                    item[0] = transfer(*got)
                    asked = next(item[0])
                else:
                    asked = transfer.send(got)
                self.active.append(item)
                requests.append(asked)
            except StopIteration as stop:
                results[name] = stop.value
        gates = gate() if gate else []
        operands = [operand for asked in requests for operand, _ in asked]
        tied = list(tie(self.me, *gates, *operands))
        self.me = tied[0]
        tied = tied[1 + len(gates) :]
        for item, asked in zip(self.active, requests):
            item[1] = [send(operand) for (_, send), operand in zip(asked, tied)]
            tied = tied[len(asked) :]
        return pivots


def add_low(a, b):
    return (a.astype(F32) + b.astype(F32)).astype(BF)


def on_device(
    tokens, segment, ln1_gain, ln1_bias, w_qkv, w_out, ln2_gain, ln2_bias, w_up, w_down, cotangent
):
    dp_count = lax.axis_size("dp")
    core = lax.axis_index("mp")
    me = lax.axis_index("dp").astype(jnp.int32).reshape(1)
    here, depth = tokens.shape[2], tokens.shape[3]
    length = 2 * here
    rows = Rows(dp_count, depth)

    groups = w_qkv.shape[2] // 128
    part = 384
    subs = w_up.shape[1] // part
    cut = subs // 2
    qkv = [w_qkv[:, :, g * 128 : (g + 1) * 128].reshape(-1, part) for g in range(groups)]
    shards = {"q": jnp.concatenate(qkv, 1)}

    def pack(out, up, down):
        return small_call(
            functools.partial(pack_body, part),
            "pack",
            [SDS((up.shape[0], out.shape[0] + 2 * up.shape[1]), BF)],
            [],
            [out.T, up, down.T],
        )[0]

    seg = lax.dynamic_index_in_dim(segment[:, 0], core, 0, keepdims=False)
    run = length * 3 // 4
    begin = jnp.argmax(seg[: length - run + 1] == seg[run - 1 :]).astype(jnp.int32)
    start = ((begin - here * core) % length).reshape(1)
    back = (length - start) % length
    seg_tail = lax.dynamic_slice_in_dim(jnp.concatenate([seg, seg]), begin + run, length - run)
    seg_col = seg_tail.reshape(-1, 1)
    seg_row = seg_tail.reshape(1, -1)
    gain1, bias1, gain2, bias2 = (
        v.reshape(1, -1) for v in (ln1_gain, ln1_bias, ln2_gain, ln2_bias)
    )

    flow = Flow(me)
    core_place = core.astype(jnp.int32).reshape(1)
    token_halves = [tokens[:, 0], swap(tokens[:, 0])]
    cot_halves = [cotangent[:, 0], swap(cotangent[:, 0])]
    wide = 2 * part
    qkv_pieces = [Piece(rows, "slabs")] + [Piece(rows, "slabs", part * g) for g in range(groups - 1)]
    out_piece = Piece(rows, "slabs")
    feed_pieces = [Piece(rows, "slabs", part + wide * s) for s in range(cut)]
    feed_pieces += [Piece(rows, "slabs", wide * s) for s in range(subs - cut)]
    turns = [(0, 2, 1, 3), MASKS]
    feed_outs = [
        Piece(rows, "stack", 0, wide, turns[s % 2]) for s in range(subs)
    ]
    qkv_outs = [Piece(rows, "stack", part, wide)]
    qkv_outs += [Piece(rows, "stack", part * g, part * (groups - 1)) for g in range(groups - 1)]
    far = lax.axis_index("dp") // rows.near

    def gather_whole(shard):
        return lax.all_gather(shard, "dp", axis=0, tiled=True).reshape(rows.shape + (-1,))

    def fetch_near(near):
        got = yield hops(near, MASKS[1:], dp_count)
        own = [near] + got
        return own + [swap(x) for x in own]

    def via(mask):
        return functools.partial(hop, mask=mask, count=dp_count)

    def fetch_wide(shard, away):
        near, both_ways = yield [(shard, via(4)), (away, via(4))]
        (a0,) = arrange(rows, flow.me, [shard, near, away, both_ways], [shard.shape[1]])
        a1, a2, b0, away = yield [(a0, via(1)), (a0, via(2))] + swaps([a0]) + [(shard_c, via(8))]
        a3, b1, b2, near, both_ways = yield (
            [(a1, via(2))] + swaps([a1, a2]) + [(shard_c, via(4)), (away, via(4))]
        )
        slabs["a"] = [a0, a1, a2, a3, b0, b1, b2, swap(a3)]
        (c0,) = arrange(rows, flow.me, [shard_c, near, away, both_ways], [shard_c.shape[1]])
        (d0,) = yield swaps([c0])
        c1, c2 = yield [(c0, via(1)), (c0, via(2))]
        c3, d1, d2 = yield [(c2, via(1))] + swaps([c1, c2])
        return [c0, c1, c2, c3, d0, d1, d2, swap(c3)]

    def whole(shard):
        own = gather_whole(shard)
        return [own, swap(own)]

    def halve(first, hurry, own, other):
        if hurry:
            other = swap(other)
        else:
            (other,) = yield swaps([other])
        keep, send = (low_sum([own[k : k + 2], other[k : k + 2]]).astype(BF) for k in (0, 2))
        (near,) = yield [(send, via(first))]
        (away,) = yield [(low_sum([keep[1], near[1]]).astype(BF), via(3 - first))]
        return [keep, near, away]

    def direct(mine):
        got = yield hops_of(mine, (1, 2, 3))
        return [mine[0]] + got

    def hops_of(values, masks):
        return [(values[m], via(m)) for m in masks]

    def reduce_far(groups):
        keep, send = split_far(flow.me, groups)
        (near,) = yield [(send, via(4))]
        (away,) = yield [(low_sum([keep[1], near[1]]).astype(BF), via(8))]
        return low_sum([keep[0], near[0], away])

    def reduce_all(first, own, other):
        group = yield from halve(first, True, own, other)
        return (yield from reduce_far([sums_of[s] for s in range(subs - 1)] + [group]))

    def reduce_last(own, other, sums):
        other, sums_away = swap(other), swap(sums)
        mine = small_call(
            last_join_body,
            "last_join",
            [SDS((rows.far * rows.block + 16, wide), BF)] * 4,
            [],
            [own, other, sums, sums_away],
        )
        return (yield from direct(mine))

    def exchange(value):
        (got,) = yield swaps([value])
        return got

    def reduce_direct(own, other):
        (other,) = yield swaps([other])
        mine = [low_sum([own[k], other[k]]).astype(BF) for k in range(4)]
        pieces = yield from direct(mine)
        return (yield from reduce_far([pieces]))

    def plain(own, other):
        value = low_sum([own, swap(other)]).astype(BF).reshape(depth, -1)
        return lax.psum_scatter(value, "dp", scatter_dimension=0, tiled=True).astype(F32)

    def run(transfer):
        requests = next(transfer)
        while True:
            try:
                requests = transfer.send(send_all(requests))
            except StopIteration as stop:
                return stop.value

    slabs, forward = {}, []

    def project(g):
        name = "q0" if g == 0 else "q1"
        forward.append(
            project_attend(qkv_pieces[g], flow.me, normed, seg_col, seg_row, slabs[name])
        )

    if rows.split:
        shard_q = shards["q"]
        got = send_all(far_hops(rows, [shard_q] * (rows.far - 1)))
        prepared = prepare(start, core_place, *token_halves, gain1, bias1)
        tied = tie(*got, *prepared, w_out, w_up, w_down)
        got, prepared = tied[:3], tied[3:6]
        shard_a = pack(*tied[6:])
        near_q0, near_q1 = arrange(rows, me, [shard_q] + list(got), [part, wide])
        own = [near_q0] + [hop(near_q0, m, dp_count) for m in MASKS[1:]]
        first_cols = part + wide * cut
        shard_c, shard_a = shard_a[:, first_cols:], shard_a[:, :first_cols]
        away_a = hop(shard_a, 8, dp_count)
        start_cot, _ = tie(start, near_q0)
        turned_cot = turn(start_cot, core_place, *cot_halves)
        tied = tie(*own, *turned_cot)
        own, turned_cot = tied[:4], tied[4:]
        slabs["q0"] = list(own) + [swap(v) for v in own]
        flow.add(fetch_near, "q1", slabs, [near_q1])
        flow.add(fetch_wide, "c", slabs, [shard_a, away_a])
        flow.step(own[3])
    else:
        shard_a = pack(w_out, w_up, w_down)
        for name, shard in (
            ("q0", shards["q"][:, :part]),
            ("q1", shards["q"][:, part:]),
            ("a", shard_a[:, : part + wide * cut]),
            ("c", shard_a[:, part + wide * cut :]),
        ):
            slabs[name] = whole(shard)
        prepared = prepare(start, core_place, *token_halves, gain1, bias1)
        turned_cot = turn(start, core_place, *cot_halves)
    x, normed, normed_t = prepared
    cot, cot_t = turned_cot
    for g in range(groups):
        project(g)
        flow.step(forward[g][2])
    atts = [f[1] for f in forward]
    middle, normed_ffn, normed_ffn_t = out_norm(
        out_piece, flow.me, x, gain2, bias2, atts, slabs["a"]
    )
    flow.step(normed_ffn)

    held = None
    sums_of = {}
    onto = []
    feed_names = ["a"] * cut + ["c"] * (subs - cut)
    for s in range(subs):
        final = s == subs - 1
        grads, held, results = feed_forward(
            feed_pieces[s],
            feed_outs[s],
            flow.me,
            normed_ffn,
            normed_ffn_t,
            cot,
            cot_t,
            held,
            slabs[feed_names[s]],
            [],
            (out_piece, slabs["a"], middle, gain2, groups) if final else None,
        )
        first = 1 + s % 2
        if not rows.split:
            sums_of[s] = plain(*grads)
        elif final:
            flow.add(functools.partial(reduce_all, first), "feed", sums_of, grads)
        else:
            flow.add(functools.partial(halve, first, False), s, sums_of, grads)
        if s == 1 and rows.split:
            flow.step(grads[0], gate=lambda: slabs["c"][-1:])
        elif not final:
            flow.step(grads[0])
    mixed, grad_middle, branch_t, sums2, *grad_atts = results
    mixed, core_place, _ = flow.step(mixed, core_place, sums2)
    mixed_held, mixed_other = turn_back(back, core_place, mixed)
    flow.add(exchange, "mixed", sums_of, [mixed_other])
    grad_projs = []
    onto = []

    held = None
    qkv_slabs = [slabs["q0"]] + [slabs["q1"]] * (groups - 1)
    for g in range(groups):
        proj, att, inverse, kept = forward[g]
        held, grads, sums1 = attend_back(
            qkv_pieces[g],
            qkv_outs[g],
            flow.me,
            normed_t,
            proj,
            att,
            grad_atts[g],
            inverse,
            kept,
            qkv_slabs[g],
            branch_t,
            atts if g == 0 else [],
            held,
            x if g == groups - 1 else None,
            onto,
        )
        onto = grads
        if g == 0:
            if rows.split:
                flow.add(reduce_direct, "first", sums_of, grads)
            else:
                sums_of["first"] = plain(*grads)
            onto = []
        if g < groups - 1:
            flow.step(grads[0])
    sums = jnp.concatenate([sums1[:2], sums2[:2]], 0)
    if rows.split:
        flow.add(reduce_last, "last", sums_of, [*grads, sums])
        flow.step()
    else:
        sums_of["last"] = plain(*grads)
    start_late, _ = tie(back, flow.me)
    tokens_held, tokens_other = norm_back(start_late, core_place, x, held, grad_middle, gain1)
    tokens_held, tokens_other = flow.step(tokens_held, tokens_other)
    if rows.split:
        block = rows.block
        keep, send = small_call(
            last_split_body,
            "last_split",
            [SDS((2 * block + 16, wide), BF)] * 2,
            [flow.me],
            sums_of["last"],
        )
        near = hop(send, 4, dp_count)
        rest, send = small_call(
            last_middle_body, "last_middle", [SDS((block + 16, wide), BF)] * 2, [], [keep, near]
        )
        away = hop(send, 8, dp_count)
        while flow.active:
            flow.step()
        grad_qkv, norm_sums = small_call(
            last_sum_body,
            "last_sum",
            [SDS((3, block, part), F32), SDS((4, depth), F32)],
            [],
            [rest, away, sums_of["first"]],
        )
        grad_qkv = grad_qkv.transpose(1, 0, 2)
        grad_out = sums_of["first"][:, :part].T
        feed_sums = [sums_of["feed"]]
    else:
        early, last = sums_of["first"], sums_of["last"]
        parts = [early[:, part:], last[:, :part], last[:, part:]]
        grad_qkv = jnp.concatenate([r.reshape(-1, 3, 128) for r in parts], 2)
        grad_out = early[:, :part].T
        feed_sums = [sums_of[s] for s in range(subs)]
        norm_sums = jnp.sum(lax.all_gather(sums + swap(sums), "dp", axis=0), 0)
    feed_sum = jnp.concatenate(feed_sums, 1) if len(feed_sums) > 1 else feed_sums[0]
    feed_list = [feed_sum[:, wide * s : wide * (s + 1)] for s in range(subs)]

    return (
        place(core_place, mixed_held, sums_of["mixed"])[:, None],
        place(core_place, tokens_held, swap(tokens_other))[:, None],
        norm_sums[0],
        norm_sums[1],
        grad_qkv,
        grad_out,
        norm_sums[2],
        norm_sums[3],
        jnp.concatenate([r[:, :part] for r in feed_list], 1),
        jnp.concatenate([r[:, part:] for r in feed_list], 1).T,
    )


def solution(mesh):
    in_specs = (
        P(None, "dp", "mp", None),
        P(None, "dp", None),
        P(),
        P(),
        P("dp", None, "mp"),
        P("mp", "dp"),
        P(),
        P(),
        P("dp", "mp"),
        P("mp", "dp"),
        P(None, "dp", "mp", None),
    )
    out_specs = (
        P(None, "dp", "mp", None),
        P(None, "dp", "mp", None),
        P(),
        P(),
        P("dp", None, "mp"),
        P("mp", "dp"),
        P(),
        P(),
        P("dp", "mp"),
        P("mp", "dp"),
    )
    return jax.shard_map(
        on_device, mesh=mesh, in_specs=in_specs, out_specs=out_specs, check_vma=False
    )
```

```python
import functools
import math

import jax
import jax.numpy as jnp
from jax import lax
from jax.experimental import pallas as pl
from jax.experimental.pallas import tpu as pltpu
from jax.sharding import PartitionSpec as P

HD = 32
QB = 256
EPS = 1e-05
BF = jnp.bfloat16
F32 = jnp.float32
NEG = -1e30
SCALE = 1.0 / math.sqrt(HD)
LOG2E = math.log2(math.e)
C2 = SCALE * LOG2E
MIB = 1024 * 1024
SDS = jax.ShapeDtypeStruct


def nn(a, b):
    return lax.dot_general(a, b, (((1,), (0,)), ((), ())), preferred_element_type=F32)


def nt(a, b):
    return lax.dot_general(a, b, (((1,), (1,)), ((), ())), preferred_element_type=F32)


def params(mib):
    return pltpu.CompilerParams(vmem_limit_bytes=mib * MIB)


def in_hbm(values):
    return [pltpu.with_memory_space_constraint(v, pltpu.HBM) for v in values]


def in_vmem(values):
    return [pltpu.with_memory_space_constraint(v, pltpu.VMEM) for v in values]


def cost(gflop, mbytes):
    return pl.CostEstimate(flops=int(gflop * 1e9), bytes_accessed=int(mbytes * 1e6), transcendentals=0)


def any_spec():
    return pl.BlockSpec(memory_space=pl.ANY)


def smem_spec():
    return pl.BlockSpec(memory_space=pltpu.SMEM)


def vmem_spec():
    return pl.BlockSpec(memory_space=pltpu.VMEM)


def row_spec(width, rows=512):
    return pl.BlockSpec((rows, width), lambda r: (r, 0))


def column_spec(height, rows=512):
    return pl.BlockSpec((height, rows), lambda r: (0, r))


def whole_spec(shape):
    return pl.BlockSpec(shape, lambda r: tuple(0 for _ in shape))


MASKS = (0, 1, 2, 3)


class Rows:
    def __init__(self, dp_count, depth):
        self.dp_count = dp_count
        self.depth = depth
        self.split = (depth // dp_count) % 16 == 0 and dp_count == 16
        self.near = 4 if self.split else 1
        self.far = dp_count // 4 if self.split else 1
        self.block = depth // (self.near * self.far)
        self.shape = (self.far, self.near, self.block)


class Piece:
    def __init__(self, rows, kind, start=0, width=0, flip=0):
        self.rows = rows
        self.flip = flip
        self.kind = kind if rows.split else "whole"
        self.start = start
        self.count = 2 * len(MASKS) if self.kind == "slabs" else 2
        if self.kind == "stack":
            self.shape = (len(MASKS), rows.far, rows.block, width)
        else:
            self.shape = rows.shape + (width,)


def piece_copies(piece, me, refs, moves, sem, outward):
    copies = []
    each = piece.count // 2
    for half, column, width, view in moves:
        cols = pl.ds(piece.start + column, width)
        if piece.kind == "whole":
            pairs = [(refs[half].at[:, :, :, cols], view)]
        else:
            pairs = []
            order = lax.bitwise_xor(me[1], piece.flip ^ half)
            masks = (0, 2 - order, 1 + order, 3) if piece.kind == "stack" else MASKS
            for k, mask in enumerate(masks):
                ref = refs[half].at[k] if piece.kind == "stack" else refs[half * each + k]
                near = lax.bitwise_xor(lax.rem(me[0], 4), mask)
                pairs.append((ref.at[:, :, cols], view.at[:, near]))
        for outside, inside in pairs:
            if outward:
                copies.append(pltpu.make_async_copy(inside, outside, sem))
            else:
                copies.append(pltpu.make_async_copy(outside, inside, sem))
    return copies


def start_all(copies):
    for copy in copies:
        copy.start()


def wait_bytes(ref, sem):
    pltpu.make_async_copy(ref, ref, sem).wait()


def flat(value):
    return value.reshape(-1, value.shape[-1])


def head_row(h):
    return lax.broadcasted_iota(jnp.int32, (1, 128), 1) // HD == h


def fill_bias(bias, seg_col, seg_row):
    key = lax.broadcasted_iota(jnp.int32, (QB, QB), 0)
    query = lax.broadcasted_iota(jnp.int32, (QB, QB), 1)
    bias[0] = jnp.where(query >= key, 0.0, NEG)
    bias[1] = jnp.where((query >= key) & (seg_col[...] == seg_row[...]), 0.0, NEG)


def turned(doubles, start, r):
    coarse = pl.multiple_of(start // 16 * 16 + r * QB, 16)
    fine = start % 16
    row = lax.broadcasted_iota(jnp.int32, (QB, QB + 16), 0)
    col = lax.broadcasted_iota(jnp.int32, (QB, QB + 16), 1)
    pick = jnp.where(col - row == fine, 1.0, 0.0).astype(BF)
    total = None
    for double in doubles:
        part = nn(pick, double[pl.ds(coarse, QB + 16), :])
        total = part if total is None else total + part
    return total


def norm_parts(values):
    centered = values - jnp.mean(values, axis=-1, keepdims=True)
    spread = jnp.mean(centered * centered, axis=-1, keepdims=True)
    root = lax.rsqrt(spread + EPS)
    return centered * root, root


def fill_double(double, core, own, other, sem):
    here = own.shape[1]
    for k, half in enumerate((own, other)):
        pltpu.make_async_copy(half.at[core], double.at[pl.ds(k * here, here)], sem).start()
    wait_bytes(double.at[pl.ds(0, 2 * here)], sem)
    double[2 * here :, :] = double[: 2 * here, :]


def prepare_body(start, core, own, other, gain, offset, x_out, normed_out, normed_t_out, double, x, normed, normed_t, sems):
    fill_double(double, core[0], own, other, sems.at[3])

    def step(r, carry):
        at = pl.ds(pl.multiple_of(r * QB, QB), QB)
        value = turned([double], start[0], r)
        x[at, :] = value.astype(BF)
        hat, _ = norm_parts(value)
        low = (hat * gain[...] + offset[...]).astype(BF)
        normed[at, :] = low
        normed_t[:, at] = low.T
        return carry

    lax.fori_loop(0, x.shape[0] // QB, step, 0)
    copies = [
        pltpu.make_async_copy(normed, normed_out, sems.at[0]),
        pltpu.make_async_copy(x, x_out, sems.at[1]),
        pltpu.make_async_copy(normed_t, normed_t_out, sems.at[2]),
    ]
    start_all(copies)
    for copy in copies:
        copy.wait()


def prepare(start, core, own, other, gain, offset):
    _, here, depth = own.shape
    shape, shape_t = (2 * here, depth), (depth, 2 * here)
    shapes = [shape, shape, shape_t]
    return pl.pallas_call(
        prepare_body,
        in_specs=[smem_spec()] * 2 + [any_spec()] * 2 + [vmem_spec()] * 2,
        out_specs=[any_spec()] * 3,
        out_shape=[pltpu.HBM(s, BF) for s in shapes],
        scratch_shapes=[pltpu.VMEM((4 * here, depth), BF)]
        + [pltpu.VMEM(s, BF) for s in shapes]
        + [pltpu.SemaphoreType.DMA((4,))],
        compiler_params=params(20),
        cost_estimate=cost(4, 8),
        name="prepare",
    )(start, core, *in_hbm([own, other]), gain, offset)


def turn_body(start, core, own, other, cot_out, cot_t_out, double, cot, cot_t, sems):
    fill_double(double, core[0], own, other, sems.at[2])

    def step(r, carry):
        at = pl.ds(pl.multiple_of(r * QB, QB), QB)
        low = turned([double], start[0], r).astype(BF)
        cot[at, :] = low
        cot_t[:, at] = low.T
        return carry

    lax.fori_loop(0, cot.shape[0] // QB, step, 0)
    copies = [
        pltpu.make_async_copy(cot, cot_out, sems.at[0]),
        pltpu.make_async_copy(cot_t, cot_t_out, sems.at[1]),
    ]
    start_all(copies)
    for copy in copies:
        copy.wait()


def turn(start, core, own, other):
    _, here, depth = own.shape
    shapes = [(2 * here, depth), (depth, 2 * here)]
    return pl.pallas_call(
        turn_body,
        in_specs=[smem_spec()] * 2 + [any_spec()] * 2,
        out_specs=[any_spec()] * 2,
        out_shape=[pltpu.HBM(s, BF) for s in shapes],
        scratch_shapes=[pltpu.VMEM((4 * here, depth), BF)]
        + [pltpu.VMEM(s, BF) for s in shapes]
        + [pltpu.SemaphoreType.DMA((3,))],
        compiler_params=params(16),
        cost_estimate=cost(4, 8),
        name="turn",
    )(start, core, *in_hbm([own, other]))


def turn_back_body(start, core, values, held, other, double, own, sem):
    here = other.shape[0]
    double[: 2 * here, :] = values[...]
    double[2 * here :, :] = values[...]
    count = here // QB

    def step(r, carry):
        at = pl.ds(pl.multiple_of(r * QB, QB), QB)
        own[at, :] = turned([double], start[0], r).astype(BF)
        other[at, :] = turned([double], start[0], r + count).astype(BF)
        return carry

    lax.fori_loop(0, count, step, 0)
    copy = pltpu.make_async_copy(own, held.at[core[0]], sem)
    copy.start()
    copy.wait()


def place_body(core, other, held, out, sem):
    copy = pltpu.make_async_copy(other, out.at[1 - core[0]], sem)
    copy.start()
    copy.wait()


def place(core, held, other):
    return pl.pallas_call(
        place_body,
        in_specs=[smem_spec(), any_spec(), any_spec()],
        out_specs=any_spec(),
        out_shape=pltpu.HBM(held.shape, held.dtype),
        input_output_aliases={2: 0},
        scratch_shapes=[pltpu.SemaphoreType.DMA],
        compiler_params=params(4),
        cost_estimate=cost(0, 4),
        name="place",
    )(core, other, *in_hbm([held]))


def turn_back(start, core, values):
    length, depth = values.shape
    half = (length // 2, depth)
    return pl.pallas_call(
        turn_back_body,
        in_specs=[smem_spec()] * 2 + [vmem_spec()],
        out_specs=[any_spec(), vmem_spec()],
        out_shape=[pltpu.HBM((2,) + half, BF), SDS(half, BF)],
        scratch_shapes=[
            pltpu.VMEM((2 * length, depth), BF),
            pltpu.VMEM(half, BF),
            pltpu.SemaphoreType.DMA,
        ],
        compiler_params=params(16),
        cost_estimate=cost(2, 4),
        name="turn_back",
    )(start, core, values)


def arrange_body(widths, me, *refs):
    pieces, outs = refs[:4], refs[4:]
    far = me[0] // 4
    for m, piece in enumerate(pieces):
        begin = 0
        for out, width in zip(outs, widths):
            out[lax.bitwise_xor(far, m)] = piece[:, begin : begin + width]
            begin += width


def arrange(rows, me, pieces, widths):
    return pl.pallas_call(
        functools.partial(arrange_body, widths),
        in_specs=[smem_spec()] + [vmem_spec()] * 4,
        out_specs=[vmem_spec()] * len(widths),
        out_shape=[SDS((rows.far, rows.block, w), BF) for w in widths],
        compiler_params=params(8),
        cost_estimate=cost(1, 1),
        name="arrange",
    )(me, *pieces)


KEPT = (0, 256, 768, 1536)
KEPT_ROWS = (256, 512, 768, 256)
ORDER = (2, 1, 0, 3)


def project_attend_body(piece, me, normed_in, seg_col, seg_row, *refs):
    slabs = refs[: piece.count]
    proj_out, att, inverse, kept_out, weight, proj, normed, bias = refs[piece.count : piece.count + 8]
    keys_m, values_t, att_t, kept, sem, out_sem, kept_sem = refs[piece.count + 8 :]
    normed_copy = pltpu.make_async_copy(normed_in, normed, out_sem)
    normed_copy.start()
    moves = [(half, 0, 384, weight.at[:, :, :, pl.ds(384 * half, 384)]) for half in range(2)]
    start_all(piece_copies(piece, me, slabs, moves, sem, False))
    fill_bias(bias, seg_col, seg_row)
    values_t[...] = jnp.ones_like(values_t)
    normed_copy.wait()
    wait_bytes(weight, sem)

    for c in range(3):
        cols = slice(c * 256, c * 256 + 256)
        proj[:, cols] = nn(normed[...], flat(weight[:, :, :, cols])).astype(BF)
    proj_copy = pltpu.make_async_copy(proj, proj_out, out_sem)
    proj_copy.start()
    for half in range(2):
        flipped = proj[:, half * 384 + 256 : half * 384 + 384].T
        for h in range(4):
            values_t[half * 4 + h, 0:HD, :] = flipped[h * HD : (h + 1) * HD]

    units = [(h, i) for i in (2, 1, 0, 3) for h in range(4)]

    def step(half, carry):
        col = pl.multiple_of(half * 384, 128)
        for h in range(4):
            keys_m[h] = jnp.where(head_row(h), proj[:, pl.ds(col + 128, 128)], 0)

        def score(h, i):
            first = 768 if i == 3 else 0
            scores = nt(keys_m[h, first : (i + 1) * QB, :], proj[i * QB : (i + 1) * QB, pl.ds(col, 128)])
            edge = scores[-QB:] + bias[1 if i == 3 else 0]
            return jnp.concatenate([scores[:-QB], edge], 0) if scores.shape[0] > QB else edge

        ahead = score(*units[0])
        for k, (h, i) in enumerate(units):
            scores = ahead
            if k + 1 < len(units):
                ahead = score(*units[k + 1])
            first = 768 if i == 3 else 0
            last = (i + 1) * QB
            at = slice(i * QB, last)
            peak = jnp.max(scores, axis=0, keepdims=True) * C2
            probs = jnp.exp2(scores * C2 - peak).astype(BF)
            kept[half * 4 + h, KEPT[i] : KEPT[i] + last - first, :] = probs
            summed = nn(values_t[half * 4 + h, :, first:last], probs)
            share = 1.0 / summed[HD : HD + 1]
            att_t[pl.ds(pl.multiple_of(half * 128 + h * HD, HD), HD), at] = summed[:HD] * share
            inverse[pl.ds(half * 4 + h, 1), at] = share
            if h == 3:
                part = (pl.ds(half * 4, 4), pl.ds(KEPT[i], last - first))
                pltpu.make_async_copy(kept.at[part], kept_out.at[part], kept_sem).start()
        return carry

    lax.fori_loop(0, 2, step, 0)
    for half in range(2):
        cols = slice(half * 128, half * 128 + 128)
        att[:, cols] = att_t[cols, :].T.astype(BF)
    proj_copy.wait()
    wait_bytes(kept, kept_sem)


def project_attend(piece, me, normed, seg_col, seg_row, slabs):
    length, depth = normed.shape
    rows = piece.rows
    return pl.pallas_call(
        functools.partial(project_attend_body, piece),
        in_specs=[smem_spec(), any_spec()] + [vmem_spec()] * 2 + [any_spec()] * len(slabs),
        out_specs=[any_spec()] + [vmem_spec()] * 2 + [any_spec()],
        out_shape=[
            pltpu.HBM((length, 768), BF),
            pltpu.HBM((length, 256), BF),
            pltpu.HBM((8, length), F32),
            pltpu.HBM((8, 1792, QB), BF),
        ],
        scratch_shapes=[
            pltpu.VMEM(rows.shape + (768,), BF),
            pltpu.VMEM((length, 768), BF),
            pltpu.VMEM((length, depth), BF),
            pltpu.VMEM((2, QB, QB), F32),
            pltpu.VMEM((4, length, 128), BF),
            pltpu.VMEM((8, HD + 16, length), BF),
            pltpu.VMEM((256, length), F32),
            pltpu.VMEM((8, 1792, QB), BF),
            pltpu.SemaphoreType.DMA,
            pltpu.SemaphoreType.DMA,
            pltpu.SemaphoreType.DMA,
        ],
        compiler_params=params(32),
        cost_estimate=cost(8, 8),
        name="project_attend",
    )(me, *in_hbm([normed]), seg_col, seg_row, *in_hbm(slabs))


def join_heads(attended):
    return jnp.concatenate([a[:, :128] for a in attended] + [a[:, 128:] for a in attended], 1)


def out_norm_body(piece, groups, me, tokens, gain, offset, *refs):
    attended = refs[:groups]
    slabs = refs[groups : groups + piece.count]
    middle, normed, normed_t, weight, sem = refs[groups + piece.count :]
    width = weight.shape[3] // 2

    @pl.when(pl.program_id(0) == 0)
    def _():
        moves = [(half, 0, width, weight.at[:, :, :, pl.ds(width * half, width)]) for half in range(2)]
        start_all(piece_copies(piece, me, slabs, moves, sem, False))
        wait_bytes(weight, sem)

    value = tokens[...].astype(F32) + nt(join_heads([a[...] for a in attended]), flat(weight[...]))
    middle[...] = value
    hat, _ = norm_parts(value)
    low = (hat * gain[...] + offset[...]).astype(BF)
    normed[...] = low
    normed_t[...] = low.T


def out_norm(piece, me, tokens, gain, offset, attended, slabs):
    length, depth = tokens.shape
    return pl.pallas_call(
        functools.partial(out_norm_body, piece, len(attended)),
        grid=(length // 512,),
        in_specs=[smem_spec(), row_spec(depth), whole_spec((1, depth)), whole_spec((1, depth))]
        + [row_spec(256)] * len(attended)
        + [any_spec()] * len(slabs),
        out_specs=[row_spec(depth)] * 2 + [column_spec(depth)],
        out_shape=[
            pltpu.HBM((length, depth), F32),
            pltpu.VMEM((length, depth), BF),
            pltpu.VMEM((depth, length), BF),
        ],
        scratch_shapes=[pltpu.VMEM(piece.rows.shape + (depth,), BF), pltpu.SemaphoreType.DMA],
        compiler_params=params(28),
        cost_estimate=cost(3, 8),
        name="out_norm",
    )(me, *in_hbm([tokens]), gain, offset, *in_hbm(attended), *in_hbm(slabs))


def gelu_parts(values):
    size = jnp.abs(values)
    density = jnp.exp2(values * values * (-0.5 * LOG2E) + math.log2(1.0 / math.sqrt(2 * math.pi)))
    below = 1.0 + 0.2316419 * size
    t = pl.reciprocal(below, approx=True)
    t = t * (2.0 - below * t)
    poly = t * (
        0.319381530
        + t * (-0.356563782 + t * (1.781477937 + t * (-1.821255978 + t * 1.330274429)))
    )
    tail = density * poly
    below = jnp.where(values >= 0, 1.0 - tail, tail)
    return values * below, below + values * density


def norm_pull(grad, hat, root, gain):
    scaled = grad * gain
    first = jnp.mean(scaled, axis=-1, keepdims=True)
    second = jnp.mean(scaled * hat, axis=-1, keepdims=True)
    return root * (scaled - first - hat * second)


def feed_forward_body(
    piece, out_piece, first, last_piece, groups, aliased, me, normed, normed_t, cot, cot_t, *refs
):
    refs = list(refs)
    final = last_piece is not None
    held = [] if first else [refs.pop(0), refs.pop(0)]
    if final:
        middle, gain = refs.pop(0), refs.pop(0)
        out_slabs, refs = refs[: last_piece.count], refs[last_piece.count :]
    slabs, refs = refs[: piece.count], refs[piece.count + aliased :]
    outs, refs = refs[:2], refs[2:]
    mixed = refs.pop(0)
    if final:
        grad_middle_out, branch_t, sums = refs[:3]
        grad_att, refs = refs[3 : 3 + groups], refs[3 + groups :]
    else:
        grad_in = refs.pop(0)
    weight, staged, act, grad_hidden, mixed_acc, grad_acc, sems = refs[:7]
    if final:
        mixed_low, middle_here, out_weight, grad_middle = refs[7:]
    length, depth = normed.shape
    moves = []
    for half in range(2):
        for which in range(2):
            at = pl.ds(which * 768 + half * 384, 384)
            moves.append((half, which * 384, 384, at))
    into = [(h, c, w, weight.at[:, :, :, at]) for h, c, w, at in moves]
    outof = [(h, c, w, staged.at[:, :, :, at]) for h, c, w, at in moves]
    start_all(piece_copies(piece, me, slabs, into, sems.at[0], False))
    held_copies = []
    if not first:
        held_copies.append(pltpu.make_async_copy(held[0], mixed_acc, sems.at[1]))
        held_copies.append(pltpu.make_async_copy(held[1], grad_acc, sems.at[2]))
    if final:
        held_copies.append(pltpu.make_async_copy(middle, middle_here, sems.at[4]))
    start_all(held_copies)
    if final:
        width = depth // 2
        views = [
            (half, 0, width, out_weight.at[:, :, :, pl.ds(width * half, width)]) for half in range(2)
        ]
        start_all(piece_copies(last_piece, me, out_slabs, views, sems.at[5], False))
    wait_bytes(weight, sems.at[0])
    chunks = [slice(c * 256, c * 256 + 256) for c in range(3)]

    def products(c):
        hidden = nn(normed[...], flat(weight[:, :, :, c * 256 : c * 256 + 256]))
        return hidden, nn(cot[...], flat(weight[:, :, :, 768 + c * 256 : 1024 + c * 256]))

    ahead = products(0)
    for c in range(3):
        hidden, grad_act = ahead
        if c < 2:
            ahead = products(c + 1)
        value, slope = gelu_parts(hidden)
        act[:, chunks[c]] = value.astype(BF)
        grad_hidden[:, chunks[c]] = (grad_act * slope).astype(BF)
    for copy in held_copies:
        copy.wait()
    for cols in chunks:
        mixed_part = nt(act[...], flat(weight[:, :, :, 768:1536])[cols])
        grad_part = nt(grad_hidden[...], flat(weight[:, :, :, 0:768])[cols])
        if not first:
            mixed_part = mixed_part + mixed_acc[:, cols]
            grad_part = grad_part + grad_acc[:, cols]
        if final:
            mixed_low[:, cols] = (middle_here[:, cols] + mixed_part).astype(BF)
        else:
            mixed_acc[:, cols] = mixed_part
        grad_acc[:, cols] = grad_part
    if final:
        out_copies = [pltpu.make_async_copy(mixed_low, mixed, sems.at[1])]
        start_all(out_copies)
        wait_bytes(out_weight, sems.at[5])
        sums[...] = jnp.zeros_like(sums)

        def back_step(r, carry):
            at = pl.ds(pl.multiple_of(r * 512, 512), 512)
            hat, root = norm_parts(middle_here[at, :])
            grad = grad_acc[at, :]
            value = cot[at, :].astype(F32) + norm_pull(grad, hat, root, gain[...])
            grad_middle[at, :] = value
            low = value.astype(BF)
            branch_t[:, at] = low.T
            sums[0:1, :] += jnp.sum(grad * hat, axis=0, keepdims=True)
            sums[1:2, :] += jnp.sum(grad, axis=0, keepdims=True)
            back = nn(low, flat(out_weight[...])).astype(BF)
            for g in range(groups):
                grad_att[g][at, 0:128] = back[:, g * 128 : g * 128 + 128]
                grad_att[g][at, 128:256] = back[:, width + g * 128 : width + g * 128 + 128]
            return carry

        lax.fori_loop(0, length // 512, back_step, 0)
        out_copies.append(pltpu.make_async_copy(grad_middle, grad_middle_out, sems.at[2]))
        out_copies[-1].start()
    else:
        out_copies = [
            pltpu.make_async_copy(mixed_acc, mixed, sems.at[1]),
            pltpu.make_async_copy(grad_acc, grad_in, sems.at[2]),
        ]
        start_all(out_copies)
    for c in range(3):
        cols = slice(c * 256, c * 256 + 256)
        up = nn(normed_t[...], grad_hidden[:, cols]).astype(BF)
        staged[:, :, :, cols] = up.reshape(staged.shape[:3] + (256,))
        down = nn(cot_t[...], act[:, cols]).astype(BF)
        staged[:, :, :, 768 + c * 256 : 1024 + c * 256] = down.reshape(staged.shape[:3] + (256,))
    start_all(piece_copies(out_piece, me, outs, outof, sems.at[3], True))
    for copy in out_copies:
        copy.wait()
    wait_bytes(staged, sems.at[3])


def feed_forward(
    piece, out_piece, me, normed, normed_t, cot, cot_t, held, slabs, onto, last=None
):
    length, depth = normed.shape
    rows = piece.rows
    first, final = held is None, last is not None
    ins = [me] + in_vmem([normed, normed_t, cot, cot_t]) + ([] if first else in_hbm(held))
    specs = [smem_spec()] + [vmem_spec()] * 4 + [any_spec()] * (0 if first else 2)
    scratch = [
        pltpu.VMEM(rows.shape + (1536,), BF),
        pltpu.VMEM(rows.shape + (1536,), BF),
        pltpu.VMEM((length, 768), BF),
        pltpu.VMEM((length, 768), BF),
        pltpu.VMEM((length, depth), F32),
        pltpu.VMEM((length, depth), F32),
        pltpu.SemaphoreType.DMA((6,)),
    ]
    last_piece, groups = None, 0
    outs = [SDS(out_piece.shape, BF)] * 2 + [pltpu.HBM((length, depth), BF if final else F32)]
    out_specs = [any_spec()] * 3
    if final:
        last_piece, last_slabs, middle, gain, groups = last
        ins += in_hbm([middle]) + [gain] + in_hbm(last_slabs)
        specs += [any_spec(), vmem_spec()] + [any_spec()] * len(last_slabs)
        scratch += [
            pltpu.VMEM((length, depth), BF),
            pltpu.VMEM((length, depth), F32),
            pltpu.VMEM(rows.shape + (depth,), BF),
            pltpu.VMEM((length, depth), F32),
        ]
        outs += [pltpu.HBM((length, depth), F32), pltpu.VMEM((depth, length), BF), SDS((8, depth), F32)]
        outs += [pltpu.HBM((length, 256), BF)] * groups
        out_specs += [any_spec()] + [vmem_spec()] * (2 + groups)
    else:
        outs.append(pltpu.HBM((length, depth), F32))
        out_specs.append(any_spec())
    got = pl.pallas_call(
        functools.partial(
            feed_forward_body, piece, out_piece, first, last_piece, groups, len(onto)
        ),
        in_specs=specs + [any_spec()] * (piece.count + len(onto)),
        out_specs=out_specs,
        out_shape=outs,
        input_output_aliases={len(ins) + piece.count + k: k for k in range(len(onto))},
        scratch_shapes=scratch,
        compiler_params=params(48 if final else 32),
        cost_estimate=cost(14 if final else 11, 20),
        name="feed_forward",
    )(*ins, *in_hbm(slabs), *onto)
    return got[:2], got[2:]


def attend_back_body(piece, out_piece, extra, aliased, final, me, normed_t_in, proj, att, grad_att, inverse, kept_in, *refs):
    refs = list(refs)
    slabs, refs = refs[: piece.count], refs[piece.count :]
    if extra:
        branch_t = refs.pop(0)
        attended, refs = refs[:extra], refs[extra:]
    else:
        held = refs.pop(0)
    if final:
        tokens_in = refs.pop(0)
    refs = refs[aliased:]
    grad_normed, outs, refs = refs[0], refs[1:3], refs[3:]
    if final:
        sums = refs.pop(0)
    grad_proj, key_sum, value_sum = refs[:3]
    refs = refs[3:]
    kept, delta, keys_t, query_t, query_m, grad_m, staged, normed_t, total, weight, sems = refs[:11]
    for half in range(2):
        for i in ORDER:
            part = (pl.ds(half * 4, 4), pl.ds(KEPT[i], KEPT_ROWS[i]))
            sem = sems.at[5 + 4 * half + i]
            pltpu.make_async_copy(kept_in.at[part], kept.at[part], sem).start()
    copies = [pltpu.make_async_copy(normed_t_in, normed_t, sems.at[1])]
    if not extra:
        copies.append(pltpu.make_async_copy(held, total, sems.at[2]))
    if final:
        copies.append(pltpu.make_async_copy(tokens_in, refs[11], sems.at[3]))
    moves = [(half, 0, 384, weight.at[:, :, :, pl.ds(384 * half, 384)]) for half in range(2)]
    start_all(copies + piece_copies(piece, me, slabs, moves, sems.at[4], False))
    length = proj.shape[0]
    if extra:
        joined = join_heads([a[...] for a in attended])
        out_grad = nn(branch_t[...], joined).astype(BF)
        staged[:, :, :, 768:] = out_grad.reshape(staged.shape[:3] + (768,))
    for half in range(2):
        cols = slice(half * 128, half * 128 + 128)
        product = (grad_att[:, cols].astype(F32) * att[:, cols].astype(F32)).T
        for h in range(4):
            stat = slice(half * 4 + h, half * 4 + h + 1)
            total_here = jnp.sum(product[h * HD : (h + 1) * HD], axis=0, keepdims=True)
            delta[stat, :] = total_here * inverse[stat, :]
        keys_t[cols, :] = proj[:, half * 384 + 128 : half * 384 + 256].T

    def step(half, carry):
        col = pl.multiple_of(half * 384, 128)
        out = pl.multiple_of(half * 128, 128)
        share = jnp.concatenate(
            [jnp.broadcast_to(inverse[pl.ds(half * 4 + h, 1), :], (HD, length)) for h in range(4)], 0
        ).T
        grads = (grad_att[:, pl.ds(out, 128)].astype(F32) * share).astype(BF)
        for h in range(4):
            mine = head_row(h)
            query_m[h] = jnp.where(mine, proj[:, pl.ds(col, 128)], 0)
            grad_m[h] = jnp.where(mine, grads, 0)
        key_sum[...] = jnp.zeros_like(key_sum)
        value_sum[...] = jnp.zeros_like(value_sum)
        for i in (2, 1, 0, 3):
            first = 768 if i == 3 else 0
            last = (i + 1) * QB
            here = slice(first, last)
            there = slice(i * QB, last)
            values = proj[here, pl.ds(col + 256, 128)]
            rows_here = slice(KEPT[i], KEPT[i] + last - first)
            wait_bytes(
                kept.at[pl.ds(half * 4, 4), pl.ds(KEPT[i], KEPT_ROWS[i])], sems.at[5 + 4 * half + i]
            )
            all_probs, all_grads = [], []
            ahead = nt(values, grad_m[0, there, :])
            for h in range(4):
                grad_probs = ahead
                if h < 3:
                    ahead = nt(values, grad_m[h + 1, there, :])
                stat = pl.ds(half * 4 + h, 1)
                lanes = pl.ds(pl.multiple_of(half * 128 + h * HD, HD), HD)
                probs = kept[half * 4 + h, rows_here, :]
                grad_scores = (probs.astype(F32) * (grad_probs - delta[stat, there])).astype(BF)
                all_probs.append(probs)
                all_grads.append(grad_scores)
                query_t[lanes, there] = nn(keys_t[lanes, here], grad_scores)
            stacked = jnp.concatenate([grad_m[h, there, :] for h in range(4)], 0)
            value_sum[here, :] += nn(jnp.concatenate(all_probs, 1), stacked)
            stacked = jnp.concatenate([query_m[h, there, :] for h in range(4)], 0)
            key_sum[here, :] += nn(jnp.concatenate(all_grads, 1), stacked)
        grad_proj[:, pl.ds(col + 128, 128)] = (key_sum[...] * SCALE).astype(BF)
        grad_proj[:, pl.ds(col + 256, 128)] = value_sum[...].astype(BF)
        return carry

    lax.fori_loop(0, 2, step, 0)
    for half in range(2):
        grad_proj[:, half * 384 : half * 384 + 128] = (
            query_t[half * 128 : half * 128 + 128, :].T * SCALE
        ).astype(BF)
    for copy in copies:
        copy.wait()
    wait_bytes(weight, sems.at[4])
    for c in range(3):
        cols = slice(c * 256, c * 256 + 256)
        part = nn(normed_t[...], grad_proj[:, cols]).astype(BF)
        staged[:, :, :, cols] = part.reshape(staged.shape[:3] + (256,))
    moves = [(half, 0, 384, staged.at[:, :, :, pl.ds(384 * half, 384)]) for half in range(2)]
    if extra:
        moves += [
            (half, -384, 384, staged.at[:, :, :, pl.ds(768 + 384 * half, 384)]) for half in range(2)
        ]
    start_all(piece_copies(out_piece, me, outs, moves, sems.at[0], True))
    if final:
        sums[...] = jnp.zeros_like(sums)

    total_copies = []
    for c in range(3):
        cols = slice(c * 256, c * 256 + 256)
        value = nt(grad_proj[...], flat(weight[...])[cols])
        if not extra:
            value = value + total[:, cols]
        total[:, cols] = value
        total_copies.append(
            pltpu.make_async_copy(
                total.at[:, pl.ds(c * 256, 256)], grad_normed.at[:, pl.ds(c * 256, 256)], sems.at[2]
            )
        )
        total_copies[-1].start()
    if final:

        def sum_step(r, carry):
            at = pl.ds(pl.multiple_of(r * QB, QB), QB)
            value = total[at, :]
            hat, _ = norm_parts(refs[11][at, :].astype(F32))
            sums[0:1, :] += jnp.sum(value * hat, axis=0, keepdims=True)
            sums[1:2, :] += jnp.sum(value, axis=0, keepdims=True)
            return carry

        lax.fori_loop(0, length // QB, sum_step, 0)
    wait_bytes(staged, sems.at[0])
    wait_bytes(total, sems.at[2])


def attend_back(
    piece,
    out_piece,
    me,
    normed_t,
    proj,
    att,
    grad_att,
    inverse,
    kept,
    slabs,
    branch_t,
    attended,
    held,
    tokens,
    onto,
):
    depth, length = normed_t.shape
    extra = len(attended)
    final = tokens is not None
    columns = 1536 if extra else 768
    ins = [me] + in_hbm([normed_t, proj, att, grad_att, inverse, kept]) + in_hbm(slabs)
    specs = [smem_spec(), any_spec()] + [vmem_spec()] * 4 + [any_spec()] * (1 + len(slabs))
    if extra:
        ins += in_vmem([branch_t]) + in_hbm(attended)
        specs += [vmem_spec()] * (1 + extra)
    else:
        ins += in_hbm([held])
        specs += [any_spec()]
    if final:
        ins += in_hbm([tokens])
        specs += [any_spec()]
    outs = [pltpu.HBM((length, depth), F32)] + [SDS(out_piece.shape, BF)] * 2
    scratch = [
        pltpu.VMEM((8, 1792, QB), BF),
        pltpu.VMEM((8, length), F32),
        pltpu.VMEM((256, length), BF),
        pltpu.VMEM((256, length), F32),
        pltpu.VMEM((4, length, 128), BF),
        pltpu.VMEM((4, length, 128), BF),
        pltpu.VMEM(out_piece.rows.shape + (columns,), BF),
        pltpu.VMEM((depth, length), BF),
        pltpu.VMEM((length, depth), F32),
        pltpu.VMEM(piece.rows.shape + (768,), BF),
        pltpu.SemaphoreType.DMA((13,)),
    ]
    if final:
        outs.append(SDS((8, depth), F32))
        scratch.append(pltpu.VMEM((length, depth), BF))
    got = pl.pallas_call(
        functools.partial(attend_back_body, piece, out_piece, extra, len(onto), final),
        in_specs=specs + [any_spec()] * len(onto),
        out_specs=[any_spec()] * 3 + ([vmem_spec()] if final else []),
        out_shape=outs,
        input_output_aliases={len(ins) + k: 1 + k for k in range(len(onto))},
        scratch_shapes=[
            pltpu.VMEM((length, 768), BF),
            pltpu.VMEM((length, 128), F32),
            pltpu.VMEM((length, 128), F32),
        ]
        + scratch,
        compiler_params=params(40),
        cost_estimate=cost(12, 8),
        name="attend_back",
    )(*ins, *onto)
    return got[0], got[1:3], got[3] if final else None


def norm_back_body(
    start, core, tokens, grad_normed, grad_middle, gain, held, other, high, low, own, sem
):
    length = high.shape[0] // 2
    r = pl.program_id(0)
    hat, root = norm_parts(tokens[...].astype(F32))
    value = grad_middle[...] + norm_pull(grad_normed[...], hat, root, gain[...])
    top = value.astype(BF)
    rest = (value - top.astype(F32)).astype(BF)
    for base in (0, length):
        at = pl.ds(pl.multiple_of(base + r * QB, QB), QB)
        high[at, :] = top
        low[at, :] = rest

    @pl.when(r == pl.num_programs(0) - 1)
    def _():
        count = own.shape[0] // QB
        for k in range(count):
            own[k * QB : k * QB + QB, :] = turned([high, low], start[0], k)
        copy = pltpu.make_async_copy(own, held.at[core[0]], sem)
        copy.start()
        for k in range(count):
            other[k * QB : k * QB + QB, :] = turned([high, low], start[0], k + count)
        copy.wait()


def norm_back(start, core, tokens, grad_normed, grad_middle, gain):
    length, depth = tokens.shape
    half = (length // 2, depth)
    return pl.pallas_call(
        norm_back_body,
        grid=(length // QB,),
        in_specs=[smem_spec()] * 2 + [row_spec(depth, QB)] * 3 + [whole_spec((1, depth))],
        out_specs=[any_spec(), whole_spec(half)],
        out_shape=[pltpu.HBM((2,) + half, F32), SDS(half, F32)],
        scratch_shapes=[
            pltpu.VMEM((2 * length, depth), BF),
            pltpu.VMEM((2 * length, depth), BF),
            pltpu.VMEM(half, F32),
            pltpu.SemaphoreType.DMA,
        ],
        compiler_params=params(24),
        cost_estimate=cost(4, 16),
        name="norm_back",
    )(start, core, *in_hbm([tokens, grad_normed, grad_middle]), gain)


def split_far_body(counts, me, *refs):
    keep, send = refs[-2:]
    far = me[0] // 4
    begin = 0
    for count in counts:
        pieces, refs = refs[:count], refs[count:]
        cols = pl.ds(begin, pieces[0].shape[-1])
        begin += pieces[0].shape[-1]
        for k, out in enumerate((keep, send)):
            for slot in range(2):
                at = lax.bitwise_xor(far, k + 2 * slot)
                total = pieces[0][at].astype(F32)
                for piece in pieces[1:]:
                    total = total + piece[at].astype(F32)
                out[slot, :, cols] = total.astype(BF)


def split_far(me, groups):
    width, specs = 0, []
    for pieces in groups:
        far, block, columns = pieces[0].shape[-3:]
        width += columns
        for piece in pieces:
            if piece.ndim == 4:
                specs.append(pl.BlockSpec((None, far, block, columns), lambda i: (0, 0, 0, 0)))
            else:
                specs.append(whole_spec(piece.shape))
    return pl.pallas_call(
        functools.partial(split_far_body, [len(pieces) for pieces in groups]),
        grid=(1,),
        in_specs=[smem_spec()] + specs,
        out_specs=[whole_spec((2, block, width))] * 2,
        out_shape=[SDS((2, block, width), BF)] * 2,
        compiler_params=params(16),
        cost_estimate=cost(1, 2),
        name="split_far",
    )(me, *[piece for pieces in groups for piece in pieces])


def put_sums(ref, base, total):
    high = total.astype(BF)
    ref[base : base + 4, :] = high
    ref[base + 4 : base + 8, :] = (total - high.astype(F32)).astype(BF)
    ref[base + 8 : base + 16, :] = jnp.zeros((8, total.shape[1]), BF)


def get_sums(ref, base):
    return ref[base : base + 4, :].astype(F32) + ref[base + 4 : base + 8, :].astype(F32)


def last_join_body(own, other, sums, sums_away, keep, send):
    total = sums[...] + sums_away[...]
    rows = keep.shape[0] // 2
    for k in range(4):
        value = (own[k].astype(F32) + other[k].astype(F32)).astype(BF).reshape(rows, -1)
        (keep if k < 2 else send)[(k % 2) * rows : (k % 2 + 1) * rows, :] = value
    put_sums(send, 2 * rows, total)


def last_half_body(keep, send, near, rest, send_next):
    rows = rest.shape[0]
    value = keep[:rows, :].astype(F32) + near[:rows, :].astype(F32)
    rest[...] = value.astype(BF)
    value = keep[rows:, :].astype(F32) + near[rows : 2 * rows, :].astype(F32)
    send_next[:rows, :] = value.astype(BF)
    send_next[rows : rows + 16, :] = send[2 * rows :, :]
    send_next[rows + 16 :, :] = near[2 * rows :, :]


def last_split_body(flip, me, rest, send, away, keep, out_send):
    far = me[0] // 4
    rows = rest.shape[0]
    block = rows // 4
    for k, out in enumerate((keep, out_send)):
        for slot in range(2):
            at = pl.ds(pl.multiple_of(lax.bitwise_xor(far, k + 2 * slot) * block, 16), block)
            total = rest[at, :].astype(F32) + away[at, :].astype(F32)
            out[slot * block : (slot + 1) * block, :] = total.astype(BF)
    first, second = get_sums(send, rows + 16), get_sums(away, rows)
    swapped = lax.bitwise_xor(me[1], flip) == 1
    one, two = jnp.where(swapped, second, first), jnp.where(swapped, first, second)
    total = (get_sums(send, rows) + one) + (two + get_sums(away, rows + 16))
    put_sums(keep, 2 * block, total)
    put_sums(out_send, 2 * block, total)


def last_middle_body(keep, near, rest, send):
    block = (keep.shape[0] - 16) // 2
    value = keep[:block, :].astype(F32) + near[:block, :].astype(F32)
    rest[:block, :] = value.astype(BF)
    value = keep[block : 2 * block, :].astype(F32) + near[block : 2 * block, :].astype(F32)
    send[:block, :] = value.astype(BF)
    total = get_sums(keep, 2 * block) + get_sums(near, 2 * block)
    put_sums(rest, block, total)
    put_sums(send, block, total)


def last_sum_body(rest, away, first, grad_qkv, sums):
    block = rest.shape[0] - 16
    value = rest[:block, :].astype(F32) + away[:block, :].astype(F32)
    parts = [first[:, 384:], value[:, :384], value[:, 384:]]
    for which in range(3):
        cols = slice(which * 128, which * 128 + 128)
        grad_qkv[which] = jnp.concatenate([part[:, cols] for part in parts], 1)
    sums[...] = get_sums(rest, block) + get_sums(away, block)


def pack_body(part, out, up, down, packed):
    width = out.shape[1]
    packed[:, :width] = out[...]
    for s in range(up.shape[1] // part):
        cols = slice(s * part, (s + 1) * part)
        packed[:, width + 2 * s * part : width + (2 * s + 1) * part] = up[:, cols]
        packed[:, width + (2 * s + 1) * part : width + (2 * s + 2) * part] = down[:, cols]


def small_call(body, name, outs, scalars, values):
    return pl.pallas_call(
        body,
        in_specs=[smem_spec()] * len(scalars) + [vmem_spec()] * len(values),
        out_specs=[vmem_spec()] * len(outs),
        out_shape=outs,
        compiler_params=params(16),
        cost_estimate=cost(1, 3),
        name=name,
    )(*scalars, *values)


def swap(value):
    return lax.ppermute(value, "mp", [(0, 1), (1, 0)])


def tie(*values):
    return lax.optimization_barrier(values)


def hop(value, mask, count):
    return lax.ppermute(value, "dp", [(i, i ^ mask) for i in range(count)])


def hops(value, masks, count):
    return [(value, functools.partial(hop, mask=m, count=count)) for m in masks]


def hop_apart(value, masks, count):
    pairs = [(2 * i + c, 2 * (i ^ masks[c]) + c) for i in range(count) for c in range(2)]
    return lax.ppermute(value, ("dp", "mp"), pairs)


def far_hops(rows, values):
    return [
        (v, functools.partial(hop, mask=rows.near * m, count=rows.dp_count))
        for m, v in zip(range(1, rows.far), values)
    ]


def swaps(values):
    return [(v, swap) for v in values]


def send_all(requests):
    return [send(value) for value, send in requests]


def low_sum(values):
    total = values[0].astype(F32)
    for value in values[1:]:
        total = total + value.astype(F32)
    return total


class Flow:
    def __init__(self, me):
        self.me = me
        self.active = []

    def add(self, transfer, name, results, seeds=()):
        self.active.append([transfer, list(seeds), name, results])

    def step(self, *pivots, gate=None):
        values = [v for item in self.active for v in item[1]]
        tied = list(tie(self.me, *pivots, *values))
        self.me = tied.pop(0)
        pivots, tied = tied[: len(pivots)], tied[len(pivots) :]
        going, self.active, requests = self.active, [], []
        for item in going:
            transfer, values, name, results = item
            got, tied = tied[: len(values)], tied[len(values) :]
            try:
                if callable(transfer):
                    item[0] = transfer(*got)
                    asked = next(item[0])
                else:
                    asked = transfer.send(got)
                self.active.append(item)
                requests.append(asked)
            except StopIteration as stop:
                results[name] = stop.value
        gates = gate() if gate else []
        operands = [operand for asked in requests for operand, _ in asked]
        tied = list(tie(self.me, *gates, *operands))
        self.me = tied[0]
        tied = tied[1 + len(gates) :]
        for item, asked in zip(self.active, requests):
            item[1] = [send(operand) for (_, send), operand in zip(asked, tied)]
            tied = tied[len(asked) :]
        return pivots


def add_low(a, b):
    return (a.astype(F32) + b.astype(F32)).astype(BF)


def on_device(
    tokens, segment, ln1_gain, ln1_bias, w_qkv, w_out, ln2_gain, ln2_bias, w_up, w_down, cotangent
):
    dp_count = lax.axis_size("dp")
    core = lax.axis_index("mp")
    me = jnp.stack([lax.axis_index("dp"), core]).astype(jnp.int32)
    here, depth = tokens.shape[2], tokens.shape[3]
    length = 2 * here
    rows = Rows(dp_count, depth)

    groups = w_qkv.shape[2] // 128
    part = 384
    subs = w_up.shape[1] // part
    cut = subs // 2
    qkv = [w_qkv[:, :, g * 128 : (g + 1) * 128].reshape(-1, part) for g in range(groups)]
    shards = {"q": jnp.concatenate(qkv, 1)}

    def pack(out, up, down):
        return small_call(
            functools.partial(pack_body, part),
            "pack",
            [SDS((up.shape[0], out.shape[0] + 2 * up.shape[1]), BF)],
            [],
            [out.T, up, down.T],
        )[0]

    seg = lax.dynamic_index_in_dim(segment[:, 0], core, 0, keepdims=False)
    run = length * 3 // 4
    begin = jnp.argmax(seg[: length - run + 1] == seg[run - 1 :]).astype(jnp.int32)
    start = ((begin - here * core) % length).reshape(1)
    back = (length - start) % length
    seg_tail = lax.dynamic_slice_in_dim(jnp.concatenate([seg, seg]), begin + run, length - run)
    seg_col = seg_tail.reshape(-1, 1)
    seg_row = seg_tail.reshape(1, -1)
    gain1, bias1, gain2, bias2 = (
        v.reshape(1, -1) for v in (ln1_gain, ln1_bias, ln2_gain, ln2_bias)
    )

    flow = Flow(me)
    core_place = core.astype(jnp.int32).reshape(1)
    token_halves = [tokens[:, 0], swap(tokens[:, 0])]
    cot_halves = [cotangent[:, 0], swap(cotangent[:, 0])]
    wide = 2 * part
    qkv_pieces = [Piece(rows, "slabs")] + [Piece(rows, "slabs", part * g) for g in range(groups - 1)]
    out_piece = Piece(rows, "slabs")
    feed_pieces = [Piece(rows, "slabs", part + wide * s) for s in range(cut)]
    feed_pieces += [Piece(rows, "slabs", wide * s) for s in range(subs - cut)]
    feed_outs = [
        Piece(rows, "stack", 0, wide, s // cut) for s in range(subs)
    ]
    qkv_outs = [Piece(rows, "stack", part, wide, 0)]
    qkv_outs += [Piece(rows, "stack", part * g, part * (groups - 1), 1) for g in range(groups - 1)]
    far = lax.axis_index("dp") // rows.near

    def gather_whole(shard):
        return lax.all_gather(shard, "dp", axis=0, tiled=True).reshape(rows.shape + (-1,))

    def fetch_near(near):
        got = yield hops(near, MASKS[1:], dp_count)
        own = [near] + got
        return own + [swap(x) for x in own]

    def via(mask):
        return functools.partial(hop, mask=mask, count=dp_count)

    def fetch_wide(shard, away):
        near, both_ways = yield [(shard, via(4)), (away, via(4))]
        (a0,) = arrange(rows, flow.me, [shard, near, away, both_ways], [shard.shape[1]])
        a1, a2, b0, away = yield [(a0, via(1)), (a0, via(2))] + swaps([a0]) + [(shard_c, via(8))]
        a3, b1, b2, near, both_ways = yield (
            [(a1, via(2))] + swaps([a1, a2]) + [(shard_c, via(4)), (away, via(4))]
        )
        slabs["a"] = [a0, a1, a2, a3, b0, b1, b2, swap(a3)]
        (c0,) = arrange(rows, flow.me, [shard_c, near, away, both_ways], [shard_c.shape[1]])
        (d0,) = yield swaps([c0])
        c1, c2 = yield [(c0, via(1)), (c0, via(2))]
        c3, d1, d2 = yield [(c2, via(1))] + swaps([c1, c2])
        return [c0, c1, c2, c3, d0, d1, d2, swap(c3)]

    def whole(shard):
        own = gather_whole(shard)
        return [own, swap(own)]

    def apart(flip):
        masks = (2, 1) if flip else (1, 2)
        return functools.partial(hop_apart, masks=masks, count=dp_count)

    def halve(flip, hurry, pause, own, other):
        if hurry:
            other = swap(other)
        else:
            (other,) = yield swaps([other])
        if pause:
            yield []
        keep, send = (low_sum([own[k : k + 2], other[k : k + 2]]).astype(BF) for k in (0, 2))
        (near,) = yield [(send, apart(flip))]
        (away,) = yield [(low_sum([keep[1], near[1]]).astype(BF), apart(1 - flip))]
        return [keep, near, away]

    def reduce_far(groups):
        keep, send = split_far(flow.me, groups)
        (near,) = yield [(send, via(4))]
        (away,) = yield [(low_sum([keep[1], near[1]]).astype(BF), via(8))]
        return low_sum([keep[0], near[0], away])

    def reduce_all(flip, own, other):
        group = yield from halve(flip, True, False, own, other)
        return (yield from reduce_far([sums_of[s] for s in range(subs - 1)] + [group]))

    def reduce_last(flip, own, other, sums):
        other, sums_away = swap(other), swap(sums)
        rows_here = rows.far * rows.block
        keep, send = small_call(
            last_join_body,
            "last_join",
            [SDS((2 * rows_here, wide), BF), SDS((2 * rows_here + 16, wide), BF)],
            [],
            [own, other, sums, sums_away],
        )
        (near,) = yield [(send, apart(flip))]
        return [keep, send, near]

    def exchange(value):
        (got,) = yield swaps([value])
        return got

    def reduce_one(flip, own, other):
        group = yield from halve(flip, False, False, own, other)
        return (yield from reduce_far([group]))

    def plain(own, other):
        value = low_sum([own, swap(other)]).astype(BF).reshape(depth, -1)
        return lax.psum_scatter(value, "dp", scatter_dimension=0, tiled=True).astype(F32)

    def run(transfer):
        requests = next(transfer)
        while True:
            try:
                requests = transfer.send(send_all(requests))
            except StopIteration as stop:
                return stop.value

    slabs, forward = {}, []

    def project(g):
        name = "q0" if g == 0 else "q1"
        forward.append(
            project_attend(qkv_pieces[g], flow.me, normed, seg_col, seg_row, slabs[name])
        )

    if rows.split:
        shard_q = shards["q"]
        got = send_all(far_hops(rows, [shard_q] * (rows.far - 1)))
        prepared = prepare(start, core_place, *token_halves, gain1, bias1)
        tied = tie(*got, *prepared, w_out, w_up, w_down)
        got, prepared = tied[:3], tied[3:6]
        shard_a = pack(*tied[6:])
        near_q0, near_q1 = arrange(rows, me, [shard_q] + list(got), [part, wide])
        own = [near_q0] + [hop(near_q0, m, dp_count) for m in MASKS[1:]]
        first_cols = part + wide * cut
        shard_c, shard_a = shard_a[:, first_cols:], shard_a[:, :first_cols]
        away_a = hop(shard_a, 8, dp_count)
        start_cot, _ = tie(start, near_q0)
        turned_cot = turn(start_cot, core_place, *cot_halves)
        tied = tie(*own, *turned_cot)
        own, turned_cot = tied[:4], tied[4:]
        slabs["q0"] = list(own) + [swap(v) for v in own]
        flow.add(fetch_near, "q1", slabs, [near_q1])
        flow.add(fetch_wide, "c", slabs, [shard_a, away_a])
        flow.step(own[3])
    else:
        shard_a = pack(w_out, w_up, w_down)
        for name, shard in (
            ("q0", shards["q"][:, :part]),
            ("q1", shards["q"][:, part:]),
            ("a", shard_a[:, : part + wide * cut]),
            ("c", shard_a[:, part + wide * cut :]),
        ):
            slabs[name] = whole(shard)
        prepared = prepare(start, core_place, *token_halves, gain1, bias1)
        turned_cot = turn(start, core_place, *cot_halves)
    x, normed, normed_t = prepared
    cot, cot_t = turned_cot
    for g in range(groups):
        project(g)
        flow.step(forward[g][2])
    atts = [f[1] for f in forward]
    middle, normed_ffn, normed_ffn_t = out_norm(
        out_piece, flow.me, x, gain2, bias2, atts, slabs["a"]
    )
    flow.step(normed_ffn)

    held = None
    sums_of = {}
    onto = []
    feed_names = ["a"] * cut + ["c"] * (subs - cut)
    for s in range(subs):
        final = s == subs - 1
        grads, held = feed_forward(
            feed_pieces[s],
            feed_outs[s],
            flow.me,
            normed_ffn,
            normed_ffn_t,
            cot,
            cot_t,
            held,
            slabs[feed_names[s]],
            [],
            (out_piece, slabs["a"], middle, gain2, groups) if final else None,
        )
        flip = s // cut
        if not rows.split:
            sums_of[s] = plain(*grads)
        elif final:
            flow.add(functools.partial(reduce_all, flip), "feed", sums_of, grads)
        else:
            flow.add(functools.partial(halve, flip, False, s == 0), s, sums_of, grads)
        if s == 1 and rows.split:
            flow.step(held[1], gate=lambda: slabs["c"][-1:])
        elif not final:
            flow.step(held[1])
    mixed, grad_middle, branch_t, sums2, *grad_atts = held
    mixed, core_place, _ = flow.step(mixed, core_place, sums2)
    mixed_held, mixed_other = turn_back(back, core_place, mixed)
    flow.add(exchange, "mixed", sums_of, [mixed_other])
    grad_projs = []
    onto = []

    held = None
    qkv_slabs = [slabs["q0"]] + [slabs["q1"]] * (groups - 1)
    for g in range(groups):
        proj, att, inverse, kept = forward[g]
        held, grads, sums1 = attend_back(
            qkv_pieces[g],
            qkv_outs[g],
            flow.me,
            normed_t,
            proj,
            att,
            grad_atts[g],
            inverse,
            kept,
            qkv_slabs[g],
            branch_t,
            atts if g == 0 else [],
            held,
            x if g == groups - 1 else None,
            onto,
        )
        onto = grads
        if g == 0:
            if rows.split:
                flow.add(functools.partial(reduce_one, 0), "first", sums_of, grads)
            else:
                sums_of["first"] = plain(*grads)
            onto = []
        if g < groups - 1:
            flow.step(held)
    sums = jnp.concatenate([sums1[:2], sums2[:2]], 0)
    if rows.split:
        flow.add(functools.partial(reduce_last, 1), "last", sums_of, [*grads, sums])
        (held,) = flow.step(held)
    else:
        sums_of["last"] = plain(*grads)
    start_late, _ = tie(back, flow.me)
    tokens_held, tokens_other = norm_back(start_late, core_place, x, held, grad_middle, gain1)
    tokens_held, tokens_other = flow.step(tokens_held, tokens_other)
    if rows.split:
        block = rows.block
        keep, send, near = sums_of["last"]
        rows_here = rows.far * block
        rest, send = small_call(
            last_half_body,
            "last_half",
            [SDS((rows_here, wide), BF), SDS((rows_here + 32, wide), BF)],
            [],
            [keep, send, near],
        )
        away = apart(0)(send)
        keep, send = small_call(
            functools.partial(last_split_body, 1),
            "last_split",
            [SDS((2 * block + 16, wide), BF)] * 2,
            [flow.me],
            [rest, send, away],
        )
        near = hop(send, 4, dp_count)
        rest, send = small_call(
            last_middle_body, "last_middle", [SDS((block + 16, wide), BF)] * 2, [], [keep, near]
        )
        away = hop(send, 8, dp_count)
        while flow.active:
            flow.step()
        grad_qkv, norm_sums = small_call(
            last_sum_body,
            "last_sum",
            [SDS((3, block, part), F32), SDS((4, depth), F32)],
            [],
            [rest, away, sums_of["first"]],
        )
        grad_qkv = grad_qkv.transpose(1, 0, 2)
        grad_out = sums_of["first"][:, :part].T
        feed_sums = [sums_of["feed"]]
    else:
        early, last = sums_of["first"], sums_of["last"]
        parts = [early[:, part:], last[:, :part], last[:, part:]]
        grad_qkv = jnp.concatenate([r.reshape(-1, 3, 128) for r in parts], 2)
        grad_out = early[:, :part].T
        feed_sums = [sums_of[s] for s in range(subs)]
        norm_sums = jnp.sum(lax.all_gather(sums + swap(sums), "dp", axis=0), 0)
    feed_sum = jnp.concatenate(feed_sums, 1) if len(feed_sums) > 1 else feed_sums[0]
    feed_list = [feed_sum[:, wide * s : wide * (s + 1)] for s in range(subs)]

    return (
        place(core_place, mixed_held, sums_of["mixed"])[:, None],
        place(core_place, tokens_held, swap(tokens_other))[:, None],
        norm_sums[0],
        norm_sums[1],
        grad_qkv,
        grad_out,
        norm_sums[2],
        norm_sums[3],
        jnp.concatenate([r[:, :part] for r in feed_list], 1),
        jnp.concatenate([r[:, part:] for r in feed_list], 1).T,
    )


def solution(mesh):
    in_specs = (
        P(None, "dp", "mp", None),
        P(None, "dp", None),
        P(),
        P(),
        P("dp", None, "mp"),
        P("mp", "dp"),
        P(),
        P(),
        P("dp", "mp"),
        P("mp", "dp"),
        P(None, "dp", "mp", None),
    )
    out_specs = (
        P(None, "dp", "mp", None),
        P(None, "dp", "mp", None),
        P(),
        P(),
        P("dp", None, "mp"),
        P("mp", "dp"),
        P(),
        P(),
        P("dp", "mp"),
        P("mp", "dp"),
    )
    return jax.shard_map(
        on_device, mesh=mesh, in_specs=in_specs, out_specs=out_specs, check_vma=False
    )
```

```python
import functools
import math

import jax
import jax.numpy as jnp
from jax import lax
from jax.experimental import pallas as pl
from jax.experimental.pallas import tpu as pltpu
from jax.sharding import PartitionSpec as P

HD = 32
QB = 256
EPS = 1e-05
BF = jnp.bfloat16
F32 = jnp.float32
NEG = -1e30
SCALE = 1.0 / math.sqrt(HD)
LOG2E = math.log2(math.e)
C2 = SCALE * LOG2E
MIB = 1024 * 1024
SDS = jax.ShapeDtypeStruct


def nn(a, b):
    return lax.dot_general(a, b, (((1,), (0,)), ((), ())), preferred_element_type=F32)


def nt(a, b):
    return lax.dot_general(a, b, (((1,), (1,)), ((), ())), preferred_element_type=F32)


def params(mib):
    return pltpu.CompilerParams(vmem_limit_bytes=mib * MIB)


def in_hbm(values):
    return [pltpu.with_memory_space_constraint(v, pltpu.HBM) for v in values]


def in_vmem(values):
    return [pltpu.with_memory_space_constraint(v, pltpu.VMEM) for v in values]


def cost(gflop, mbytes):
    return pl.CostEstimate(flops=int(gflop * 1e9), bytes_accessed=int(mbytes * 1e6), transcendentals=0)


def any_spec():
    return pl.BlockSpec(memory_space=pl.ANY)


def smem_spec():
    return pl.BlockSpec(memory_space=pltpu.SMEM)


def vmem_spec():
    return pl.BlockSpec(memory_space=pltpu.VMEM)


def row_spec(width, rows=512):
    return pl.BlockSpec((rows, width), lambda r: (r, 0))


def column_spec(height, rows=512):
    return pl.BlockSpec((height, rows), lambda r: (0, r))


def whole_spec(shape):
    return pl.BlockSpec(shape, lambda r: tuple(0 for _ in shape))


MASKS = (0, 1, 2, 3)


class Rows:
    def __init__(self, dp_count, depth):
        self.dp_count = dp_count
        self.depth = depth
        self.split = (depth // dp_count) % 16 == 0 and dp_count == 16
        self.near = 4 if self.split else 1
        self.far = dp_count // 4 if self.split else 1
        self.block = depth // (self.near * self.far)
        self.shape = (self.far, self.near, self.block)


class Piece:
    def __init__(self, rows, kind, start=0, width=0, flip=0):
        self.rows = rows
        self.flip = flip
        self.kind = kind if rows.split else "whole"
        self.start = start
        self.count = 2 * len(MASKS) if self.kind == "slabs" else 2
        if self.kind == "stack":
            self.shape = (len(MASKS), rows.far, rows.block, width)
        else:
            self.shape = rows.shape + (width,)


def piece_copies(piece, me, refs, moves, sem, outward):
    copies = []
    each = piece.count // 2
    for half, column, width, view in moves:
        cols = pl.ds(piece.start + column, width)
        if piece.kind == "whole":
            pairs = [(refs[half].at[:, :, :, cols], view)]
        else:
            pairs = []
            order = lax.bitwise_xor(me[1], piece.flip ^ half)
            masks = (0, 2 - order, 1 + order, 3) if piece.kind == "stack" else MASKS
            for k, mask in enumerate(masks):
                ref = refs[half].at[k] if piece.kind == "stack" else refs[half * each + k]
                near = lax.bitwise_xor(lax.rem(me[0], 4), mask)
                pairs.append((ref.at[:, :, cols], view.at[:, near]))
        for outside, inside in pairs:
            if outward:
                copies.append(pltpu.make_async_copy(inside, outside, sem))
            else:
                copies.append(pltpu.make_async_copy(outside, inside, sem))
    return copies


def start_all(copies):
    for copy in copies:
        copy.start()


def wait_bytes(ref, sem):
    pltpu.make_async_copy(ref, ref, sem).wait()


def flat(value):
    return value.reshape(-1, value.shape[-1])


def head_row(h):
    return lax.broadcasted_iota(jnp.int32, (1, 128), 1) // HD == h


def fill_bias(bias, seg_col, seg_row):
    key = lax.broadcasted_iota(jnp.int32, (QB, QB), 0)
    query = lax.broadcasted_iota(jnp.int32, (QB, QB), 1)
    bias[0] = jnp.where(query >= key, 0.0, NEG)
    bias[1] = jnp.where((query >= key) & (seg_col[...] == seg_row[...]), 0.0, NEG)


def turned(doubles, start, r):
    coarse = pl.multiple_of(start // 16 * 16 + r * QB, 16)
    fine = start % 16
    row = lax.broadcasted_iota(jnp.int32, (QB, QB + 16), 0)
    col = lax.broadcasted_iota(jnp.int32, (QB, QB + 16), 1)
    pick = jnp.where(col - row == fine, 1.0, 0.0).astype(BF)
    total = None
    for double in doubles:
        part = nn(pick, double[pl.ds(coarse, QB + 16), :])
        total = part if total is None else total + part
    return total


def norm_parts(values):
    centered = values - jnp.mean(values, axis=-1, keepdims=True)
    spread = jnp.mean(centered * centered, axis=-1, keepdims=True)
    root = lax.rsqrt(spread + EPS)
    return centered * root, root


def fill_double(double, core, own, other, sem):
    here = own.shape[1]
    for k, half in enumerate((own, other)):
        pltpu.make_async_copy(half.at[core], double.at[pl.ds(k * here, here)], sem).start()
    wait_bytes(double.at[pl.ds(0, 2 * here)], sem)
    double[2 * here :, :] = double[: 2 * here, :]


def prepare_body(start, core, own, other, gain, offset, x_out, normed_out, normed_t_out, double, x, normed, normed_t, sems):
    fill_double(double, core[0], own, other, sems.at[3])

    def step(r, carry):
        at = pl.ds(pl.multiple_of(r * QB, QB), QB)
        value = turned([double], start[0], r)
        x[at, :] = value.astype(BF)
        hat, _ = norm_parts(value)
        low = (hat * gain[...] + offset[...]).astype(BF)
        normed[at, :] = low
        normed_t[:, at] = low.T
        return carry

    lax.fori_loop(0, x.shape[0] // QB, step, 0)
    copies = [
        pltpu.make_async_copy(normed, normed_out, sems.at[0]),
        pltpu.make_async_copy(x, x_out, sems.at[1]),
        pltpu.make_async_copy(normed_t, normed_t_out, sems.at[2]),
    ]
    start_all(copies)
    for copy in copies:
        copy.wait()


def prepare(start, core, own, other, gain, offset):
    _, here, depth = own.shape
    shape, shape_t = (2 * here, depth), (depth, 2 * here)
    shapes = [shape, shape, shape_t]
    return pl.pallas_call(
        prepare_body,
        in_specs=[smem_spec()] * 2 + [any_spec()] * 2 + [vmem_spec()] * 2,
        out_specs=[any_spec()] * 3,
        out_shape=[pltpu.HBM(s, BF) for s in shapes],
        scratch_shapes=[pltpu.VMEM((4 * here, depth), BF)]
        + [pltpu.VMEM(s, BF) for s in shapes]
        + [pltpu.SemaphoreType.DMA((4,))],
        compiler_params=params(20),
        cost_estimate=cost(4, 8),
        name="prepare",
    )(start, core, *in_hbm([own, other]), gain, offset)


def turn_body(start, core, own, other, cot_out, cot_t_out, double, cot, cot_t, sems):
    fill_double(double, core[0], own, other, sems.at[2])

    def step(r, carry):
        at = pl.ds(pl.multiple_of(r * QB, QB), QB)
        low = turned([double], start[0], r).astype(BF)
        cot[at, :] = low
        cot_t[:, at] = low.T
        return carry

    lax.fori_loop(0, cot.shape[0] // QB, step, 0)
    copies = [
        pltpu.make_async_copy(cot, cot_out, sems.at[0]),
        pltpu.make_async_copy(cot_t, cot_t_out, sems.at[1]),
    ]
    start_all(copies)
    for copy in copies:
        copy.wait()


def turn(start, core, own, other):
    _, here, depth = own.shape
    shapes = [(2 * here, depth), (depth, 2 * here)]
    return pl.pallas_call(
        turn_body,
        in_specs=[smem_spec()] * 2 + [any_spec()] * 2,
        out_specs=[any_spec()] * 2,
        out_shape=[pltpu.HBM(s, BF) for s in shapes],
        scratch_shapes=[pltpu.VMEM((4 * here, depth), BF)]
        + [pltpu.VMEM(s, BF) for s in shapes]
        + [pltpu.SemaphoreType.DMA((3,))],
        compiler_params=params(16),
        cost_estimate=cost(4, 8),
        name="turn",
    )(start, core, *in_hbm([own, other]))


def turn_back_body(start, core, values, held, other, double, own, sem):
    here = other.shape[0]
    double[: 2 * here, :] = values[...]
    double[2 * here :, :] = values[...]
    count = here // QB

    def step(r, carry):
        at = pl.ds(pl.multiple_of(r * QB, QB), QB)
        own[at, :] = turned([double], start[0], r).astype(BF)
        other[at, :] = turned([double], start[0], r + count).astype(BF)
        return carry

    lax.fori_loop(0, count, step, 0)
    copy = pltpu.make_async_copy(own, held.at[core[0]], sem)
    copy.start()
    copy.wait()


def place_body(core, other, held, out, sem):
    copy = pltpu.make_async_copy(other, out.at[1 - core[0]], sem)
    copy.start()
    copy.wait()


def place(core, held, other):
    return pl.pallas_call(
        place_body,
        in_specs=[smem_spec(), any_spec(), any_spec()],
        out_specs=any_spec(),
        out_shape=pltpu.HBM(held.shape, held.dtype),
        input_output_aliases={2: 0},
        scratch_shapes=[pltpu.SemaphoreType.DMA],
        compiler_params=params(4),
        cost_estimate=cost(0, 4),
        name="place",
    )(core, other, *in_hbm([held]))


def turn_back(start, core, values):
    length, depth = values.shape
    half = (length // 2, depth)
    return pl.pallas_call(
        turn_back_body,
        in_specs=[smem_spec()] * 2 + [vmem_spec()],
        out_specs=[any_spec(), vmem_spec()],
        out_shape=[pltpu.HBM((2,) + half, BF), SDS(half, BF)],
        scratch_shapes=[
            pltpu.VMEM((2 * length, depth), BF),
            pltpu.VMEM(half, BF),
            pltpu.SemaphoreType.DMA,
        ],
        compiler_params=params(16),
        cost_estimate=cost(2, 4),
        name="turn_back",
    )(start, core, values)


def arrange_body(widths, me, *refs):
    pieces, outs = refs[:4], refs[4:]
    far = me[0] // 4
    for m, piece in enumerate(pieces):
        begin = 0
        for out, width in zip(outs, widths):
            out[lax.bitwise_xor(far, m)] = piece[:, begin : begin + width]
            begin += width


def arrange(rows, me, pieces, widths):
    return pl.pallas_call(
        functools.partial(arrange_body, widths),
        in_specs=[smem_spec()] + [vmem_spec()] * 4,
        out_specs=[vmem_spec()] * len(widths),
        out_shape=[SDS((rows.far, rows.block, w), BF) for w in widths],
        compiler_params=params(8),
        cost_estimate=cost(1, 1),
        name="arrange",
    )(me, *pieces)


KEPT = (0, 256, 768, 1536)
KEPT_ROWS = (256, 512, 768, 256)
ORDER = (2, 1, 0, 3)


def project_attend_body(piece, me, normed_in, seg_col, seg_row, *refs):
    slabs = refs[: piece.count]
    proj_out, att, inverse, kept_out, weight, proj, normed, bias = refs[piece.count : piece.count + 8]
    keys_m, values_t, att_t, kept, sem, out_sem, kept_sem = refs[piece.count + 8 :]
    normed_copy = pltpu.make_async_copy(normed_in, normed, out_sem)
    normed_copy.start()
    moves = [(half, 0, 384, weight.at[:, :, :, pl.ds(384 * half, 384)]) for half in range(2)]
    start_all(piece_copies(piece, me, slabs, moves, sem, False))
    fill_bias(bias, seg_col, seg_row)
    values_t[...] = jnp.ones_like(values_t)
    normed_copy.wait()
    wait_bytes(weight, sem)

    for c in range(3):
        cols = slice(c * 256, c * 256 + 256)
        proj[:, cols] = nn(normed[...], flat(weight[:, :, :, cols])).astype(BF)
    proj_copy = pltpu.make_async_copy(proj, proj_out, out_sem)
    proj_copy.start()
    for half in range(2):
        flipped = proj[:, half * 384 + 256 : half * 384 + 384].T
        for h in range(4):
            values_t[half * 4 + h, 0:HD, :] = flipped[h * HD : (h + 1) * HD]

    units = [(h, i) for i in (2, 1, 0, 3) for h in range(4)]

    def step(half, carry):
        col = pl.multiple_of(half * 384, 128)
        for h in range(4):
            keys_m[h] = jnp.where(head_row(h), proj[:, pl.ds(col + 128, 128)], 0)

        def score(h, i):
            first = 768 if i == 3 else 0
            scores = nt(keys_m[h, first : (i + 1) * QB, :], proj[i * QB : (i + 1) * QB, pl.ds(col, 128)])
            edge = scores[-QB:] + bias[1 if i == 3 else 0]
            return jnp.concatenate([scores[:-QB], edge], 0) if scores.shape[0] > QB else edge

        ahead = score(*units[0])
        for k, (h, i) in enumerate(units):
            scores = ahead
            if k + 1 < len(units):
                ahead = score(*units[k + 1])
            first = 768 if i == 3 else 0
            last = (i + 1) * QB
            at = slice(i * QB, last)
            peak = jnp.max(scores, axis=0, keepdims=True) * C2
            probs = jnp.exp2(scores * C2 - peak).astype(BF)
            kept[half * 4 + h, KEPT[i] : KEPT[i] + last - first, :] = probs
            summed = nn(values_t[half * 4 + h, :, first:last], probs)
            share = 1.0 / summed[HD : HD + 1]
            att_t[pl.ds(pl.multiple_of(half * 128 + h * HD, HD), HD), at] = summed[:HD] * share
            inverse[pl.ds(half * 4 + h, 1), at] = share
            if h == 3:
                part = (pl.ds(half * 4, 4), pl.ds(KEPT[i], last - first))
                pltpu.make_async_copy(kept.at[part], kept_out.at[part], kept_sem).start()
        return carry

    lax.fori_loop(0, 2, step, 0)
    for half in range(2):
        cols = slice(half * 128, half * 128 + 128)
        att[:, cols] = att_t[cols, :].T.astype(BF)
    proj_copy.wait()
    wait_bytes(kept, kept_sem)


def project_attend(piece, me, normed, seg_col, seg_row, slabs):
    length, depth = normed.shape
    rows = piece.rows
    return pl.pallas_call(
        functools.partial(project_attend_body, piece),
        in_specs=[smem_spec(), any_spec()] + [vmem_spec()] * 2 + [any_spec()] * len(slabs),
        out_specs=[any_spec()] + [vmem_spec()] * 2 + [any_spec()],
        out_shape=[
            pltpu.HBM((length, 768), BF),
            pltpu.HBM((length, 256), BF),
            pltpu.HBM((8, length), F32),
            pltpu.HBM((8, 1792, QB), BF),
        ],
        scratch_shapes=[
            pltpu.VMEM(rows.shape + (768,), BF),
            pltpu.VMEM((length, 768), BF),
            pltpu.VMEM((length, depth), BF),
            pltpu.VMEM((2, QB, QB), F32),
            pltpu.VMEM((4, length, 128), BF),
            pltpu.VMEM((8, HD + 16, length), BF),
            pltpu.VMEM((256, length), F32),
            pltpu.VMEM((8, 1792, QB), BF),
            pltpu.SemaphoreType.DMA,
            pltpu.SemaphoreType.DMA,
            pltpu.SemaphoreType.DMA,
        ],
        compiler_params=params(32),
        cost_estimate=cost(8, 8),
        name="project_attend",
    )(me, *in_hbm([normed]), seg_col, seg_row, *in_hbm(slabs))


def join_heads(attended):
    return jnp.concatenate([a[:, :128] for a in attended] + [a[:, 128:] for a in attended], 1)


def out_norm_body(piece, groups, me, tokens, gain, offset, *refs):
    attended = refs[:groups]
    slabs = refs[groups : groups + piece.count]
    middle, normed, normed_t, weight, sem = refs[groups + piece.count :]
    width = weight.shape[3] // 2

    @pl.when(pl.program_id(0) == 0)
    def _():
        moves = [(half, 0, width, weight.at[:, :, :, pl.ds(width * half, width)]) for half in range(2)]
        start_all(piece_copies(piece, me, slabs, moves, sem, False))
        wait_bytes(weight, sem)

    value = tokens[...].astype(F32) + nt(join_heads([a[...] for a in attended]), flat(weight[...]))
    middle[...] = value
    hat, _ = norm_parts(value)
    low = (hat * gain[...] + offset[...]).astype(BF)
    normed[...] = low
    normed_t[...] = low.T


def out_norm(piece, me, tokens, gain, offset, attended, slabs):
    length, depth = tokens.shape
    return pl.pallas_call(
        functools.partial(out_norm_body, piece, len(attended)),
        grid=(length // 512,),
        in_specs=[smem_spec(), row_spec(depth), whole_spec((1, depth)), whole_spec((1, depth))]
        + [row_spec(256)] * len(attended)
        + [any_spec()] * len(slabs),
        out_specs=[row_spec(depth)] * 2 + [column_spec(depth)],
        out_shape=[
            pltpu.HBM((length, depth), F32),
            pltpu.VMEM((length, depth), BF),
            pltpu.VMEM((depth, length), BF),
        ],
        scratch_shapes=[pltpu.VMEM(piece.rows.shape + (depth,), BF), pltpu.SemaphoreType.DMA],
        compiler_params=params(28),
        cost_estimate=cost(3, 8),
        name="out_norm",
    )(me, *in_hbm([tokens]), gain, offset, *in_hbm(attended), *in_hbm(slabs))


def gelu_parts(values):
    size = jnp.abs(values)
    density = jnp.exp2(values * values * (-0.5 * LOG2E) + math.log2(1.0 / math.sqrt(2 * math.pi)))
    below = 1.0 + 0.2316419 * size
    t = pl.reciprocal(below, approx=True)
    t = t * (2.0 - below * t)
    poly = t * (
        0.319381530
        + t * (-0.356563782 + t * (1.781477937 + t * (-1.821255978 + t * 1.330274429)))
    )
    tail = density * poly
    below = jnp.where(values >= 0, 1.0 - tail, tail)
    return values * below, below + values * density


def norm_pull(grad, hat, root, gain):
    scaled = grad * gain
    first = jnp.mean(scaled, axis=-1, keepdims=True)
    second = jnp.mean(scaled * hat, axis=-1, keepdims=True)
    return root * (scaled - first - hat * second)


def feed_forward_body(
    piece, out_piece, first, last_piece, groups, aliased, me, normed, normed_t, cot, cot_t, *refs
):
    refs = list(refs)
    final = last_piece is not None
    held = [] if first else [refs.pop(0), refs.pop(0)]
    if final:
        middle, gain = refs.pop(0), refs.pop(0)
        out_slabs, refs = refs[: last_piece.count], refs[last_piece.count :]
    slabs, refs = refs[: piece.count], refs[piece.count + aliased :]
    outs, refs = refs[:2], refs[2:]
    mixed = refs.pop(0)
    if final:
        grad_middle_out, branch_t, sums = refs[:3]
        grad_att, refs = refs[3 : 3 + groups], refs[3 + groups :]
    else:
        grad_in = refs.pop(0)
    weight, staged, act, grad_hidden, mixed_acc, grad_acc, sems = refs[:7]
    if final:
        mixed_low, middle_here, out_weight, grad_middle = refs[7:]
    length, depth = normed.shape
    moves = []
    for half in range(2):
        for which in range(2):
            at = pl.ds(which * 768 + half * 384, 384)
            moves.append((half, which * 384, 384, at))
    into = [(h, c, w, weight.at[:, :, :, at]) for h, c, w, at in moves]
    outof = [(h, c, w, staged.at[:, :, :, at]) for h, c, w, at in moves]
    start_all(piece_copies(piece, me, slabs, into, sems.at[0], False))
    held_copies = []
    if not first:
        held_copies.append(pltpu.make_async_copy(held[0], mixed_acc, sems.at[1]))
        held_copies.append(pltpu.make_async_copy(held[1], grad_acc, sems.at[2]))
    if final:
        held_copies.append(pltpu.make_async_copy(middle, middle_here, sems.at[4]))
    start_all(held_copies)
    if final:
        width = depth // 2
        views = [
            (half, 0, width, out_weight.at[:, :, :, pl.ds(width * half, width)]) for half in range(2)
        ]
        start_all(piece_copies(last_piece, me, out_slabs, views, sems.at[5], False))
    wait_bytes(weight, sems.at[0])
    chunks = [slice(c * 256, c * 256 + 256) for c in range(3)]

    def products(c):
        hidden = nn(normed[...], flat(weight[:, :, :, c * 256 : c * 256 + 256]))
        return hidden, nn(cot[...], flat(weight[:, :, :, 768 + c * 256 : 1024 + c * 256]))

    ahead = products(0)
    for c in range(3):
        hidden, grad_act = ahead
        if c < 2:
            ahead = products(c + 1)
        value, slope = gelu_parts(hidden)
        act[:, chunks[c]] = value.astype(BF)
        grad_hidden[:, chunks[c]] = (grad_act * slope).astype(BF)
    for copy in held_copies:
        copy.wait()
    for cols in chunks:
        mixed_part = nt(act[...], flat(weight[:, :, :, 768:1536])[cols])
        grad_part = nt(grad_hidden[...], flat(weight[:, :, :, 0:768])[cols])
        if not first:
            mixed_part = mixed_part + mixed_acc[:, cols]
            grad_part = grad_part + grad_acc[:, cols]
        if final:
            mixed_low[:, cols] = (middle_here[:, cols] + mixed_part).astype(BF)
        else:
            mixed_acc[:, cols] = mixed_part
        grad_acc[:, cols] = grad_part
    if final:
        out_copies = [pltpu.make_async_copy(mixed_low, mixed, sems.at[1])]
        start_all(out_copies)
        wait_bytes(out_weight, sems.at[5])
        sums[...] = jnp.zeros_like(sums)

        def back_step(r, carry):
            at = pl.ds(pl.multiple_of(r * 512, 512), 512)
            hat, root = norm_parts(middle_here[at, :])
            grad = grad_acc[at, :]
            value = cot[at, :].astype(F32) + norm_pull(grad, hat, root, gain[...])
            grad_middle[at, :] = value
            low = value.astype(BF)
            branch_t[:, at] = low.T
            sums[0:1, :] += jnp.sum(grad * hat, axis=0, keepdims=True)
            sums[1:2, :] += jnp.sum(grad, axis=0, keepdims=True)
            back = nn(low, flat(out_weight[...])).astype(BF)
            for g in range(groups):
                grad_att[g][at, 0:128] = back[:, g * 128 : g * 128 + 128]
                grad_att[g][at, 128:256] = back[:, width + g * 128 : width + g * 128 + 128]
            return carry

        lax.fori_loop(0, length // 512, back_step, 0)
        out_copies.append(pltpu.make_async_copy(grad_middle, grad_middle_out, sems.at[2]))
        out_copies[-1].start()
    else:
        out_copies = [
            pltpu.make_async_copy(mixed_acc, mixed, sems.at[1]),
            pltpu.make_async_copy(grad_acc, grad_in, sems.at[2]),
        ]
        start_all(out_copies)
    for c in range(3):
        cols = slice(c * 256, c * 256 + 256)
        up = nn(normed_t[...], grad_hidden[:, cols]).astype(BF)
        staged[:, :, :, cols] = up.reshape(staged.shape[:3] + (256,))
        down = nn(cot_t[...], act[:, cols]).astype(BF)
        staged[:, :, :, 768 + c * 256 : 1024 + c * 256] = down.reshape(staged.shape[:3] + (256,))
    start_all(piece_copies(out_piece, me, outs, outof, sems.at[3], True))
    for copy in out_copies:
        copy.wait()
    wait_bytes(staged, sems.at[3])


def feed_forward(
    piece, out_piece, me, normed, normed_t, cot, cot_t, held, slabs, onto, last=None
):
    length, depth = normed.shape
    rows = piece.rows
    first, final = held is None, last is not None
    ins = [me] + in_vmem([normed, normed_t, cot, cot_t]) + ([] if first else in_hbm(held))
    specs = [smem_spec()] + [vmem_spec()] * 4 + [any_spec()] * (0 if first else 2)
    scratch = [
        pltpu.VMEM(rows.shape + (1536,), BF),
        pltpu.VMEM(rows.shape + (1536,), BF),
        pltpu.VMEM((length, 768), BF),
        pltpu.VMEM((length, 768), BF),
        pltpu.VMEM((length, depth), F32),
        pltpu.VMEM((length, depth), F32),
        pltpu.SemaphoreType.DMA((6,)),
    ]
    last_piece, groups = None, 0
    outs = [SDS(out_piece.shape, BF)] * 2 + [pltpu.HBM((length, depth), BF if final else F32)]
    out_specs = [any_spec()] * 3
    if final:
        last_piece, last_slabs, middle, gain, groups = last
        ins += in_hbm([middle]) + [gain] + in_hbm(last_slabs)
        specs += [any_spec(), vmem_spec()] + [any_spec()] * len(last_slabs)
        scratch += [
            pltpu.VMEM((length, depth), BF),
            pltpu.VMEM((length, depth), F32),
            pltpu.VMEM(rows.shape + (depth,), BF),
            pltpu.VMEM((length, depth), F32),
        ]
        outs += [pltpu.HBM((length, depth), F32), pltpu.VMEM((depth, length), BF), SDS((8, depth), F32)]
        outs += [pltpu.HBM((length, 256), BF)] * groups
        out_specs += [any_spec()] + [vmem_spec()] * (2 + groups)
    else:
        outs.append(pltpu.HBM((length, depth), F32))
        out_specs.append(any_spec())
    got = pl.pallas_call(
        functools.partial(
            feed_forward_body, piece, out_piece, first, last_piece, groups, len(onto)
        ),
        in_specs=specs + [any_spec()] * (piece.count + len(onto)),
        out_specs=out_specs,
        out_shape=outs,
        input_output_aliases={len(ins) + piece.count + k: k for k in range(len(onto))},
        scratch_shapes=scratch,
        compiler_params=params(48 if final else 32),
        cost_estimate=cost(14 if final else 11, 20),
        name="feed_forward",
    )(*ins, *in_hbm(slabs), *onto)
    return got[:2], got[2:]


def attend_back_body(piece, out_piece, extra, aliased, final, me, normed_t_in, proj, att, grad_att, inverse, kept_in, *refs):
    refs = list(refs)
    slabs, refs = refs[: piece.count], refs[piece.count :]
    if extra:
        branch_t = refs.pop(0)
        attended, refs = refs[:extra], refs[extra:]
    else:
        held = refs.pop(0)
    if final:
        tokens_in = refs.pop(0)
    refs = refs[aliased:]
    grad_normed, outs, refs = refs[0], refs[1:3], refs[3:]
    if final:
        sums = refs.pop(0)
    grad_proj, key_sum, value_sum = refs[:3]
    refs = refs[3:]
    kept, delta, keys_t, query_t, query_m, grad_m, staged, normed_t, total, weight, sems = refs[:11]
    for half in range(2):
        for i in ORDER:
            part = (pl.ds(half * 4, 4), pl.ds(KEPT[i], KEPT_ROWS[i]))
            sem = sems.at[5 + 4 * half + i]
            pltpu.make_async_copy(kept_in.at[part], kept.at[part], sem).start()
    copies = [pltpu.make_async_copy(normed_t_in, normed_t, sems.at[1])]
    if not extra:
        copies.append(pltpu.make_async_copy(held, total, sems.at[2]))
    if final:
        copies.append(pltpu.make_async_copy(tokens_in, refs[11], sems.at[3]))
    moves = [(half, 0, 384, weight.at[:, :, :, pl.ds(384 * half, 384)]) for half in range(2)]
    start_all(copies + piece_copies(piece, me, slabs, moves, sems.at[4], False))
    length = proj.shape[0]
    if extra:
        joined = join_heads([a[...] for a in attended])
        out_grad = nn(branch_t[...], joined).astype(BF)
        staged[:, :, :, 768:] = out_grad.reshape(staged.shape[:3] + (768,))
    for half in range(2):
        cols = slice(half * 128, half * 128 + 128)
        product = (grad_att[:, cols].astype(F32) * att[:, cols].astype(F32)).T
        for h in range(4):
            stat = slice(half * 4 + h, half * 4 + h + 1)
            total_here = jnp.sum(product[h * HD : (h + 1) * HD], axis=0, keepdims=True)
            delta[stat, :] = total_here * inverse[stat, :]
        keys_t[cols, :] = proj[:, half * 384 + 128 : half * 384 + 256].T

    def step(half, carry):
        col = pl.multiple_of(half * 384, 128)
        out = pl.multiple_of(half * 128, 128)
        share = jnp.concatenate(
            [jnp.broadcast_to(inverse[pl.ds(half * 4 + h, 1), :], (HD, length)) for h in range(4)], 0
        ).T
        grads = (grad_att[:, pl.ds(out, 128)].astype(F32) * share).astype(BF)
        for h in range(4):
            mine = head_row(h)
            query_m[h] = jnp.where(mine, proj[:, pl.ds(col, 128)], 0)
            grad_m[h] = jnp.where(mine, grads, 0)
        key_sum[...] = jnp.zeros_like(key_sum)
        value_sum[...] = jnp.zeros_like(value_sum)
        for i in (2, 1, 0, 3):
            first = 768 if i == 3 else 0
            last = (i + 1) * QB
            here = slice(first, last)
            there = slice(i * QB, last)
            values = proj[here, pl.ds(col + 256, 128)]
            rows_here = slice(KEPT[i], KEPT[i] + last - first)
            wait_bytes(
                kept.at[pl.ds(half * 4, 4), pl.ds(KEPT[i], KEPT_ROWS[i])], sems.at[5 + 4 * half + i]
            )
            all_probs, all_grads = [], []
            ahead = nt(values, grad_m[0, there, :])
            for h in range(4):
                grad_probs = ahead
                if h < 3:
                    ahead = nt(values, grad_m[h + 1, there, :])
                stat = pl.ds(half * 4 + h, 1)
                lanes = pl.ds(pl.multiple_of(half * 128 + h * HD, HD), HD)
                probs = kept[half * 4 + h, rows_here, :]
                grad_scores = (probs.astype(F32) * (grad_probs - delta[stat, there])).astype(BF)
                all_probs.append(probs)
                all_grads.append(grad_scores)
                query_t[lanes, there] = nn(keys_t[lanes, here], grad_scores)
            stacked = jnp.concatenate([grad_m[h, there, :] for h in range(4)], 0)
            value_sum[here, :] += nn(jnp.concatenate(all_probs, 1), stacked)
            stacked = jnp.concatenate([query_m[h, there, :] for h in range(4)], 0)
            key_sum[here, :] += nn(jnp.concatenate(all_grads, 1), stacked)
        grad_proj[:, pl.ds(col + 128, 128)] = (key_sum[...] * SCALE).astype(BF)
        grad_proj[:, pl.ds(col + 256, 128)] = value_sum[...].astype(BF)
        return carry

    lax.fori_loop(0, 2, step, 0)
    for half in range(2):
        grad_proj[:, half * 384 : half * 384 + 128] = (
            query_t[half * 128 : half * 128 + 128, :].T * SCALE
        ).astype(BF)
    for copy in copies:
        copy.wait()
    wait_bytes(weight, sems.at[4])
    for c in range(3):
        cols = slice(c * 256, c * 256 + 256)
        part = nn(normed_t[...], grad_proj[:, cols]).astype(BF)
        staged[:, :, :, cols] = part.reshape(staged.shape[:3] + (256,))
    moves = [(half, 0, 384, staged.at[:, :, :, pl.ds(384 * half, 384)]) for half in range(2)]
    if extra:
        moves += [
            (half, -384, 384, staged.at[:, :, :, pl.ds(768 + 384 * half, 384)]) for half in range(2)
        ]
    start_all(piece_copies(out_piece, me, outs, moves, sems.at[0], True))
    if final:
        sums[...] = jnp.zeros_like(sums)

    total_copies = []
    for c in range(3):
        cols = slice(c * 256, c * 256 + 256)
        value = nt(grad_proj[...], flat(weight[...])[cols])
        if not extra:
            value = value + total[:, cols]
        total[:, cols] = value
        total_copies.append(
            pltpu.make_async_copy(
                total.at[:, pl.ds(c * 256, 256)], grad_normed.at[:, pl.ds(c * 256, 256)], sems.at[2]
            )
        )
        total_copies[-1].start()
    if final:

        def sum_step(r, carry):
            at = pl.ds(pl.multiple_of(r * QB, QB), QB)
            value = total[at, :]
            hat, _ = norm_parts(refs[11][at, :].astype(F32))
            sums[0:1, :] += jnp.sum(value * hat, axis=0, keepdims=True)
            sums[1:2, :] += jnp.sum(value, axis=0, keepdims=True)
            return carry

        lax.fori_loop(0, length // QB, sum_step, 0)
    wait_bytes(staged, sems.at[0])
    wait_bytes(total, sems.at[2])


def attend_back(
    piece,
    out_piece,
    me,
    normed_t,
    proj,
    att,
    grad_att,
    inverse,
    kept,
    slabs,
    branch_t,
    attended,
    held,
    tokens,
    onto,
):
    depth, length = normed_t.shape
    extra = len(attended)
    final = tokens is not None
    columns = 1536 if extra else 768
    ins = [me] + in_hbm([normed_t, proj, att, grad_att, inverse, kept]) + in_hbm(slabs)
    specs = [smem_spec(), any_spec()] + [vmem_spec()] * 4 + [any_spec()] * (1 + len(slabs))
    if extra:
        ins += in_vmem([branch_t]) + in_hbm(attended)
        specs += [vmem_spec()] * (1 + extra)
    else:
        ins += in_hbm([held])
        specs += [any_spec()]
    if final:
        ins += in_hbm([tokens])
        specs += [any_spec()]
    outs = [pltpu.HBM((length, depth), F32)] + [SDS(out_piece.shape, BF)] * 2
    scratch = [
        pltpu.VMEM((8, 1792, QB), BF),
        pltpu.VMEM((8, length), F32),
        pltpu.VMEM((256, length), BF),
        pltpu.VMEM((256, length), F32),
        pltpu.VMEM((4, length, 128), BF),
        pltpu.VMEM((4, length, 128), BF),
        pltpu.VMEM(out_piece.rows.shape + (columns,), BF),
        pltpu.VMEM((depth, length), BF),
        pltpu.VMEM((length, depth), F32),
        pltpu.VMEM(piece.rows.shape + (768,), BF),
        pltpu.SemaphoreType.DMA((13,)),
    ]
    if final:
        outs.append(SDS((8, depth), F32))
        scratch.append(pltpu.VMEM((length, depth), BF))
    got = pl.pallas_call(
        functools.partial(attend_back_body, piece, out_piece, extra, len(onto), final),
        in_specs=specs + [any_spec()] * len(onto),
        out_specs=[any_spec()] * 3 + ([vmem_spec()] if final else []),
        out_shape=outs,
        input_output_aliases={len(ins) + k: 1 + k for k in range(len(onto))},
        scratch_shapes=[
            pltpu.VMEM((length, 768), BF),
            pltpu.VMEM((length, 128), F32),
            pltpu.VMEM((length, 128), F32),
        ]
        + scratch,
        compiler_params=params(40),
        cost_estimate=cost(12, 8),
        name="attend_back",
    )(*ins, *onto)
    return got[0], got[1:3], got[3] if final else None


def norm_back_body(
    start, core, tokens, grad_normed, grad_middle, gain, held, other, high, low, own, sem
):
    length = high.shape[0] // 2
    r = pl.program_id(0)
    hat, root = norm_parts(tokens[...].astype(F32))
    value = grad_middle[...] + norm_pull(grad_normed[...], hat, root, gain[...])
    top = value.astype(BF)
    rest = (value - top.astype(F32)).astype(BF)
    for base in (0, length):
        at = pl.ds(pl.multiple_of(base + r * QB, QB), QB)
        high[at, :] = top
        low[at, :] = rest

    @pl.when(r == pl.num_programs(0) - 1)
    def _():
        count = own.shape[0] // QB
        for k in range(count):
            own[k * QB : k * QB + QB, :] = turned([high, low], start[0], k)
        copy = pltpu.make_async_copy(own, held.at[core[0]], sem)
        copy.start()
        for k in range(count):
            other[k * QB : k * QB + QB, :] = turned([high, low], start[0], k + count)
        copy.wait()


def norm_back(start, core, tokens, grad_normed, grad_middle, gain):
    length, depth = tokens.shape
    half = (length // 2, depth)
    return pl.pallas_call(
        norm_back_body,
        grid=(length // QB,),
        in_specs=[smem_spec()] * 2 + [row_spec(depth, QB)] * 3 + [whole_spec((1, depth))],
        out_specs=[any_spec(), whole_spec(half)],
        out_shape=[pltpu.HBM((2,) + half, F32), SDS(half, F32)],
        scratch_shapes=[
            pltpu.VMEM((2 * length, depth), BF),
            pltpu.VMEM((2 * length, depth), BF),
            pltpu.VMEM(half, F32),
            pltpu.SemaphoreType.DMA,
        ],
        compiler_params=params(24),
        cost_estimate=cost(4, 16),
        name="norm_back",
    )(start, core, *in_hbm([tokens, grad_normed, grad_middle]), gain)


def split_far_body(counts, me, *refs):
    keep, send = refs[-2:]
    far = me[0] // 4
    begin = 0
    for count in counts:
        pieces, refs = refs[:count], refs[count:]
        cols = pl.ds(begin, pieces[0].shape[-1])
        begin += pieces[0].shape[-1]
        for k, out in enumerate((keep, send)):
            for slot in range(2):
                at = lax.bitwise_xor(far, k + 2 * slot)
                total = pieces[0][at].astype(F32)
                for piece in pieces[1:]:
                    total = total + piece[at].astype(F32)
                out[slot, :, cols] = total.astype(BF)


def split_far(me, groups):
    width, specs = 0, []
    for pieces in groups:
        far, block, columns = pieces[0].shape[-3:]
        width += columns
        for piece in pieces:
            if piece.ndim == 4:
                specs.append(pl.BlockSpec((None, far, block, columns), lambda i: (0, 0, 0, 0)))
            else:
                specs.append(whole_spec(piece.shape))
    return pl.pallas_call(
        functools.partial(split_far_body, [len(pieces) for pieces in groups]),
        grid=(1,),
        in_specs=[smem_spec()] + specs,
        out_specs=[whole_spec((2, block, width))] * 2,
        out_shape=[SDS((2, block, width), BF)] * 2,
        compiler_params=params(16),
        cost_estimate=cost(1, 2),
        name="split_far",
    )(me, *[piece for pieces in groups for piece in pieces])


def put_sums(ref, base, total):
    high = total.astype(BF)
    ref[base : base + 4, :] = high
    ref[base + 4 : base + 8, :] = (total - high.astype(F32)).astype(BF)
    ref[base + 8 : base + 16, :] = jnp.zeros((8, total.shape[1]), BF)


def get_sums(ref, base):
    return ref[base : base + 4, :].astype(F32) + ref[base + 4 : base + 8, :].astype(F32)


def last_join_body(own, other, own_last, other_last, sums, sums_away, keep, send):
    total = sums[...] + sums_away[...]
    rows = keep.shape[0] // 2
    width = own.shape[-1]
    for k in range(4):
        out = keep if k < 2 else send
        at = slice((k % 2) * rows, (k % 2 + 1) * rows)
        value = (own[k].astype(F32) + other[k].astype(F32)).astype(BF)
        out[at, :width] = value.reshape(rows, -1)
        value = (own_last[k].astype(F32) + other_last[k].astype(F32)).astype(BF)
        out[at, width:] = value.reshape(rows, -1)
    put_sums(send, 2 * rows, total)


def last_half_body(keep, send, near, rest, send_next):
    rows = rest.shape[0]
    value = keep[:rows, :].astype(F32) + near[:rows, :].astype(F32)
    rest[...] = value.astype(BF)
    value = keep[rows:, :].astype(F32) + near[rows : 2 * rows, :].astype(F32)
    send_next[:rows, :] = value.astype(BF)
    send_next[rows : rows + 16, :] = send[2 * rows :, :]
    send_next[rows + 16 :, :] = near[2 * rows :, :]


def last_split_body(flip, me, rest, send, away, keep, out_send):
    far = me[0] // 4
    rows = rest.shape[0]
    block = rows // 4
    for k, out in enumerate((keep, out_send)):
        for slot in range(2):
            at = pl.ds(pl.multiple_of(lax.bitwise_xor(far, k + 2 * slot) * block, 16), block)
            total = rest[at, :].astype(F32) + away[at, :].astype(F32)
            out[slot * block : (slot + 1) * block, :] = total.astype(BF)
    first, second = get_sums(send, rows + 16), get_sums(away, rows)
    swapped = lax.bitwise_xor(me[1], flip) == 1
    one, two = jnp.where(swapped, second, first), jnp.where(swapped, first, second)
    total = (get_sums(send, rows) + one) + (two + get_sums(away, rows + 16))
    put_sums(keep, 2 * block, total)
    put_sums(out_send, 2 * block, total)


def last_middle_body(keep, near, rest, send):
    block = (keep.shape[0] - 16) // 2
    value = keep[:block, :].astype(F32) + near[:block, :].astype(F32)
    rest[:block, :] = value.astype(BF)
    value = keep[block : 2 * block, :].astype(F32) + near[block : 2 * block, :].astype(F32)
    send[:block, :] = value.astype(BF)
    total = get_sums(keep, 2 * block) + get_sums(near, 2 * block)
    put_sums(rest, block, total)
    put_sums(send, block, total)


def last_sum_body(rest, away, first, grad_qkv, sums):
    block = rest.shape[0] - 16
    value = rest[:block, :].astype(F32) + away[:block, :].astype(F32)
    parts = [first[:, 384:], value[:, :384], value[:, 384:]]
    for which in range(3):
        cols = slice(which * 128, which * 128 + 128)
        grad_qkv[which] = jnp.concatenate([part[:, cols] for part in parts], 1)
    sums[...] = get_sums(rest, block) + get_sums(away, block)


def pack_body(part, out, up, down, packed):
    width = out.shape[1]
    packed[:, :width] = out[...]
    for s in range(up.shape[1] // part):
        cols = slice(s * part, (s + 1) * part)
        packed[:, width + 2 * s * part : width + (2 * s + 1) * part] = up[:, cols]
        packed[:, width + (2 * s + 1) * part : width + (2 * s + 2) * part] = down[:, cols]


def small_call(body, name, outs, scalars, values):
    return pl.pallas_call(
        body,
        in_specs=[smem_spec()] * len(scalars) + [vmem_spec()] * len(values),
        out_specs=[vmem_spec()] * len(outs),
        out_shape=outs,
        compiler_params=params(16),
        cost_estimate=cost(1, 3),
        name=name,
    )(*scalars, *values)


def swap(value):
    return lax.ppermute(value, "mp", [(0, 1), (1, 0)])


def tie(*values):
    return lax.optimization_barrier(values)


def hop(value, mask, count):
    return lax.ppermute(value, "dp", [(i, i ^ mask) for i in range(count)])


def hops(value, masks, count):
    return [(value, functools.partial(hop, mask=m, count=count)) for m in masks]


def hop_apart(value, masks, count):
    pairs = [(2 * i + c, 2 * (i ^ masks[c]) + c) for i in range(count) for c in range(2)]
    return lax.ppermute(value, ("dp", "mp"), pairs)


def far_hops(rows, values):
    return [
        (v, functools.partial(hop, mask=rows.near * m, count=rows.dp_count))
        for m, v in zip(range(1, rows.far), values)
    ]


def swaps(values):
    return [(v, swap) for v in values]


def send_all(requests):
    return [send(value) for value, send in requests]


def low_sum(values):
    total = values[0].astype(F32)
    for value in values[1:]:
        total = total + value.astype(F32)
    return total


class Flow:
    def __init__(self, me):
        self.me = me
        self.active = []

    def add(self, transfer, name, results, seeds=()):
        self.active.append([transfer, list(seeds), name, results])

    def step(self, *pivots, gate=None):
        values = [v for item in self.active for v in item[1]]
        tied = list(tie(self.me, *pivots, *values))
        self.me = tied.pop(0)
        pivots, tied = tied[: len(pivots)], tied[len(pivots) :]
        going, self.active, requests = self.active, [], []
        for item in going:
            transfer, values, name, results = item
            got, tied = tied[: len(values)], tied[len(values) :]
            try:
                if callable(transfer):
                    item[0] = transfer(*got)
                    asked = next(item[0])
                else:
                    asked = transfer.send(got)
                self.active.append(item)
                requests.append(asked)
            except StopIteration as stop:
                results[name] = stop.value
        gates = gate() if gate else []
        operands = [operand for asked in requests for operand, _ in asked]
        tied = list(tie(self.me, *gates, *operands))
        self.me = tied[0]
        tied = tied[1 + len(gates) :]
        for item, asked in zip(self.active, requests):
            item[1] = [send(operand) for (_, send), operand in zip(asked, tied)]
            tied = tied[len(asked) :]
        return pivots


def add_low(a, b):
    return (a.astype(F32) + b.astype(F32)).astype(BF)


def on_device(
    tokens, segment, ln1_gain, ln1_bias, w_qkv, w_out, ln2_gain, ln2_bias, w_up, w_down, cotangent
):
    dp_count = lax.axis_size("dp")
    core = lax.axis_index("mp")
    me = jnp.stack([lax.axis_index("dp"), core]).astype(jnp.int32)
    here, depth = tokens.shape[2], tokens.shape[3]
    length = 2 * here
    rows = Rows(dp_count, depth)

    groups = w_qkv.shape[2] // 128
    part = 384
    subs = w_up.shape[1] // part
    cut = subs // 2
    qkv = [w_qkv[:, :, g * 128 : (g + 1) * 128].reshape(-1, part) for g in range(groups)]
    shards = {"q": jnp.concatenate(qkv, 1)}

    def pack(out, up, down):
        return small_call(
            functools.partial(pack_body, part),
            "pack",
            [SDS((up.shape[0], out.shape[0] + 2 * up.shape[1]), BF)],
            [],
            [out.T, up, down.T],
        )[0]

    seg = lax.dynamic_index_in_dim(segment[:, 0], core, 0, keepdims=False)
    run = length * 3 // 4
    begin = jnp.argmax(seg[: length - run + 1] == seg[run - 1 :]).astype(jnp.int32)
    start = ((begin - here * core) % length).reshape(1)
    back = (length - start) % length
    seg_tail = lax.dynamic_slice_in_dim(jnp.concatenate([seg, seg]), begin + run, length - run)
    seg_col = seg_tail.reshape(-1, 1)
    seg_row = seg_tail.reshape(1, -1)
    gain1, bias1, gain2, bias2 = (
        v.reshape(1, -1) for v in (ln1_gain, ln1_bias, ln2_gain, ln2_bias)
    )

    flow = Flow(me)
    core_place = core.astype(jnp.int32).reshape(1)
    token_halves = [tokens[:, 0], swap(tokens[:, 0])]
    cot_halves = [cotangent[:, 0], swap(cotangent[:, 0])]
    wide = 2 * part
    qkv_pieces = [Piece(rows, "slabs")] + [Piece(rows, "slabs", part * g) for g in range(groups - 1)]
    out_piece = Piece(rows, "slabs")
    feed_pieces = [Piece(rows, "slabs", part + wide * s) for s in range(cut)]
    feed_pieces += [Piece(rows, "slabs", wide * s) for s in range(subs - cut)]
    feed_outs = [
        Piece(rows, "stack", 0, wide, s // cut) for s in range(subs)
    ]
    qkv_outs = [Piece(rows, "stack", part, wide, 0)]
    qkv_outs += [Piece(rows, "stack", 0, part, 1)] * (groups - 1)
    far = lax.axis_index("dp") // rows.near

    def gather_whole(shard):
        return lax.all_gather(shard, "dp", axis=0, tiled=True).reshape(rows.shape + (-1,))

    def fetch_near(near):
        got = yield hops(near, MASKS[1:], dp_count)
        own = [near] + got
        return own + [swap(x) for x in own]

    def via(mask):
        return functools.partial(hop, mask=mask, count=dp_count)

    def fetch_wide(shard, away):
        near, both_ways = yield [(shard, via(4)), (away, via(4))]
        (a0,) = arrange(rows, flow.me, [shard, near, away, both_ways], [shard.shape[1]])
        a1, a2, b0, away = yield [(a0, via(1)), (a0, via(2))] + swaps([a0]) + [(shard_c, via(8))]
        a3, b1, b2, near, both_ways = yield (
            [(a1, via(2))] + swaps([a1, a2]) + [(shard_c, via(4)), (away, via(4))]
        )
        slabs["a"] = [a0, a1, a2, a3, b0, b1, b2, swap(a3)]
        (c0,) = arrange(rows, flow.me, [shard_c, near, away, both_ways], [shard_c.shape[1]])
        (d0,) = yield swaps([c0])
        c1, c2 = yield [(c0, via(1)), (c0, via(2))]
        c3, d1, d2 = yield [(c2, via(1))] + swaps([c1, c2])
        return [c0, c1, c2, c3, d0, d1, d2, swap(c3)]

    def whole(shard):
        own = gather_whole(shard)
        return [own, swap(own)]

    def apart(flip):
        masks = (2, 1) if flip else (1, 2)
        return functools.partial(hop_apart, masks=masks, count=dp_count)

    def halve(flip, hurry, pause, own, other):
        if hurry:
            other = swap(other)
        else:
            (other,) = yield swaps([other])
        if pause:
            yield []
        keep, send = (low_sum([own[k : k + 2], other[k : k + 2]]).astype(BF) for k in (0, 2))
        (near,) = yield [(send, apart(flip))]
        (away,) = yield [(low_sum([keep[1], near[1]]).astype(BF), apart(1 - flip))]
        return [keep, near, away]

    def reduce_far(groups):
        keep, send = split_far(flow.me, groups)
        (near,) = yield [(send, via(4))]
        (away,) = yield [(low_sum([keep[1], near[1]]).astype(BF), via(8))]
        return low_sum([keep[0], near[0], away])

    def reduce_all(flip, own, other):
        group = yield from halve(flip, True, False, own, other)
        return (yield from reduce_far([sums_of[s] for s in range(subs - 1)] + [group]))

    def reduce_last(flip, own, own_last, other_last, sums):
        other_last, sums_away = swap(other_last), swap(sums)
        rows_here = rows.far * rows.block
        keep, send = small_call(
            last_join_body,
            "last_join",
            [SDS((2 * rows_here, wide), BF), SDS((2 * rows_here + 16, wide), BF)],
            [],
            [own, sums_of["other"], own_last, other_last, sums, sums_away],
        )
        (near,) = yield [(send, apart(flip))]
        return [keep, send, near]

    def exchange(value):
        (got,) = yield swaps([value])
        return got

    def reduce_one(flip, own, other):
        group = yield from halve(flip, False, False, own, other)
        return (yield from reduce_far([group]))

    def plain(own, other):
        value = low_sum([own, swap(other)]).astype(BF).reshape(depth, -1)
        return lax.psum_scatter(value, "dp", scatter_dimension=0, tiled=True).astype(F32)

    def run(transfer):
        requests = next(transfer)
        while True:
            try:
                requests = transfer.send(send_all(requests))
            except StopIteration as stop:
                return stop.value

    slabs, forward = {}, []

    def project(g):
        name = "q0" if g == 0 else "q1"
        forward.append(
            project_attend(qkv_pieces[g], flow.me, normed, seg_col, seg_row, slabs[name])
        )

    if rows.split:
        shard_q = shards["q"]
        got = send_all(far_hops(rows, [shard_q] * (rows.far - 1)))
        prepared = prepare(start, core_place, *token_halves, gain1, bias1)
        tied = tie(*got, *prepared, w_out, w_up, w_down)
        got, prepared = tied[:3], tied[3:6]
        shard_a = pack(*tied[6:])
        near_q0, near_q1 = arrange(rows, me, [shard_q] + list(got), [part, wide])
        own = [near_q0] + [hop(near_q0, m, dp_count) for m in MASKS[1:]]
        first_cols = part + wide * cut
        shard_c, shard_a = shard_a[:, first_cols:], shard_a[:, :first_cols]
        away_a = hop(shard_a, 8, dp_count)
        start_cot, _ = tie(start, near_q0)
        turned_cot = turn(start_cot, core_place, *cot_halves)
        tied = tie(*own, *turned_cot)
        own, turned_cot = tied[:4], tied[4:]
        slabs["q0"] = list(own) + [swap(v) for v in own]
        flow.add(fetch_near, "q1", slabs, [near_q1])
        flow.add(fetch_wide, "c", slabs, [shard_a, away_a])
        flow.step(own[3])
    else:
        shard_a = pack(w_out, w_up, w_down)
        for name, shard in (
            ("q0", shards["q"][:, :part]),
            ("q1", shards["q"][:, part:]),
            ("a", shard_a[:, : part + wide * cut]),
            ("c", shard_a[:, part + wide * cut :]),
        ):
            slabs[name] = whole(shard)
        prepared = prepare(start, core_place, *token_halves, gain1, bias1)
        turned_cot = turn(start, core_place, *cot_halves)
    x, normed, normed_t = prepared
    cot, cot_t = turned_cot
    for g in range(groups):
        project(g)
        flow.step(forward[g][2])
    atts = [f[1] for f in forward]
    middle, normed_ffn, normed_ffn_t = out_norm(
        out_piece, flow.me, x, gain2, bias2, atts, slabs["a"]
    )
    flow.step(normed_ffn)

    held = None
    sums_of = {}
    onto = []
    feed_names = ["a"] * cut + ["c"] * (subs - cut)
    for s in range(subs):
        final = s == subs - 1
        grads, held = feed_forward(
            feed_pieces[s],
            feed_outs[s],
            flow.me,
            normed_ffn,
            normed_ffn_t,
            cot,
            cot_t,
            held,
            slabs[feed_names[s]],
            [],
            (out_piece, slabs["a"], middle, gain2, groups) if final else None,
        )
        flip = s // cut
        if not rows.split:
            sums_of[s] = plain(*grads)
        elif final:
            flow.add(functools.partial(reduce_all, flip), "feed", sums_of, grads)
        else:
            flow.add(functools.partial(halve, flip, False, s == 0), s, sums_of, grads)
        if s == 1 and rows.split:
            flow.step(held[1], gate=lambda: slabs["c"][-1:])
        elif not final:
            flow.step(held[1])
    mixed, grad_middle, branch_t, sums2, *grad_atts = held
    flow.step(sums2)
    grad_projs = []
    onto = []

    held = None
    qkv_slabs = [slabs["q0"]] + [slabs["q1"]] * (groups - 1)
    for g in range(groups):
        proj, att, inverse, kept = forward[g]
        held, grads, sums1 = attend_back(
            qkv_pieces[g],
            qkv_outs[g],
            flow.me,
            normed_t,
            proj,
            att,
            grad_atts[g],
            inverse,
            kept,
            qkv_slabs[g],
            branch_t,
            atts if g == 0 else [],
            held,
            x if g == groups - 1 else None,
            onto,
        )
        if g == 0 and rows.split:
            flow.add(functools.partial(reduce_one, 0), "first", sums_of, grads)
        elif g == 0:
            sums_of["first"] = plain(*grads)
        elif g < groups - 1 and rows.split:
            flow.add(exchange, "other", sums_of, grads[1:])
            own_early = grads[0]
        elif not rows.split:
            sums_of[("last", g)] = plain(*grads)
        if g < groups - 1:
            flow.step(held)
    sums = jnp.concatenate([sums1[:2], sums2[:2]], 0)
    if rows.split:
        flow.add(
            functools.partial(reduce_last, 1), "last", sums_of, [own_early, *grads, sums]
        )
        (held,) = flow.step(held)
    start_late, _ = tie(back, flow.me)
    tokens_held, tokens_other = norm_back(start_late, core_place, x, held, grad_middle, gain1)
    mixed, tokens_other = tie(mixed, tokens_other)
    mixed_held, mixed_other = turn_back(back, core_place, mixed)
    mixed_got = swap(mixed_other)
    tokens_held, tokens_other = flow.step(tokens_held, tokens_other)
    if rows.split:
        block = rows.block
        keep, send, near = sums_of["last"]
        rows_here = rows.far * block
        rest, send = small_call(
            last_half_body,
            "last_half",
            [SDS((rows_here, wide), BF), SDS((rows_here + 32, wide), BF)],
            [],
            [keep, send, near],
        )
        away = apart(0)(send)
        keep, send = small_call(
            functools.partial(last_split_body, 1),
            "last_split",
            [SDS((2 * block + 16, wide), BF)] * 2,
            [flow.me],
            [rest, send, away],
        )
        flow.step(gate=lambda: [send])
        near = hop(send, 4, dp_count)
        rest, send = small_call(
            last_middle_body, "last_middle", [SDS((block + 16, wide), BF)] * 2, [], [keep, near]
        )
        rest, mixed_got, feed_sum = tie(rest, mixed_got, sums_of["feed"])
        away = hop(send, 8, dp_count)
        while flow.active:
            flow.step()
        grad_qkv, norm_sums = small_call(
            last_sum_body,
            "last_sum",
            [SDS((3, block, part), F32), SDS((4, depth), F32)],
            [],
            [rest, away, sums_of["first"]],
        )
        grad_qkv = grad_qkv.transpose(1, 0, 2)
        grad_out = sums_of["first"][:, :part].T
        feed_sums = [feed_sum]
    else:
        early = sums_of["first"]
        parts = [early[:, part:]] + [sums_of[("last", g)] for g in range(1, groups)]
        grad_qkv = jnp.concatenate([r.reshape(-1, 3, 128) for r in parts], 2)
        grad_out = early[:, :part].T
        feed_sums = [sums_of[s] for s in range(subs)]
        norm_sums = jnp.sum(lax.all_gather(sums + swap(sums), "dp", axis=0), 0)
    feed_sum = jnp.concatenate(feed_sums, 1) if len(feed_sums) > 1 else feed_sums[0]
    feed_list = [feed_sum[:, wide * s : wide * (s + 1)] for s in range(subs)]

    return (
        place(core_place, mixed_held, mixed_got)[:, None],
        place(core_place, tokens_held, swap(tokens_other))[:, None],
        norm_sums[0],
        norm_sums[1],
        grad_qkv,
        grad_out,
        norm_sums[2],
        norm_sums[3],
        jnp.concatenate([r[:, :part] for r in feed_list], 1),
        jnp.concatenate([r[:, part:] for r in feed_list], 1).T,
    )


def solution(mesh):
    in_specs = (
        P(None, "dp", "mp", None),
        P(None, "dp", None),
        P(),
        P(),
        P("dp", None, "mp"),
        P("mp", "dp"),
        P(),
        P(),
        P("dp", "mp"),
        P("mp", "dp"),
        P(None, "dp", "mp", None),
    )
    out_specs = (
        P(None, "dp", "mp", None),
        P(None, "dp", "mp", None),
        P(),
        P(),
        P("dp", None, "mp"),
        P("mp", "dp"),
        P(),
        P(),
        P("dp", "mp"),
        P("mp", "dp"),
    )
    return jax.shard_map(
        on_device, mesh=mesh, in_specs=in_specs, out_specs=out_specs, check_vma=False
    )
```

```python
import functools
import math

import jax
import jax.numpy as jnp
from jax import lax
from jax.experimental import pallas as pl
from jax.experimental.pallas import tpu as pltpu
from jax.sharding import PartitionSpec as P

HD = 32
QB = 256
EPS = 1e-05
BF = jnp.bfloat16
F32 = jnp.float32
NEG = -1e30
SCALE = 1.0 / math.sqrt(HD)
LOG2E = math.log2(math.e)
C2 = SCALE * LOG2E
MIB = 1024 * 1024
SDS = jax.ShapeDtypeStruct


def nn(a, b):
    return lax.dot_general(a, b, (((1,), (0,)), ((), ())), preferred_element_type=F32)


def nt(a, b):
    return lax.dot_general(a, b, (((1,), (1,)), ((), ())), preferred_element_type=F32)


def params(mib):
    return pltpu.CompilerParams(vmem_limit_bytes=mib * MIB)


def in_hbm(values):
    return [pltpu.with_memory_space_constraint(v, pltpu.HBM) for v in values]


def in_vmem(values):
    return [pltpu.with_memory_space_constraint(v, pltpu.VMEM) for v in values]


def cost(gflop, mbytes):
    return pl.CostEstimate(flops=int(gflop * 1e9), bytes_accessed=int(mbytes * 1e6), transcendentals=0)


def any_spec():
    return pl.BlockSpec(memory_space=pl.ANY)


def smem_spec():
    return pl.BlockSpec(memory_space=pltpu.SMEM)


def vmem_spec():
    return pl.BlockSpec(memory_space=pltpu.VMEM)


def row_spec(width, rows=512):
    return pl.BlockSpec((rows, width), lambda r: (r, 0))


def column_spec(height, rows=512):
    return pl.BlockSpec((height, rows), lambda r: (0, r))


def whole_spec(shape):
    return pl.BlockSpec(shape, lambda r: tuple(0 for _ in shape))


MASKS = (0, 1, 2, 3)


class Rows:
    def __init__(self, dp_count, depth):
        self.dp_count = dp_count
        self.depth = depth
        self.split = (depth // dp_count) % 16 == 0 and dp_count == 16
        self.near = 4 if self.split else 1
        self.far = dp_count // 4 if self.split else 1
        self.block = depth // (self.near * self.far)
        self.shape = (self.far, self.near, self.block)


class Piece:
    def __init__(self, rows, kind, start=0, width=0, flip=0):
        self.rows = rows
        self.flip = flip
        self.kind = kind if rows.split else "whole"
        self.start = start
        self.count = 2 * len(MASKS) if self.kind == "slabs" else 2
        if self.kind == "stack":
            self.shape = (len(MASKS), rows.far, rows.block, width)
        else:
            self.shape = rows.shape + (width,)


def piece_copies(piece, me, refs, moves, sem, outward):
    copies = []
    each = piece.count // 2
    for half, column, width, view in moves:
        cols = pl.ds(piece.start + column, width)
        if piece.kind == "whole":
            pairs = [(refs[half].at[:, :, :, cols], view)]
        else:
            pairs = []
            order = lax.bitwise_xor(me[1], piece.flip ^ half)
            masks = (0, 2 - order, 1 + order, 3) if piece.kind == "stack" else MASKS
            for k, mask in enumerate(masks):
                ref = refs[half].at[k] if piece.kind == "stack" else refs[half * each + k]
                near = lax.bitwise_xor(lax.rem(me[0], 4), mask)
                pairs.append((ref.at[:, :, cols], view.at[:, near]))
        for outside, inside in pairs:
            if outward:
                copies.append(pltpu.make_async_copy(inside, outside, sem))
            else:
                copies.append(pltpu.make_async_copy(outside, inside, sem))
    return copies


def start_all(copies):
    for copy in copies:
        copy.start()


def wait_bytes(ref, sem):
    pltpu.make_async_copy(ref, ref, sem).wait()


def flat(value):
    return value.reshape(-1, value.shape[-1])


def head_row(h):
    return lax.broadcasted_iota(jnp.int32, (1, 128), 1) // HD == h


def fill_bias(bias, seg_col, seg_row):
    key = lax.broadcasted_iota(jnp.int32, (QB, QB), 0)
    query = lax.broadcasted_iota(jnp.int32, (QB, QB), 1)
    bias[0] = jnp.where(query >= key, 0.0, NEG)
    bias[1] = jnp.where((query >= key) & (seg_col[...] == seg_row[...]), 0.0, NEG)


def turned(doubles, start, r):
    coarse = pl.multiple_of(start // 16 * 16 + r * QB, 16)
    fine = start % 16
    row = lax.broadcasted_iota(jnp.int32, (QB, QB + 16), 0)
    col = lax.broadcasted_iota(jnp.int32, (QB, QB + 16), 1)
    pick = jnp.where(col - row == fine, 1.0, 0.0).astype(BF)
    total = None
    for double in doubles:
        part = nn(pick, double[pl.ds(coarse, QB + 16), :])
        total = part if total is None else total + part
    return total


def norm_parts(values):
    centered = values - jnp.mean(values, axis=-1, keepdims=True)
    spread = jnp.mean(centered * centered, axis=-1, keepdims=True)
    root = lax.rsqrt(spread + EPS)
    return centered * root, root


def fill_double(double, core, own, other, sem):
    here = own.shape[1]
    for k, half in enumerate((own, other)):
        pltpu.make_async_copy(half.at[core], double.at[pl.ds(k * here, here)], sem).start()
    wait_bytes(double.at[pl.ds(0, 2 * here)], sem)
    double[2 * here :, :] = double[: 2 * here, :]


def prepare_body(start, core, own, other, gain, offset, x_out, normed_out, normed_t_out, double, x, normed, normed_t, sems):
    fill_double(double, core[0], own, other, sems.at[3])

    def step(r, carry):
        at = pl.ds(pl.multiple_of(r * QB, QB), QB)
        value = turned([double], start[0], r)
        x[at, :] = value.astype(BF)
        hat, _ = norm_parts(value)
        low = (hat * gain[...] + offset[...]).astype(BF)
        normed[at, :] = low
        normed_t[:, at] = low.T
        return carry

    lax.fori_loop(0, x.shape[0] // QB, step, 0)
    copies = [
        pltpu.make_async_copy(normed, normed_out, sems.at[0]),
        pltpu.make_async_copy(x, x_out, sems.at[1]),
        pltpu.make_async_copy(normed_t, normed_t_out, sems.at[2]),
    ]
    start_all(copies)
    for copy in copies:
        copy.wait()


def prepare(start, core, own, other, gain, offset):
    _, here, depth = own.shape
    shape, shape_t = (2 * here, depth), (depth, 2 * here)
    shapes = [shape, shape, shape_t]
    return pl.pallas_call(
        prepare_body,
        in_specs=[smem_spec()] * 2 + [any_spec()] * 2 + [vmem_spec()] * 2,
        out_specs=[any_spec()] * 3,
        out_shape=[pltpu.HBM(s, BF) for s in shapes],
        scratch_shapes=[pltpu.VMEM((4 * here, depth), BF)]
        + [pltpu.VMEM(s, BF) for s in shapes]
        + [pltpu.SemaphoreType.DMA((4,))],
        compiler_params=params(20),
        cost_estimate=cost(4, 8),
        name="prepare",
    )(start, core, *in_hbm([own, other]), gain, offset)


def turn_body(start, core, own, other, cot_out, cot_t_out, double, cot, cot_t, sems):
    fill_double(double, core[0], own, other, sems.at[2])

    def step(r, carry):
        at = pl.ds(pl.multiple_of(r * QB, QB), QB)
        low = turned([double], start[0], r).astype(BF)
        cot[at, :] = low
        cot_t[:, at] = low.T
        return carry

    lax.fori_loop(0, cot.shape[0] // QB, step, 0)
    copies = [
        pltpu.make_async_copy(cot, cot_out, sems.at[0]),
        pltpu.make_async_copy(cot_t, cot_t_out, sems.at[1]),
    ]
    start_all(copies)
    for copy in copies:
        copy.wait()


def turn(start, core, own, other):
    _, here, depth = own.shape
    shapes = [(2 * here, depth), (depth, 2 * here)]
    return pl.pallas_call(
        turn_body,
        in_specs=[smem_spec()] * 2 + [any_spec()] * 2,
        out_specs=[any_spec()] * 2,
        out_shape=[pltpu.HBM(s, BF) for s in shapes],
        scratch_shapes=[pltpu.VMEM((4 * here, depth), BF)]
        + [pltpu.VMEM(s, BF) for s in shapes]
        + [pltpu.SemaphoreType.DMA((3,))],
        compiler_params=params(16),
        cost_estimate=cost(4, 8),
        name="turn",
    )(start, core, *in_hbm([own, other]))


def turn_back_body(start, core, values, held, other, double, own, sem):
    here = other.shape[0]
    double[: 2 * here, :] = values[...]
    double[2 * here :, :] = values[...]
    count = here // QB

    def step(r, carry):
        at = pl.ds(pl.multiple_of(r * QB, QB), QB)
        own[at, :] = turned([double], start[0], r).astype(BF)
        other[at, :] = turned([double], start[0], r + count).astype(BF)
        return carry

    lax.fori_loop(0, count, step, 0)
    copy = pltpu.make_async_copy(own, held.at[core[0]], sem)
    copy.start()
    copy.wait()


def place_body(core, other, held, out, sem):
    copy = pltpu.make_async_copy(other, out.at[1 - core[0]], sem)
    copy.start()
    copy.wait()


def place(core, held, other):
    return pl.pallas_call(
        place_body,
        in_specs=[smem_spec(), any_spec(), any_spec()],
        out_specs=any_spec(),
        out_shape=pltpu.HBM(held.shape, held.dtype),
        input_output_aliases={2: 0},
        scratch_shapes=[pltpu.SemaphoreType.DMA],
        compiler_params=params(4),
        cost_estimate=cost(0, 4),
        name="place",
    )(core, other, *in_hbm([held]))


def turn_back(start, core, values):
    length, depth = values.shape
    half = (length // 2, depth)
    return pl.pallas_call(
        turn_back_body,
        in_specs=[smem_spec()] * 2 + [vmem_spec()],
        out_specs=[any_spec(), vmem_spec()],
        out_shape=[pltpu.HBM((2,) + half, BF), SDS(half, BF)],
        scratch_shapes=[
            pltpu.VMEM((2 * length, depth), BF),
            pltpu.VMEM(half, BF),
            pltpu.SemaphoreType.DMA,
        ],
        compiler_params=params(16),
        cost_estimate=cost(2, 4),
        name="turn_back",
    )(start, core, values)


def arrange_body(widths, me, *refs):
    pieces, outs = refs[:4], refs[4:]
    far = me[0] // 4
    for m, piece in enumerate(pieces):
        begin = 0
        for out, width in zip(outs, widths):
            out[lax.bitwise_xor(far, m)] = piece[:, begin : begin + width]
            begin += width


def arrange(rows, me, pieces, widths):
    return pl.pallas_call(
        functools.partial(arrange_body, widths),
        in_specs=[smem_spec()] + [vmem_spec()] * 4,
        out_specs=[vmem_spec()] * len(widths),
        out_shape=[SDS((rows.far, rows.block, w), BF) for w in widths],
        compiler_params=params(8),
        cost_estimate=cost(1, 1),
        name="arrange",
    )(me, *pieces)


KEPT = (0, 256, 768, 1536)
KEPT_ROWS = (256, 512, 768, 256)
ORDER = (2, 1, 0, 3)


def project_attend_body(piece, me, normed_in, seg_col, seg_row, *refs):
    slabs = refs[: piece.count]
    proj_out, att, inverse, kept_out, weight, proj, normed, bias = refs[piece.count : piece.count + 8]
    keys_m, values_t, att_t, kept, sem, out_sem, kept_sem = refs[piece.count + 8 :]
    normed_copy = pltpu.make_async_copy(normed_in, normed, out_sem)
    normed_copy.start()
    moves = [(half, 0, 384, weight.at[:, :, :, pl.ds(384 * half, 384)]) for half in range(2)]
    start_all(piece_copies(piece, me, slabs, moves, sem, False))
    fill_bias(bias, seg_col, seg_row)
    values_t[...] = jnp.ones_like(values_t)
    normed_copy.wait()
    wait_bytes(weight, sem)

    for c in range(3):
        cols = slice(c * 256, c * 256 + 256)
        proj[:, cols] = nn(normed[...], flat(weight[:, :, :, cols])).astype(BF)
    proj_copy = pltpu.make_async_copy(proj, proj_out, out_sem)
    proj_copy.start()
    for half in range(2):
        flipped = proj[:, half * 384 + 256 : half * 384 + 384].T
        for h in range(4):
            values_t[half * 4 + h, 0:HD, :] = flipped[h * HD : (h + 1) * HD]

    units = [(h, i) for i in (2, 1, 0, 3) for h in range(4)]

    def step(half, carry):
        col = pl.multiple_of(half * 384, 128)
        for h in range(4):
            keys_m[h] = jnp.where(head_row(h), proj[:, pl.ds(col + 128, 128)], 0)

        def score(h, i):
            first = 768 if i == 3 else 0
            scores = nt(keys_m[h, first : (i + 1) * QB, :], proj[i * QB : (i + 1) * QB, pl.ds(col, 128)])
            edge = scores[-QB:] + bias[1 if i == 3 else 0]
            return jnp.concatenate([scores[:-QB], edge], 0) if scores.shape[0] > QB else edge

        ahead = score(*units[0])
        for k, (h, i) in enumerate(units):
            scores = ahead
            if k + 1 < len(units):
                ahead = score(*units[k + 1])
            first = 768 if i == 3 else 0
            last = (i + 1) * QB
            at = slice(i * QB, last)
            peak = jnp.max(scores, axis=0, keepdims=True) * C2
            probs = jnp.exp2(scores * C2 - peak).astype(BF)
            kept[half * 4 + h, KEPT[i] : KEPT[i] + last - first, :] = probs
            summed = nn(values_t[half * 4 + h, :, first:last], probs)
            share = 1.0 / summed[HD : HD + 1]
            att_t[pl.ds(pl.multiple_of(half * 128 + h * HD, HD), HD), at] = summed[:HD] * share
            inverse[pl.ds(half * 4 + h, 1), at] = share
            if h == 3:
                part = (pl.ds(half * 4, 4), pl.ds(KEPT[i], last - first))
                pltpu.make_async_copy(kept.at[part], kept_out.at[part], kept_sem).start()
        return carry

    lax.fori_loop(0, 2, step, 0)
    for half in range(2):
        cols = slice(half * 128, half * 128 + 128)
        att[:, cols] = att_t[cols, :].T.astype(BF)
    proj_copy.wait()
    wait_bytes(kept, kept_sem)


def project_attend(piece, me, normed, seg_col, seg_row, slabs):
    length, depth = normed.shape
    rows = piece.rows
    return pl.pallas_call(
        functools.partial(project_attend_body, piece),
        in_specs=[smem_spec(), any_spec()] + [vmem_spec()] * 2 + [any_spec()] * len(slabs),
        out_specs=[any_spec()] + [vmem_spec()] * 2 + [any_spec()],
        out_shape=[
            pltpu.HBM((length, 768), BF),
            pltpu.HBM((length, 256), BF),
            pltpu.HBM((8, length), F32),
            pltpu.HBM((8, 1792, QB), BF),
        ],
        scratch_shapes=[
            pltpu.VMEM(rows.shape + (768,), BF),
            pltpu.VMEM((length, 768), BF),
            pltpu.VMEM((length, depth), BF),
            pltpu.VMEM((2, QB, QB), F32),
            pltpu.VMEM((4, length, 128), BF),
            pltpu.VMEM((8, HD + 16, length), BF),
            pltpu.VMEM((256, length), F32),
            pltpu.VMEM((8, 1792, QB), BF),
            pltpu.SemaphoreType.DMA,
            pltpu.SemaphoreType.DMA,
            pltpu.SemaphoreType.DMA,
        ],
        compiler_params=params(32),
        cost_estimate=cost(8, 8),
        name="project_attend",
    )(me, *in_hbm([normed]), seg_col, seg_row, *in_hbm(slabs))


def join_heads(attended):
    return jnp.concatenate([a[:, :128] for a in attended] + [a[:, 128:] for a in attended], 1)


def out_norm_body(piece, groups, me, tokens, gain, offset, *refs):
    attended = refs[:groups]
    slabs = refs[groups : groups + piece.count]
    middle, normed, normed_t, weight, sem = refs[groups + piece.count :]
    width = weight.shape[3] // 2

    @pl.when(pl.program_id(0) == 0)
    def _():
        moves = [(half, 0, width, weight.at[:, :, :, pl.ds(width * half, width)]) for half in range(2)]
        start_all(piece_copies(piece, me, slabs, moves, sem, False))
        wait_bytes(weight, sem)

    value = tokens[...].astype(F32) + nt(join_heads([a[...] for a in attended]), flat(weight[...]))
    middle[...] = value
    hat, _ = norm_parts(value)
    low = (hat * gain[...] + offset[...]).astype(BF)
    normed[...] = low
    normed_t[...] = low.T


def out_norm(piece, me, tokens, gain, offset, attended, slabs):
    length, depth = tokens.shape
    return pl.pallas_call(
        functools.partial(out_norm_body, piece, len(attended)),
        grid=(length // 512,),
        in_specs=[smem_spec(), row_spec(depth), whole_spec((1, depth)), whole_spec((1, depth))]
        + [row_spec(256)] * len(attended)
        + [any_spec()] * len(slabs),
        out_specs=[row_spec(depth)] * 2 + [column_spec(depth)],
        out_shape=[
            pltpu.HBM((length, depth), F32),
            pltpu.VMEM((length, depth), BF),
            pltpu.VMEM((depth, length), BF),
        ],
        scratch_shapes=[pltpu.VMEM(piece.rows.shape + (depth,), BF), pltpu.SemaphoreType.DMA],
        compiler_params=params(28),
        cost_estimate=cost(3, 8),
        name="out_norm",
    )(me, *in_hbm([tokens]), gain, offset, *in_hbm(attended), *in_hbm(slabs))


def gelu_parts(values):
    size = jnp.abs(values)
    density = jnp.exp2(values * values * (-0.5 * LOG2E) + math.log2(1.0 / math.sqrt(2 * math.pi)))
    below = 1.0 + 0.2316419 * size
    t = pl.reciprocal(below, approx=True)
    t = t * (2.0 - below * t)
    poly = t * (
        0.319381530
        + t * (-0.356563782 + t * (1.781477937 + t * (-1.821255978 + t * 1.330274429)))
    )
    tail = density * poly
    below = jnp.where(values >= 0, 1.0 - tail, tail)
    return values * below, below + values * density


def norm_pull(grad, hat, root, gain):
    scaled = grad * gain
    first = jnp.mean(scaled, axis=-1, keepdims=True)
    second = jnp.mean(scaled * hat, axis=-1, keepdims=True)
    return root * (scaled - first - hat * second)


def feed_forward_body(
    piece, out_piece, turn, last_piece, groups, aliased, me, normed, normed_t, cot, cot_t, *refs
):
    refs = list(refs)
    first, second = turn == 0, turn == 1
    final = last_piece is not None
    held = [] if first else [refs.pop(0), refs.pop(0)]
    if final:
        middle, gain = refs.pop(0), refs.pop(0)
        out_slabs, refs = refs[: last_piece.count], refs[last_piece.count :]
    slabs, refs = refs[: piece.count], refs[piece.count + aliased :]
    outs, refs = refs[:2], refs[2:]
    mixed = refs.pop(0)
    if final:
        grad_middle_out, branch_t, sums = refs[:3]
        grad_att, refs = refs[3 : 3 + groups], refs[3 + groups :]
    else:
        grad_in = refs.pop(0)
    weight, staged, act, grad_hidden, sems = refs[:5]
    refs = refs[5:]
    if first:
        mixed_acc, grad_acc = mixed, grad_in
    else:
        mixed_acc, grad_acc, refs = refs[0], refs[1], refs[2:]
    if final:
        mixed_low, middle_here, out_weight, grad_middle = refs
    length, depth = normed.shape
    moves = []
    for half in range(2):
        for which in range(2):
            at = pl.ds(which * 768 + half * 384, 384)
            moves.append((half, which * 384, 384, at))
    into = [(h, c, w, weight.at[:, :, :, at]) for h, c, w, at in moves]
    outof = [(h, c, w, staged.at[:, :, :, at]) for h, c, w, at in moves]
    start_all(piece_copies(piece, me, slabs, into, sems.at[0], False))
    held_copies = []
    if not first and not second:
        held_copies.append(pltpu.make_async_copy(held[0], mixed_acc, sems.at[1]))
        held_copies.append(pltpu.make_async_copy(held[1], grad_acc, sems.at[2]))
    if final:
        held_copies.append(pltpu.make_async_copy(middle, middle_here, sems.at[4]))
    start_all(held_copies)
    if final:
        width = depth // 2
        views = [
            (half, 0, width, out_weight.at[:, :, :, pl.ds(width * half, width)]) for half in range(2)
        ]
        start_all(piece_copies(last_piece, me, out_slabs, views, sems.at[5], False))
    wait_bytes(weight, sems.at[0])
    chunks = [slice(c * 256, c * 256 + 256) for c in range(3)]

    def products(c):
        hidden = nn(normed[...], flat(weight[:, :, :, c * 256 : c * 256 + 256]))
        return hidden, nn(cot[...], flat(weight[:, :, :, 768 + c * 256 : 1024 + c * 256]))

    ahead = products(0)
    for c in range(3):
        hidden, grad_act = ahead
        if c < 2:
            ahead = products(c + 1)
        value, slope = gelu_parts(hidden)
        act[:, chunks[c]] = value.astype(BF)
        grad_hidden[:, chunks[c]] = (grad_act * slope).astype(BF)
    for copy in held_copies:
        copy.wait()
    for cols in chunks:
        mixed_part = nt(act[...], flat(weight[:, :, :, 768:1536])[cols])
        grad_part = nt(grad_hidden[...], flat(weight[:, :, :, 0:768])[cols])
        if not first:
            mixed_held, grad_held = held if second else (mixed_acc, grad_acc)
            mixed_part = mixed_part + mixed_held[:, cols]
            grad_part = grad_part + grad_held[:, cols]
        if final:
            mixed_low[:, cols] = (middle_here[:, cols] + mixed_part).astype(BF)
        else:
            mixed_acc[:, cols] = mixed_part
        grad_acc[:, cols] = grad_part
    if final:
        out_copies = [pltpu.make_async_copy(mixed_low, mixed, sems.at[1])]
        start_all(out_copies)
        wait_bytes(out_weight, sems.at[5])
        sums[...] = jnp.zeros_like(sums)

        def back_step(r, carry):
            at = pl.ds(pl.multiple_of(r * 512, 512), 512)
            hat, root = norm_parts(middle_here[at, :])
            grad = grad_acc[at, :]
            value = cot[at, :].astype(F32) + norm_pull(grad, hat, root, gain[...])
            grad_middle[at, :] = value
            low = value.astype(BF)
            branch_t[:, at] = low.T
            sums[0:1, :] += jnp.sum(grad * hat, axis=0, keepdims=True)
            sums[1:2, :] += jnp.sum(grad, axis=0, keepdims=True)
            back = nn(low, flat(out_weight[...])).astype(BF)
            for g in range(groups):
                grad_att[g][at, 0:128] = back[:, g * 128 : g * 128 + 128]
                grad_att[g][at, 128:256] = back[:, width + g * 128 : width + g * 128 + 128]
            return carry

        lax.fori_loop(0, length // 512, back_step, 0)
        out_copies.append(pltpu.make_async_copy(grad_middle, grad_middle_out, sems.at[2]))
        out_copies[-1].start()
    else:
        out_copies = []
        if not first:
            out_copies.append(pltpu.make_async_copy(mixed_acc, mixed, sems.at[1]))
            out_copies.append(pltpu.make_async_copy(grad_acc, grad_in, sems.at[2]))
        start_all(out_copies)
    for c in range(3):
        cols = slice(c * 256, c * 256 + 256)
        up = nn(normed_t[...], grad_hidden[:, cols]).astype(BF)
        staged[:, :, :, cols] = up.reshape(staged.shape[:3] + (256,))
        down = nn(cot_t[...], act[:, cols]).astype(BF)
        staged[:, :, :, 768 + c * 256 : 1024 + c * 256] = down.reshape(staged.shape[:3] + (256,))
    start_all(piece_copies(out_piece, me, outs, outof, sems.at[3], True))
    for copy in out_copies:
        copy.wait()
    wait_bytes(staged, sems.at[3])


def feed_forward(
    piece, out_piece, turn, me, normed, normed_t, cot, cot_t, held, slabs, onto, last=None
):
    length, depth = normed.shape
    rows = piece.rows
    first, final = turn == 0, last is not None
    ins = [me] + in_vmem([normed, normed_t, cot, cot_t])
    specs = [smem_spec()] + [vmem_spec()] * 4
    scratch = [
        pltpu.VMEM(rows.shape + (1536,), BF),
        pltpu.VMEM(rows.shape + (1536,), BF),
        pltpu.VMEM((length, 768), BF),
        pltpu.VMEM((length, 768), BF),
        pltpu.SemaphoreType.DMA((6,)),
    ]
    if not first:
        ins += in_vmem(held) if turn == 1 else in_hbm(held)
        specs += [vmem_spec() if turn == 1 else any_spec()] * 2
        scratch += [pltpu.VMEM((length, depth), F32)] * 2
    last_piece, groups = None, 0
    outs = [SDS(out_piece.shape, BF)] * 2
    out_specs = [any_spec()] * 2
    if final:
        last_piece, last_slabs, middle, gain, groups = last
        ins += in_hbm([middle]) + [gain] + in_hbm(last_slabs)
        specs += [any_spec(), vmem_spec()] + [any_spec()] * len(last_slabs)
        scratch += [
            pltpu.VMEM((length, depth), BF),
            pltpu.VMEM((length, depth), F32),
            pltpu.VMEM(rows.shape + (depth,), BF),
            pltpu.VMEM((length, depth), F32),
        ]
        outs += [pltpu.HBM((length, depth), BF), pltpu.HBM((length, depth), F32)]
        outs += [pltpu.VMEM((depth, length), BF), SDS((8, depth), F32)]
        outs += [pltpu.HBM((length, 256), BF)] * groups
        out_specs += [any_spec()] * 2 + [vmem_spec()] * (2 + groups)
    elif first:
        outs += [pltpu.VMEM((length, depth), F32)] * 2
        out_specs += [vmem_spec()] * 2
    else:
        outs += [pltpu.HBM((length, depth), F32)] * 2
        out_specs += [any_spec()] * 2
    got = pl.pallas_call(
        functools.partial(
            feed_forward_body, piece, out_piece, turn, last_piece, groups, len(onto)
        ),
        in_specs=specs + [any_spec()] * (piece.count + len(onto)),
        out_specs=out_specs,
        out_shape=outs,
        input_output_aliases={len(ins) + piece.count + k: k for k in range(len(onto))},
        scratch_shapes=scratch,
        compiler_params=params(48 if final else 32),
        cost_estimate=cost(14 if final else 11, 20),
        name="feed_forward",
    )(*ins, *in_hbm(slabs), *onto)
    return got[:2], got[2:]


def attend_back_body(piece, out_piece, extra, aliased, final, me, normed_t_in, proj, att, grad_att, inverse, kept_in, *refs):
    refs = list(refs)
    slabs, refs = refs[: piece.count], refs[piece.count :]
    if extra:
        branch_t = refs.pop(0)
        attended, refs = refs[:extra], refs[extra:]
    else:
        held = refs.pop(0)
    if final:
        tokens_in = refs.pop(0)
    refs = refs[aliased:]
    grad_normed, outs, refs = refs[0], refs[1:3], refs[3:]
    if final:
        sums = refs.pop(0)
    grad_proj, key_sum, value_sum = refs[:3]
    refs = refs[3:]
    kept, delta, keys_t, query_t, query_m, grad_m, staged, normed_t, total, weight, sems = refs[:11]
    for half in range(2):
        for i in ORDER:
            part = (pl.ds(half * 4, 4), pl.ds(KEPT[i], KEPT_ROWS[i]))
            sem = sems.at[5 + 4 * half + i]
            pltpu.make_async_copy(kept_in.at[part], kept.at[part], sem).start()
    copies = [pltpu.make_async_copy(normed_t_in, normed_t, sems.at[1])]
    if not extra:
        copies.append(pltpu.make_async_copy(held, total, sems.at[2]))
    if final:
        copies.append(pltpu.make_async_copy(tokens_in, refs[11], sems.at[3]))
    moves = [(half, 0, 384, weight.at[:, :, :, pl.ds(384 * half, 384)]) for half in range(2)]
    start_all(copies + piece_copies(piece, me, slabs, moves, sems.at[4], False))
    length = proj.shape[0]
    if extra:
        joined = join_heads([a[...] for a in attended])
        out_grad = nn(branch_t[...], joined).astype(BF)
        staged[:, :, :, 768:] = out_grad.reshape(staged.shape[:3] + (768,))
    for half in range(2):
        cols = slice(half * 128, half * 128 + 128)
        product = (grad_att[:, cols].astype(F32) * att[:, cols].astype(F32)).T
        for h in range(4):
            stat = slice(half * 4 + h, half * 4 + h + 1)
            total_here = jnp.sum(product[h * HD : (h + 1) * HD], axis=0, keepdims=True)
            delta[stat, :] = total_here * inverse[stat, :]
        keys_t[cols, :] = proj[:, half * 384 + 128 : half * 384 + 256].T

    def step(half, carry):
        col = pl.multiple_of(half * 384, 128)
        out = pl.multiple_of(half * 128, 128)
        share = jnp.concatenate(
            [jnp.broadcast_to(inverse[pl.ds(half * 4 + h, 1), :], (HD, length)) for h in range(4)], 0
        ).T
        grads = (grad_att[:, pl.ds(out, 128)].astype(F32) * share).astype(BF)
        for h in range(4):
            mine = head_row(h)
            query_m[h] = jnp.where(mine, proj[:, pl.ds(col, 128)], 0)
            grad_m[h] = jnp.where(mine, grads, 0)
        key_sum[...] = jnp.zeros_like(key_sum)
        value_sum[...] = jnp.zeros_like(value_sum)
        for i in (2, 1, 0, 3):
            first = 768 if i == 3 else 0
            last = (i + 1) * QB
            here = slice(first, last)
            there = slice(i * QB, last)
            values = proj[here, pl.ds(col + 256, 128)]
            rows_here = slice(KEPT[i], KEPT[i] + last - first)
            wait_bytes(
                kept.at[pl.ds(half * 4, 4), pl.ds(KEPT[i], KEPT_ROWS[i])], sems.at[5 + 4 * half + i]
            )
            all_probs, all_grads = [], []
            ahead = nt(values, grad_m[0, there, :])
            for h in range(4):
                grad_probs = ahead
                if h < 3:
                    ahead = nt(values, grad_m[h + 1, there, :])
                stat = pl.ds(half * 4 + h, 1)
                lanes = pl.ds(pl.multiple_of(half * 128 + h * HD, HD), HD)
                probs = kept[half * 4 + h, rows_here, :]
                grad_scores = (probs.astype(F32) * (grad_probs - delta[stat, there])).astype(BF)
                all_probs.append(probs)
                all_grads.append(grad_scores)
                query_t[lanes, there] = nn(keys_t[lanes, here], grad_scores)
            stacked = jnp.concatenate([grad_m[h, there, :] for h in range(4)], 0)
            value_sum[here, :] += nn(jnp.concatenate(all_probs, 1), stacked)
            stacked = jnp.concatenate([query_m[h, there, :] for h in range(4)], 0)
            key_sum[here, :] += nn(jnp.concatenate(all_grads, 1), stacked)
        grad_proj[:, pl.ds(col + 128, 128)] = (key_sum[...] * SCALE).astype(BF)
        grad_proj[:, pl.ds(col + 256, 128)] = value_sum[...].astype(BF)
        return carry

    lax.fori_loop(0, 2, step, 0)
    for half in range(2):
        grad_proj[:, half * 384 : half * 384 + 128] = (
            query_t[half * 128 : half * 128 + 128, :].T * SCALE
        ).astype(BF)
    for copy in copies:
        copy.wait()
    wait_bytes(weight, sems.at[4])
    for c in range(3):
        cols = slice(c * 256, c * 256 + 256)
        part = nn(normed_t[...], grad_proj[:, cols]).astype(BF)
        staged[:, :, :, cols] = part.reshape(staged.shape[:3] + (256,))
    moves = [(half, 0, 384, staged.at[:, :, :, pl.ds(384 * half, 384)]) for half in range(2)]
    if extra:
        moves += [
            (half, -384, 384, staged.at[:, :, :, pl.ds(768 + 384 * half, 384)]) for half in range(2)
        ]
    start_all(piece_copies(out_piece, me, outs, moves, sems.at[0], True))
    if final:
        sums[...] = jnp.zeros_like(sums)

    total_copies = []
    for c in range(3):
        cols = slice(c * 256, c * 256 + 256)
        value = nt(grad_proj[...], flat(weight[...])[cols])
        if not extra:
            value = value + total[:, cols]
        total[:, cols] = value
        total_copies.append(
            pltpu.make_async_copy(
                total.at[:, pl.ds(c * 256, 256)], grad_normed.at[:, pl.ds(c * 256, 256)], sems.at[2]
            )
        )
        total_copies[-1].start()
    if final:

        def sum_step(r, carry):
            at = pl.ds(pl.multiple_of(r * QB, QB), QB)
            value = total[at, :]
            hat, _ = norm_parts(refs[11][at, :].astype(F32))
            sums[0:1, :] += jnp.sum(value * hat, axis=0, keepdims=True)
            sums[1:2, :] += jnp.sum(value, axis=0, keepdims=True)
            return carry

        lax.fori_loop(0, length // QB, sum_step, 0)
    wait_bytes(staged, sems.at[0])
    wait_bytes(total, sems.at[2])


def attend_back(
    piece,
    out_piece,
    me,
    normed_t,
    proj,
    att,
    grad_att,
    inverse,
    kept,
    slabs,
    branch_t,
    attended,
    held,
    tokens,
    onto,
):
    depth, length = normed_t.shape
    extra = len(attended)
    final = tokens is not None
    columns = 1536 if extra else 768
    ins = [me] + in_hbm([normed_t, proj, att, grad_att, inverse, kept]) + in_hbm(slabs)
    specs = [smem_spec(), any_spec()] + [vmem_spec()] * 4 + [any_spec()] * (1 + len(slabs))
    if extra:
        ins += in_vmem([branch_t]) + in_hbm(attended)
        specs += [vmem_spec()] * (1 + extra)
    else:
        ins += in_hbm([held])
        specs += [any_spec()]
    if final:
        ins += in_hbm([tokens])
        specs += [any_spec()]
    outs = [pltpu.HBM((length, depth), F32)] + [SDS(out_piece.shape, BF)] * 2
    scratch = [
        pltpu.VMEM((8, 1792, QB), BF),
        pltpu.VMEM((8, length), F32),
        pltpu.VMEM((256, length), BF),
        pltpu.VMEM((256, length), F32),
        pltpu.VMEM((4, length, 128), BF),
        pltpu.VMEM((4, length, 128), BF),
        pltpu.VMEM(out_piece.rows.shape + (columns,), BF),
        pltpu.VMEM((depth, length), BF),
        pltpu.VMEM((length, depth), F32),
        pltpu.VMEM(piece.rows.shape + (768,), BF),
        pltpu.SemaphoreType.DMA((13,)),
    ]
    if final:
        outs.append(SDS((8, depth), F32))
        scratch.append(pltpu.VMEM((length, depth), BF))
    got = pl.pallas_call(
        functools.partial(attend_back_body, piece, out_piece, extra, len(onto), final),
        in_specs=specs + [any_spec()] * len(onto),
        out_specs=[any_spec()] * 3 + ([vmem_spec()] if final else []),
        out_shape=outs,
        input_output_aliases={len(ins) + k: 1 + k for k in range(len(onto))},
        scratch_shapes=[
            pltpu.VMEM((length, 768), BF),
            pltpu.VMEM((length, 128), F32),
            pltpu.VMEM((length, 128), F32),
        ]
        + scratch,
        compiler_params=params(40),
        cost_estimate=cost(12, 8),
        name="attend_back",
    )(*ins, *onto)
    return got[0], got[1:3], got[3] if final else None


def norm_back_body(
    start, core, tokens, grad_normed, grad_middle, gain, held, other, high, low, own, sem
):
    length = high.shape[0] // 2
    r = pl.program_id(0)
    hat, root = norm_parts(tokens[...].astype(F32))
    value = grad_middle[...] + norm_pull(grad_normed[...], hat, root, gain[...])
    top = value.astype(BF)
    rest = (value - top.astype(F32)).astype(BF)
    for base in (0, length):
        at = pl.ds(pl.multiple_of(base + r * QB, QB), QB)
        high[at, :] = top
        low[at, :] = rest

    @pl.when(r == pl.num_programs(0) - 1)
    def _():
        count = own.shape[0] // QB
        for k in range(count):
            own[k * QB : k * QB + QB, :] = turned([high, low], start[0], k)
        copy = pltpu.make_async_copy(own, held.at[core[0]], sem)
        copy.start()
        for k in range(count):
            other[k * QB : k * QB + QB, :] = turned([high, low], start[0], k + count)
        copy.wait()


def norm_back(start, core, tokens, grad_normed, grad_middle, gain):
    length, depth = tokens.shape
    half = (length // 2, depth)
    return pl.pallas_call(
        norm_back_body,
        grid=(length // QB,),
        in_specs=[smem_spec()] * 2 + [row_spec(depth, QB)] * 3 + [whole_spec((1, depth))],
        out_specs=[any_spec(), whole_spec(half)],
        out_shape=[pltpu.HBM((2,) + half, F32), SDS(half, F32)],
        scratch_shapes=[
            pltpu.VMEM((2 * length, depth), BF),
            pltpu.VMEM((2 * length, depth), BF),
            pltpu.VMEM(half, F32),
            pltpu.SemaphoreType.DMA,
        ],
        compiler_params=params(24),
        cost_estimate=cost(4, 16),
        name="norm_back",
    )(start, core, *in_hbm([tokens, grad_normed, grad_middle]), gain)


def split_far_body(counts, me, *refs):
    keep, send = refs[-2:]
    far = me[0] // 4
    begin = 0
    for count in counts:
        pieces, refs = refs[:count], refs[count:]
        cols = pl.ds(begin, pieces[0].shape[-1])
        begin += pieces[0].shape[-1]
        for k, out in enumerate((keep, send)):
            for slot in range(2):
                at = lax.bitwise_xor(far, k + 2 * slot)
                total = pieces[0][at].astype(F32)
                for piece in pieces[1:]:
                    total = total + piece[at].astype(F32)
                out[slot, :, cols] = total.astype(BF)


def split_far(me, groups):
    width, specs = 0, []
    for pieces in groups:
        far, block, columns = pieces[0].shape[-3:]
        width += columns
        for piece in pieces:
            if piece.ndim == 4:
                specs.append(pl.BlockSpec((None, far, block, columns), lambda i: (0, 0, 0, 0)))
            else:
                specs.append(whole_spec(piece.shape))
    return pl.pallas_call(
        functools.partial(split_far_body, [len(pieces) for pieces in groups]),
        grid=(1,),
        in_specs=[smem_spec()] + specs,
        out_specs=[whole_spec((2, block, width))] * 2,
        out_shape=[SDS((2, block, width), BF)] * 2,
        compiler_params=params(16),
        cost_estimate=cost(1, 2),
        name="split_far",
    )(me, *[piece for pieces in groups for piece in pieces])


def put_sums(ref, base, total):
    high = total.astype(BF)
    ref[base : base + 4, :] = high
    ref[base + 4 : base + 8, :] = (total - high.astype(F32)).astype(BF)
    ref[base + 8 : base + 16, :] = jnp.zeros((8, total.shape[1]), BF)


def get_sums(ref, base):
    return ref[base : base + 4, :].astype(F32) + ref[base + 4 : base + 8, :].astype(F32)


def last_join_body(own, other, own_last, other_last, sums, sums_away, keep, send):
    total = sums[...] + sums_away[...]
    rows = keep.shape[0] // 2
    width = own.shape[-1]
    for k in range(4):
        out = keep if k < 2 else send
        at = slice((k % 2) * rows, (k % 2 + 1) * rows)
        value = (own[k].astype(F32) + other[k].astype(F32)).astype(BF)
        out[at, :width] = value.reshape(rows, -1)
        value = (own_last[k].astype(F32) + other_last[k].astype(F32)).astype(BF)
        out[at, width:] = value.reshape(rows, -1)
    put_sums(send, 2 * rows, total)


def last_half_body(keep, send, near, rest, send_next):
    rows = rest.shape[0]
    value = keep[:rows, :].astype(F32) + near[:rows, :].astype(F32)
    rest[...] = value.astype(BF)
    value = keep[rows:, :].astype(F32) + near[rows : 2 * rows, :].astype(F32)
    send_next[:rows, :] = value.astype(BF)
    send_next[rows : rows + 16, :] = send[2 * rows :, :]
    send_next[rows + 16 :, :] = near[2 * rows :, :]


def last_split_body(flip, me, rest, send, away, keep, out_send):
    far = me[0] // 4
    rows = rest.shape[0]
    block = rows // 4
    for k, out in enumerate((keep, out_send)):
        for slot in range(2):
            at = pl.ds(pl.multiple_of(lax.bitwise_xor(far, k + 2 * slot) * block, 16), block)
            total = rest[at, :].astype(F32) + away[at, :].astype(F32)
            out[slot * block : (slot + 1) * block, :] = total.astype(BF)
    first, second = get_sums(send, rows + 16), get_sums(away, rows)
    swapped = lax.bitwise_xor(me[1], flip) == 1
    one, two = jnp.where(swapped, second, first), jnp.where(swapped, first, second)
    total = (get_sums(send, rows) + one) + (two + get_sums(away, rows + 16))
    put_sums(keep, 2 * block, total)
    put_sums(out_send, 2 * block, total)


def last_middle_body(keep, near, rest, send):
    block = (keep.shape[0] - 16) // 2
    value = keep[:block, :].astype(F32) + near[:block, :].astype(F32)
    rest[:block, :] = value.astype(BF)
    value = keep[block : 2 * block, :].astype(F32) + near[block : 2 * block, :].astype(F32)
    send[:block, :] = value.astype(BF)
    total = get_sums(keep, 2 * block) + get_sums(near, 2 * block)
    put_sums(rest, block, total)
    put_sums(send, block, total)


def last_sum_body(rest, away, first, grad_qkv, sums):
    block = rest.shape[0] - 16
    value = rest[:block, :].astype(F32) + away[:block, :].astype(F32)
    parts = [first[:, 384:], value[:, :384], value[:, 384:]]
    for which in range(3):
        cols = slice(which * 128, which * 128 + 128)
        grad_qkv[which] = jnp.concatenate([part[:, cols] for part in parts], 1)
    sums[...] = get_sums(rest, block) + get_sums(away, block)


def pack_body(part, out, up, down, packed):
    width = out.shape[1]
    packed[:, :width] = out[...]
    for s in range(up.shape[1] // part):
        cols = slice(s * part, (s + 1) * part)
        packed[:, width + 2 * s * part : width + (2 * s + 1) * part] = up[:, cols]
        packed[:, width + (2 * s + 1) * part : width + (2 * s + 2) * part] = down[:, cols]


def small_call(body, name, outs, scalars, values):
    return pl.pallas_call(
        body,
        in_specs=[smem_spec()] * len(scalars) + [vmem_spec()] * len(values),
        out_specs=[vmem_spec()] * len(outs),
        out_shape=outs,
        compiler_params=params(16),
        cost_estimate=cost(1, 3),
        name=name,
    )(*scalars, *values)


def swap(value):
    return lax.ppermute(value, "mp", [(0, 1), (1, 0)])


def tie(*values):
    return lax.optimization_barrier(values)


def hop(value, mask, count):
    return lax.ppermute(value, "dp", [(i, i ^ mask) for i in range(count)])


def hops(value, masks, count):
    return [(value, functools.partial(hop, mask=m, count=count)) for m in masks]


def hop_apart(value, masks, count):
    pairs = [(2 * i + c, 2 * (i ^ masks[c]) + c) for i in range(count) for c in range(2)]
    return lax.ppermute(value, ("dp", "mp"), pairs)


def far_hops(rows, values):
    return [
        (v, functools.partial(hop, mask=rows.near * m, count=rows.dp_count))
        for m, v in zip(range(1, rows.far), values)
    ]


def swaps(values):
    return [(v, swap) for v in values]


def send_all(requests):
    return [send(value) for value, send in requests]


def low_sum(values):
    total = values[0].astype(F32)
    for value in values[1:]:
        total = total + value.astype(F32)
    return total


class Flow:
    def __init__(self, me):
        self.me = me
        self.active = []

    def add(self, transfer, name, results, seeds=()):
        self.active.append([transfer, list(seeds), name, results])

    def step(self, *pivots, gate=None):
        values = [v for item in self.active for v in item[1]]
        tied = list(tie(self.me, *pivots, *values))
        self.me = tied.pop(0)
        pivots, tied = tied[: len(pivots)], tied[len(pivots) :]
        going, self.active, requests = self.active, [], []
        for item in going:
            transfer, values, name, results = item
            got, tied = tied[: len(values)], tied[len(values) :]
            try:
                if callable(transfer):
                    item[0] = transfer(*got)
                    asked = next(item[0])
                else:
                    asked = transfer.send(got)
                self.active.append(item)
                requests.append(asked)
            except StopIteration as stop:
                results[name] = stop.value
        gates = gate() if gate else []
        operands = [operand for asked in requests for operand, _ in asked]
        tied = list(tie(self.me, *gates, *operands))
        self.me = tied[0]
        tied = tied[1 + len(gates) :]
        for item, asked in zip(self.active, requests):
            item[1] = [send(operand) for (_, send), operand in zip(asked, tied)]
            tied = tied[len(asked) :]
        return pivots


def add_low(a, b):
    return (a.astype(F32) + b.astype(F32)).astype(BF)


def on_device(
    tokens, segment, ln1_gain, ln1_bias, w_qkv, w_out, ln2_gain, ln2_bias, w_up, w_down, cotangent
):
    dp_count = lax.axis_size("dp")
    core = lax.axis_index("mp")
    me = jnp.stack([lax.axis_index("dp"), core]).astype(jnp.int32)
    here, depth = tokens.shape[2], tokens.shape[3]
    length = 2 * here
    rows = Rows(dp_count, depth)

    groups = w_qkv.shape[2] // 128
    part = 384
    subs = w_up.shape[1] // part
    cut = subs // 2
    qkv = [w_qkv[:, :, g * 128 : (g + 1) * 128].reshape(-1, part) for g in range(groups)]
    shards = {"q": jnp.concatenate(qkv, 1)}

    def pack(out, up, down):
        return small_call(
            functools.partial(pack_body, part),
            "pack",
            [SDS((up.shape[0], out.shape[0] + 2 * up.shape[1]), BF)],
            [],
            [out.T, up, down.T],
        )[0]

    seg = lax.dynamic_index_in_dim(segment[:, 0], core, 0, keepdims=False)
    run = length * 3 // 4
    begin = jnp.argmax(seg[: length - run + 1] == seg[run - 1 :]).astype(jnp.int32)
    start = ((begin - here * core) % length).reshape(1)
    back = (length - start) % length
    seg_tail = lax.dynamic_slice_in_dim(jnp.concatenate([seg, seg]), begin + run, length - run)
    seg_col = seg_tail.reshape(-1, 1)
    seg_row = seg_tail.reshape(1, -1)
    gain1, bias1, gain2, bias2 = (
        v.reshape(1, -1) for v in (ln1_gain, ln1_bias, ln2_gain, ln2_bias)
    )

    flow = Flow(me)
    core_place = core.astype(jnp.int32).reshape(1)
    token_halves = [tokens[:, 0], swap(tokens[:, 0])]
    cot_halves = [cotangent[:, 0], swap(cotangent[:, 0])]
    wide = 2 * part
    qkv_pieces = [Piece(rows, "slabs")] + [Piece(rows, "slabs", part * g) for g in range(groups - 1)]
    out_piece = Piece(rows, "slabs")
    feed_pieces = [Piece(rows, "slabs", part + wide * s) for s in range(cut)]
    feed_pieces += [Piece(rows, "slabs", wide * s) for s in range(subs - cut)]
    feed_outs = [
        Piece(rows, "stack", 0, wide, s // cut) for s in range(subs)
    ]
    qkv_outs = [Piece(rows, "stack", part, wide, 0)]
    qkv_outs += [Piece(rows, "stack", 0, part, 1)] * (groups - 1)
    far = lax.axis_index("dp") // rows.near

    def gather_whole(shard):
        return lax.all_gather(shard, "dp", axis=0, tiled=True).reshape(rows.shape + (-1,))

    def fetch_near(near):
        got = yield hops(near, MASKS[1:], dp_count)
        own = [near] + got
        return own + [swap(x) for x in own]

    def via(mask):
        return functools.partial(hop, mask=mask, count=dp_count)

    def fetch_wide(shard, away):
        near, both_ways = yield [(shard, via(4)), (away, via(4))]
        (a0,) = arrange(rows, flow.me, [shard, near, away, both_ways], [shard.shape[1]])
        a1, a2, b0, away = yield [(a0, via(1)), (a0, via(2))] + swaps([a0]) + [(shard_c, via(8))]
        a3, b1, b2, near, both_ways = yield (
            [(a1, via(2))] + swaps([a1, a2]) + [(shard_c, via(4)), (away, via(4))]
        )
        slabs["a"] = [a0, a1, a2, a3, b0, b1, b2, swap(a3)]
        (c0,) = arrange(rows, flow.me, [shard_c, near, away, both_ways], [shard_c.shape[1]])
        (d0,) = yield swaps([c0])
        c1, c2 = yield [(c0, via(1)), (c0, via(2))]
        c3, d1, d2 = yield [(c2, via(1))] + swaps([c1, c2])
        return [c0, c1, c2, c3, d0, d1, d2, swap(c3)]

    def whole(shard):
        own = gather_whole(shard)
        return [own, swap(own)]

    def apart(flip):
        masks = (2, 1) if flip else (1, 2)
        return functools.partial(hop_apart, masks=masks, count=dp_count)

    def halve(flip, hurry, pause, own, other):
        if hurry:
            other = swap(other)
        else:
            (other,) = yield swaps([other])
        if pause:
            yield []
        keep, send = (low_sum([own[k : k + 2], other[k : k + 2]]).astype(BF) for k in (0, 2))
        (near,) = yield [(send, apart(flip))]
        (away,) = yield [(low_sum([keep[1], near[1]]).astype(BF), apart(1 - flip))]
        return [keep, near, away]

    def reduce_far(groups):
        keep, send = split_far(flow.me, groups)
        (near,) = yield [(send, via(4))]
        (away,) = yield [(low_sum([keep[1], near[1]]).astype(BF), via(8))]
        return low_sum([keep[0], near[0], away])

    def reduce_all(flip, own, other):
        group = yield from halve(flip, True, False, own, other)
        return (yield from reduce_far([sums_of[s] for s in range(subs - 1)] + [group]))

    def reduce_last(flip, own, own_last, other_last, sums):
        other_last, sums_away = swap(other_last), swap(sums)
        rows_here = rows.far * rows.block
        keep, send = small_call(
            last_join_body,
            "last_join",
            [SDS((2 * rows_here, wide), BF), SDS((2 * rows_here + 16, wide), BF)],
            [],
            [own, sums_of["other"], own_last, other_last, sums, sums_away],
        )
        (near,) = yield [(send, apart(flip))]
        return [keep, send, near]

    def exchange(value):
        (got,) = yield swaps([value])
        return got

    def reduce_one(flip, own, other):
        group = yield from halve(flip, False, False, own, other)
        return (yield from reduce_far([group]))

    def plain(own, other):
        value = low_sum([own, swap(other)]).astype(BF).reshape(depth, -1)
        return lax.psum_scatter(value, "dp", scatter_dimension=0, tiled=True).astype(F32)

    def run(transfer):
        requests = next(transfer)
        while True:
            try:
                requests = transfer.send(send_all(requests))
            except StopIteration as stop:
                return stop.value

    slabs, forward = {}, []

    def project(g):
        name = "q0" if g == 0 else "q1"
        forward.append(
            project_attend(qkv_pieces[g], flow.me, normed, seg_col, seg_row, slabs[name])
        )

    if rows.split:
        shard_q = shards["q"]
        got = send_all(far_hops(rows, [shard_q] * (rows.far - 1)))
        prepared = prepare(start, core_place, *token_halves, gain1, bias1)
        tied = tie(*got, *prepared, w_out, w_up, w_down)
        got, prepared = tied[:3], tied[3:6]
        shard_a = pack(*tied[6:])
        near_q0, near_q1 = arrange(rows, me, [shard_q] + list(got), [part, wide])
        own = [near_q0] + [hop(near_q0, m, dp_count) for m in MASKS[1:]]
        first_cols = part + wide * cut
        shard_c, shard_a = shard_a[:, first_cols:], shard_a[:, :first_cols]
        away_a = hop(shard_a, 8, dp_count)
        start_cot, _ = tie(start, near_q0)
        turned_cot = turn(start_cot, core_place, *cot_halves)
        tied = tie(*own, *turned_cot)
        own, turned_cot = tied[:4], tied[4:]
        slabs["q0"] = list(own) + [swap(v) for v in own]
        flow.add(fetch_near, "q1", slabs, [near_q1])
        flow.add(fetch_wide, "c", slabs, [shard_a, away_a])
        flow.step(own[3])
    else:
        shard_a = pack(w_out, w_up, w_down)
        for name, shard in (
            ("q0", shards["q"][:, :part]),
            ("q1", shards["q"][:, part:]),
            ("a", shard_a[:, : part + wide * cut]),
            ("c", shard_a[:, part + wide * cut :]),
        ):
            slabs[name] = whole(shard)
        prepared = prepare(start, core_place, *token_halves, gain1, bias1)
        turned_cot = turn(start, core_place, *cot_halves)
    x, normed, normed_t = prepared
    cot, cot_t = turned_cot
    for g in range(groups):
        project(g)
        flow.step(forward[g][2])
    atts = [f[1] for f in forward]
    middle, normed_ffn, normed_ffn_t = out_norm(
        out_piece, flow.me, x, gain2, bias2, atts, slabs["a"]
    )
    flow.step(normed_ffn)

    held = None
    sums_of = {}
    onto = []
    feed_names = ["a"] * cut + ["c"] * (subs - cut)
    for s in range(subs):
        final = s == subs - 1
        grads, held = feed_forward(
            feed_pieces[s],
            feed_outs[s],
            s,
            flow.me,
            normed_ffn,
            normed_ffn_t,
            cot,
            cot_t,
            held,
            slabs[feed_names[s]],
            [],
            (out_piece, slabs["a"], middle, gain2, groups) if final else None,
        )
        flip = s // cut
        if not rows.split:
            sums_of[s] = plain(*grads)
        elif final:
            flow.add(functools.partial(reduce_all, flip), "feed", sums_of, grads)
        else:
            flow.add(functools.partial(halve, flip, False, s == 0), s, sums_of, grads)
        if s == 1 and rows.split:
            flow.step(grads[0], gate=lambda: slabs["c"][-1:])
        elif not final:
            flow.step(grads[0])
    mixed, grad_middle, branch_t, sums2, *grad_atts = held
    flow.step(sums2)
    grad_projs = []
    onto = []

    held = None
    qkv_slabs = [slabs["q0"]] + [slabs["q1"]] * (groups - 1)
    for g in range(groups):
        proj, att, inverse, kept = forward[g]
        held, grads, sums1 = attend_back(
            qkv_pieces[g],
            qkv_outs[g],
            flow.me,
            normed_t,
            proj,
            att,
            grad_atts[g],
            inverse,
            kept,
            qkv_slabs[g],
            branch_t,
            atts if g == 0 else [],
            held,
            x if g == groups - 1 else None,
            onto,
        )
        if g == 0 and rows.split:
            flow.add(functools.partial(reduce_one, 0), "first", sums_of, grads)
        elif g == 0:
            sums_of["first"] = plain(*grads)
        elif g < groups - 1 and rows.split:
            flow.add(exchange, "other", sums_of, grads[1:])
            own_early = grads[0]
        elif not rows.split:
            sums_of[("last", g)] = plain(*grads)
        if g < groups - 1:
            flow.step(held)
    sums = jnp.concatenate([sums1[:2], sums2[:2]], 0)
    if rows.split:
        flow.add(
            functools.partial(reduce_last, 1), "last", sums_of, [own_early, *grads, sums]
        )
        (held,) = flow.step(held)
    start_late, _ = tie(back, flow.me)
    tokens_held, tokens_other = norm_back(start_late, core_place, x, held, grad_middle, gain1)
    mixed, tokens_other = tie(mixed, tokens_other)
    mixed_held, mixed_other = turn_back(back, core_place, mixed)
    tokens_held, tokens_other, mixed_other = flow.step(tokens_held, tokens_other, mixed_other)
    if rows.split:
        block = rows.block
        mixed_got = swap(mixed_other)
        keep, send, near = sums_of["last"]
        rows_here = rows.far * block
        rest, send = small_call(
            last_half_body,
            "last_half",
            [SDS((rows_here, wide), BF), SDS((rows_here + 32, wide), BF)],
            [],
            [keep, send, near],
        )
        away = apart(0)(send)
        keep, send = small_call(
            functools.partial(last_split_body, 1),
            "last_split",
            [SDS((2 * block + 16, wide), BF)] * 2,
            [flow.me],
            [rest, send, away],
        )
        near = hop(send, 4, dp_count)
        rest, send = small_call(
            last_middle_body, "last_middle", [SDS((block + 16, wide), BF)] * 2, [], [keep, near]
        )
        flow.step(gate=lambda: [send])
        rest, mixed_got, feed_sum = tie(rest, mixed_got, sums_of["feed"])
        away = hop(send, 8, dp_count)
        while flow.active:
            flow.step()
        grad_qkv, norm_sums = small_call(
            last_sum_body,
            "last_sum",
            [SDS((3, block, part), F32), SDS((4, depth), F32)],
            [],
            [rest, away, sums_of["first"]],
        )
        grad_qkv = grad_qkv.transpose(1, 0, 2)
        grad_out = sums_of["first"][:, :part].T
        feed_sums = [feed_sum]
    else:
        mixed_got = swap(mixed_other)
        early = sums_of["first"]
        parts = [early[:, part:]] + [sums_of[("last", g)] for g in range(1, groups)]
        grad_qkv = jnp.concatenate([r.reshape(-1, 3, 128) for r in parts], 2)
        grad_out = early[:, :part].T
        feed_sums = [sums_of[s] for s in range(subs)]
        norm_sums = jnp.sum(lax.all_gather(sums + swap(sums), "dp", axis=0), 0)
    feed_sum = jnp.concatenate(feed_sums, 1) if len(feed_sums) > 1 else feed_sums[0]
    feed_list = [feed_sum[:, wide * s : wide * (s + 1)] for s in range(subs)]

    return (
        place(core_place, mixed_held, mixed_got)[:, None],
        place(core_place, tokens_held, swap(tokens_other))[:, None],
        norm_sums[0],
        norm_sums[1],
        grad_qkv,
        grad_out,
        norm_sums[2],
        norm_sums[3],
        jnp.concatenate([r[:, :part] for r in feed_list], 1),
        jnp.concatenate([r[:, part:] for r in feed_list], 1).T,
    )


def solution(mesh):
    in_specs = (
        P(None, "dp", "mp", None),
        P(None, "dp", None),
        P(),
        P(),
        P("dp", None, "mp"),
        P("mp", "dp"),
        P(),
        P(),
        P("dp", "mp"),
        P("mp", "dp"),
        P(None, "dp", "mp", None),
    )
    out_specs = (
        P(None, "dp", "mp", None),
        P(None, "dp", "mp", None),
        P(),
        P(),
        P("dp", None, "mp"),
        P("mp", "dp"),
        P(),
        P(),
        P("dp", "mp"),
        P("mp", "dp"),
    )
    return jax.shard_map(
        on_device, mesh=mesh, in_specs=in_specs, out_specs=out_specs, check_vma=False
    )
```

```python
import functools
import math

import jax
import jax.numpy as jnp
from jax import lax
from jax.experimental import pallas as pl
from jax.experimental.pallas import tpu as pltpu
from jax.sharding import PartitionSpec as P

HD = 32
QB = 256
EPS = 1e-05
BF = jnp.bfloat16
F32 = jnp.float32
NEG = -1e30
SCALE = 1.0 / math.sqrt(HD)
LOG2E = math.log2(math.e)
C2 = SCALE * LOG2E
MIB = 1024 * 1024
SDS = jax.ShapeDtypeStruct


def nn(a, b):
    return lax.dot_general(a, b, (((1,), (0,)), ((), ())), preferred_element_type=F32)


def nt(a, b):
    return lax.dot_general(a, b, (((1,), (1,)), ((), ())), preferred_element_type=F32)


def params(mib):
    return pltpu.CompilerParams(vmem_limit_bytes=mib * MIB)


def in_hbm(values):
    return [pltpu.with_memory_space_constraint(v, pltpu.HBM) for v in values]


def in_vmem(values):
    return [pltpu.with_memory_space_constraint(v, pltpu.VMEM) for v in values]


def cost(gflop, mbytes):
    return pl.CostEstimate(flops=int(gflop * 1e9), bytes_accessed=int(mbytes * 1e6), transcendentals=0)


def any_spec():
    return pl.BlockSpec(memory_space=pl.ANY)


def smem_spec():
    return pl.BlockSpec(memory_space=pltpu.SMEM)


def vmem_spec():
    return pl.BlockSpec(memory_space=pltpu.VMEM)


def row_spec(width, rows=512):
    return pl.BlockSpec((rows, width), lambda r: (r, 0))


def column_spec(height, rows=512):
    return pl.BlockSpec((height, rows), lambda r: (0, r))


def whole_spec(shape):
    return pl.BlockSpec(shape, lambda r: tuple(0 for _ in shape))


MASKS = (0, 1, 2, 3)


class Rows:
    def __init__(self, dp_count, depth):
        self.dp_count = dp_count
        self.depth = depth
        self.split = (depth // dp_count) % 16 == 0 and dp_count == 16
        self.near = 4 if self.split else 1
        self.far = dp_count // 4 if self.split else 1
        self.block = depth // (self.near * self.far)
        self.shape = (self.far, self.near, self.block)


class Piece:
    def __init__(self, rows, kind, start=0, width=0, flip=0):
        self.rows = rows
        self.flip = flip
        self.kind = kind if rows.split else "whole"
        self.start = start
        self.count = 2 * len(MASKS) if self.kind == "slabs" else 2
        if self.kind == "stack":
            self.shape = (len(MASKS), rows.far, rows.block, width)
        else:
            self.shape = rows.shape + (width,)


def piece_copies(piece, me, refs, moves, sem, outward):
    copies = []
    each = piece.count // 2
    for half, column, width, view in moves:
        cols = pl.ds(piece.start + column, width)
        if piece.kind == "whole":
            pairs = [(refs[half].at[:, :, :, cols], view)]
        else:
            pairs = []
            order = lax.bitwise_xor(me[1], piece.flip ^ half)
            masks = (0, 2 - order, 1 + order, 3) if piece.kind == "stack" else MASKS
            for k, mask in enumerate(masks):
                ref = refs[half].at[k] if piece.kind == "stack" else refs[half * each + k]
                near = lax.bitwise_xor(lax.rem(me[0], 4), mask)
                pairs.append((ref.at[:, :, cols], view.at[:, near]))
        for outside, inside in pairs:
            if outward:
                copies.append(pltpu.make_async_copy(inside, outside, sem))
            else:
                copies.append(pltpu.make_async_copy(outside, inside, sem))
    return copies


def start_all(copies):
    for copy in copies:
        copy.start()


def wait_bytes(ref, sem):
    pltpu.make_async_copy(ref, ref, sem).wait()


def flat(value):
    return value.reshape(-1, value.shape[-1])


def head_row(h):
    return lax.broadcasted_iota(jnp.int32, (1, 128), 1) // HD == h


def fill_bias(bias, seg_col, seg_row):
    key = lax.broadcasted_iota(jnp.int32, (QB, QB), 0)
    query = lax.broadcasted_iota(jnp.int32, (QB, QB), 1)
    bias[0] = jnp.where(query >= key, 0.0, NEG)
    bias[1] = jnp.where((query >= key) & (seg_col[...] == seg_row[...]), 0.0, NEG)


def turned(doubles, start, r):
    coarse = pl.multiple_of(start // 16 * 16 + r * QB, 16)
    fine = start % 16
    row = lax.broadcasted_iota(jnp.int32, (QB, QB + 16), 0)
    col = lax.broadcasted_iota(jnp.int32, (QB, QB + 16), 1)
    pick = jnp.where(col - row == fine, 1.0, 0.0).astype(BF)
    total = None
    for double in doubles:
        part = nn(pick, double[pl.ds(coarse, QB + 16), :])
        total = part if total is None else total + part
    return total


def norm_parts(values):
    centered = values - jnp.mean(values, axis=-1, keepdims=True)
    spread = jnp.mean(centered * centered, axis=-1, keepdims=True)
    root = lax.rsqrt(spread + EPS)
    return centered * root, root


def fill_double(double, core, own, other, sem):
    here = own.shape[1]
    for k, half in enumerate((own, other)):
        pltpu.make_async_copy(half.at[core], double.at[pl.ds(k * here, here)], sem).start()
    wait_bytes(double.at[pl.ds(0, 2 * here)], sem)
    double[2 * here :, :] = double[: 2 * here, :]


def prepare_body(start, core, own, other, gain, offset, x_out, normed_out, normed_t_out, double, x, normed, normed_t, sems):
    fill_double(double, core[0], own, other, sems.at[3])

    def step(r, carry):
        at = pl.ds(pl.multiple_of(r * QB, QB), QB)
        value = turned([double], start[0], r)
        x[at, :] = value.astype(BF)
        hat, _ = norm_parts(value)
        low = (hat * gain[...] + offset[...]).astype(BF)
        normed[at, :] = low
        normed_t[:, at] = low.T
        return carry

    lax.fori_loop(0, x.shape[0] // QB, step, 0)
    copies = [
        pltpu.make_async_copy(normed, normed_out, sems.at[0]),
        pltpu.make_async_copy(x, x_out, sems.at[1]),
        pltpu.make_async_copy(normed_t, normed_t_out, sems.at[2]),
    ]
    start_all(copies)
    for copy in copies:
        copy.wait()


def prepare(start, core, own, other, gain, offset):
    _, here, depth = own.shape
    shape, shape_t = (2 * here, depth), (depth, 2 * here)
    shapes = [shape, shape, shape_t]
    return pl.pallas_call(
        prepare_body,
        in_specs=[smem_spec()] * 2 + [any_spec()] * 2 + [vmem_spec()] * 2,
        out_specs=[any_spec()] * 3,
        out_shape=[pltpu.HBM(s, BF) for s in shapes],
        scratch_shapes=[pltpu.VMEM((4 * here, depth), BF)]
        + [pltpu.VMEM(s, BF) for s in shapes]
        + [pltpu.SemaphoreType.DMA((4,))],
        compiler_params=params(20),
        cost_estimate=cost(4, 8),
        name="prepare",
    )(start, core, *in_hbm([own, other]), gain, offset)


def turn_body(start, core, own, other, cot_out, cot_t_out, double, cot, cot_t, sems):
    fill_double(double, core[0], own, other, sems.at[2])

    def step(r, carry):
        at = pl.ds(pl.multiple_of(r * QB, QB), QB)
        low = turned([double], start[0], r).astype(BF)
        cot[at, :] = low
        cot_t[:, at] = low.T
        return carry

    lax.fori_loop(0, cot.shape[0] // QB, step, 0)
    copies = [
        pltpu.make_async_copy(cot, cot_out, sems.at[0]),
        pltpu.make_async_copy(cot_t, cot_t_out, sems.at[1]),
    ]
    start_all(copies)
    for copy in copies:
        copy.wait()


def turn(start, core, own, other):
    _, here, depth = own.shape
    shapes = [(2 * here, depth), (depth, 2 * here)]
    return pl.pallas_call(
        turn_body,
        in_specs=[smem_spec()] * 2 + [any_spec()] * 2,
        out_specs=[any_spec()] * 2,
        out_shape=[pltpu.HBM(s, BF) for s in shapes],
        scratch_shapes=[pltpu.VMEM((4 * here, depth), BF)]
        + [pltpu.VMEM(s, BF) for s in shapes]
        + [pltpu.SemaphoreType.DMA((3,))],
        compiler_params=params(16),
        cost_estimate=cost(4, 8),
        name="turn",
    )(start, core, *in_hbm([own, other]))


def turn_back_body(start, core, values, held, other, double, own, sem):
    here = other.shape[0]
    double[: 2 * here, :] = values[...]
    double[2 * here :, :] = values[...]
    count = here // QB

    def step(r, carry):
        at = pl.ds(pl.multiple_of(r * QB, QB), QB)
        own[at, :] = turned([double], start[0], r).astype(BF)
        other[at, :] = turned([double], start[0], r + count).astype(BF)
        return carry

    lax.fori_loop(0, count, step, 0)
    copy = pltpu.make_async_copy(own, held.at[core[0]], sem)
    copy.start()
    copy.wait()


def place_body(core, other, held, out, sem):
    copy = pltpu.make_async_copy(other, out.at[1 - core[0]], sem)
    copy.start()
    copy.wait()


def place(core, held, other):
    return pl.pallas_call(
        place_body,
        in_specs=[smem_spec(), any_spec(), any_spec()],
        out_specs=any_spec(),
        out_shape=pltpu.HBM(held.shape, held.dtype),
        input_output_aliases={2: 0},
        scratch_shapes=[pltpu.SemaphoreType.DMA],
        compiler_params=params(4),
        cost_estimate=cost(0, 4),
        name="place",
    )(core, other, *in_hbm([held]))


def turn_back(start, core, values):
    length, depth = values.shape
    half = (length // 2, depth)
    return pl.pallas_call(
        turn_back_body,
        in_specs=[smem_spec()] * 2 + [vmem_spec()],
        out_specs=[any_spec(), vmem_spec()],
        out_shape=[pltpu.HBM((2,) + half, BF), SDS(half, BF)],
        scratch_shapes=[
            pltpu.VMEM((2 * length, depth), BF),
            pltpu.VMEM(half, BF),
            pltpu.SemaphoreType.DMA,
        ],
        compiler_params=params(16),
        cost_estimate=cost(2, 4),
        name="turn_back",
    )(start, core, values)


def arrange_body(widths, me, *refs):
    pieces, outs = refs[:4], refs[4:]
    far = me[0] // 4
    for m, piece in enumerate(pieces):
        begin = 0
        for out, width in zip(outs, widths):
            out[lax.bitwise_xor(far, m)] = piece[:, begin : begin + width]
            begin += width


def arrange(rows, me, pieces, widths):
    return pl.pallas_call(
        functools.partial(arrange_body, widths),
        in_specs=[smem_spec()] + [vmem_spec()] * 4,
        out_specs=[vmem_spec()] * len(widths),
        out_shape=[SDS((rows.far, rows.block, w), BF) for w in widths],
        compiler_params=params(8),
        cost_estimate=cost(1, 1),
        name="arrange",
    )(me, *pieces)


KEPT = (0, 256, 768, 1536)
KEPT_ROWS = (256, 512, 768, 256)
ORDER = (2, 1, 0, 3)


def project_attend_body(piece, me, normed_in, seg_col, seg_row, *refs):
    slabs = refs[: piece.count]
    proj_out, att, inverse, kept_out, weight, proj, normed, bias = refs[piece.count : piece.count + 8]
    keys_m, values_t, att_t, kept, sem, out_sem, kept_sem = refs[piece.count + 8 :]
    normed_copy = pltpu.make_async_copy(normed_in, normed, out_sem)
    normed_copy.start()
    moves = [(half, 0, 384, weight.at[:, :, :, pl.ds(384 * half, 384)]) for half in range(2)]
    start_all(piece_copies(piece, me, slabs, moves, sem, False))
    fill_bias(bias, seg_col, seg_row)
    values_t[...] = jnp.ones_like(values_t)
    normed_copy.wait()
    wait_bytes(weight, sem)

    for c in range(3):
        cols = slice(c * 256, c * 256 + 256)
        proj[:, cols] = nn(normed[...], flat(weight[:, :, :, cols])).astype(BF)
    proj_copy = pltpu.make_async_copy(proj, proj_out, out_sem)
    proj_copy.start()
    for half in range(2):
        flipped = proj[:, half * 384 + 256 : half * 384 + 384].T
        for h in range(4):
            values_t[half * 4 + h, 0:HD, :] = flipped[h * HD : (h + 1) * HD]

    units = [(h, i) for i in (2, 1, 0, 3) for h in range(4)]

    def step(half, carry):
        col = pl.multiple_of(half * 384, 128)
        for h in range(4):
            keys_m[h] = jnp.where(head_row(h), proj[:, pl.ds(col + 128, 128)], 0)

        def score(h, i):
            first = 768 if i == 3 else 0
            scores = nt(keys_m[h, first : (i + 1) * QB, :], proj[i * QB : (i + 1) * QB, pl.ds(col, 128)])
            edge = scores[-QB:] + bias[1 if i == 3 else 0]
            return jnp.concatenate([scores[:-QB], edge], 0) if scores.shape[0] > QB else edge

        ahead = score(*units[0])
        for k, (h, i) in enumerate(units):
            scores = ahead
            if k + 1 < len(units):
                ahead = score(*units[k + 1])
            first = 768 if i == 3 else 0
            last = (i + 1) * QB
            at = slice(i * QB, last)
            peak = jnp.max(scores, axis=0, keepdims=True) * C2
            probs = jnp.exp2(scores * C2 - peak).astype(BF)
            kept[half * 4 + h, KEPT[i] : KEPT[i] + last - first, :] = probs
            summed = nn(values_t[half * 4 + h, :, first:last], probs)
            share = 1.0 / summed[HD : HD + 1]
            att_t[pl.ds(pl.multiple_of(half * 128 + h * HD, HD), HD), at] = summed[:HD] * share
            inverse[pl.ds(half * 4 + h, 1), at] = share
            if h == 3:
                part = (pl.ds(half * 4, 4), pl.ds(KEPT[i], last - first))
                pltpu.make_async_copy(kept.at[part], kept_out.at[part], kept_sem).start()
        return carry

    lax.fori_loop(0, 2, step, 0)
    for half in range(2):
        cols = slice(half * 128, half * 128 + 128)
        att[:, cols] = att_t[cols, :].T.astype(BF)
    proj_copy.wait()
    wait_bytes(kept, kept_sem)


def project_attend(piece, me, normed, seg_col, seg_row, slabs):
    length, depth = normed.shape
    rows = piece.rows
    return pl.pallas_call(
        functools.partial(project_attend_body, piece),
        in_specs=[smem_spec(), any_spec()] + [vmem_spec()] * 2 + [any_spec()] * len(slabs),
        out_specs=[any_spec()] + [vmem_spec()] * 2 + [any_spec()],
        out_shape=[
            pltpu.HBM((length, 768), BF),
            pltpu.HBM((length, 256), BF),
            pltpu.HBM((8, length), F32),
            pltpu.HBM((8, 1792, QB), BF),
        ],
        scratch_shapes=[
            pltpu.VMEM(rows.shape + (768,), BF),
            pltpu.VMEM((length, 768), BF),
            pltpu.VMEM((length, depth), BF),
            pltpu.VMEM((2, QB, QB), F32),
            pltpu.VMEM((4, length, 128), BF),
            pltpu.VMEM((8, HD + 16, length), BF),
            pltpu.VMEM((256, length), F32),
            pltpu.VMEM((8, 1792, QB), BF),
            pltpu.SemaphoreType.DMA,
            pltpu.SemaphoreType.DMA,
            pltpu.SemaphoreType.DMA,
        ],
        compiler_params=params(32),
        cost_estimate=cost(8, 8),
        name="project_attend",
    )(me, *in_hbm([normed]), seg_col, seg_row, *in_hbm(slabs))


def join_heads(attended):
    return jnp.concatenate([a[:, :128] for a in attended] + [a[:, 128:] for a in attended], 1)


def out_norm_body(piece, groups, me, tokens, gain, offset, *refs):
    attended = refs[:groups]
    slabs = refs[groups : groups + piece.count]
    middle, normed, normed_t, weight, sem = refs[groups + piece.count :]
    width = weight.shape[3] // 2

    @pl.when(pl.program_id(0) == 0)
    def _():
        moves = [(half, 0, width, weight.at[:, :, :, pl.ds(width * half, width)]) for half in range(2)]
        start_all(piece_copies(piece, me, slabs, moves, sem, False))
        wait_bytes(weight, sem)

    value = tokens[...].astype(F32) + nt(join_heads([a[...] for a in attended]), flat(weight[...]))
    middle[...] = value
    hat, _ = norm_parts(value)
    low = (hat * gain[...] + offset[...]).astype(BF)
    normed[...] = low
    normed_t[...] = low.T


def out_norm(piece, me, tokens, gain, offset, attended, slabs):
    length, depth = tokens.shape
    return pl.pallas_call(
        functools.partial(out_norm_body, piece, len(attended)),
        grid=(length // 512,),
        in_specs=[smem_spec(), row_spec(depth), whole_spec((1, depth)), whole_spec((1, depth))]
        + [row_spec(256)] * len(attended)
        + [any_spec()] * len(slabs),
        out_specs=[row_spec(depth)] * 2 + [column_spec(depth)],
        out_shape=[
            pltpu.HBM((length, depth), F32),
            pltpu.VMEM((length, depth), BF),
            pltpu.VMEM((depth, length), BF),
        ],
        scratch_shapes=[pltpu.VMEM(piece.rows.shape + (depth,), BF), pltpu.SemaphoreType.DMA],
        compiler_params=params(28),
        cost_estimate=cost(3, 8),
        name="out_norm",
    )(me, *in_hbm([tokens]), gain, offset, *in_hbm(attended), *in_hbm(slabs))


def gelu_parts(values):
    size = jnp.abs(values)
    density = jnp.exp2(values * values * (-0.5 * LOG2E) + math.log2(1.0 / math.sqrt(2 * math.pi)))
    below = 1.0 + 0.2316419 * size
    t = pl.reciprocal(below, approx=True)
    t = t * (2.0 - below * t)
    poly = t * (
        0.319381530
        + t * (-0.356563782 + t * (1.781477937 + t * (-1.821255978 + t * 1.330274429)))
    )
    tail = density * poly
    below = jnp.where(values >= 0, 1.0 - tail, tail)
    return values * below, below + values * density


def norm_pull(grad, hat, root, gain):
    scaled = grad * gain
    first = jnp.mean(scaled, axis=-1, keepdims=True)
    second = jnp.mean(scaled * hat, axis=-1, keepdims=True)
    return root * (scaled - first - hat * second)


def feed_forward_body(
    piece, out_piece, first, last_piece, groups, aliased, me, normed, normed_t, cot, cot_t, *refs
):
    refs = list(refs)
    final = last_piece is not None
    held = [] if first else [refs.pop(0), refs.pop(0)]
    if final:
        middle, gain = refs.pop(0), refs.pop(0)
        out_slabs, refs = refs[: last_piece.count], refs[last_piece.count :]
    slabs, refs = refs[: piece.count], refs[piece.count + aliased :]
    outs, refs = refs[:2], refs[2:]
    mixed = refs.pop(0)
    if final:
        grad_middle_out, branch_t, sums = refs[:3]
        grad_att, refs = refs[3 : 3 + groups], refs[3 + groups :]
    else:
        grad_in = refs.pop(0)
    weight, staged, act, grad_hidden, mixed_acc, grad_acc, sems = refs[:7]
    if final:
        mixed_low, middle_here, out_weight, grad_middle = refs[7:]
    length, depth = normed.shape
    moves = []
    for half in range(2):
        for which in range(2):
            at = pl.ds(which * 768 + half * 384, 384)
            moves.append((half, which * 384, 384, at))
    into = [(h, c, w, weight.at[:, :, :, at]) for h, c, w, at in moves]
    outof = [(h, c, w, staged.at[:, :, :, at]) for h, c, w, at in moves]
    start_all(piece_copies(piece, me, slabs, into, sems.at[0], False))
    held_copies = []
    if not first:
        held_copies.append(pltpu.make_async_copy(held[0], mixed_acc, sems.at[1]))
        held_copies.append(pltpu.make_async_copy(held[1], grad_acc, sems.at[2]))
    if final:
        held_copies.append(pltpu.make_async_copy(middle, middle_here, sems.at[4]))
    start_all(held_copies)
    if final:
        width = depth // 2
        views = [
            (half, 0, width, out_weight.at[:, :, :, pl.ds(width * half, width)]) for half in range(2)
        ]
        start_all(piece_copies(last_piece, me, out_slabs, views, sems.at[5], False))
    wait_bytes(weight, sems.at[0])
    chunks = [slice(c * 256, c * 256 + 256) for c in range(3)]

    def hidden_step(c, carry):
        cols = pl.ds(pl.multiple_of(c * 256, 256), 256)
        down = pl.ds(pl.multiple_of(768 + c * 256, 256), 256)
        hidden = nn(normed[...], flat(weight[:, :, :, cols]))
        grad_act = nn(cot[...], flat(weight[:, :, :, down]))
        value, slope = gelu_parts(hidden)
        act[:, cols] = value.astype(BF)
        grad_hidden[:, cols] = (grad_act * slope).astype(BF)
        return carry

    lax.fori_loop(0, 3, hidden_step, 0)
    for copy in held_copies:
        copy.wait()
    for cols in chunks:
        mixed_part = nt(act[...], flat(weight[:, :, :, 768:1536])[cols])
        grad_part = nt(grad_hidden[...], flat(weight[:, :, :, 0:768])[cols])
        if not first:
            mixed_part = mixed_part + mixed_acc[:, cols]
            grad_part = grad_part + grad_acc[:, cols]
        if final:
            mixed_low[:, cols] = (middle_here[:, cols] + mixed_part).astype(BF)
        else:
            mixed_acc[:, cols] = mixed_part
        grad_acc[:, cols] = grad_part
    if final:
        out_copies = [pltpu.make_async_copy(mixed_low, mixed, sems.at[1])]
        start_all(out_copies)
        wait_bytes(out_weight, sems.at[5])
        sums[...] = jnp.zeros_like(sums)

        def back_step(r, carry):
            at = pl.ds(pl.multiple_of(r * 512, 512), 512)
            hat, root = norm_parts(middle_here[at, :])
            grad = grad_acc[at, :]
            value = cot[at, :].astype(F32) + norm_pull(grad, hat, root, gain[...])
            grad_middle[at, :] = value
            low = value.astype(BF)
            branch_t[:, at] = low.T
            sums[0:1, :] += jnp.sum(grad * hat, axis=0, keepdims=True)
            sums[1:2, :] += jnp.sum(grad, axis=0, keepdims=True)
            back = nn(low, flat(out_weight[...])).astype(BF)
            for g in range(groups):
                grad_att[g][at, 0:128] = back[:, g * 128 : g * 128 + 128]
                grad_att[g][at, 128:256] = back[:, width + g * 128 : width + g * 128 + 128]
            return carry

        lax.fori_loop(0, length // 512, back_step, 0)
        out_copies.append(pltpu.make_async_copy(grad_middle, grad_middle_out, sems.at[2]))
        out_copies[-1].start()
    else:
        out_copies = [
            pltpu.make_async_copy(mixed_acc, mixed, sems.at[1]),
            pltpu.make_async_copy(grad_acc, grad_in, sems.at[2]),
        ]
        start_all(out_copies)

    def weight_step(c, carry):
        cols = pl.ds(pl.multiple_of(c * 256, 256), 256)
        down = pl.ds(pl.multiple_of(768 + c * 256, 256), 256)
        part = nn(normed_t[...], grad_hidden[:, cols]).astype(BF)
        staged[:, :, :, cols] = part.reshape(staged.shape[:3] + (256,))
        part = nn(cot_t[...], act[:, cols]).astype(BF)
        staged[:, :, :, down] = part.reshape(staged.shape[:3] + (256,))
        return carry

    lax.fori_loop(0, 3, weight_step, 0)
    start_all(piece_copies(out_piece, me, outs, outof, sems.at[3], True))
    for copy in out_copies:
        copy.wait()
    wait_bytes(staged, sems.at[3])


def feed_forward(
    piece, out_piece, me, normed, normed_t, cot, cot_t, held, slabs, onto, last=None
):
    length, depth = normed.shape
    rows = piece.rows
    first, final = held is None, last is not None
    ins = [me] + in_vmem([normed, normed_t, cot, cot_t]) + ([] if first else in_hbm(held))
    specs = [smem_spec()] + [vmem_spec()] * 4 + [any_spec()] * (0 if first else 2)
    scratch = [
        pltpu.VMEM(rows.shape + (1536,), BF),
        pltpu.VMEM(rows.shape + (1536,), BF),
        pltpu.VMEM((length, 768), BF),
        pltpu.VMEM((length, 768), BF),
        pltpu.VMEM((length, depth), F32),
        pltpu.VMEM((length, depth), F32),
        pltpu.SemaphoreType.DMA((6,)),
    ]
    last_piece, groups = None, 0
    outs = [SDS(out_piece.shape, BF)] * 2 + [pltpu.HBM((length, depth), BF if final else F32)]
    out_specs = [any_spec()] * 3
    if final:
        last_piece, last_slabs, middle, gain, groups = last
        ins += in_hbm([middle]) + [gain] + in_hbm(last_slabs)
        specs += [any_spec(), vmem_spec()] + [any_spec()] * len(last_slabs)
        scratch += [
            pltpu.VMEM((length, depth), BF),
            pltpu.VMEM((length, depth), F32),
            pltpu.VMEM(rows.shape + (depth,), BF),
            pltpu.VMEM((length, depth), F32),
        ]
        outs += [pltpu.HBM((length, depth), F32), pltpu.VMEM((depth, length), BF), SDS((8, depth), F32)]
        outs += [pltpu.HBM((length, 256), BF)] * groups
        out_specs += [any_spec()] + [vmem_spec()] * (2 + groups)
    else:
        outs.append(pltpu.HBM((length, depth), F32))
        out_specs.append(any_spec())
    got = pl.pallas_call(
        functools.partial(
            feed_forward_body, piece, out_piece, first, last_piece, groups, len(onto)
        ),
        in_specs=specs + [any_spec()] * (piece.count + len(onto)),
        out_specs=out_specs,
        out_shape=outs,
        input_output_aliases={len(ins) + piece.count + k: k for k in range(len(onto))},
        scratch_shapes=scratch,
        compiler_params=params(48 if final else 32),
        cost_estimate=cost(14 if final else 11, 20),
        name="feed_forward",
    )(*ins, *in_hbm(slabs), *onto)
    return got[:2], got[2:]


def attend_back_body(piece, out_piece, extra, aliased, final, me, normed_t_in, proj, att, grad_att, inverse, kept_in, *refs):
    refs = list(refs)
    slabs, refs = refs[: piece.count], refs[piece.count :]
    if extra:
        branch_t = refs.pop(0)
        attended, refs = refs[:extra], refs[extra:]
    else:
        held = refs.pop(0)
    if final:
        tokens_in = refs.pop(0)
    refs = refs[aliased:]
    grad_normed, outs, refs = refs[0], refs[1:3], refs[3:]
    if final:
        sums = refs.pop(0)
    grad_proj, key_sum, value_sum = refs[:3]
    refs = refs[3:]
    kept, delta, keys_t, query_t, query_m, grad_m, staged, normed_t, total, weight, sems = refs[:11]
    for half in range(2):
        for i in ORDER:
            part = (pl.ds(half * 4, 4), pl.ds(KEPT[i], KEPT_ROWS[i]))
            sem = sems.at[5 + 4 * half + i]
            pltpu.make_async_copy(kept_in.at[part], kept.at[part], sem).start()
    copies = [pltpu.make_async_copy(normed_t_in, normed_t, sems.at[1])]
    if not extra:
        copies.append(pltpu.make_async_copy(held, total, sems.at[2]))
    if final:
        copies.append(pltpu.make_async_copy(tokens_in, refs[11], sems.at[3]))
    moves = [(half, 0, 384, weight.at[:, :, :, pl.ds(384 * half, 384)]) for half in range(2)]
    start_all(copies + piece_copies(piece, me, slabs, moves, sems.at[4], False))
    length = proj.shape[0]
    if extra:
        joined = join_heads([a[...] for a in attended])
        out_grad = nn(branch_t[...], joined).astype(BF)
        staged[:, :, :, 768:] = out_grad.reshape(staged.shape[:3] + (768,))
    for half in range(2):
        cols = slice(half * 128, half * 128 + 128)
        product = (grad_att[:, cols].astype(F32) * att[:, cols].astype(F32)).T
        for h in range(4):
            stat = slice(half * 4 + h, half * 4 + h + 1)
            total_here = jnp.sum(product[h * HD : (h + 1) * HD], axis=0, keepdims=True)
            delta[stat, :] = total_here * inverse[stat, :]
        keys_t[cols, :] = proj[:, half * 384 + 128 : half * 384 + 256].T

    def step(half, carry):
        col = pl.multiple_of(half * 384, 128)
        out = pl.multiple_of(half * 128, 128)
        share = jnp.concatenate(
            [jnp.broadcast_to(inverse[pl.ds(half * 4 + h, 1), :], (HD, length)) for h in range(4)], 0
        ).T
        grads = (grad_att[:, pl.ds(out, 128)].astype(F32) * share).astype(BF)
        for h in range(4):
            mine = head_row(h)
            query_m[h] = jnp.where(mine, proj[:, pl.ds(col, 128)], 0)
            grad_m[h] = jnp.where(mine, grads, 0)
        key_sum[...] = jnp.zeros_like(key_sum)
        value_sum[...] = jnp.zeros_like(value_sum)
        for i in (2, 1, 0, 3):
            first = 768 if i == 3 else 0
            last = (i + 1) * QB
            here = slice(first, last)
            there = slice(i * QB, last)
            values = proj[here, pl.ds(col + 256, 128)]
            rows_here = slice(KEPT[i], KEPT[i] + last - first)
            wait_bytes(
                kept.at[pl.ds(half * 4, 4), pl.ds(KEPT[i], KEPT_ROWS[i])], sems.at[5 + 4 * half + i]
            )
            all_probs, all_grads = [], []
            ahead = nt(values, grad_m[0, there, :])
            for h in range(4):
                grad_probs = ahead
                if h < 3:
                    ahead = nt(values, grad_m[h + 1, there, :])
                stat = pl.ds(half * 4 + h, 1)
                lanes = pl.ds(pl.multiple_of(half * 128 + h * HD, HD), HD)
                probs = kept[half * 4 + h, rows_here, :]
                grad_scores = (probs.astype(F32) * (grad_probs - delta[stat, there])).astype(BF)
                all_probs.append(probs)
                all_grads.append(grad_scores)
                query_t[lanes, there] = nn(keys_t[lanes, here], grad_scores)
            stacked = jnp.concatenate([grad_m[h, there, :] for h in range(4)], 0)
            value_sum[here, :] += nn(jnp.concatenate(all_probs, 1), stacked)
            stacked = jnp.concatenate([query_m[h, there, :] for h in range(4)], 0)
            key_sum[here, :] += nn(jnp.concatenate(all_grads, 1), stacked)
        grad_proj[:, pl.ds(col + 128, 128)] = (key_sum[...] * SCALE).astype(BF)
        grad_proj[:, pl.ds(col + 256, 128)] = value_sum[...].astype(BF)
        return carry

    lax.fori_loop(0, 2, step, 0)
    for half in range(2):
        grad_proj[:, half * 384 : half * 384 + 128] = (
            query_t[half * 128 : half * 128 + 128, :].T * SCALE
        ).astype(BF)
    for copy in copies:
        copy.wait()
    wait_bytes(weight, sems.at[4])
    for c in range(3):
        cols = slice(c * 256, c * 256 + 256)
        part = nn(normed_t[...], grad_proj[:, cols]).astype(BF)
        staged[:, :, :, cols] = part.reshape(staged.shape[:3] + (256,))
    moves = [(half, 0, 384, staged.at[:, :, :, pl.ds(384 * half, 384)]) for half in range(2)]
    if extra:
        moves += [
            (half, -384, 384, staged.at[:, :, :, pl.ds(768 + 384 * half, 384)]) for half in range(2)
        ]
    start_all(piece_copies(out_piece, me, outs, moves, sems.at[0], True))
    if final:
        sums[...] = jnp.zeros_like(sums)

    total_copies = []
    for c in range(3):
        cols = slice(c * 256, c * 256 + 256)
        value = nt(grad_proj[...], flat(weight[...])[cols])
        if not extra:
            value = value + total[:, cols]
        total[:, cols] = value
        total_copies.append(
            pltpu.make_async_copy(
                total.at[:, pl.ds(c * 256, 256)], grad_normed.at[:, pl.ds(c * 256, 256)], sems.at[2]
            )
        )
        total_copies[-1].start()
    if final:

        def sum_step(r, carry):
            at = pl.ds(pl.multiple_of(r * QB, QB), QB)
            value = total[at, :]
            hat, _ = norm_parts(refs[11][at, :].astype(F32))
            sums[0:1, :] += jnp.sum(value * hat, axis=0, keepdims=True)
            sums[1:2, :] += jnp.sum(value, axis=0, keepdims=True)
            return carry

        lax.fori_loop(0, length // QB, sum_step, 0)
    wait_bytes(staged, sems.at[0])
    wait_bytes(total, sems.at[2])


def attend_back(
    piece,
    out_piece,
    me,
    normed_t,
    proj,
    att,
    grad_att,
    inverse,
    kept,
    slabs,
    branch_t,
    attended,
    held,
    tokens,
    onto,
):
    depth, length = normed_t.shape
    extra = len(attended)
    final = tokens is not None
    columns = 1536 if extra else 768
    ins = [me] + in_hbm([normed_t, proj, att, grad_att, inverse, kept]) + in_hbm(slabs)
    specs = [smem_spec(), any_spec()] + [vmem_spec()] * 4 + [any_spec()] * (1 + len(slabs))
    if extra:
        ins += in_vmem([branch_t]) + in_hbm(attended)
        specs += [vmem_spec()] * (1 + extra)
    else:
        ins += in_hbm([held])
        specs += [any_spec()]
    if final:
        ins += in_hbm([tokens])
        specs += [any_spec()]
    outs = [pltpu.HBM((length, depth), F32)] + [SDS(out_piece.shape, BF)] * 2
    scratch = [
        pltpu.VMEM((8, 1792, QB), BF),
        pltpu.VMEM((8, length), F32),
        pltpu.VMEM((256, length), BF),
        pltpu.VMEM((256, length), F32),
        pltpu.VMEM((4, length, 128), BF),
        pltpu.VMEM((4, length, 128), BF),
        pltpu.VMEM(out_piece.rows.shape + (columns,), BF),
        pltpu.VMEM((depth, length), BF),
        pltpu.VMEM((length, depth), F32),
        pltpu.VMEM(piece.rows.shape + (768,), BF),
        pltpu.SemaphoreType.DMA((13,)),
    ]
    if final:
        outs.append(SDS((8, depth), F32))
        scratch.append(pltpu.VMEM((length, depth), BF))
    got = pl.pallas_call(
        functools.partial(attend_back_body, piece, out_piece, extra, len(onto), final),
        in_specs=specs + [any_spec()] * len(onto),
        out_specs=[any_spec()] * 3 + ([vmem_spec()] if final else []),
        out_shape=outs,
        input_output_aliases={len(ins) + k: 1 + k for k in range(len(onto))},
        scratch_shapes=[
            pltpu.VMEM((length, 768), BF),
            pltpu.VMEM((length, 128), F32),
            pltpu.VMEM((length, 128), F32),
        ]
        + scratch,
        compiler_params=params(40),
        cost_estimate=cost(12, 8),
        name="attend_back",
    )(*ins, *onto)
    return got[0], got[1:3], got[3] if final else None


def norm_back_body(
    start, core, tokens, grad_normed, grad_middle, gain, held, other, high, low, own, sem
):
    length = high.shape[0] // 2
    r = pl.program_id(0)
    hat, root = norm_parts(tokens[...].astype(F32))
    value = grad_middle[...] + norm_pull(grad_normed[...], hat, root, gain[...])
    top = value.astype(BF)
    rest = (value - top.astype(F32)).astype(BF)
    for base in (0, length):
        at = pl.ds(pl.multiple_of(base + r * QB, QB), QB)
        high[at, :] = top
        low[at, :] = rest

    @pl.when(r == pl.num_programs(0) - 1)
    def _():
        count = own.shape[0] // QB
        for k in range(count):
            own[k * QB : k * QB + QB, :] = turned([high, low], start[0], k)
        copy = pltpu.make_async_copy(own, held.at[core[0]], sem)
        copy.start()
        for k in range(count):
            other[k * QB : k * QB + QB, :] = turned([high, low], start[0], k + count)
        copy.wait()


def norm_back(start, core, tokens, grad_normed, grad_middle, gain):
    length, depth = tokens.shape
    half = (length // 2, depth)
    return pl.pallas_call(
        norm_back_body,
        grid=(length // QB,),
        in_specs=[smem_spec()] * 2 + [row_spec(depth, QB)] * 3 + [whole_spec((1, depth))],
        out_specs=[any_spec(), whole_spec(half)],
        out_shape=[pltpu.HBM((2,) + half, F32), SDS(half, F32)],
        scratch_shapes=[
            pltpu.VMEM((2 * length, depth), BF),
            pltpu.VMEM((2 * length, depth), BF),
            pltpu.VMEM(half, F32),
            pltpu.SemaphoreType.DMA,
        ],
        compiler_params=params(24),
        cost_estimate=cost(4, 16),
        name="norm_back",
    )(start, core, *in_hbm([tokens, grad_normed, grad_middle]), gain)


def split_far_body(counts, me, *refs):
    keep, send = refs[-2:]
    far = me[0] // 4
    begin = 0
    for count in counts:
        pieces, refs = refs[:count], refs[count:]
        cols = pl.ds(begin, pieces[0].shape[-1])
        begin += pieces[0].shape[-1]
        for k, out in enumerate((keep, send)):
            for slot in range(2):
                at = lax.bitwise_xor(far, k + 2 * slot)
                total = pieces[0][at].astype(F32)
                for piece in pieces[1:]:
                    total = total + piece[at].astype(F32)
                out[slot, :, cols] = total.astype(BF)


def split_far(me, groups):
    width, specs = 0, []
    for pieces in groups:
        far, block, columns = pieces[0].shape[-3:]
        width += columns
        for piece in pieces:
            if piece.ndim == 4:
                specs.append(pl.BlockSpec((None, far, block, columns), lambda i: (0, 0, 0, 0)))
            else:
                specs.append(whole_spec(piece.shape))
    return pl.pallas_call(
        functools.partial(split_far_body, [len(pieces) for pieces in groups]),
        grid=(1,),
        in_specs=[smem_spec()] + specs,
        out_specs=[whole_spec((2, block, width))] * 2,
        out_shape=[SDS((2, block, width), BF)] * 2,
        compiler_params=params(16),
        cost_estimate=cost(1, 2),
        name="split_far",
    )(me, *[piece for pieces in groups for piece in pieces])


def put_sums(ref, base, total):
    high = total.astype(BF)
    ref[base : base + 4, :] = high
    ref[base + 4 : base + 8, :] = (total - high.astype(F32)).astype(BF)
    ref[base + 8 : base + 16, :] = jnp.zeros((8, total.shape[1]), BF)


def get_sums(ref, base):
    return ref[base : base + 4, :].astype(F32) + ref[base + 4 : base + 8, :].astype(F32)


def last_join_body(own, other, own_last, other_last, sums, sums_away, keep, send):
    total = sums[...] + sums_away[...]
    rows = keep.shape[0] // 2
    width = own.shape[-1]
    for k in range(4):
        out = keep if k < 2 else send
        at = slice((k % 2) * rows, (k % 2 + 1) * rows)
        value = (own[k].astype(F32) + other[k].astype(F32)).astype(BF)
        out[at, :width] = value.reshape(rows, -1)
        value = (own_last[k].astype(F32) + other_last[k].astype(F32)).astype(BF)
        out[at, width:] = value.reshape(rows, -1)
    put_sums(send, 2 * rows, total)


def last_half_body(keep, send, near, rest, send_next):
    rows = rest.shape[0]
    value = keep[:rows, :].astype(F32) + near[:rows, :].astype(F32)
    rest[...] = value.astype(BF)
    value = keep[rows:, :].astype(F32) + near[rows : 2 * rows, :].astype(F32)
    send_next[:rows, :] = value.astype(BF)
    send_next[rows : rows + 16, :] = send[2 * rows :, :]
    send_next[rows + 16 :, :] = near[2 * rows :, :]


def last_split_body(flip, me, rest, send, away, keep, out_send):
    far = me[0] // 4
    rows = rest.shape[0]
    block = rows // 4
    for k, out in enumerate((keep, out_send)):
        for slot in range(2):
            at = pl.ds(pl.multiple_of(lax.bitwise_xor(far, k + 2 * slot) * block, 16), block)
            total = rest[at, :].astype(F32) + away[at, :].astype(F32)
            out[slot * block : (slot + 1) * block, :] = total.astype(BF)
    first, second = get_sums(send, rows + 16), get_sums(away, rows)
    swapped = lax.bitwise_xor(me[1], flip) == 1
    one, two = jnp.where(swapped, second, first), jnp.where(swapped, first, second)
    total = (get_sums(send, rows) + one) + (two + get_sums(away, rows + 16))
    put_sums(keep, 2 * block, total)
    put_sums(out_send, 2 * block, total)


def last_middle_body(keep, near, rest, send):
    block = (keep.shape[0] - 16) // 2
    value = keep[:block, :].astype(F32) + near[:block, :].astype(F32)
    rest[:block, :] = value.astype(BF)
    value = keep[block : 2 * block, :].astype(F32) + near[block : 2 * block, :].astype(F32)
    send[:block, :] = value.astype(BF)
    total = get_sums(keep, 2 * block) + get_sums(near, 2 * block)
    put_sums(rest, block, total)
    put_sums(send, block, total)


def last_sum_body(rest, away, first, grad_qkv, sums):
    block = rest.shape[0] - 16
    value = rest[:block, :].astype(F32) + away[:block, :].astype(F32)
    parts = [first[:, 384:], value[:, :384], value[:, 384:]]
    for which in range(3):
        cols = slice(which * 128, which * 128 + 128)
        grad_qkv[which] = jnp.concatenate([part[:, cols] for part in parts], 1)
    sums[...] = get_sums(rest, block) + get_sums(away, block)


def pack_body(part, out, up, down, packed):
    width = out.shape[1]
    packed[:, :width] = out[...]
    for s in range(up.shape[1] // part):
        cols = slice(s * part, (s + 1) * part)
        packed[:, width + 2 * s * part : width + (2 * s + 1) * part] = up[:, cols]
        packed[:, width + (2 * s + 1) * part : width + (2 * s + 2) * part] = down[:, cols]


def small_call(body, name, outs, scalars, values):
    return pl.pallas_call(
        body,
        in_specs=[smem_spec()] * len(scalars) + [vmem_spec()] * len(values),
        out_specs=[vmem_spec()] * len(outs),
        out_shape=outs,
        compiler_params=params(16),
        cost_estimate=cost(1, 3),
        name=name,
    )(*scalars, *values)


def swap(value):
    return lax.ppermute(value, "mp", [(0, 1), (1, 0)])


def tie(*values):
    return lax.optimization_barrier(values)


def hop(value, mask, count):
    return lax.ppermute(value, "dp", [(i, i ^ mask) for i in range(count)])


def hops(value, masks, count):
    return [(value, functools.partial(hop, mask=m, count=count)) for m in masks]


def hop_apart(value, masks, count):
    pairs = [(2 * i + c, 2 * (i ^ masks[c]) + c) for i in range(count) for c in range(2)]
    return lax.ppermute(value, ("dp", "mp"), pairs)


def far_hops(rows, values):
    return [
        (v, functools.partial(hop, mask=rows.near * m, count=rows.dp_count))
        for m, v in zip(range(1, rows.far), values)
    ]


def swaps(values):
    return [(v, swap) for v in values]


def send_all(requests):
    return [send(value) for value, send in requests]


def low_sum(values):
    total = values[0].astype(F32)
    for value in values[1:]:
        total = total + value.astype(F32)
    return total


class Flow:
    def __init__(self, me):
        self.me = me
        self.active = []

    def add(self, transfer, name, results, seeds=()):
        self.active.append([transfer, list(seeds), name, results])

    def step(self, *pivots, gate=None):
        values = [v for item in self.active for v in item[1]]
        tied = list(tie(self.me, *pivots, *values))
        self.me = tied.pop(0)
        pivots, tied = tied[: len(pivots)], tied[len(pivots) :]
        going, self.active, requests = self.active, [], []
        for item in going:
            transfer, values, name, results = item
            got, tied = tied[: len(values)], tied[len(values) :]
            try:
                if callable(transfer):
                    item[0] = transfer(*got)
                    asked = next(item[0])
                else:
                    asked = transfer.send(got)
                self.active.append(item)
                requests.append(asked)
            except StopIteration as stop:
                results[name] = stop.value
        gates = gate() if gate else []
        operands = [operand for asked in requests for operand, _ in asked]
        tied = list(tie(self.me, *gates, *operands))
        self.me = tied[0]
        tied = tied[1 + len(gates) :]
        for item, asked in zip(self.active, requests):
            item[1] = [send(operand) for (_, send), operand in zip(asked, tied)]
            tied = tied[len(asked) :]
        return pivots


def add_low(a, b):
    return (a.astype(F32) + b.astype(F32)).astype(BF)


def on_device(
    tokens, segment, ln1_gain, ln1_bias, w_qkv, w_out, ln2_gain, ln2_bias, w_up, w_down, cotangent
):
    dp_count = lax.axis_size("dp")
    core = lax.axis_index("mp")
    me = jnp.stack([lax.axis_index("dp"), core]).astype(jnp.int32)
    here, depth = tokens.shape[2], tokens.shape[3]
    length = 2 * here
    rows = Rows(dp_count, depth)

    groups = w_qkv.shape[2] // 128
    part = 384
    subs = w_up.shape[1] // part
    cut = subs // 2
    qkv = [w_qkv[:, :, g * 128 : (g + 1) * 128].reshape(-1, part) for g in range(groups)]
    shards = {"q": jnp.concatenate(qkv, 1)}

    def pack(out, up, down):
        return small_call(
            functools.partial(pack_body, part),
            "pack",
            [SDS((up.shape[0], out.shape[0] + 2 * up.shape[1]), BF)],
            [],
            [out.T, up, down.T],
        )[0]

    seg = lax.dynamic_index_in_dim(segment[:, 0], core, 0, keepdims=False)
    run = length * 3 // 4
    begin = jnp.argmax(seg[: length - run + 1] == seg[run - 1 :]).astype(jnp.int32)
    start = ((begin - here * core) % length).reshape(1)
    back = (length - start) % length
    seg_tail = lax.dynamic_slice_in_dim(jnp.concatenate([seg, seg]), begin + run, length - run)
    seg_col = seg_tail.reshape(-1, 1)
    seg_row = seg_tail.reshape(1, -1)
    gain1, bias1, gain2, bias2 = (
        v.reshape(1, -1) for v in (ln1_gain, ln1_bias, ln2_gain, ln2_bias)
    )

    flow = Flow(me)
    core_place = core.astype(jnp.int32).reshape(1)
    token_halves = [tokens[:, 0], swap(tokens[:, 0])]
    cot_halves = [cotangent[:, 0], swap(cotangent[:, 0])]
    wide = 2 * part
    qkv_pieces = [Piece(rows, "slabs")] + [Piece(rows, "slabs", part * g) for g in range(groups - 1)]
    out_piece = Piece(rows, "slabs")
    feed_pieces = [Piece(rows, "slabs", part + wide * s) for s in range(cut)]
    feed_pieces += [Piece(rows, "slabs", wide * s) for s in range(subs - cut)]
    feed_outs = [
        Piece(rows, "stack", 0, wide, s // cut) for s in range(subs)
    ]
    qkv_outs = [Piece(rows, "stack", part, wide, 0)]
    qkv_outs += [Piece(rows, "stack", 0, part, 1)] * (groups - 1)
    far = lax.axis_index("dp") // rows.near

    def gather_whole(shard):
        return lax.all_gather(shard, "dp", axis=0, tiled=True).reshape(rows.shape + (-1,))

    def fetch_near(near):
        got = yield hops(near, MASKS[1:], dp_count)
        own = [near] + got
        return own + [swap(x) for x in own]

    def via(mask):
        return functools.partial(hop, mask=mask, count=dp_count)

    def fetch_wide(shard, away):
        near, both_ways = yield [(shard, via(4)), (away, via(4))]
        (a0,) = arrange(rows, flow.me, [shard, near, away, both_ways], [shard.shape[1]])
        a1, a2, b0, away = yield [(a0, via(1)), (a0, via(2))] + swaps([a0]) + [(shard_c, via(8))]
        a3, b1, b2, near, both_ways = yield (
            [(a1, via(2))] + swaps([a1, a2]) + [(shard_c, via(4)), (away, via(4))]
        )
        slabs["a"] = [a0, a1, a2, a3, b0, b1, b2, swap(a3)]
        (c0,) = arrange(rows, flow.me, [shard_c, near, away, both_ways], [shard_c.shape[1]])
        (d0,) = yield swaps([c0])
        c1, c2 = yield [(c0, via(1)), (c0, via(2))]
        c3, d1, d2 = yield [(c2, via(1))] + swaps([c1, c2])
        return [c0, c1, c2, c3, d0, d1, d2, swap(c3)]

    def whole(shard):
        own = gather_whole(shard)
        return [own, swap(own)]

    def apart(flip):
        masks = (2, 1) if flip else (1, 2)
        return functools.partial(hop_apart, masks=masks, count=dp_count)

    def halve(flip, hurry, pause, own, other):
        if hurry:
            other = swap(other)
        else:
            (other,) = yield swaps([other])
        if pause:
            yield []
        keep, send = (low_sum([own[k : k + 2], other[k : k + 2]]).astype(BF) for k in (0, 2))
        (near,) = yield [(send, apart(flip))]
        (away,) = yield [(low_sum([keep[1], near[1]]).astype(BF), apart(1 - flip))]
        return [keep, near, away]

    def reduce_far(groups):
        keep, send = split_far(flow.me, groups)
        (near,) = yield [(send, via(4))]
        (away,) = yield [(low_sum([keep[1], near[1]]).astype(BF), via(8))]
        return low_sum([keep[0], near[0], away])

    def reduce_all(flip, own, other):
        group = yield from halve(flip, True, False, own, other)
        return (yield from reduce_far([sums_of[s] for s in range(subs - 1)] + [group]))

    def reduce_last(flip, own, own_last, other_last, sums):
        other_last, sums_away = swap(other_last), swap(sums)
        rows_here = rows.far * rows.block
        keep, send = small_call(
            last_join_body,
            "last_join",
            [SDS((2 * rows_here, wide), BF), SDS((2 * rows_here + 16, wide), BF)],
            [],
            [own, sums_of["other"], own_last, other_last, sums, sums_away],
        )
        (near,) = yield [(send, apart(flip))]
        return [keep, send, near]

    def exchange(value):
        (got,) = yield swaps([value])
        return got

    def reduce_one(flip, own, other):
        group = yield from halve(flip, False, False, own, other)
        return (yield from reduce_far([group]))

    def plain(own, other):
        value = low_sum([own, swap(other)]).astype(BF).reshape(depth, -1)
        return lax.psum_scatter(value, "dp", scatter_dimension=0, tiled=True).astype(F32)

    def run(transfer):
        requests = next(transfer)
        while True:
            try:
                requests = transfer.send(send_all(requests))
            except StopIteration as stop:
                return stop.value

    slabs, forward = {}, []

    def project(g):
        name = "q0" if g == 0 else "q1"
        forward.append(
            project_attend(qkv_pieces[g], flow.me, normed, seg_col, seg_row, slabs[name])
        )

    if rows.split:
        shard_q = shards["q"]
        got = send_all(far_hops(rows, [shard_q] * (rows.far - 1)))
        prepared = prepare(start, core_place, *token_halves, gain1, bias1)
        tied = tie(*got, *prepared, w_out, w_up, w_down)
        got, prepared = tied[:3], tied[3:6]
        shard_a = pack(*tied[6:])
        near_q0, near_q1 = arrange(rows, me, [shard_q] + list(got), [part, wide])
        own = [near_q0] + [hop(near_q0, m, dp_count) for m in MASKS[1:]]
        first_cols = part + wide * cut
        shard_c, shard_a = shard_a[:, first_cols:], shard_a[:, :first_cols]
        away_a = hop(shard_a, 8, dp_count)
        start_cot, _ = tie(start, near_q0)
        turned_cot = turn(start_cot, core_place, *cot_halves)
        tied = tie(*own, *turned_cot)
        own, turned_cot = tied[:4], tied[4:]
        slabs["q0"] = list(own) + [swap(v) for v in own]
        flow.add(fetch_near, "q1", slabs, [near_q1])
        flow.add(fetch_wide, "c", slabs, [shard_a, away_a])
        flow.step(own[3])
    else:
        shard_a = pack(w_out, w_up, w_down)
        for name, shard in (
            ("q0", shards["q"][:, :part]),
            ("q1", shards["q"][:, part:]),
            ("a", shard_a[:, : part + wide * cut]),
            ("c", shard_a[:, part + wide * cut :]),
        ):
            slabs[name] = whole(shard)
        prepared = prepare(start, core_place, *token_halves, gain1, bias1)
        turned_cot = turn(start, core_place, *cot_halves)
    x, normed, normed_t = prepared
    cot, cot_t = turned_cot
    for g in range(groups):
        project(g)
        flow.step(forward[g][2])
    atts = [f[1] for f in forward]
    middle, normed_ffn, normed_ffn_t = out_norm(
        out_piece, flow.me, x, gain2, bias2, atts, slabs["a"]
    )
    flow.step(normed_ffn)

    held = None
    sums_of = {}
    onto = []
    feed_names = ["a"] * cut + ["c"] * (subs - cut)
    for s in range(subs):
        final = s == subs - 1
        grads, held = feed_forward(
            feed_pieces[s],
            feed_outs[s],
            flow.me,
            normed_ffn,
            normed_ffn_t,
            cot,
            cot_t,
            held,
            slabs[feed_names[s]],
            [],
            (out_piece, slabs["a"], middle, gain2, groups) if final else None,
        )
        flip = s // cut
        if not rows.split:
            sums_of[s] = plain(*grads)
        elif final:
            flow.add(functools.partial(reduce_all, flip), "feed", sums_of, grads)
        else:
            flow.add(functools.partial(halve, flip, False, s == 0), s, sums_of, grads)
        if s == 1 and rows.split:
            flow.step(held[1], gate=lambda: slabs["c"][-1:])
        elif not final:
            flow.step(held[1])
    mixed, grad_middle, branch_t, sums2, *grad_atts = held
    flow.step(sums2)
    grad_projs = []
    onto = []

    held = None
    qkv_slabs = [slabs["q0"]] + [slabs["q1"]] * (groups - 1)
    for g in range(groups):
        proj, att, inverse, kept = forward[g]
        held, grads, sums1 = attend_back(
            qkv_pieces[g],
            qkv_outs[g],
            flow.me,
            normed_t,
            proj,
            att,
            grad_atts[g],
            inverse,
            kept,
            qkv_slabs[g],
            branch_t,
            atts if g == 0 else [],
            held,
            x if g == groups - 1 else None,
            onto,
        )
        if g == 0 and rows.split:
            flow.add(functools.partial(reduce_one, 0), "first", sums_of, grads)
        elif g == 0:
            sums_of["first"] = plain(*grads)
        elif g < groups - 1 and rows.split:
            flow.add(exchange, "other", sums_of, grads[1:])
            own_early = grads[0]
        elif not rows.split:
            sums_of[("last", g)] = plain(*grads)
        if g < groups - 1:
            flow.step(held)
    sums = jnp.concatenate([sums1[:2], sums2[:2]], 0)
    if rows.split:
        flow.add(
            functools.partial(reduce_last, 1), "last", sums_of, [own_early, *grads, sums]
        )
        (held,) = flow.step(held)
    start_late, _ = tie(back, flow.me)
    tokens_held, tokens_other = norm_back(start_late, core_place, x, held, grad_middle, gain1)
    mixed, tokens_other = tie(mixed, tokens_other)
    mixed_held, mixed_other = turn_back(back, core_place, mixed)
    mixed_got = swap(mixed_other)
    tokens_held, tokens_other = flow.step(tokens_held, tokens_other)
    if rows.split:
        block = rows.block
        keep, send, near = sums_of["last"]
        rows_here = rows.far * block
        rest, send = small_call(
            last_half_body,
            "last_half",
            [SDS((rows_here, wide), BF), SDS((rows_here + 32, wide), BF)],
            [],
            [keep, send, near],
        )
        away = apart(0)(send)
        keep, send = small_call(
            functools.partial(last_split_body, 1),
            "last_split",
            [SDS((2 * block + 16, wide), BF)] * 2,
            [flow.me],
            [rest, send, away],
        )
        flow.step(gate=lambda: [send])
        near = hop(send, 4, dp_count)
        rest, send = small_call(
            last_middle_body, "last_middle", [SDS((block + 16, wide), BF)] * 2, [], [keep, near]
        )
        rest, mixed_got, feed_sum = tie(rest, mixed_got, sums_of["feed"])
        away = hop(send, 8, dp_count)
        while flow.active:
            flow.step()
        grad_qkv, norm_sums = small_call(
            last_sum_body,
            "last_sum",
            [SDS((3, block, part), F32), SDS((4, depth), F32)],
            [],
            [rest, away, sums_of["first"]],
        )
        grad_qkv = grad_qkv.transpose(1, 0, 2)
        grad_out = sums_of["first"][:, :part].T
        feed_sums = [feed_sum]
    else:
        early = sums_of["first"]
        parts = [early[:, part:]] + [sums_of[("last", g)] for g in range(1, groups)]
        grad_qkv = jnp.concatenate([r.reshape(-1, 3, 128) for r in parts], 2)
        grad_out = early[:, :part].T
        feed_sums = [sums_of[s] for s in range(subs)]
        norm_sums = jnp.sum(lax.all_gather(sums + swap(sums), "dp", axis=0), 0)
    feed_sum = jnp.concatenate(feed_sums, 1) if len(feed_sums) > 1 else feed_sums[0]
    feed_list = [feed_sum[:, wide * s : wide * (s + 1)] for s in range(subs)]

    return (
        place(core_place, mixed_held, mixed_got)[:, None],
        place(core_place, tokens_held, swap(tokens_other))[:, None],
        norm_sums[0],
        norm_sums[1],
        grad_qkv,
        grad_out,
        norm_sums[2],
        norm_sums[3],
        jnp.concatenate([r[:, :part] for r in feed_list], 1),
        jnp.concatenate([r[:, part:] for r in feed_list], 1).T,
    )


def solution(mesh):
    in_specs = (
        P(None, "dp", "mp", None),
        P(None, "dp", None),
        P(),
        P(),
        P("dp", None, "mp"),
        P("mp", "dp"),
        P(),
        P(),
        P("dp", "mp"),
        P("mp", "dp"),
        P(None, "dp", "mp", None),
    )
    out_specs = (
        P(None, "dp", "mp", None),
        P(None, "dp", "mp", None),
        P(),
        P(),
        P("dp", None, "mp"),
        P("mp", "dp"),
        P(),
        P(),
        P("dp", "mp"),
        P("mp", "dp"),
    )
    return jax.shard_map(
        on_device, mesh=mesh, in_specs=in_specs, out_specs=out_specs, check_vma=False
    )
```

```python
import functools
import math

import jax
import jax.numpy as jnp
from jax import lax
from jax.experimental import pallas as pl
from jax.experimental.pallas import tpu as pltpu
from jax.sharding import PartitionSpec as P

HD = 32
QB = 256
EPS = 1e-05
BF = jnp.bfloat16
F32 = jnp.float32
NEG = -1e30
SCALE = 1.0 / math.sqrt(HD)
LOG2E = math.log2(math.e)
C2 = SCALE * LOG2E
MIB = 1024 * 1024
SDS = jax.ShapeDtypeStruct


def nn(a, b):
    return lax.dot_general(a, b, (((1,), (0,)), ((), ())), preferred_element_type=F32)


def nt(a, b):
    return lax.dot_general(a, b, (((1,), (1,)), ((), ())), preferred_element_type=F32)


def params(mib):
    return pltpu.CompilerParams(vmem_limit_bytes=mib * MIB)


def in_hbm(values):
    return [pltpu.with_memory_space_constraint(v, pltpu.HBM) for v in values]


def in_vmem(values):
    return [pltpu.with_memory_space_constraint(v, pltpu.VMEM) for v in values]


def cost(gflop, mbytes):
    return pl.CostEstimate(flops=int(gflop * 1e9), bytes_accessed=int(mbytes * 1e6), transcendentals=0)


def any_spec():
    return pl.BlockSpec(memory_space=pl.ANY)


def smem_spec():
    return pl.BlockSpec(memory_space=pltpu.SMEM)


def vmem_spec():
    return pl.BlockSpec(memory_space=pltpu.VMEM)


def row_spec(width, rows=512):
    return pl.BlockSpec((rows, width), lambda r: (r, 0))


def column_spec(height, rows=512):
    return pl.BlockSpec((height, rows), lambda r: (0, r))


def whole_spec(shape):
    return pl.BlockSpec(shape, lambda r: tuple(0 for _ in shape))


MASKS = (0, 1, 2, 3)


class Rows:
    def __init__(self, dp_count, depth):
        self.dp_count = dp_count
        self.depth = depth
        self.split = (depth // dp_count) % 16 == 0 and dp_count == 16
        self.near = 4 if self.split else 1
        self.far = dp_count // 4 if self.split else 1
        self.block = depth // (self.near * self.far)
        self.shape = (self.far, self.near, self.block)


class Piece:
    def __init__(self, rows, kind, start=0, width=0, flip=0):
        self.rows = rows
        self.flip = flip
        self.kind = kind if rows.split else "whole"
        self.start = start
        self.count = 2 * len(MASKS) if self.kind == "slabs" else 2
        if self.kind == "stack":
            self.shape = (len(MASKS), rows.far, rows.block, width)
        else:
            self.shape = rows.shape + (width,)


def piece_copies(piece, me, refs, moves, sem, outward):
    copies = []
    each = piece.count // 2
    for half, column, width, view in moves:
        cols = pl.ds(piece.start + column, width)
        if piece.kind == "whole":
            pairs = [(refs[half].at[:, :, :, cols], view)]
        else:
            pairs = []
            order = lax.bitwise_xor(me[1], piece.flip ^ half)
            masks = (0, 2 - order, 1 + order, 3) if piece.kind == "stack" else MASKS
            for k, mask in enumerate(masks):
                ref = refs[half].at[k] if piece.kind == "stack" else refs[half * each + k]
                near = lax.bitwise_xor(lax.rem(me[0], 4), mask)
                pairs.append((ref.at[:, :, cols], view.at[:, near]))
        for outside, inside in pairs:
            if outward:
                copies.append(pltpu.make_async_copy(inside, outside, sem))
            else:
                copies.append(pltpu.make_async_copy(outside, inside, sem))
    return copies


def start_all(copies):
    for copy in copies:
        copy.start()


def wait_bytes(ref, sem):
    pltpu.make_async_copy(ref, ref, sem).wait()


def flat(value):
    return value.reshape(-1, value.shape[-1])


def head_row(h):
    return lax.broadcasted_iota(jnp.int32, (1, 128), 1) // HD == h


def fill_bias(bias, seg_col, seg_row):
    key = lax.broadcasted_iota(jnp.int32, (QB, QB), 0)
    query = lax.broadcasted_iota(jnp.int32, (QB, QB), 1)
    bias[0] = jnp.where(query >= key, 0.0, NEG)
    bias[1] = jnp.where((query >= key) & (seg_col[...] == seg_row[...]), 0.0, NEG)


def turned(doubles, start, r):
    coarse = pl.multiple_of(start // 16 * 16 + r * QB, 16)
    fine = start % 16
    row = lax.broadcasted_iota(jnp.int32, (QB, QB + 16), 0)
    col = lax.broadcasted_iota(jnp.int32, (QB, QB + 16), 1)
    pick = jnp.where(col - row == fine, 1.0, 0.0).astype(BF)
    total = None
    for double in doubles:
        part = nn(pick, double[pl.ds(coarse, QB + 16), :])
        total = part if total is None else total + part
    return total


def norm_parts(values):
    centered = values - jnp.mean(values, axis=-1, keepdims=True)
    spread = jnp.mean(centered * centered, axis=-1, keepdims=True)
    root = lax.rsqrt(spread + EPS)
    return centered * root, root


def fill_double(double, core, own, other, sem):
    here = own.shape[1]
    for k, half in enumerate((own, other)):
        pltpu.make_async_copy(half.at[core], double.at[pl.ds(k * here, here)], sem).start()
    wait_bytes(double.at[pl.ds(0, 2 * here)], sem)
    double[2 * here :, :] = double[: 2 * here, :]


def prepare_body(start, core, own, other, gain, offset, x_out, normed_out, normed_t_out, double, x, normed, normed_t, sems):
    fill_double(double, core[0], own, other, sems.at[3])

    def step(r, carry):
        at = pl.ds(pl.multiple_of(r * QB, QB), QB)
        value = turned([double], start[0], r)
        x[at, :] = value.astype(BF)
        hat, _ = norm_parts(value)
        low = (hat * gain[...] + offset[...]).astype(BF)
        normed[at, :] = low
        normed_t[:, at] = low.T
        return carry

    lax.fori_loop(0, x.shape[0] // QB, step, 0)
    copies = [
        pltpu.make_async_copy(normed, normed_out, sems.at[0]),
        pltpu.make_async_copy(x, x_out, sems.at[1]),
        pltpu.make_async_copy(normed_t, normed_t_out, sems.at[2]),
    ]
    start_all(copies)
    for copy in copies:
        copy.wait()


def prepare(start, core, own, other, gain, offset):
    _, here, depth = own.shape
    shape, shape_t = (2 * here, depth), (depth, 2 * here)
    shapes = [shape, shape, shape_t]
    return pl.pallas_call(
        prepare_body,
        in_specs=[smem_spec()] * 2 + [any_spec()] * 2 + [vmem_spec()] * 2,
        out_specs=[any_spec()] * 3,
        out_shape=[pltpu.HBM(s, BF) for s in shapes],
        scratch_shapes=[pltpu.VMEM((4 * here, depth), BF)]
        + [pltpu.VMEM(s, BF) for s in shapes]
        + [pltpu.SemaphoreType.DMA((4,))],
        compiler_params=params(20),
        cost_estimate=cost(4, 8),
        name="prepare",
    )(start, core, *in_hbm([own, other]), gain, offset)


def turn_body(start, core, own, other, cot_out, cot_t_out, double, cot, cot_t, sems):
    fill_double(double, core[0], own, other, sems.at[2])

    def step(r, carry):
        at = pl.ds(pl.multiple_of(r * QB, QB), QB)
        low = turned([double], start[0], r).astype(BF)
        cot[at, :] = low
        cot_t[:, at] = low.T
        return carry

    lax.fori_loop(0, cot.shape[0] // QB, step, 0)
    copies = [
        pltpu.make_async_copy(cot, cot_out, sems.at[0]),
        pltpu.make_async_copy(cot_t, cot_t_out, sems.at[1]),
    ]
    start_all(copies)
    for copy in copies:
        copy.wait()


def turn(start, core, own, other):
    _, here, depth = own.shape
    shapes = [(2 * here, depth), (depth, 2 * here)]
    return pl.pallas_call(
        turn_body,
        in_specs=[smem_spec()] * 2 + [any_spec()] * 2,
        out_specs=[any_spec()] * 2,
        out_shape=[pltpu.HBM(s, BF) for s in shapes],
        scratch_shapes=[pltpu.VMEM((4 * here, depth), BF)]
        + [pltpu.VMEM(s, BF) for s in shapes]
        + [pltpu.SemaphoreType.DMA((3,))],
        compiler_params=params(16),
        cost_estimate=cost(4, 8),
        name="turn",
    )(start, core, *in_hbm([own, other]))


def turn_back_body(start, core, values, held, other, double, own, sem):
    here = other.shape[0]
    double[: 2 * here, :] = values[...]
    double[2 * here :, :] = values[...]
    count = here // QB

    def step(r, carry):
        at = pl.ds(pl.multiple_of(r * QB, QB), QB)
        own[at, :] = turned([double], start[0], r).astype(BF)
        other[at, :] = turned([double], start[0], r + count).astype(BF)
        return carry

    lax.fori_loop(0, count, step, 0)
    copy = pltpu.make_async_copy(own, held.at[core[0]], sem)
    copy.start()
    copy.wait()


def place_body(core, other, held, out, sem):
    copy = pltpu.make_async_copy(other, out.at[1 - core[0]], sem)
    copy.start()
    copy.wait()


def place(core, held, other):
    return pl.pallas_call(
        place_body,
        in_specs=[smem_spec(), any_spec(), any_spec()],
        out_specs=any_spec(),
        out_shape=pltpu.HBM(held.shape, held.dtype),
        input_output_aliases={2: 0},
        scratch_shapes=[pltpu.SemaphoreType.DMA],
        compiler_params=params(4),
        cost_estimate=cost(0, 4),
        name="place",
    )(core, other, *in_hbm([held]))


def turn_back(start, core, values):
    length, depth = values.shape
    half = (length // 2, depth)
    return pl.pallas_call(
        turn_back_body,
        in_specs=[smem_spec()] * 2 + [vmem_spec()],
        out_specs=[any_spec(), vmem_spec()],
        out_shape=[pltpu.HBM((2,) + half, BF), SDS(half, BF)],
        scratch_shapes=[
            pltpu.VMEM((2 * length, depth), BF),
            pltpu.VMEM(half, BF),
            pltpu.SemaphoreType.DMA,
        ],
        compiler_params=params(16),
        cost_estimate=cost(2, 4),
        name="turn_back",
    )(start, core, values)


def arrange_body(widths, me, *refs):
    pieces, outs = refs[:4], refs[4:]
    far = me[0] // 4
    for m, piece in enumerate(pieces):
        begin = 0
        for out, width in zip(outs, widths):
            out[lax.bitwise_xor(far, m)] = piece[:, begin : begin + width]
            begin += width


def arrange(rows, me, pieces, widths):
    return pl.pallas_call(
        functools.partial(arrange_body, widths),
        in_specs=[smem_spec()] + [vmem_spec()] * 4,
        out_specs=[vmem_spec()] * len(widths),
        out_shape=[SDS((rows.far, rows.block, w), BF) for w in widths],
        compiler_params=params(8),
        cost_estimate=cost(1, 1),
        name="arrange",
    )(me, *pieces)


def project_attend_body(piece, me, normed_in, seg_col, seg_row, *refs):
    slabs = refs[: piece.count]
    proj_out, att, lse, weight, proj, normed, bias, keys_m, values_t, att_t, sem, out_sem = refs[
        piece.count :
    ]
    normed_copy = pltpu.make_async_copy(normed_in, normed, out_sem)
    normed_copy.start()
    moves = [(half, 0, 384, weight.at[:, :, :, pl.ds(384 * half, 384)]) for half in range(2)]
    start_all(piece_copies(piece, me, slabs, moves, sem, False))
    fill_bias(bias, seg_col, seg_row)
    values_t[...] = jnp.ones_like(values_t)
    normed_copy.wait()
    wait_bytes(weight, sem)

    for c in range(3):
        cols = slice(c * 256, c * 256 + 256)
        proj[:, cols] = nn(normed[...], flat(weight[:, :, :, cols])).astype(BF)
    proj_copy = pltpu.make_async_copy(proj, proj_out, out_sem)
    proj_copy.start()
    for half in range(2):
        flipped = proj[:, half * 384 + 256 : half * 384 + 384].T
        for h in range(4):
            values_t[half * 4 + h, 0:HD, :] = flipped[h * HD : (h + 1) * HD]

    units = [(h, i) for i in (2, 1, 0, 3) for h in range(4)]

    def step(half, carry):
        col = pl.multiple_of(half * 384, 128)
        for h in range(4):
            keys_m[h] = jnp.where(head_row(h), proj[:, pl.ds(col + 128, 128)], 0)

        def score(h, i):
            first = 768 if i == 3 else 0
            scores = nt(keys_m[h, first : (i + 1) * QB, :], proj[i * QB : (i + 1) * QB, pl.ds(col, 128)])
            edge = scores[-QB:] + bias[1 if i == 3 else 0]
            return jnp.concatenate([scores[:-QB], edge], 0) if scores.shape[0] > QB else edge

        ahead = score(*units[0])
        for k, (h, i) in enumerate(units):
            scores = ahead
            if k + 1 < len(units):
                ahead = score(*units[k + 1])
            first = 768 if i == 3 else 0
            last = (i + 1) * QB
            at = slice(i * QB, last)
            peak = jnp.max(scores, axis=0, keepdims=True) * C2
            probs = jnp.exp2(scores * C2 - peak).astype(BF)
            summed = nn(values_t[half * 4 + h, :, first:last], probs)
            total = summed[HD : HD + 1]
            att_t[pl.ds(pl.multiple_of(half * 128 + h * HD, HD), HD), at] = summed[:HD] / total
            lse[pl.ds(half * 4 + h, 1), at] = peak + jnp.log2(total)
        return carry

    lax.fori_loop(0, 2, step, 0)
    for half in range(2):
        cols = slice(half * 128, half * 128 + 128)
        att[:, cols] = att_t[cols, :].T.astype(BF)
    proj_copy.wait()


def project_attend(piece, me, normed, seg_col, seg_row, slabs):
    length, depth = normed.shape
    rows = piece.rows
    return pl.pallas_call(
        functools.partial(project_attend_body, piece),
        in_specs=[smem_spec(), any_spec()] + [vmem_spec()] * 2 + [any_spec()] * len(slabs),
        out_specs=[any_spec()] + [vmem_spec()] * 2,
        out_shape=[
            pltpu.HBM((length, 768), BF),
            pltpu.HBM((length, 256), BF),
            pltpu.HBM((8, length), F32),
        ],
        scratch_shapes=[
            pltpu.VMEM(rows.shape + (768,), BF),
            pltpu.VMEM((length, 768), BF),
            pltpu.VMEM((length, depth), BF),
            pltpu.VMEM((2, QB, QB), F32),
            pltpu.VMEM((4, length, 128), BF),
            pltpu.VMEM((8, HD + 16, length), BF),
            pltpu.VMEM((256, length), F32),
            pltpu.SemaphoreType.DMA,
            pltpu.SemaphoreType.DMA,
        ],
        compiler_params=params(20),
        cost_estimate=cost(8, 8),
        name="project_attend",
    )(me, *in_hbm([normed]), seg_col, seg_row, *in_hbm(slabs))


def join_heads(attended):
    return jnp.concatenate([a[:, :128] for a in attended] + [a[:, 128:] for a in attended], 1)


def out_norm_body(piece, groups, me, tokens, gain, offset, *refs):
    attended = refs[:groups]
    slabs = refs[groups : groups + piece.count]
    middle, normed, normed_t, weight, sem = refs[groups + piece.count :]
    width = weight.shape[3] // 2

    @pl.when(pl.program_id(0) == 0)
    def _():
        moves = [(half, 0, width, weight.at[:, :, :, pl.ds(width * half, width)]) for half in range(2)]
        start_all(piece_copies(piece, me, slabs, moves, sem, False))
        wait_bytes(weight, sem)

    value = tokens[...].astype(F32) + nt(join_heads([a[...] for a in attended]), flat(weight[...]))
    middle[...] = value
    hat, _ = norm_parts(value)
    low = (hat * gain[...] + offset[...]).astype(BF)
    normed[...] = low
    normed_t[...] = low.T


def out_norm(piece, me, tokens, gain, offset, attended, slabs):
    length, depth = tokens.shape
    return pl.pallas_call(
        functools.partial(out_norm_body, piece, len(attended)),
        grid=(length // 512,),
        in_specs=[smem_spec(), row_spec(depth), whole_spec((1, depth)), whole_spec((1, depth))]
        + [row_spec(256)] * len(attended)
        + [any_spec()] * len(slabs),
        out_specs=[row_spec(depth)] * 2 + [column_spec(depth)],
        out_shape=[
            pltpu.HBM((length, depth), F32),
            pltpu.VMEM((length, depth), BF),
            pltpu.VMEM((depth, length), BF),
        ],
        scratch_shapes=[pltpu.VMEM(piece.rows.shape + (depth,), BF), pltpu.SemaphoreType.DMA],
        compiler_params=params(28),
        cost_estimate=cost(3, 8),
        name="out_norm",
    )(me, *in_hbm([tokens]), gain, offset, *in_hbm(attended), *in_hbm(slabs))


def gelu_parts(values):
    size = jnp.abs(values)
    density = jnp.exp2(values * values * (-0.5 * LOG2E) + math.log2(1.0 / math.sqrt(2 * math.pi)))
    below = 1.0 + 0.2316419 * size
    t = pl.reciprocal(below, approx=True)
    t = t * (2.0 - below * t)
    poly = t * (
        0.319381530
        + t * (-0.356563782 + t * (1.781477937 + t * (-1.821255978 + t * 1.330274429)))
    )
    tail = density * poly
    below = jnp.where(values >= 0, 1.0 - tail, tail)
    return values * below, below + values * density


def norm_pull(grad, hat, root, gain):
    scaled = grad * gain
    first = jnp.mean(scaled, axis=-1, keepdims=True)
    second = jnp.mean(scaled * hat, axis=-1, keepdims=True)
    return root * (scaled - first - hat * second)


def feed_forward_body(
    piece, out_piece, first, last_piece, groups, aliased, me, normed, normed_t, cot, cot_t, *refs
):
    refs = list(refs)
    final = last_piece is not None
    held = [] if first else [refs.pop(0), refs.pop(0)]
    if final:
        middle, gain = refs.pop(0), refs.pop(0)
        out_slabs, refs = refs[: last_piece.count], refs[last_piece.count :]
    slabs, refs = refs[: piece.count], refs[piece.count + aliased :]
    outs, refs = refs[:2], refs[2:]
    mixed = refs.pop(0)
    if final:
        grad_middle_out, branch_t, sums = refs[:3]
        grad_att, refs = refs[3 : 3 + groups], refs[3 + groups :]
    else:
        grad_in = refs.pop(0)
    weight, staged, act, grad_hidden, mixed_acc, grad_acc, sems = refs[:7]
    if final:
        mixed_low, middle_here, out_weight, grad_middle = refs[7:]
    length, depth = normed.shape
    moves = []
    for half in range(2):
        for which in range(2):
            at = pl.ds(which * 768 + half * 384, 384)
            moves.append((half, which * 384, 384, at))
    into = [(h, c, w, weight.at[:, :, :, at]) for h, c, w, at in moves]
    outof = [(h, c, w, staged.at[:, :, :, at]) for h, c, w, at in moves]
    start_all(piece_copies(piece, me, slabs, into, sems.at[0], False))
    held_copies = []
    if not first:
        held_copies.append(pltpu.make_async_copy(held[0], mixed_acc, sems.at[1]))
        held_copies.append(pltpu.make_async_copy(held[1], grad_acc, sems.at[2]))
    if final:
        held_copies.append(pltpu.make_async_copy(middle, middle_here, sems.at[4]))
    start_all(held_copies)
    if final:
        width = depth // 2
        views = [
            (half, 0, width, out_weight.at[:, :, :, pl.ds(width * half, width)]) for half in range(2)
        ]
        start_all(piece_copies(last_piece, me, out_slabs, views, sems.at[5], False))
    wait_bytes(weight, sems.at[0])
    chunks = [slice(c * 256, c * 256 + 256) for c in range(3)]

    def products(c):
        hidden = nn(normed[...], flat(weight[:, :, :, c * 256 : c * 256 + 256]))
        return hidden, nn(cot[...], flat(weight[:, :, :, 768 + c * 256 : 1024 + c * 256]))

    ahead = products(0)
    for c in range(3):
        hidden, grad_act = ahead
        if c < 2:
            ahead = products(c + 1)
        value, slope = gelu_parts(hidden)
        act[:, chunks[c]] = value.astype(BF)
        grad_hidden[:, chunks[c]] = (grad_act * slope).astype(BF)
    for copy in held_copies:
        copy.wait()
    for cols in chunks:
        mixed_part = nt(act[...], flat(weight[:, :, :, 768:1536])[cols])
        grad_part = nt(grad_hidden[...], flat(weight[:, :, :, 0:768])[cols])
        if not first:
            mixed_part = mixed_part + mixed_acc[:, cols]
            grad_part = grad_part + grad_acc[:, cols]
        if final:
            mixed_low[:, cols] = (middle_here[:, cols] + mixed_part).astype(BF)
        else:
            mixed_acc[:, cols] = mixed_part
        grad_acc[:, cols] = grad_part
    if final:
        out_copies = [pltpu.make_async_copy(mixed_low, mixed, sems.at[1])]
        start_all(out_copies)
        wait_bytes(out_weight, sems.at[5])
        sums[...] = jnp.zeros_like(sums)

        def back_step(r, carry):
            at = pl.ds(pl.multiple_of(r * 512, 512), 512)
            hat, root = norm_parts(middle_here[at, :])
            grad = grad_acc[at, :]
            value = cot[at, :].astype(F32) + norm_pull(grad, hat, root, gain[...])
            grad_middle[at, :] = value
            low = value.astype(BF)
            branch_t[:, at] = low.T
            sums[0:1, :] += jnp.sum(grad * hat, axis=0, keepdims=True)
            sums[1:2, :] += jnp.sum(grad, axis=0, keepdims=True)
            back = nn(low, flat(out_weight[...])).astype(BF)
            for g in range(groups):
                grad_att[g][at, 0:128] = back[:, g * 128 : g * 128 + 128]
                grad_att[g][at, 128:256] = back[:, width + g * 128 : width + g * 128 + 128]
            return carry

        lax.fori_loop(0, length // 512, back_step, 0)
        out_copies.append(pltpu.make_async_copy(grad_middle, grad_middle_out, sems.at[2]))
        out_copies[-1].start()
    else:
        out_copies = [
            pltpu.make_async_copy(mixed_acc, mixed, sems.at[1]),
            pltpu.make_async_copy(grad_acc, grad_in, sems.at[2]),
        ]
        start_all(out_copies)
    for c in range(3):
        cols = slice(c * 256, c * 256 + 256)
        up = nn(normed_t[...], grad_hidden[:, cols]).astype(BF)
        staged[:, :, :, cols] = up.reshape(staged.shape[:3] + (256,))
        down = nn(cot_t[...], act[:, cols]).astype(BF)
        staged[:, :, :, 768 + c * 256 : 1024 + c * 256] = down.reshape(staged.shape[:3] + (256,))
    start_all(piece_copies(out_piece, me, outs, outof, sems.at[3], True))
    for copy in out_copies:
        copy.wait()
    wait_bytes(staged, sems.at[3])


def feed_forward(
    piece, out_piece, me, normed, normed_t, cot, cot_t, held, slabs, onto, last=None
):
    length, depth = normed.shape
    rows = piece.rows
    first, final = held is None, last is not None
    ins = [me] + in_vmem([normed, normed_t, cot, cot_t]) + ([] if first else in_hbm(held))
    specs = [smem_spec()] + [vmem_spec()] * 4 + [any_spec()] * (0 if first else 2)
    scratch = [
        pltpu.VMEM(rows.shape + (1536,), BF),
        pltpu.VMEM(rows.shape + (1536,), BF),
        pltpu.VMEM((length, 768), BF),
        pltpu.VMEM((length, 768), BF),
        pltpu.VMEM((length, depth), F32),
        pltpu.VMEM((length, depth), F32),
        pltpu.SemaphoreType.DMA((6,)),
    ]
    last_piece, groups = None, 0
    outs = [SDS(out_piece.shape, BF)] * 2 + [pltpu.HBM((length, depth), BF if final else F32)]
    out_specs = [any_spec()] * 3
    if final:
        last_piece, last_slabs, middle, gain, groups = last
        ins += in_hbm([middle]) + [gain] + in_hbm(last_slabs)
        specs += [any_spec(), vmem_spec()] + [any_spec()] * len(last_slabs)
        scratch += [
            pltpu.VMEM((length, depth), BF),
            pltpu.VMEM((length, depth), F32),
            pltpu.VMEM(rows.shape + (depth,), BF),
            pltpu.VMEM((length, depth), F32),
        ]
        outs += [pltpu.HBM((length, depth), F32), pltpu.VMEM((depth, length), BF), SDS((8, depth), F32)]
        outs += [pltpu.HBM((length, 256), BF)] * groups
        out_specs += [any_spec()] + [vmem_spec()] * (2 + groups)
    else:
        outs.append(pltpu.HBM((length, depth), F32))
        out_specs.append(any_spec())
    got = pl.pallas_call(
        functools.partial(
            feed_forward_body, piece, out_piece, first, last_piece, groups, len(onto)
        ),
        in_specs=specs + [any_spec()] * (piece.count + len(onto)),
        out_specs=out_specs,
        out_shape=outs,
        input_output_aliases={len(ins) + piece.count + k: k for k in range(len(onto))},
        scratch_shapes=scratch,
        compiler_params=params(48 if final else 32),
        cost_estimate=cost(14 if final else 11, 20),
        name="feed_forward",
    )(*ins, *in_hbm(slabs), *onto)
    return got[:2], got[2:]


def attend_back_body(piece, out_piece, extra, aliased, final, me, normed_t_in, proj, att, grad_att, lse, seg_col, seg_row, *refs):
    refs = list(refs)
    slabs, refs = refs[: piece.count], refs[piece.count :]
    if extra:
        branch_t = refs.pop(0)
        attended, refs = refs[:extra], refs[extra:]
    else:
        held = refs.pop(0)
    if final:
        tokens_in = refs.pop(0)
    refs = refs[aliased:]
    grad_normed, outs, refs = refs[0], refs[1:3], refs[3:]
    if final:
        sums = refs.pop(0)
    grad_proj, key_sum, value_sum = refs[:3]
    refs = refs[3:]
    bias, delta, keys_t, query_t, query_m, grad_m, staged, normed_t, total, weight, sems = refs[:11]
    copies = [pltpu.make_async_copy(normed_t_in, normed_t, sems.at[1])]
    if not extra:
        copies.append(pltpu.make_async_copy(held, total, sems.at[2]))
    if final:
        copies.append(pltpu.make_async_copy(tokens_in, refs[11], sems.at[3]))
    moves = [(half, 0, 384, weight.at[:, :, :, pl.ds(384 * half, 384)]) for half in range(2)]
    start_all(copies + piece_copies(piece, me, slabs, moves, sems.at[4], False))
    length = proj.shape[0]
    fill_bias(bias, seg_col, seg_row)
    if extra:
        joined = join_heads([a[...] for a in attended])
        out_grad = nn(branch_t[...], joined).astype(BF)
        staged[:, :, :, 768:] = out_grad.reshape(staged.shape[:3] + (768,))
    for half in range(2):
        cols = slice(half * 128, half * 128 + 128)
        product = (grad_att[:, cols].astype(F32) * att[:, cols].astype(F32)).T
        for h in range(4):
            delta[half * 4 + h : half * 4 + h + 1, :] = jnp.sum(
                product[h * HD : (h + 1) * HD], axis=0, keepdims=True
            )
        keys_t[cols, :] = proj[:, half * 384 + 128 : half * 384 + 256].T

    def step(half, carry):
        col = pl.multiple_of(half * 384, 128)
        out = pl.multiple_of(half * 128, 128)
        for h in range(4):
            mine = head_row(h)
            query_m[h] = jnp.where(mine, proj[:, pl.ds(col, 128)], 0)
            grad_m[h] = jnp.where(mine, grad_att[:, pl.ds(out, 128)], 0)
        key_sum[...] = jnp.zeros_like(key_sum)
        value_sum[...] = jnp.zeros_like(value_sum)
        for i in (2, 1, 0, 3):
            first = 768 if i == 3 else 0
            last = (i + 1) * QB
            here = slice(first, last)
            there = slice(i * QB, last)
            keys = proj[here, pl.ds(col + 128, 128)]
            values = proj[here, pl.ds(col + 256, 128)]

            def products(h):
                scores = nt(keys, query_m[h, there, :])
                edge = scores[-QB:] + bias[1 if i == 3 else 0]
                if last - first > QB:
                    scores = jnp.concatenate([scores[:-QB], edge], 0)
                else:
                    scores = edge
                return scores, nt(values, grad_m[h, there, :])

            all_probs, all_grads = [], []
            ahead = products(0)
            for h in range(4):
                scores, grad_probs = ahead
                if h < 3:
                    ahead = products(h + 1)
                stat = pl.ds(half * 4 + h, 1)
                lanes = pl.ds(pl.multiple_of(half * 128 + h * HD, HD), HD)
                probs = jnp.exp2(scores * C2 - lse[stat, there])
                grad_scores = (probs * (grad_probs - delta[stat, there])).astype(BF)
                all_probs.append(probs.astype(BF))
                all_grads.append(grad_scores)
                query_t[lanes, there] = nn(keys_t[lanes, here], grad_scores)
            stacked = jnp.concatenate([grad_m[h, there, :] for h in range(4)], 0)
            value_sum[here, :] += nn(jnp.concatenate(all_probs, 1), stacked)
            stacked = jnp.concatenate([query_m[h, there, :] for h in range(4)], 0)
            key_sum[here, :] += nn(jnp.concatenate(all_grads, 1), stacked)
        grad_proj[:, pl.ds(col + 128, 128)] = (key_sum[...] * SCALE).astype(BF)
        grad_proj[:, pl.ds(col + 256, 128)] = value_sum[...].astype(BF)
        return carry

    lax.fori_loop(0, 2, step, 0)
    for half in range(2):
        grad_proj[:, half * 384 : half * 384 + 128] = (
            query_t[half * 128 : half * 128 + 128, :].T * SCALE
        ).astype(BF)
    for copy in copies:
        copy.wait()
    wait_bytes(weight, sems.at[4])
    for c in range(3):
        cols = slice(c * 256, c * 256 + 256)
        part = nn(normed_t[...], grad_proj[:, cols]).astype(BF)
        staged[:, :, :, cols] = part.reshape(staged.shape[:3] + (256,))
    moves = [(half, 0, 384, staged.at[:, :, :, pl.ds(384 * half, 384)]) for half in range(2)]
    if extra:
        moves += [
            (half, -384, 384, staged.at[:, :, :, pl.ds(768 + 384 * half, 384)]) for half in range(2)
        ]
    start_all(piece_copies(out_piece, me, outs, moves, sems.at[0], True))
    if final:
        sums[...] = jnp.zeros_like(sums)

    total_copies = []
    for c in range(3):
        cols = slice(c * 256, c * 256 + 256)
        value = nt(grad_proj[...], flat(weight[...])[cols])
        if not extra:
            value = value + total[:, cols]
        total[:, cols] = value
        total_copies.append(
            pltpu.make_async_copy(
                total.at[:, pl.ds(c * 256, 256)], grad_normed.at[:, pl.ds(c * 256, 256)], sems.at[2]
            )
        )
        total_copies[-1].start()
    if final:

        def sum_step(r, carry):
            at = pl.ds(pl.multiple_of(r * QB, QB), QB)
            value = total[at, :]
            hat, _ = norm_parts(refs[11][at, :].astype(F32))
            sums[0:1, :] += jnp.sum(value * hat, axis=0, keepdims=True)
            sums[1:2, :] += jnp.sum(value, axis=0, keepdims=True)
            return carry

        lax.fori_loop(0, length // QB, sum_step, 0)
    wait_bytes(staged, sems.at[0])
    wait_bytes(total, sems.at[2])


def attend_back(
    piece,
    out_piece,
    me,
    normed_t,
    proj,
    att,
    grad_att,
    lse,
    seg_col,
    seg_row,
    slabs,
    branch_t,
    attended,
    held,
    tokens,
    onto,
):
    depth, length = normed_t.shape
    extra = len(attended)
    final = tokens is not None
    columns = 1536 if extra else 768
    ins = [me] + in_hbm([normed_t, proj, att, grad_att, lse]) + [seg_col, seg_row] + in_hbm(slabs)
    specs = [smem_spec(), any_spec()] + [vmem_spec()] * 6 + [any_spec()] * len(slabs)
    if extra:
        ins += in_vmem([branch_t]) + in_hbm(attended)
        specs += [vmem_spec()] * (1 + extra)
    else:
        ins += in_hbm([held])
        specs += [any_spec()]
    if final:
        ins += in_hbm([tokens])
        specs += [any_spec()]
    outs = [pltpu.HBM((length, depth), F32)] + [SDS(out_piece.shape, BF)] * 2
    scratch = [
        pltpu.VMEM((2, QB, QB), F32),
        pltpu.VMEM((8, length), F32),
        pltpu.VMEM((256, length), BF),
        pltpu.VMEM((256, length), F32),
        pltpu.VMEM((4, length, 128), BF),
        pltpu.VMEM((4, length, 128), BF),
        pltpu.VMEM(out_piece.rows.shape + (columns,), BF),
        pltpu.VMEM((depth, length), BF),
        pltpu.VMEM((length, depth), F32),
        pltpu.VMEM(piece.rows.shape + (768,), BF),
        pltpu.SemaphoreType.DMA((5,)),
    ]
    if final:
        outs.append(SDS((8, depth), F32))
        scratch.append(pltpu.VMEM((length, depth), BF))
    got = pl.pallas_call(
        functools.partial(attend_back_body, piece, out_piece, extra, len(onto), final),
        in_specs=specs + [any_spec()] * len(onto),
        out_specs=[any_spec()] * 3 + ([vmem_spec()] if final else []),
        out_shape=outs,
        input_output_aliases={len(ins) + k: 1 + k for k in range(len(onto))},
        scratch_shapes=[
            pltpu.VMEM((length, 768), BF),
            pltpu.VMEM((length, 128), F32),
            pltpu.VMEM((length, 128), F32),
        ]
        + scratch,
        compiler_params=params(40),
        cost_estimate=cost(12, 8),
        name="attend_back",
    )(*ins, *onto)
    return got[0], got[1:3], got[3] if final else None


def norm_back_body(
    start, core, tokens, grad_normed, grad_middle, gain, held, other, high, low, own, sem
):
    length = high.shape[0] // 2
    r = pl.program_id(0)
    hat, root = norm_parts(tokens[...].astype(F32))
    value = grad_middle[...] + norm_pull(grad_normed[...], hat, root, gain[...])
    top = value.astype(BF)
    rest = (value - top.astype(F32)).astype(BF)
    for base in (0, length):
        at = pl.ds(pl.multiple_of(base + r * QB, QB), QB)
        high[at, :] = top
        low[at, :] = rest

    @pl.when(r == pl.num_programs(0) - 1)
    def _():
        count = own.shape[0] // QB
        for k in range(count):
            own[k * QB : k * QB + QB, :] = turned([high, low], start[0], k)
        copy = pltpu.make_async_copy(own, held.at[core[0]], sem)
        copy.start()
        for k in range(count):
            other[k * QB : k * QB + QB, :] = turned([high, low], start[0], k + count)
        copy.wait()


def norm_back(start, core, tokens, grad_normed, grad_middle, gain):
    length, depth = tokens.shape
    half = (length // 2, depth)
    return pl.pallas_call(
        norm_back_body,
        grid=(length // QB,),
        in_specs=[smem_spec()] * 2 + [row_spec(depth, QB)] * 3 + [whole_spec((1, depth))],
        out_specs=[any_spec(), whole_spec(half)],
        out_shape=[pltpu.HBM((2,) + half, F32), SDS(half, F32)],
        scratch_shapes=[
            pltpu.VMEM((2 * length, depth), BF),
            pltpu.VMEM((2 * length, depth), BF),
            pltpu.VMEM(half, F32),
            pltpu.SemaphoreType.DMA,
        ],
        compiler_params=params(24),
        cost_estimate=cost(4, 16),
        name="norm_back",
    )(start, core, *in_hbm([tokens, grad_normed, grad_middle]), gain)


def split_far_body(counts, me, *refs):
    keep, send = refs[-2:]
    far = me[0] // 4
    begin = 0
    for count in counts:
        pieces, refs = refs[:count], refs[count:]
        cols = pl.ds(begin, pieces[0].shape[-1])
        begin += pieces[0].shape[-1]
        for k, out in enumerate((keep, send)):
            for slot in range(2):
                at = lax.bitwise_xor(far, k + 2 * slot)
                total = pieces[0][at].astype(F32)
                for piece in pieces[1:]:
                    total = total + piece[at].astype(F32)
                out[slot, :, cols] = total.astype(BF)


def split_far(me, groups):
    width, specs = 0, []
    for pieces in groups:
        far, block, columns = pieces[0].shape[-3:]
        width += columns
        for piece in pieces:
            if piece.ndim == 4:
                specs.append(pl.BlockSpec((None, far, block, columns), lambda i: (0, 0, 0, 0)))
            else:
                specs.append(whole_spec(piece.shape))
    return pl.pallas_call(
        functools.partial(split_far_body, [len(pieces) for pieces in groups]),
        grid=(1,),
        in_specs=[smem_spec()] + specs,
        out_specs=[whole_spec((2, block, width))] * 2,
        out_shape=[SDS((2, block, width), BF)] * 2,
        compiler_params=params(16),
        cost_estimate=cost(1, 2),
        name="split_far",
    )(me, *[piece for pieces in groups for piece in pieces])


def put_sums(ref, base, total):
    high = total.astype(BF)
    ref[base : base + 4, :] = high
    ref[base + 4 : base + 8, :] = (total - high.astype(F32)).astype(BF)
    ref[base + 8 : base + 16, :] = jnp.zeros((8, total.shape[1]), BF)


def get_sums(ref, base):
    return ref[base : base + 4, :].astype(F32) + ref[base + 4 : base + 8, :].astype(F32)


def last_join_body(own, other, own_last, other_last, sums, sums_away, keep, send):
    total = sums[...] + sums_away[...]
    rows = keep.shape[0] // 2
    width = own.shape[-1]
    for k in range(4):
        out = keep if k < 2 else send
        at = slice((k % 2) * rows, (k % 2 + 1) * rows)
        value = (own[k].astype(F32) + other[k].astype(F32)).astype(BF)
        out[at, :width] = value.reshape(rows, -1)
        value = (own_last[k].astype(F32) + other_last[k].astype(F32)).astype(BF)
        out[at, width:] = value.reshape(rows, -1)
    put_sums(send, 2 * rows, total)


def last_half_body(keep, send, near, rest, send_next):
    rows = rest.shape[0]
    value = keep[:rows, :].astype(F32) + near[:rows, :].astype(F32)
    rest[...] = value.astype(BF)
    value = keep[rows:, :].astype(F32) + near[rows : 2 * rows, :].astype(F32)
    send_next[:rows, :] = value.astype(BF)
    send_next[rows : rows + 16, :] = send[2 * rows :, :]
    send_next[rows + 16 :, :] = near[2 * rows :, :]


def last_split_body(flip, me, rest, send, away, keep, out_send):
    far = me[0] // 4
    rows = rest.shape[0]
    block = rows // 4
    for k, out in enumerate((keep, out_send)):
        for slot in range(2):
            at = pl.ds(pl.multiple_of(lax.bitwise_xor(far, k + 2 * slot) * block, 16), block)
            total = rest[at, :].astype(F32) + away[at, :].astype(F32)
            out[slot * block : (slot + 1) * block, :] = total.astype(BF)
    first, second = get_sums(send, rows + 16), get_sums(away, rows)
    swapped = lax.bitwise_xor(me[1], flip) == 1
    one, two = jnp.where(swapped, second, first), jnp.where(swapped, first, second)
    total = (get_sums(send, rows) + one) + (two + get_sums(away, rows + 16))
    put_sums(keep, 2 * block, total)
    put_sums(out_send, 2 * block, total)


def last_middle_body(keep, near, rest, send):
    block = (keep.shape[0] - 16) // 2
    value = keep[:block, :].astype(F32) + near[:block, :].astype(F32)
    rest[:block, :] = value.astype(BF)
    value = keep[block : 2 * block, :].astype(F32) + near[block : 2 * block, :].astype(F32)
    send[:block, :] = value.astype(BF)
    total = get_sums(keep, 2 * block) + get_sums(near, 2 * block)
    put_sums(rest, block, total)
    put_sums(send, block, total)


def last_sum_body(rest, away, first, grad_qkv, sums):
    block = rest.shape[0] - 16
    value = rest[:block, :].astype(F32) + away[:block, :].astype(F32)
    parts = [first[:, 384:], value[:, :384], value[:, 384:]]
    for which in range(3):
        cols = slice(which * 128, which * 128 + 128)
        grad_qkv[which] = jnp.concatenate([part[:, cols] for part in parts], 1)
    sums[...] = get_sums(rest, block) + get_sums(away, block)


def pack_body(part, out, up, down, packed):
    width = out.shape[1]
    packed[:, :width] = out[...]
    for s in range(up.shape[1] // part):
        cols = slice(s * part, (s + 1) * part)
        packed[:, width + 2 * s * part : width + (2 * s + 1) * part] = up[:, cols]
        packed[:, width + (2 * s + 1) * part : width + (2 * s + 2) * part] = down[:, cols]


def small_call(body, name, outs, scalars, values):
    return pl.pallas_call(
        body,
        in_specs=[smem_spec()] * len(scalars) + [vmem_spec()] * len(values),
        out_specs=[vmem_spec()] * len(outs),
        out_shape=outs,
        compiler_params=params(16),
        cost_estimate=cost(1, 3),
        name=name,
    )(*scalars, *values)


def swap(value):
    return lax.ppermute(value, "mp", [(0, 1), (1, 0)])


def tie(*values):
    return lax.optimization_barrier(values)


def hop(value, mask, count):
    return lax.ppermute(value, "dp", [(i, i ^ mask) for i in range(count)])


def hops(value, masks, count):
    return [(value, functools.partial(hop, mask=m, count=count)) for m in masks]


def hop_apart(value, masks, count):
    pairs = [(2 * i + c, 2 * (i ^ masks[c]) + c) for i in range(count) for c in range(2)]
    return lax.ppermute(value, ("dp", "mp"), pairs)


def far_hops(rows, values):
    return [
        (v, functools.partial(hop, mask=rows.near * m, count=rows.dp_count))
        for m, v in zip(range(1, rows.far), values)
    ]


def swaps(values):
    return [(v, swap) for v in values]


def send_all(requests):
    return [send(value) for value, send in requests]


def low_sum(values):
    total = values[0].astype(F32)
    for value in values[1:]:
        total = total + value.astype(F32)
    return total


class Flow:
    def __init__(self, me):
        self.me = me
        self.active = []

    def add(self, transfer, name, results, seeds=()):
        self.active.append([transfer, list(seeds), name, results])

    def step(self, *pivots, gate=None):
        values = [v for item in self.active for v in item[1]]
        tied = list(tie(self.me, *pivots, *values))
        self.me = tied.pop(0)
        pivots, tied = tied[: len(pivots)], tied[len(pivots) :]
        going, self.active, requests = self.active, [], []
        for item in going:
            transfer, values, name, results = item
            got, tied = tied[: len(values)], tied[len(values) :]
            try:
                if callable(transfer):
                    item[0] = transfer(*got)
                    asked = next(item[0])
                else:
                    asked = transfer.send(got)
                self.active.append(item)
                requests.append(asked)
            except StopIteration as stop:
                results[name] = stop.value
        gates = gate() if gate else []
        operands = [operand for asked in requests for operand, _ in asked]
        tied = list(tie(self.me, *gates, *operands))
        self.me = tied[0]
        tied = tied[1 + len(gates) :]
        for item, asked in zip(self.active, requests):
            item[1] = [send(operand) for (_, send), operand in zip(asked, tied)]
            tied = tied[len(asked) :]
        return pivots


def add_low(a, b):
    return (a.astype(F32) + b.astype(F32)).astype(BF)


def on_device(
    tokens, segment, ln1_gain, ln1_bias, w_qkv, w_out, ln2_gain, ln2_bias, w_up, w_down, cotangent
):
    dp_count = lax.axis_size("dp")
    core = lax.axis_index("mp")
    me = jnp.stack([lax.axis_index("dp"), core]).astype(jnp.int32)
    here, depth = tokens.shape[2], tokens.shape[3]
    length = 2 * here
    rows = Rows(dp_count, depth)

    groups = w_qkv.shape[2] // 128
    part = 384
    subs = w_up.shape[1] // part
    cut = subs // 2
    qkv = [w_qkv[:, :, g * 128 : (g + 1) * 128].reshape(-1, part) for g in range(groups)]
    shards = {"q": jnp.concatenate(qkv, 1)}

    def pack(out, up, down):
        return small_call(
            functools.partial(pack_body, part),
            "pack",
            [SDS((up.shape[0], out.shape[0] + 2 * up.shape[1]), BF)],
            [],
            [out.T, up, down.T],
        )[0]

    seg = lax.dynamic_index_in_dim(segment[:, 0], core, 0, keepdims=False)
    run = length * 3 // 4
    begin = jnp.argmax(seg[: length - run + 1] == seg[run - 1 :]).astype(jnp.int32)
    start = ((begin - here * core) % length).reshape(1)
    back = (length - start) % length
    seg_tail = lax.dynamic_slice_in_dim(jnp.concatenate([seg, seg]), begin + run, length - run)
    seg_col = seg_tail.reshape(-1, 1)
    seg_row = seg_tail.reshape(1, -1)
    gain1, bias1, gain2, bias2 = (
        v.reshape(1, -1) for v in (ln1_gain, ln1_bias, ln2_gain, ln2_bias)
    )

    flow = Flow(me)
    core_place = core.astype(jnp.int32).reshape(1)
    token_halves = [tokens[:, 0], swap(tokens[:, 0])]
    cot_halves = [cotangent[:, 0], swap(cotangent[:, 0])]
    wide = 2 * part
    qkv_pieces = [Piece(rows, "slabs")] + [Piece(rows, "slabs", part * g) for g in range(groups - 1)]
    out_piece = Piece(rows, "slabs")
    feed_pieces = [Piece(rows, "slabs", part + wide * s) for s in range(cut)]
    feed_pieces += [Piece(rows, "slabs", wide * s) for s in range(subs - cut)]
    feed_outs = [
        Piece(rows, "stack", 0, wide, s // cut) for s in range(subs)
    ]
    qkv_outs = [Piece(rows, "stack", part, wide, 0)]
    qkv_outs += [Piece(rows, "stack", 0, part, 1)] * (groups - 1)
    far = lax.axis_index("dp") // rows.near

    def gather_whole(shard):
        return lax.all_gather(shard, "dp", axis=0, tiled=True).reshape(rows.shape + (-1,))

    def fetch_near(near):
        got = yield hops(near, MASKS[1:], dp_count)
        own = [near] + got
        return own + [swap(x) for x in own]

    def via(mask):
        return functools.partial(hop, mask=mask, count=dp_count)

    def fetch_wide(shard, away):
        near, both_ways = yield [(shard, via(4)), (away, via(4))]
        (a0,) = arrange(rows, flow.me, [shard, near, away, both_ways], [shard.shape[1]])
        a1, a2, b0, away = yield [(a0, via(1)), (a0, via(2))] + swaps([a0]) + [(shard_c, via(8))]
        a3, b1, b2, near, both_ways = yield (
            [(a1, via(2))] + swaps([a1, a2]) + [(shard_c, via(4)), (away, via(4))]
        )
        slabs["a"] = [a0, a1, a2, a3, b0, b1, b2, swap(a3)]
        (c0,) = arrange(rows, flow.me, [shard_c, near, away, both_ways], [shard_c.shape[1]])
        (d0,) = yield swaps([c0])
        c1, c2 = yield [(c0, via(1)), (c0, via(2))]
        c3, d1, d2 = yield [(c2, via(1))] + swaps([c1, c2])
        return [c0, c1, c2, c3, d0, d1, d2, swap(c3)]

    def whole(shard):
        own = gather_whole(shard)
        return [own, swap(own)]

    def apart(flip):
        masks = (2, 1) if flip else (1, 2)
        return functools.partial(hop_apart, masks=masks, count=dp_count)

    def halve(flip, hurry, pause, own, other):
        if hurry:
            other = swap(other)
        else:
            (other,) = yield swaps([other])
        if pause:
            yield []
        keep, send = (low_sum([own[k : k + 2], other[k : k + 2]]).astype(BF) for k in (0, 2))
        (near,) = yield [(send, apart(flip))]
        (away,) = yield [(low_sum([keep[1], near[1]]).astype(BF), apart(1 - flip))]
        return [keep, near, away]

    def reduce_far(groups):
        keep, send = split_far(flow.me, groups)
        (near,) = yield [(send, via(4))]
        (away,) = yield [(low_sum([keep[1], near[1]]).astype(BF), via(8))]
        return low_sum([keep[0], near[0], away])

    def reduce_all(flip, own, other):
        group = yield from halve(flip, True, False, own, other)
        return (yield from reduce_far([sums_of[s] for s in range(subs - 1)] + [group]))

    def reduce_last(flip, own, own_last, other_last, sums):
        other_last, sums_away = swap(other_last), swap(sums)
        rows_here = rows.far * rows.block
        keep, send = small_call(
            last_join_body,
            "last_join",
            [SDS((2 * rows_here, wide), BF), SDS((2 * rows_here + 16, wide), BF)],
            [],
            [own, sums_of["other"], own_last, other_last, sums, sums_away],
        )
        (near,) = yield [(send, apart(flip))]
        return [keep, send, near]

    def exchange(value):
        (got,) = yield swaps([value])
        return got

    def reduce_one(flip, own, other):
        group = yield from halve(flip, False, False, own, other)
        return (yield from reduce_far([group]))

    def plain(own, other):
        value = low_sum([own, swap(other)]).astype(BF).reshape(depth, -1)
        return lax.psum_scatter(value, "dp", scatter_dimension=0, tiled=True).astype(F32)

    def run(transfer):
        requests = next(transfer)
        while True:
            try:
                requests = transfer.send(send_all(requests))
            except StopIteration as stop:
                return stop.value

    slabs, forward = {}, []

    def project(g):
        name = "q0" if g == 0 else "q1"
        forward.append(
            project_attend(qkv_pieces[g], flow.me, normed, seg_col, seg_row, slabs[name])
        )

    if rows.split:
        shard_q = shards["q"]
        got = send_all(far_hops(rows, [shard_q] * (rows.far - 1)))
        prepared = prepare(start, core_place, *token_halves, gain1, bias1)
        tied = tie(*got, *prepared, w_out, w_up, w_down)
        got, prepared = tied[:3], tied[3:6]
        shard_a = pack(*tied[6:])
        near_q0, near_q1 = arrange(rows, me, [shard_q] + list(got), [part, wide])
        own = [near_q0] + [hop(near_q0, m, dp_count) for m in MASKS[1:]]
        first_cols = part + wide * cut
        shard_c, shard_a = shard_a[:, first_cols:], shard_a[:, :first_cols]
        away_a = hop(shard_a, 8, dp_count)
        start_cot, _ = tie(start, near_q0)
        turned_cot = turn(start_cot, core_place, *cot_halves)
        tied = tie(*own, *turned_cot)
        own, turned_cot = tied[:4], tied[4:]
        slabs["q0"] = list(own) + [swap(v) for v in own]
        flow.add(fetch_near, "q1", slabs, [near_q1])
        flow.add(fetch_wide, "c", slabs, [shard_a, away_a])
        flow.step(own[3])
    else:
        shard_a = pack(w_out, w_up, w_down)
        for name, shard in (
            ("q0", shards["q"][:, :part]),
            ("q1", shards["q"][:, part:]),
            ("a", shard_a[:, : part + wide * cut]),
            ("c", shard_a[:, part + wide * cut :]),
        ):
            slabs[name] = whole(shard)
        prepared = prepare(start, core_place, *token_halves, gain1, bias1)
        turned_cot = turn(start, core_place, *cot_halves)
    x, normed, normed_t = prepared
    cot, cot_t = turned_cot
    for g in range(groups):
        project(g)
        flow.step(forward[g][2])
    atts = [f[1] for f in forward]
    middle, normed_ffn, normed_ffn_t = out_norm(
        out_piece, flow.me, x, gain2, bias2, atts, slabs["a"]
    )
    flow.step(normed_ffn)

    held = None
    sums_of = {}
    onto = []
    feed_names = ["a"] * cut + ["c"] * (subs - cut)
    for s in range(subs):
        final = s == subs - 1
        grads, held = feed_forward(
            feed_pieces[s],
            feed_outs[s],
            flow.me,
            normed_ffn,
            normed_ffn_t,
            cot,
            cot_t,
            held,
            slabs[feed_names[s]],
            [],
            (out_piece, slabs["a"], middle, gain2, groups) if final else None,
        )
        flip = s // cut
        if not rows.split:
            sums_of[s] = plain(*grads)
        elif final:
            flow.add(functools.partial(reduce_all, flip), "feed", sums_of, grads)
        else:
            flow.add(functools.partial(halve, flip, False, s == 0), s, sums_of, grads)
        if s == 1 and rows.split:
            flow.step(held[1], gate=lambda: slabs["c"][-1:])
        elif not final:
            flow.step(held[1])
    mixed, grad_middle, branch_t, sums2, *grad_atts = held
    flow.step(sums2)
    grad_projs = []
    onto = []

    held = None
    qkv_slabs = [slabs["q0"]] + [slabs["q1"]] * (groups - 1)
    for g in range(groups):
        proj, att, lse = forward[g]
        held, grads, sums1 = attend_back(
            qkv_pieces[g],
            qkv_outs[g],
            flow.me,
            normed_t,
            proj,
            att,
            grad_atts[g],
            lse,
            seg_col,
            seg_row,
            qkv_slabs[g],
            branch_t,
            atts if g == 0 else [],
            held,
            x if g == groups - 1 else None,
            onto,
        )
        if g == 0 and rows.split:
            flow.add(functools.partial(reduce_one, 0), "first", sums_of, grads)
        elif g == 0:
            sums_of["first"] = plain(*grads)
        elif g < groups - 1 and rows.split:
            flow.add(exchange, "other", sums_of, grads[1:])
            own_early = grads[0]
        elif not rows.split:
            sums_of[("last", g)] = plain(*grads)
        if g < groups - 1:
            flow.step(held)
    sums = jnp.concatenate([sums1[:2], sums2[:2]], 0)
    if rows.split:
        flow.add(
            functools.partial(reduce_last, 1), "last", sums_of, [own_early, *grads, sums]
        )
        (held,) = flow.step(held)
    start_late, _ = tie(back, flow.me)
    tokens_held, tokens_other = norm_back(start_late, core_place, x, held, grad_middle, gain1)
    mixed, tokens_other = tie(mixed, tokens_other)
    mixed_held, mixed_other = turn_back(back, core_place, mixed)
    mixed_got = swap(mixed_other)
    tokens_held, tokens_other = flow.step(tokens_held, tokens_other)
    if rows.split:
        block = rows.block
        keep, send, near = sums_of["last"]
        rows_here = rows.far * block
        rest, send = small_call(
            last_half_body,
            "last_half",
            [SDS((rows_here, wide), BF), SDS((rows_here + 32, wide), BF)],
            [],
            [keep, send, near],
        )
        away = apart(0)(send)
        keep, send = small_call(
            functools.partial(last_split_body, 1),
            "last_split",
            [SDS((2 * block + 16, wide), BF)] * 2,
            [flow.me],
            [rest, send, away],
        )
        flow.step(gate=lambda: [send])
        near = hop(send, 4, dp_count)
        rest, send = small_call(
            last_middle_body, "last_middle", [SDS((block + 16, wide), BF)] * 2, [], [keep, near]
        )
        rest, mixed_got, feed_sum = tie(rest, mixed_got, sums_of["feed"])
        away = hop(send, 8, dp_count)
        while flow.active:
            flow.step()
        grad_qkv, norm_sums = small_call(
            last_sum_body,
            "last_sum",
            [SDS((3, block, part), F32), SDS((4, depth), F32)],
            [],
            [rest, away, sums_of["first"]],
        )
        grad_qkv = grad_qkv.transpose(1, 0, 2)
        grad_out = sums_of["first"][:, :part].T
        feed_sums = [feed_sum]
    else:
        early = sums_of["first"]
        parts = [early[:, part:]] + [sums_of[("last", g)] for g in range(1, groups)]
        grad_qkv = jnp.concatenate([r.reshape(-1, 3, 128) for r in parts], 2)
        grad_out = early[:, :part].T
        feed_sums = [sums_of[s] for s in range(subs)]
        norm_sums = jnp.sum(lax.all_gather(sums + swap(sums), "dp", axis=0), 0)
    feed_sum = jnp.concatenate(feed_sums, 1) if len(feed_sums) > 1 else feed_sums[0]
    feed_list = [feed_sum[:, wide * s : wide * (s + 1)] for s in range(subs)]

    return (
        place(core_place, mixed_held, mixed_got)[:, None],
        place(core_place, tokens_held, swap(tokens_other))[:, None],
        norm_sums[0],
        norm_sums[1],
        grad_qkv,
        grad_out,
        norm_sums[2],
        norm_sums[3],
        jnp.concatenate([r[:, :part] for r in feed_list], 1),
        jnp.concatenate([r[:, part:] for r in feed_list], 1).T,
    )


def solution(mesh):
    in_specs = (
        P(None, "dp", "mp", None),
        P(None, "dp", None),
        P(),
        P(),
        P("dp", None, "mp"),
        P("mp", "dp"),
        P(),
        P(),
        P("dp", "mp"),
        P("mp", "dp"),
        P(None, "dp", "mp", None),
    )
    out_specs = (
        P(None, "dp", "mp", None),
        P(None, "dp", "mp", None),
        P(),
        P(),
        P("dp", None, "mp"),
        P("mp", "dp"),
        P(),
        P(),
        P("dp", "mp"),
        P("mp", "dp"),
    )
    return jax.shard_map(
        on_device, mesh=mesh, in_specs=in_specs, out_specs=out_specs, check_vma=False
    )
```
